32 devices in a mesh: dp: 8 (over z, y), tensor: 4 (over x, core).
Axes of the slice: x: 2, y: 2, z: 4, core: 2. Of those that a mesh axis runs over, the one named last changes fastest.
Arguments:
- hidden_in: bfloat16 [8192, 1536], P(('dp', 'tensor')), may hold values from -6 to 6
- context: bfloat16 [8, 512, 1536], P('dp', 'tensor'), may hold values from -6 to 6
- time_emb: float32 [8, 6, 1536], P('dp'), may hold values from -3 to 3
- text_lengths: int32 [8], P('dp'), may hold values from 385 to 512, as said below
- positions: int32 [3, 8192], P(None, 'dp'), may hold values from 0 to 31
- modulation: float32 [6, 1536], P(None, 'dp'), may hold values from -3 to 3
- self_query: float32 [1536, 1536], P('dp', 'tensor'), may hold values from -0.15625 to 0.15625
- self_key: float32 [1536, 1536], P('dp', 'tensor'), may hold values from -0.15625 to 0.15625
- self_value: float32 [1536, 1536], P('dp', 'tensor'), may hold values from -0.15625 to 0.15625
- self_output: float32 [1536, 1536], P('tensor', 'dp'), may hold values from -0.625 to 0.625
- self_query_gain: float32 [12, 128], P('tensor', 'dp'), may hold values from 1.3 to 1.7
- self_key_gain: float32 [12, 128], P('tensor', 'dp'), may hold values from 1.3 to 1.7
- cross_query: float32 [1536, 1536], P('dp', 'tensor'), may hold values from -0.15625 to 0.15625
- cross_key: float32 [1536, 1536], P('dp', 'tensor'), may hold values from -0.15625 to 0.15625
- cross_value: float32 [1536, 1536], P('dp', 'tensor'), may hold values from -0.15625 to 0.15625
- cross_output: float32 [1536, 1536], P('tensor', 'dp'), may hold values from -2 to 2
- cross_query_gain: float32 [12, 128], P('tensor', 'dp'), may hold values from 0.25 to 1.75
- cross_key_gain: float32 [12, 128], P('tensor', 'dp'), may hold values from 0.25 to 1.75
- norm_weight: float32 [1536], P('dp'), may hold values from 0.25 to 1.75
- norm_bias: float32 [1536], P('dp'), may hold values from -3 to 3
- ffn_up: float32 [1536, 8960], P('dp', 'tensor'), may hold values from -0.15625 to 0.15625
- ffn_down: float32 [8960, 1536], P('tensor', 'dp'), may hold values from -0.1875 to 0.1875
- out_cotangent: bfloat16 [8192, 1536], P(('dp', 'tensor')), may hold values from -6 to 6
Outputs:
- block_out: bfloat16 [8192, 1536], P(('dp', 'tensor'))
- hidden_grad: bfloat16 [8192, 1536], P(('dp', 'tensor'))
- context_grad: bfloat16 [8, 512, 1536], P('dp', 'tensor')
- time_grad: float32 [8, 6, 1536], P('dp')
- modulation_grad: float32 [6, 1536], P(None, 'dp')
- self_query_grad: float32 [1536, 1536], P('dp', 'tensor')
- self_key_grad: float32 [1536, 1536], P('dp', 'tensor')
- self_value_grad: float32 [1536, 1536], P('dp', 'tensor')
- self_output_grad: float32 [1536, 1536], P('tensor', 'dp')
- self_query_gain_grad: float32 [12, 128], P('tensor', 'dp')
- self_key_gain_grad: float32 [12, 128], P('tensor', 'dp')
- cross_query_grad: float32 [1536, 1536], P('dp', 'tensor')
- cross_key_grad: float32 [1536, 1536], P('dp', 'tensor')
- cross_value_grad: float32 [1536, 1536], P('dp', 'tensor')
- cross_output_grad: float32 [1536, 1536], P('tensor', 'dp')
- cross_query_gain_grad: float32 [12, 128], P('tensor', 'dp')
- cross_key_gain_grad: float32 [12, 128], P('tensor', 'dp')
- norm_weight_grad: float32 [1536], P('dp')
- norm_bias_grad: float32 [1536], P('dp')
- ffn_up_grad: float32 [1536, 8960], P('dp', 'tensor')
- ffn_down_grad: float32 [8960, 1536], P('tensor', 'dp')
The draws below stay inside these ranges and needn't reach their ends.
Inputs may be any that keep to these rules, and one draw needn't show every extreme that they name: text_lengths[c] counts the live text rows of clip c; the rows from that index on are padding. Some clip uses all 512 rows.
All inputs are finite; a program needn't handle non-finite values.
Results may differ from the reference program's by a relative error of at most 0.03.
Values may be sent and summed in bfloat16 or wider, within the bound.
A program may use at most 192 MiB of HBM per device.

```python
import math
import jax
import jax.numpy as jnp
from jax import lax

D = 1536
HEADS = 12
HEAD = 128
FF = 8960
TEXT = 512
CLIP = 1024
CLIPS = 8
TOKENS = 8192
TEXT_DEV = 128


def draw_text_lengths(key, part):
    first_key = jax.random.fold_in(key, 11)
    second_key = jax.random.fold_in(key, 12)
    lengths = jax.random.randint(first_key, (CLIPS,), TEXT - TEXT_DEV + 1, TEXT + 1)
    chosen = jax.random.randint(second_key, (), 0, CLIPS)
    return jnp.where(jnp.arange(CLIPS) == chosen, TEXT, lengths).astype(jnp.int32)


def set_ends(array, rng, smallest, top_value):
    shape = array.shape
    spot = [jax.random.randint(jax.random.fold_in(rng, axis), (), 0, shape[axis]) for axis in range(len(shape))]
    array = array.at[tuple(spot)].set(smallest)
    longest = shape.index(max(shape))
    spot[longest] = (spot[longest] + 1) % shape[longest]
    return array.at[tuple(spot)].set(top_value)


def steps_of(key, dims, shards, smallest, top_value):
    level, own = 1.0, jax.random.fold_in(key, 6)
    for dim, parts in shards:
        draws = jnp.exp(jax.random.uniform(jax.random.fold_in(own, dim), (parts,), jnp.float32, smallest / len(shards), top_value / len(shards)))
        level = level * jnp.repeat(draws, dims[dim] // parts).reshape([-1 if axis == dim else 1 for axis in range(len(dims))])
    return level


def scatter_about(rng, shape, scale, limit, shards=(), dtype=jnp.bfloat16):
    entries = scale * jax.random.normal(rng, shape, jnp.float32)
    if shards:
        entries = entries * steps_of(rng, shape, shards, -0.22, 0.18)
    return jnp.clip(entries, -limit, limit).astype(dtype)


def setup_inputs(seed: int = 0) -> dict:
    splits = jax.random.split(jax.random.key(seed), 24)
    hidden_in = scatter_about(splits[0], (TOKENS, D), 1.0, 6.0, ((0, 32),))
    context = scatter_about(splits[1], (CLIPS, TEXT, D), 1.0, 6.0, ((0, 8), (1, 4)))
    time_emb = scatter_about(splits[2], (CLIPS, 6, D), 0.5, 3.0, ((0, 8),), jnp.float32)
    text_lengths = draw_text_lengths(jax.random.fold_in(splits[23], 71), 0)
    positions = set_ends(jax.random.randint(splits[4], (3, TOKENS), 0, 32), jax.random.fold_in(splits[4], 1), 0, 31).astype(jnp.int32)
    modulation = scatter_about(splits[5], (6, D), 0.5, 3.0, ((1, 8),), jnp.float32)
    self_query = scatter_about(splits[6], (D, D), D ** -0.5, 0.15625, ((0, 8), (1, 4)), jnp.float32)
    self_key = scatter_about(splits[7], (D, D), D ** -0.5, 0.15625, ((0, 8), (1, 4)), jnp.float32)
    self_value = scatter_about(splits[8], (D, D), D ** -0.5, 0.15625, ((0, 8), (1, 4)), jnp.float32)
    self_output = scatter_about(splits[9], (D, D), (min(D, max(64 * D // CLIP, 1))) ** -0.5, 0.625, ((0, 4), (1, 8)), jnp.float32)
    self_query_gain = jnp.clip(1.3 + 0.4000001 * jax.random.uniform(splits[10], (HEADS, HEAD), jnp.float32) ** steps_of(splits[10], (HEADS, HEAD), ((0, 4), (1, 8)), -0.2, 0.2), 1.3, 1.7)
    self_key_gain = jnp.clip(1.3 + 0.4000001 * jax.random.uniform(splits[11], (HEADS, HEAD), jnp.float32) ** steps_of(splits[11], (HEADS, HEAD), ((0, 4), (1, 8)), -0.2, 0.2), 1.3, 1.7)
    cross_query = scatter_about(splits[12], (D, D), D ** -0.5, 0.15625, ((0, 8), (1, 4)), jnp.float32)
    cross_key = scatter_about(splits[13], (D, D), D ** -0.5, 0.15625, ((0, 8), (1, 4)), jnp.float32)
    cross_value = scatter_about(splits[14], (D, D), D ** -0.5, 0.15625, ((0, 8), (1, 4)), jnp.float32)
    cross_output = scatter_about(splits[15], (D, D), (max(3 * D // TEXT, 1)) ** -0.5, 2.0, ((0, 4), (1, 8)), jnp.float32)
    cross_query_gain = jnp.clip(1.0 + 0.15 * jax.random.normal(splits[16], (HEADS, HEAD), jnp.float32), 0.25, 1.75)
    cross_key_gain = jnp.clip(1.0 + 0.15 * jax.random.normal(splits[17], (HEADS, HEAD), jnp.float32), 0.25, 1.75)
    norm_weight = jnp.clip(1.0 + 0.15 * jax.random.normal(splits[18], (D,), jnp.float32), 0.25, 1.75)
    norm_bias = scatter_about(splits[19], (D,), 0.5, 3.0, ((0, 8),), jnp.float32)
    ffn_up = scatter_about(splits[20], (D, FF), D ** -0.5, 0.15625, ((0, 8), (1, 4)), jnp.float32)
    ffn_down = scatter_about(splits[21], (FF, D), (max(FF // 8, 1)) ** -0.5, 0.1875, ((0, 4), (1, 8)), jnp.float32)
    out_cotangent = scatter_about(splits[22], (TOKENS, D), 1.0, 6.0, ((0, 32),))
    return dict(hidden_in=hidden_in, context=context, time_emb=time_emb, text_lengths=text_lengths, positions=positions, modulation=modulation, self_query=self_query, self_key=self_key, self_value=self_value, self_output=self_output, self_query_gain=self_query_gain, self_key_gain=self_key_gain, cross_query=cross_query, cross_key=cross_key, cross_value=cross_value, cross_output=cross_output, cross_query_gain=cross_query_gain, cross_key_gain=cross_key_gain, norm_weight=norm_weight, norm_bias=norm_bias, ffn_up=ffn_up, ffn_down=ffn_down, out_cotangent=out_cotangent)


epsilon = 1e-06

@jax.custom_vjp
def low(v):
    return lax.optimization_barrier(v.astype(jnp.bfloat16)).astype(jnp.float32)

@jax.custom_vjp
def low_back(v):
    return v

def low_keep(v):
    return (low(v), None)

def low_pass(kept, grad):
    return (grad,)

def back_keep(v):
    return (v, None)

def back_low(kept, grad):
    return (low(grad),)
low.defvjp(low_keep, low_pass)
low_back.defvjp(back_keep, back_low)

def layer_norm(values):
    center = values - lax.optimization_barrier(jnp.mean(values, axis=-1, keepdims=True))
    return center * lax.rsqrt(lax.optimization_barrier(jnp.mean(center * center, axis=-1, keepdims=True)) + epsilon)

def root_norm(values, gain_row):
    return values * lax.rsqrt(lax.optimization_barrier(jnp.mean(values * values, axis=-1, keepdims=True)) + epsilon) * gain_row

def rotary_tables(positions, head_dim):
    pair_count = head_dim // 2
    side_pairs = pair_count // 3
    frame_pairs = pair_count - 2 * side_pairs
    pair_index = jnp.arange(pair_count)
    frame_mask = pair_index < frame_pairs
    height_mask = (pair_index >= frame_pairs) & (pair_index < frame_pairs + side_pairs)
    within = jnp.where(frame_mask, pair_index, jnp.where(height_mask, pair_index - frame_pairs, pair_index - frame_pairs - side_pairs))
    extent = jnp.where(frame_mask, frame_pairs, side_pairs)
    frequency = jnp.power(10000.0, -within.astype(jnp.float32) / extent.astype(jnp.float32))
    coords = positions.astype(jnp.float32)
    coordinate = jnp.where(frame_mask[None, :], coords[0][:, None], jnp.where(height_mask[None, :], coords[1][:, None], coords[2][:, None]))
    angles = jnp.repeat(coordinate * frequency[None, :], 2, axis=1)
    parity = jnp.arange(head_dim) % 2
    sign_pattern = jnp.where(parity == 0, -1.0, 1.0)
    return (jnp.cos(angles), jnp.sin(angles) * sign_pattern)

def rotate(values, cosine, sine_signed):
    next_lane = jnp.roll(values, -1, axis=-1)
    last_lane = jnp.roll(values, 1, axis=-1)
    parity = jnp.arange(values.shape[-1]) % 2
    partner = jnp.where(parity == 0, next_lane, last_lane)
    return values * cosine[:, None, :] + partner * sine_signed[:, None, :]

def project(left_side, right_side):
    return jnp.dot(left_side, right_side, precision=lax.Precision.HIGHEST)

def attention(queries, key_rows, value_rows, key_bias):
    query_rows = queries.shape[0]
    block_size = min(512, query_rows)
    blocks = queries.reshape(query_rows // block_size, block_size, queries.shape[1], queries.shape[2])
    factor = 1.0 / math.sqrt(queries.shape[2])

    def one_block(query_block):
        scores = jnp.einsum('qhd,khd->hqk', query_block, key_rows, precision=lax.Precision.HIGHEST) * factor + key_bias
        scores = low_back(scores)
        probability = low(jax.nn.softmax(scores, axis=-1))
        return jnp.einsum('hqk,khd->qhd', probability, value_rows, precision=lax.Precision.HIGHEST)
    result = lax.map(jax.checkpoint(one_block), blocks)
    return result.reshape(queries.shape)

def clip_forward(hidden, text_tokens, time_rows, length, coords, params):
    modulation, self_query, self_key, self_value, self_output, self_query_gain, self_key_gain, cross_query, cross_key, cross_value, cross_output, cross_query_gain, cross_key_gain, norm_weight, norm_bias, ffn_up, ffn_down = [low(matrix) for matrix in params]
    head_count = self_query_gain.shape[0]
    head_dim = self_query_gain.shape[1]
    clip_rows = hidden.shape[0]
    text_count = text_tokens.shape[0]
    shifts = modulation + time_rows
    cosine, sine_signed = rotary_tables(coords, head_dim)
    self_in = low(layer_norm(hidden) * (1.0 + shifts[1]) + shifts[0])
    query_raw = low_back(project(self_in, self_query))
    key_raw = low_back(project(self_in, self_key))
    value_raw = low_back(project(self_in, self_value))
    query_rot = low(rotate(root_norm(query_raw, self_query_gain.reshape(-1)).reshape(clip_rows, head_count, head_dim), cosine, sine_signed))
    key_rotated = low(rotate(root_norm(key_raw, self_key_gain.reshape(-1)).reshape(clip_rows, head_count, head_dim), cosine, sine_signed))
    value_low = low(value_raw).reshape(clip_rows, head_count, head_dim)
    open_bias = jnp.zeros((clip_rows,), jnp.float32)
    attended = low(low_back(attention(query_rot, key_rotated, value_low, open_bias))).reshape(clip_rows, -1)
    self_branch = low_back(project(attended, self_output))
    after_self = hidden + self_branch * shifts[2]
    cross_in = low(layer_norm(after_self) * norm_weight + norm_bias)
    cross_query_raw = low_back(project(cross_in, cross_query))
    cross_key_raw = low_back(project(text_tokens, cross_key))
    cross_value_raw = low_back(project(text_tokens, cross_value))
    cross_query_low = low(root_norm(cross_query_raw, cross_query_gain.reshape(-1))).reshape(clip_rows, head_count, head_dim)
    cross_key_low = low(root_norm(cross_key_raw, cross_key_gain.reshape(-1))).reshape(text_count, head_count, head_dim)
    cross_value_low = low(cross_value_raw).reshape(text_count, head_count, head_dim)
    text_bias = jnp.where(jnp.arange(text_count) < length, 0.0, -1e+30)
    cross_attended = low(low_back(attention(cross_query_low, cross_key_low, cross_value_low, text_bias))).reshape(clip_rows, -1)
    cross_branch = low_back(project(cross_attended, cross_output))
    after_cross = after_self + cross_branch
    ffn_in = low(layer_norm(after_cross) * (1.0 + shifts[4]) + shifts[3])
    hidden_pre = low_back(project(ffn_in, ffn_up))
    activated = low(jax.nn.gelu(hidden_pre, approximate=True))
    ffn_branch = low_back(project(activated, ffn_down))
    return after_cross + ffn_branch * shifts[5]

def reference(hidden_in, context, time_emb, text_lengths, positions, modulation, self_query, self_key, self_value, self_output, self_query_gain, self_key_gain, cross_query, cross_key, cross_value, cross_output, cross_query_gain, cross_key_gain, norm_weight, norm_bias, ffn_up, ffn_down, out_cotangent):
    params = (modulation, self_query, self_key, self_value, self_output, self_query_gain, self_key_gain, cross_query, cross_key, cross_value, cross_output, cross_query_gain, cross_key_gain, norm_weight, norm_bias, ffn_up, ffn_down)
    hidden_clips = hidden_in.astype(jnp.float32).reshape(CLIPS, CLIP, D)
    text_clips = context.astype(jnp.float32)
    coord_clips = positions.reshape(3, CLIPS, CLIP).transpose(1, 0, 2)
    cotangent_clips = out_cotangent.astype(jnp.float32).reshape(CLIPS, CLIP, D)
    initial = jax.tree.map(jnp.zeros_like, params)

    def one_clip(running, inputs):
        hidden, text_tokens, time_rows, length, coords, cotangent = inputs

        def forward(hidden_arg, text_arg, time_arg, param_arg):
            return clip_forward(hidden_arg, text_arg, time_arg, length, coords, param_arg)
        output, backward = jax.vjp(forward, hidden, text_tokens, time_rows, params)
        grad_hidden, grad_text, grad_time, grad_params = backward(cotangent)
        running = jax.tree.map(lambda left_grad, right_grad: left_grad + right_grad, running, grad_params)
        return (running, (output.astype(jnp.bfloat16), grad_hidden.astype(jnp.bfloat16), grad_text.astype(jnp.bfloat16), grad_time))
    param_grads, outputs = lax.scan(one_clip, initial, (hidden_clips, text_clips, time_emb, text_lengths, coord_clips, cotangent_clips))
    block_out = outputs[0].reshape(TOKENS, D)
    hidden_grad = outputs[1].reshape(TOKENS, D)
    return (block_out, hidden_grad, outputs[2], outputs[3], param_grads[0], param_grads[1], param_grads[2], param_grads[3], param_grads[4], param_grads[5], param_grads[6], param_grads[7], param_grads[8], param_grads[9], param_grads[10], param_grads[11], param_grads[12], param_grads[13], param_grads[14], param_grads[15], param_grads[16])
```

```python
import math

import jax
import jax.numpy as jnp
from jax import lax
from jax.sharding import PartitionSpec as P

D = 1536
HEAD = 128
EPS = 1e-6
BF = jnp.bfloat16
F32 = jnp.float32


def dot(a, b):
    return jnp.dot(a, b, preferred_element_type=F32)


def dot_nt(a, b):
    return lax.dot_general(a, b, (((1,), (1,)), ((), ())), preferred_element_type=F32)


def dot_tn(a, b):
    return lax.dot_general(a, b, (((0,), (0,)), ((), ())), preferred_element_type=F32)


def rotary_tables(positions, head_dim):
    pair_count = head_dim // 2
    side_pairs = pair_count // 3
    frame_pairs = pair_count - 2 * side_pairs
    pair_index = jnp.arange(pair_count)
    frame_mask = pair_index < frame_pairs
    height_mask = (pair_index >= frame_pairs) & (pair_index < frame_pairs + side_pairs)
    within = jnp.where(
        frame_mask,
        pair_index,
        jnp.where(height_mask, pair_index - frame_pairs, pair_index - frame_pairs - side_pairs),
    )
    extent = jnp.where(frame_mask, frame_pairs, side_pairs)
    frequency = jnp.power(10000.0, -within.astype(F32) / extent.astype(F32))
    coords = positions.astype(F32)
    coordinate = jnp.where(
        frame_mask[None, :],
        coords[0][:, None],
        jnp.where(height_mask[None, :], coords[1][:, None], coords[2][:, None]),
    )
    angles = jnp.repeat(coordinate * frequency[None, :], 2, axis=1)
    parity = jnp.arange(head_dim) % 2
    sign_pattern = jnp.where(parity == 0, -1.0, 1.0)
    return (jnp.cos(angles), jnp.sin(angles) * sign_pattern)


def rotate(values, cosine, sine_signed):
    next_lane = jnp.roll(values, -1, axis=-1)
    last_lane = jnp.roll(values, 1, axis=-1)
    parity = jnp.arange(values.shape[-1]) % 2
    partner = jnp.where(parity == 0, next_lane, last_lane)
    return values * cosine[:, None, :] + partner * sine_signed[:, None, :]


def norm_stats(v):
    center = v - jnp.mean(v, axis=-1, keepdims=True)
    r = lax.rsqrt(jnp.mean(center * center, axis=-1, keepdims=True) + EPS)
    return center * r, r


def norm_back(n, r, da, m):
    dn = da * m
    return r * (
        dn - jnp.mean(dn, axis=-1, keepdims=True) - n * jnp.mean(dn * n, axis=-1, keepdims=True)
    )


def attend_forward(q, k, v, bias, factor):
    s = jnp.einsum("qhd,khd->hqk", q, k, preferred_element_type=F32) * factor + bias
    top = jnp.max(s, axis=-1, keepdims=True)
    e = jnp.exp(s - top)
    total = jnp.sum(e, axis=-1, keepdims=True)
    p = (e / total).astype(BF)
    o = jnp.einsum("hqk,khd->qhd", p, v, preferred_element_type=F32)
    return o.astype(BF).reshape(q.shape[0], -1), top + jnp.log(total)


def attend_backward(q, k, v, bias, lse, do, factor):
    s = jnp.einsum("qhd,khd->hqk", q, k, preferred_element_type=F32) * factor + bias
    p = jnp.exp(s - lse)
    dp = jnp.einsum("qhd,khd->hqk", do, v, preferred_element_type=F32)
    ds = (p * (dp - jnp.sum(p * dp, axis=-1, keepdims=True))).astype(BF)
    dq = jnp.einsum("hqk,khd->qhd", ds, k, preferred_element_type=F32) * factor
    dk = jnp.einsum("hqk,qhd->khd", ds, q, preferred_element_type=F32) * factor
    dv = jnp.einsum("hqk,qhd->khd", p.astype(BF), do, preferred_element_type=F32)
    return (
        dq.reshape(q.shape[0], -1),
        dk.reshape(k.shape[0], -1),
        dv.reshape(k.shape[0], -1),
    )


def solution(mesh):
    n_dp = mesh.shape["dp"]
    n_major = n_dp // 2
    pair_perm = [(i, i ^ 1) for i in range(n_dp)]
    ring_perm = {
        t: [((((i // 2) + t) % n_major) * 2 + i % 2, i) for i in range(n_dp)]
        for t in range(1, n_major)
    }
    back_perm = {t: [(b, a) for a, b in ring_perm[t]] for t in ring_perm}
    core_perm = [(i, i ^ 1) for i in range(4)]
    x_perm = [(i, i ^ 2) for i in range(4)]

    def core_swap(v):
        return lax.ppermute(v, "tensor", core_perm)

    def x_swap(v):
        return lax.ppermute(v, "tensor", x_perm)

    def gather_dp(block):
        d = lax.axis_index("dp")
        major, minor = d // 2, d % 2
        out = jnp.zeros((n_dp,) + block.shape, block.dtype)
        for t in range(n_major):
            piece = block if t == 0 else lax.ppermute(block, "dp", ring_perm[t])
            other = lax.ppermute(piece, "dp", pair_perm)
            origin = 2 * ((major + t) % n_major)
            out = lax.dynamic_update_slice(out, piece[None], (origin + minor, 0, 0))
            out = lax.dynamic_update_slice(out, other[None], (origin + 1 - minor, 0, 0))
        return out

    def scatter_dp(full):
        d = lax.axis_index("dp")
        major, minor = d // 2, d % 2
        r, c = full.shape[1:]
        low = full.astype(BF).reshape(n_major, 2, r, c)
        theirs = lax.dynamic_slice_in_dim(low, 1 - minor, 1, axis=1)[:, 0]
        mine = lax.dynamic_slice_in_dim(low, minor, 1, axis=1)[:, 0]
        got = lax.ppermute(theirs, "dp", pair_perm)
        pair = (mine.astype(F32) + got.astype(F32)).astype(BF)
        total = lax.dynamic_slice_in_dim(pair, major, 1, axis=0)[0].astype(F32)
        for t in range(1, n_major):
            send = lax.dynamic_slice_in_dim(pair, (major + t) % n_major, 1, axis=0)[0]
            total = total + lax.ppermute(send, "dp", back_perm[t]).astype(F32)
        return total

    def sum_rows(theirs, mine):
        chip = (mine + core_swap(theirs.astype(BF)).astype(F32)).astype(BF)
        h = chip.shape[0] // 2
        r0 = x_swap(chip[h:])
        r1 = x_swap(chip[:h])
        return chip.astype(F32) + jnp.concatenate([r0, r1]).astype(F32)

    def sum_quarter(theirs, mine):
        chip = (mine + core_swap(theirs.astype(BF)).astype(F32)).astype(BF)
        h = chip.shape[0] // 2
        return chip[:h].astype(F32) + x_swap(chip[h:]).astype(F32)

    def sum_all(v):
        v = v + core_swap(v)
        return v + x_swap(v)

    def sum_vectors(v):
        h = v.shape[-1] // 2
        other = core_swap(v)
        v = v + jnp.concatenate([other[..., h:], other[..., :h]], -1)
        split = v.shape[:-1] + (2, 2, h // 2)
        return v + x_swap(v).reshape(split)[..., ::-1, :].reshape(v.shape)

    def rows_all(mine):
        return jnp.concatenate([mine, core_swap(mine)])

    def quarters(values, axis):
        t = lax.axis_index("tensor")
        step = values.shape[axis] // 4
        return jnp.concatenate(
            [
                lax.dynamic_slice_in_dim(values, (t ^ flip) * step, step, axis)
                for flip in (0, 2, 1, 3)
            ],
            axis,
        )

    def on_device(
        hidden_in, context, time_emb, text_lengths, positions, modulation,
        self_query, self_key, self_value, self_output, self_query_gain, self_key_gain,
        cross_query, cross_key, cross_value, cross_output, cross_query_gain, cross_key_gain,
        norm_weight, norm_bias, ffn_up, ffn_down, out_cotangent,
    ):
        factor = 1.0 / math.sqrt(HEAD)
        heads = self_query_gain.shape[0]
        clip_rows = positions.shape[1]
        half = clip_rows // 2
        quarter = clip_rows // 4
        wide = heads * HEAD
        r_dp = self_query.shape[0]
        hid = ffn_up.shape[1]

        gains = [self_query_gain, self_key_gain, cross_query_gain, cross_key_gain]
        small = jnp.concatenate(
            [modulation.reshape(-1), norm_weight, norm_bias] + [g.reshape(-1) for g in gains]
        ).astype(BF)
        pad = -small.shape[0] % 1024
        small_all = gather_dp(jnp.pad(small, (0, pad)).reshape(8, -1)).reshape(n_dp, -1).astype(F32)
        mods = small_all[:, : 6 * r_dp].reshape(n_dp, 6, r_dp).transpose(1, 0, 2).reshape(6, D)
        at = 6 * r_dp
        norm_gain = small_all[:, at : at + r_dp].reshape(D)
        norm_shift = small_all[:, at + r_dp : at + 2 * r_dp].reshape(D)
        at += 2 * r_dp
        g_cols = self_query_gain.shape[1]
        g_rows = []
        for i in range(4):
            g = small_all[:, at + i * heads * g_cols : at + (i + 1) * heads * g_cols]
            g_rows.append(g.reshape(n_dp, heads, g_cols).transpose(1, 0, 2).reshape(wide))
        sq_gain, sk_gain, cq_gain, ck_gain = g_rows
        shifts = mods + time_emb[0]

        w_qkv = gather_dp(
            jnp.concatenate([self_query, self_key, self_value], axis=1).astype(BF)
        ).reshape(D, 3 * wide)
        w_oT = gather_dp(self_output.T.astype(BF)).reshape(D, wide)
        w_cross = gather_dp(
            jnp.concatenate([cross_query, cross_key, cross_value, cross_output.T], axis=1).astype(BF)
        ).reshape(D, 4 * wide)
        w_cq, w_ckv, w_coT = w_cross[:, :wide], w_cross[:, wide : 3 * wide], w_cross[:, 3 * wide :]
        w_downT = gather_dp(ffn_down.T.astype(BF)).reshape(D, hid)
        w_up = gather_dp(ffn_up.astype(BF)).reshape(D, hid)

        res = jnp.concatenate([hidden_in, x_swap(hidden_in)]).astype(F32)
        g = jnp.concatenate([out_cotangent, x_swap(out_cotangent)]).astype(F32)
        ctx = context[0]
        ctx = rows_all(jnp.concatenate([ctx, x_swap(ctx)]))
        texts = ctx.shape[0]
        cosine, sine = rotary_tables(quarters(positions, 1), HEAD)
        text_bias = jnp.where(quarters(jnp.arange(texts), 0) < text_lengths[0], 0.0, -1e30)
        open_bias = jnp.zeros((clip_rows,), F32)

        def heads_of(v):
            return v.reshape(v.shape[0], heads, HEAD)

        n_self, r_self = norm_stats(res)
        self_rows = rows_all((n_self * (1.0 + shifts[1]) + shifts[0]).astype(BF))
        qkv = dot(self_rows, w_qkv)
        q_raw, k_raw, v_raw = qkv[:, :wide], qkv[:, wide : 2 * wide], qkv[:, 2 * wide :]
        sums = sum_vectors(jnp.stack([jnp.sum(q_raw * q_raw, 1), jnp.sum(k_raw * k_raw, 1)]))
        scales = lax.rsqrt(sums / D + EPS)
        q_s, k_s = scales[0][:, None], scales[1][:, None]
        q = rotate(heads_of(q_raw * q_s * sq_gain), cosine, sine).astype(BF)
        k = rotate(heads_of(k_raw * k_s * sk_gain), cosine, sine).astype(BF)
        v = heads_of(v_raw.astype(BF))
        attn, lse = attend_forward(q, k, v, open_bias, factor)
        branch = dot_nt(attn, w_oT)
        self_branch = sum_rows(branch[half:], branch[:half])
        after_self = res + self_branch * shifts[2]

        ckv = dot(ctx, w_ckv)
        ck_raw, cv_raw = ckv[:, :wide], ckv[:, wide:]
        n_cross, r_cross = norm_stats(after_self)
        cross_rows = rows_all((n_cross * norm_gain + norm_shift).astype(BF))
        cq_raw = dot(cross_rows, w_cq)
        ck_s = lax.rsqrt(sum_vectors(jnp.sum(ck_raw * ck_raw, 1)) / D + EPS)[:, None]
        cq_s = lax.rsqrt(sum_vectors(jnp.sum(cq_raw * cq_raw, 1)) / D + EPS)[:, None]
        cq = heads_of((cq_raw * cq_s * cq_gain).astype(BF))
        ck = heads_of((ck_raw * ck_s * ck_gain).astype(BF))
        cv = heads_of(cv_raw.astype(BF))
        cattn, clse = attend_forward(cq, ck, cv, text_bias, factor)
        cbranch = dot_nt(cattn, w_coT)
        after_cross = after_self + sum_rows(cbranch[half:], cbranch[:half])

        dffn = rows_all((g * shifts[5]).astype(BF))
        dact = dot(dffn, w_downT)
        n_ffn, r_ffn = norm_stats(after_cross)
        ffn_rows = rows_all((n_ffn * (1.0 + shifts[4]) + shifts[3]).astype(BF))
        pre = dot(ffn_rows, w_up)
        c0 = math.sqrt(2.0 / math.pi)
        th = jnp.tanh(c0 * (pre + 0.044715 * pre * pre * pre))
        act = (0.5 * pre * (1.0 + th)).astype(BF)
        slope = 0.5 * (1.0 + th) + 0.5 * pre * (1.0 - th * th) * c0 * (1.0 + 3 * 0.044715 * pre * pre)
        dpre = (dact * slope).astype(BF)
        dffn_part = dot_nt(dpre, w_up)
        dffn_in = sum_rows(dffn_part[half:], dffn_part[:half])
        g_c = g + norm_back(n_ffn, r_ffn, dffn_in, 1.0 + shifts[4])
        ffn_part = dot_nt(act, w_downT)
        ffn_branch = sum_quarter(ffn_part[half:], ffn_part[:half])
        block_out = (after_cross[:quarter] + ffn_branch * shifts[5]).astype(BF)
        downT_grad = scatter_dp(dot_tn(dffn, act).reshape(n_dp, r_dp, hid))
        up_grad = scatter_dp(dot_tn(ffn_rows, dpre).reshape(n_dp, r_dp, hid))

        dcross = rows_all(g_c.astype(BF))
        dcattn = dot(dcross, w_coT).astype(BF)
        dcq, dck, dcv = attend_backward(cq, ck, cv, text_bias, clse, heads_of(dcattn), factor)
        dots_q = sum_vectors(jnp.sum(cq_raw * cq_gain * dcq, 1))[:, None]
        dots_k = sum_vectors(jnp.sum(ck_raw * ck_gain * dck, 1))[:, None]
        dcq_raw = (cq_s * cq_gain * dcq - cq_raw * (cq_s**3 * dots_q / D)).astype(BF)
        dck_raw = (ck_s * ck_gain * dck - ck_raw * (ck_s**3 * dots_k / D)).astype(BF)
        cq_gain_grad = jnp.sum(cq_raw * cq_s * dcq, 0)
        ck_gain_grad = jnp.sum(ck_raw * ck_s * dck, 0)
        dckv = jnp.concatenate([dck_raw, dcv.astype(BF)], axis=1)
        dcross_part = dot_nt(dcq_raw, w_cq)
        dcross_in = sum_rows(dcross_part[half:], dcross_part[:half])
        g_s = g_c + norm_back(n_cross, r_cross, dcross_in, norm_gain)
        dctx = dot_nt(dckv, w_ckv)
        th2 = texts // 2
        context_grad = sum_quarter(dctx[th2:], dctx[:th2]).astype(BF)
        cross_grad = scatter_dp(
            jnp.concatenate(
                [dot_tn(cross_rows, dcq_raw), dot_tn(ctx, dckv), dot_tn(dcross, cattn)], axis=1
            ).reshape(n_dp, r_dp, 4 * wide)
        )

        dself = rows_all((g_s * shifts[2]).astype(BF))
        dattn = dot(dself, w_oT).astype(BF)
        oT_grad = scatter_dp(dot_tn(dself, attn).reshape(n_dp, r_dp, wide))
        dq, dk, dv = attend_backward(q, k, v, open_bias, lse, heads_of(dattn), factor)
        dq = rotate(heads_of(dq), cosine, -sine).reshape(clip_rows, wide)
        dk = rotate(heads_of(dk), cosine, -sine).reshape(clip_rows, wide)
        dots = sum_vectors(
            jnp.stack([jnp.sum(q_raw * sq_gain * dq, 1), jnp.sum(k_raw * sk_gain * dk, 1)])
        )
        dq_raw = (q_s * sq_gain * dq - q_raw * (q_s**3 * dots[0][:, None] / D)).astype(BF)
        dk_raw = (k_s * sk_gain * dk - k_raw * (k_s**3 * dots[1][:, None] / D)).astype(BF)
        sq_gain_grad = jnp.sum(q_raw * q_s * dq, 0)
        sk_gain_grad = jnp.sum(k_raw * k_s * dk, 0)
        dqkv = jnp.concatenate([dq_raw, dk_raw, dv.astype(BF)], axis=1)
        dself_part = dot_nt(dqkv, w_qkv)
        qkv_grad = scatter_dp(dot_tn(self_rows, dqkv).reshape(n_dp, r_dp, 3 * wide))
        dself_in = sum_quarter(dself_part[half:], dself_part[:half])
        n_q, r_q = n_self[:quarter], r_self[:quarter]
        hidden_grad = (
            g_s[:quarter] + norm_back(n_q, r_q, dself_in, 1.0 + shifts[1])
        ).astype(BF)

        da3, da2 = dffn_in[:quarter], dcross_in[:quarter]
        sums_own = jnp.stack(
            [
                jnp.sum(dself_in, 0),
                jnp.sum(dself_in * n_q, 0),
                jnp.sum(g_s[:quarter] * self_branch[:quarter], 0),
                jnp.sum(da3, 0),
                jnp.sum(da3 * n_ffn[:quarter], 0),
                jnp.sum(g[:quarter] * ffn_branch, 0),
                jnp.sum(da2 * n_cross[:quarter], 0),
                jnp.sum(da2, 0),
            ]
        )
        sums_clip = sum_all(sums_own)
        time_grad = sums_clip[:6]
        low_sums = sums_clip.reshape(8, n_dp, r_dp).transpose(1, 0, 2).reshape(n_dp, -1)
        gain_grads = jnp.stack([sq_gain_grad, sk_gain_grad, cq_gain_grad, ck_gain_grad])
        low_gains = gain_grads.reshape(4 * heads, n_dp, g_cols).transpose(1, 0, 2).reshape(n_dp, -1)
        packed = jnp.concatenate([low_sums, low_gains], axis=1)
        packed = jnp.pad(packed, ((0, 0), (0, pad))).reshape(n_dp, 8, -1)
        tiny = scatter_dp(packed).reshape(-1)
        eight = tiny[: 8 * r_dp].reshape(8, r_dp)
        gains_out = tiny[8 * r_dp : 8 * r_dp + 4 * heads * g_cols].reshape(4, heads, g_cols)

        return (
            block_out,
            hidden_grad,
            context_grad[None],
            time_grad[None],
            eight[:6],
            qkv_grad[:, :wide],
            qkv_grad[:, wide : 2 * wide],
            qkv_grad[:, 2 * wide :],
            oT_grad.T,
            gains_out[0],
            gains_out[1],
            cross_grad[:, :wide],
            cross_grad[:, wide : 2 * wide],
            cross_grad[:, 2 * wide : 3 * wide],
            cross_grad[:, 3 * wide :].T,
            gains_out[2],
            gains_out[3],
            eight[6],
            eight[7],
            up_grad,
            downT_grad.T,
        )

    rows = P(("dp", "tensor"), None)
    col = P("dp", "tensor")
    row = P("tensor", "dp")
    text = P("dp", "tensor", None)
    time = P("dp", None, None)
    one = P("dp")
    ins = (
        rows, text, time, one, P(None, "dp"), P(None, "dp"),
        col, col, col, row, row, row,
        col, col, col, row, row, row,
        one, one, col, row, rows,
    )
    outs = (
        rows, rows, text, time, P(None, "dp"),
        col, col, col, row, row, row,
        col, col, col, row, row, row,
        one, one, col, row,
    )
    return jax.shard_map(on_device, mesh=mesh, in_specs=ins, out_specs=outs, check_vma=False)
```

```python
import math

import jax
import jax.numpy as jnp
from jax import lax
from jax.experimental import pallas as pl
from jax.experimental.pallas import tpu as pltpu
from jax.sharding import PartitionSpec as P

D = 1536
HEAD = 128
EPS = 1e-6
BF = jnp.bfloat16
F32 = jnp.float32
FACTOR = 1.0 / math.sqrt(HEAD)
GELU = math.sqrt(2.0 / math.pi)
CUBE = 0.044715
MESH = pl.DeviceIdType.MESH


def dot_nn(a, b):
    return lax.dot_general(a, b, (((1,), (0,)), ((), ())), preferred_element_type=F32)


def dot_nt(a, b):
    return lax.dot_general(a, b, (((1,), (1,)), ((), ())), preferred_element_type=F32)


def dot_tn(a, b):
    return lax.dot_general(a, b, (((0,), (0,)), ((), ())), preferred_element_type=F32)


def shape(dims, dtype):
    return jax.ShapeDtypeStruct(dims, dtype)


def run(kernel, outs, blocks, far=(), scratch=(), flops=0, exps=0, limit=60):
    moved = sum(math.prod(v.shape) * v.dtype.itemsize for v in (*blocks, *far, *outs))
    return pl.pallas_call(
        kernel,
        out_shape=tuple(outs),
        in_specs=[pl.BlockSpec(memory_space=pltpu.VMEM)] * len(blocks)
        + [pl.BlockSpec(memory_space=pl.ANY)] * len(far),
        out_specs=tuple(pl.BlockSpec(memory_space=pltpu.VMEM) for _ in outs),
        scratch_shapes=list(scratch),
        compiler_params=pltpu.CompilerParams(vmem_limit_bytes=limit * 2**20),
        cost_estimate=pl.CostEstimate(flops=int(flops), bytes_accessed=moved, transcendentals=int(exps)),
    )(*blocks, *far)


def load(pieces, w, sems, first=0):
    n = len(pieces)
    r, c = w.shape[0] // n, w.shape[1]
    if n == 1:
        copy = pltpu.make_async_copy(pieces[0].at[:, pl.ds(first, c)], w, sems.at[0])
        copy.start()
        return [copy]
    d = lax.axis_index("dp")
    major, minor = d // 2, d % 2
    copies = []
    for i, piece in enumerate(pieces):
        t, flip = i // 2, i % 2
        block = 2 * lax.rem(major + t, n // 2) + (1 - minor if flip else minor)
        rows = pl.ds(pl.multiple_of(block * r, 16), r)
        copy = pltpu.make_async_copy(piece.at[:, pl.ds(first, c)], w.at[rows], sems.at[i])
        copy.start()
        copies.append(copy)
    return copies


def wait(copies):
    for copy in copies:
        copy.wait()


def weight(n, c):
    return [pltpu.VMEM((D, c), BF), pltpu.SemaphoreType.DMA((n,))]


def to_rows(columns, count):
    lane = lax.broadcasted_iota(jnp.int32, (count, 128), 1)
    out = jnp.zeros((count, 128), F32)
    for i, column in enumerate(columns):
        out = jnp.where(lane == i, column, out)
    return jnp.transpose(out)[:8]


def to_columns(rows):
    return jnp.transpose(jnp.concatenate([rows] * 16, axis=0))


def turn(values, cosine, sine):
    even = lax.broadcasted_iota(jnp.int32, values.shape, 1) % 2 == 0
    partner = jnp.where(even, pltpu.roll(values, HEAD - 1, 1), pltpu.roll(values, 1, 1))
    return values * cosine + partner * sine


def norm_of(v):
    center = v - jnp.mean(v, axis=-1, keepdims=True)
    r = lax.rsqrt(jnp.mean(center * center, axis=-1, keepdims=True) + EPS)
    return center * r, r


STEP = 32


def over_rows(count, body):
    def one(i, carry):
        body(pl.ds(pl.multiple_of(i * STEP, STEP), STEP))
        return carry

    lax.fori_loop(0, count // STEP, one, 0)


def norm_first(v, m, t):
    def kernel(v_ref, m_ref, t_ref, rows_ref):
        def body(s):
            n, _ = norm_of(v_ref[s].astype(F32))
            rows_ref[s] = (n * m_ref[...] + t_ref[...]).astype(BF)

        over_rows(v_ref.shape[0], body)

    return run(kernel, [shape(v.shape, BF)], [v, m, t], flops=1e9)[0]


def norm_forward(v, chip, far_chip, s, m, t):
    def kernel(v_ref, a_ref, b_ref, s_ref, m_ref, t_ref, out_ref, rows_ref):
        def body(i):
            branch = a_ref[i].astype(F32) + b_ref[i].astype(F32)
            out = v_ref[i].astype(F32) + branch * s_ref[...]
            out_ref[i] = out
            n, _ = norm_of(out)
            rows_ref[i] = (n * m_ref[...] + t_ref[...]).astype(BF)

        over_rows(v_ref.shape[0], body)

    return run(
        kernel, [shape(v.shape, F32), shape(v.shape, BF)], [v, chip, far_chip, s, m, t], flops=1e9
    )


def norm_backward(g, v, chip, far_chip, m, s):
    def kernel(g_ref, v_ref, a_ref, b_ref, m_ref, s_ref, out_ref, rows_ref, sum_ref):
        sum_ref[...] = jnp.zeros_like(sum_ref)

        def body(i):
            da = a_ref[i].astype(F32) + b_ref[i].astype(F32)
            n, r = norm_of(v_ref[i].astype(F32))
            dn = da * m_ref[...]
            mean = jnp.mean(dn, axis=-1, keepdims=True)
            along = jnp.mean(dn * n, axis=-1, keepdims=True)
            out = g_ref[i].astype(F32) + r * (dn - mean - n * along)
            out_ref[i] = out
            rows_ref[i] = (out * s_ref[...]).astype(BF)
            dan = da * n
            for k in range(STEP // 8):
                sum_ref[:8] += da[k * 8 : k * 8 + 8]
                sum_ref[8:] += dan[k * 8 : k * 8 + 8]

        over_rows(g_ref.shape[0], body)

    return run(
        kernel,
        [shape(g.shape, F32), shape(g.shape, BF), shape((16, D), F32)],
        [g, v, chip, far_chip, m, s],
        flops=1e9,
    )


def hold(v, after):
    def kernel(v_ref, *refs):
        refs[-1][...] = v_ref[...]

    return run(kernel, [shape(v.shape, v.dtype)], [v], after)[0]


def project(xs, pieces, first, squares, lows, wide):
    total = sum(x.shape[0] for x in xs)
    cols = (squares + lows) * wide
    n = len(pieces)
    outs = [shape((total, squares * wide), F32)] * (squares > 0)
    outs += [shape((total, lows * wide), BF)] * (lows > 0)
    outs += [shape((8, total), F32)] * (squares > 0)

    def kernel(*refs):
        x_refs, refs = refs[: len(xs)], refs[len(xs) :]
        piece_refs, refs = refs[:n], refs[n:]
        out_refs, (w, sems) = list(refs[:-2]), refs[-2:]
        wait(load(piece_refs, w, sems, first))
        at = 0
        for x_ref in x_refs:
            m = x_ref.shape[0]
            value = dot_nn(x_ref[...], w[...])
            columns = []
            for i in range(squares):
                part = value[:, i * wide : (i + 1) * wide]
                columns.append(jnp.sum(part * part, axis=1, keepdims=True))
            if squares:
                out_refs[0][at : at + m] = value[:, : squares * wide]
                out_refs[-1][:, at : at + m] = to_rows(columns, m)
            if lows:
                out_refs[1 if squares else 0][at : at + m] = value[:, squares * wide :].astype(BF)
            at += m

    return run(kernel, outs, xs, pieces, weight(n, cols), flops=2 * total * D * cols)


def normalize(raws, stats, gains, tables, wide):
    count = len(gains)
    parts = len(raws)
    outs = [shape((r.shape[0], wide), BF) for r in raws for _ in range(count)]

    def kernel(*refs):
        raw_refs, refs = refs[:parts], refs[parts:]
        stat_refs, refs = refs[:parts], refs[parts:]
        gain_refs, refs = refs[:count], refs[count:]
        if tables:
            cos_refs, sin_refs, refs = refs[:parts], refs[parts : 2 * parts], refs[2 * parts :]
        for p in range(parts):
            scale = lax.rsqrt(to_columns(stat_refs[p][...]) / D + EPS)
            for i in range(count):
                for h in range(wide // HEAD):
                    lanes = slice(i * wide + h * HEAD, i * wide + (h + 1) * HEAD)
                    own = slice(h * HEAD, (h + 1) * HEAD)
                    value = raw_refs[p][:, lanes] * scale[:, i : i + 1] * gain_refs[i][:, own]
                    if tables:
                        value = turn(value, cos_refs[p][...], sin_refs[p][...])
                    refs[p * count + i][:, own] = value.astype(BF)

    args = [*raws, *stats, *gains]
    if tables:
        args += [*tables[0], *tables[1]]
    return run(kernel, outs, args, flops=1e9)


QB = 256


def attend(q, ks, vs, bias, pieces, first):
    rows, wide = q.shape
    heads = wide // HEAD
    nk = sum(k.shape[0] for k in ks)
    n = len(pieces)
    parts = len(ks)
    half = rows // 2
    biases = [] if bias is None else [bias]

    def kernel(*refs):
        q_ref, k_refs, v_refs = refs[0], refs[1 : 1 + parts], refs[1 + parts : 1 + 2 * parts]
        refs = refs[1 + 2 * parts :]
        b_refs, refs = refs[: len(biases)], refs[len(biases) :]
        piece_refs, (out_ref, lse_ref, mine_ref, theirs_ref, w, sems) = refs[:n], refs[n:]
        copies = load(piece_refs, w, sems, first)
        lse_ref[...] = jnp.zeros_like(lse_ref)
        for h in range(heads):
            lanes = slice(h * HEAD, (h + 1) * HEAD)
            k = jnp.concatenate([r[:, lanes] for r in k_refs]) if parts > 1 else k_refs[0][:, lanes]
            v = jnp.concatenate([r[:, lanes] for r in v_refs]) if parts > 1 else v_refs[0][:, lanes]
            for b in range(rows // QB):
                block = slice(b * QB, (b + 1) * QB)
                s = dot_nt(k, q_ref[block, lanes]) * FACTOR
                if biases:
                    s = s + b_refs[0][...]
                top = jnp.max(s, axis=0, keepdims=True)
                e = jnp.exp(s - top)
                total = jnp.sum(e, axis=0, keepdims=True)
                lse_ref[h : h + 1, block] = top + jnp.log(total)
                o = dot_tn(v, e.astype(BF)) * (1.0 / total)
                out_ref[block, lanes] = jnp.transpose(o).astype(BF)
        wait(copies)
        mine_ref[...] = dot_nt(out_ref[:half], w[...])
        theirs_ref[...] = dot_nt(out_ref[half:], w[...]).astype(BF)

    return run(
        kernel,
        [shape((rows, wide), BF), shape((8, rows), F32), shape((half, D), F32), shape((half, D), BF)],
        [q, *ks, *vs, *biases],
        pieces,
        weight(n, wide),
        flops=2 * rows * wide * (2 * nk + D),
        exps=rows * nk * heads,
    )


def attend_back(xs, pieces, first, q, ks, vs, bias, lse, sofar):
    rows, wide = q.shape
    heads = wide // HEAD
    nk = sum(k.shape[0] for k in ks)
    n = len(pieces)
    parts = len(ks)
    biases = [] if bias is None else [bias]

    def kernel(*refs):
        x_refs, q_ref, refs = refs[:2], refs[2], refs[3:]
        k_refs, v_refs, lse_ref, refs = refs[:parts], refs[parts : 2 * parts], refs[2 * parts], refs[2 * parts + 1 :]
        b_refs, refs = refs[: len(biases)], refs[len(biases) :]
        old_refs, refs = refs[: len(sofar)], refs[len(sofar) :]
        piece_refs, (dq_ref, dk_ref, dv_ref, w, sems, do_ref) = refs[:n], refs[n:]
        wait(load(piece_refs, w, sems, first))
        for i in range(2):
            m = x_refs[i].shape[0]
            do_ref[i * m : (i + 1) * m] = dot_nn(x_refs[i][...], w[...]).astype(BF)
        for h in range(heads):
            lanes = slice(h * HEAD, (h + 1) * HEAD)
            k = jnp.concatenate([r[:, lanes] for r in k_refs]) if parts > 1 else k_refs[0][:, lanes]
            v = jnp.concatenate([r[:, lanes] for r in v_refs]) if parts > 1 else v_refs[0][:, lanes]
            for b in range(rows // QB):
                block = slice(b * QB, (b + 1) * QB)
                qb = q_ref[block, lanes]
                do = do_ref[block, lanes]
                s = dot_nt(k, qb) * FACTOR
                if biases:
                    s = s + b_refs[0][...]
                p = jnp.exp(s - lse_ref[h : h + 1, block])
                dp = dot_nt(v, do)
                center = jnp.sum(p * dp, axis=0, keepdims=True)
                ds = (p * (dp - center)).astype(BF)
                dq_ref[block, lanes] = dot_tn(ds, k) * FACTOR
                dk = dot_nn(ds, qb) * FACTOR
                dv = dot_nn(p.astype(BF), do)
                if b == 0 and not sofar:
                    dk_ref[:, lanes] = dk
                    dv_ref[:, lanes] = dv
                elif b == 0:
                    dk_ref[:, lanes] = old_refs[0][:, lanes] + dk
                    dv_ref[:, lanes] = old_refs[1][:, lanes] + dv
                else:
                    dk_ref[:, lanes] += dk
                    dv_ref[:, lanes] += dv

    return run(
        kernel,
        [shape((rows, wide), F32), shape((nk, wide), F32), shape((nk, wide), F32)],
        [*xs, q, *ks, *vs, lse, *biases, *sofar],
        pieces,
        weight(n, wide) + [pltpu.VMEM((rows, wide), BF)],
        flops=2 * rows * wide * (5 * nk + D),
        exps=rows * nk * heads,
    )


def root_dots(dys, raws, stats, gains, tables, wide):
    count = len(gains)
    outs = [shape(dy.shape, F32) for dy in dys] if tables else []
    outs += [shape((8, dy.shape[0]), F32) for dy in dys]
    outs += [shape((8, wide), F32)]

    def kernel(*refs):
        dy_refs, refs = refs[:count], refs[count:]
        raw_refs, refs = refs[:count], refs[count:]
        stat_refs, refs = refs[:count], refs[count:]
        gain_refs, refs = refs[:count], refs[count:]
        if tables:
            cos_ref, sin_ref, refs = refs[0], refs[1], refs[2:]
            turned, refs = refs[:count], refs[count:]
        dot_refs, grad_ref = refs[:count], refs[count]
        grad_ref[...] = jnp.zeros_like(grad_ref)
        for i in range(count):
            row = raws[i][2]
            m = dy_refs[i].shape[0]
            scale = lax.rsqrt(to_columns(stat_refs[i][...]) / D + EPS)[:, row : row + 1]
            dots = jnp.zeros((m, 1), F32)
            for h in range(wide // HEAD):
                own = slice(h * HEAD, (h + 1) * HEAD)
                dy = dy_refs[i][:, own]
                if tables:
                    dy = turn(dy, cos_ref[...], -sin_ref[...])
                    turned[i][:, own] = dy
                c = raws[i][1] + h * HEAD
                both = raw_refs[i][:, c : c + HEAD] * dy
                dots = dots + jnp.sum(both * gain_refs[i][:, own], axis=1, keepdims=True)
                grad_ref[i : i + 1, own] = jnp.sum(both * scale, axis=0, keepdims=True)
            dot_refs[i][...] = to_rows([dots], m)

    args = [*dys, *(r[0] for r in raws), *stats, *gains]
    if tables:
        args += [*tables]
    return run(kernel, outs, args, flops=1e9)


def root_back(dys, raws, stats, dots, gains, dv, pieces, first, wide, halves):
    count = len(gains)
    extra = 0 if dv is None else 1
    rows = dys[0].shape[0]
    cols = (count + extra) * wide
    n = len(pieces)
    part = rows // (2 * halves)
    vs = [] if dv is None else [dv]

    def kernel(*refs):
        dy_refs, refs = refs[:count], refs[count:]
        raw_refs, refs = refs[:count], refs[count:]
        stat_refs, refs = refs[:count], refs[count:]
        dot_refs, refs = refs[:count], refs[count:]
        gain_refs, refs = refs[:count], refs[count:]
        v_refs, refs = refs[:extra], refs[extra:]
        piece_refs, refs = refs[:n], refs[n:]
        low_ref, refs = refs[0], refs[1:]
        mine_refs, their_refs, (w, sems) = refs[:halves], refs[halves : 2 * halves], refs[2 * halves :]
        copies = load(piece_refs, w, sems, first)
        for i in range(count):
            row = raws[i][2]
            scale = lax.rsqrt(to_columns(stat_refs[i][...]) / D + EPS)[:, row : row + 1]
            along = scale * scale * scale * to_columns(dot_refs[i][...])[:, 0:1] / D
            for h in range(wide // HEAD):
                own = slice(h * HEAD, (h + 1) * HEAD)
                c = raws[i][1] + h * HEAD
                dx = scale * gain_refs[i][:, own] * dy_refs[i][:, own] - raw_refs[i][:, c : c + HEAD] * along
                low_ref[:, i * wide + h * HEAD : i * wide + (h + 1) * HEAD] = dx.astype(BF)
        if extra:
            low_ref[:, count * wide :] = v_refs[0][...].astype(BF)
        wait(copies)
        for j in range(halves):
            at = 2 * part * j
            mine_refs[j][...] = dot_nt(low_ref[at : at + part], w[...])
            their_refs[j][...] = dot_nt(low_ref[at + part : at + 2 * part], w[...]).astype(BF)

    return run(
        kernel,
        [shape((rows, cols), BF)]
        + [shape((part, D), F32)] * halves
        + [shape((part, D), BF)] * halves,
        [*dys, *(r[0] for r in raws), *stats, *dots, *gains, *vs],
        pieces,
        weight(n, cols),
        flops=2 * rows * cols * D,
    )


HC = 768


def expand(xs, pieces, first, hid):
    rows = sum(x.shape[0] for x in xs)
    n = len(pieces)

    def kernel(*refs):
        x_refs, piece_refs, (out_ref, w, sems) = refs[: len(xs)], refs[len(xs) : len(xs) + n], refs[len(xs) + n :]
        chunks = [load(piece_refs[j : j + 1], w.at[j], sems.at[j], first) for j in range(hid // HC)]
        for j in range(hid // HC):
            wait(chunks[j])
            at = 0
            for x_ref in x_refs:
                m = x_ref.shape[0]
                out_ref[at : at + m, j * HC : (j + 1) * HC] = dot_nn(x_ref[...], w[j]).astype(BF)
                at += m

    return run(
        kernel,
        [shape((rows, hid), BF)],
        xs,
        pieces,
        [pltpu.VMEM((hid // HC, D, HC), BF), pltpu.SemaphoreType.DMA((hid // HC, 1))],
        flops=2 * rows * D * hid,
    )[0]


def feed(xs, dact, pieces, first):
    rows, hid = dact.shape
    n = len(pieces)
    m = rows // 2

    def kernel(*refs):
        x_refs, dact_ref, piece_refs = refs[:2], refs[2], refs[3 : 3 + n]
        act_ref, dpre_ref, mine_ref, theirs_ref, w, sems = refs[3 + n :]
        chunks = [load(piece_refs[j : j + 1], w.at[j], sems.at[j], first) for j in range(hid // HC)]
        for j in range(hid // HC):
            cols = slice(j * HC, (j + 1) * HC)
            wait(chunks[j])
            for i in range(2):
                own = slice(i * m, (i + 1) * m)
                u = dot_nn(x_refs[i][...], w[j])
                sq = u * u
                th = jnp.tanh(u * (GELU + GELU * CUBE * sq))
                near = 0.5 + 0.5 * th
                act_ref[own, cols] = (u * near).astype(BF)
                slope = near + u * near * (1.0 - th) * (GELU + 3 * GELU * CUBE * sq)
                dpre_ref[own, cols] = (dact_ref[own, cols].astype(F32) * slope).astype(BF)
        for i in range(2):
            own = slice(i * m, (i + 1) * m)
            total = dot_nt(dpre_ref[own, :HC], w[0])
            for j in range(1, hid // HC):
                total = total + dot_nt(dpre_ref[own, j * HC : (j + 1) * HC], w[j])
            if i == 0:
                mine_ref[...] = total
            else:
                theirs_ref[...] = total.astype(BF)

    return run(
        kernel,
        [shape((rows, hid), BF), shape((rows, hid), BF), shape((m, D), F32), shape((m, D), BF)],
        [*xs, dact],
        pieces,
        [pltpu.VMEM((hid // HC, D, HC), BF), pltpu.SemaphoreType.DMA((hid // HC, 1))],
        flops=4 * rows * D * hid,
        exps=rows * hid,
        limit=60,
    )


def contract(act, pieces, first):
    rows, hid = act.shape
    n = len(pieces)
    m = rows // 2

    def kernel(*refs):
        act_ref, piece_refs, (mine_ref, theirs_ref, w, sems) = refs[0], refs[1 : 1 + n], refs[1 + n :]
        chunks = [load(piece_refs[j : j + 1], w.at[j], sems.at[j], first) for j in range(hid // HC)]
        for chunk in chunks:
            wait(chunk)
        for i in range(2):
            own = slice(i * m, (i + 1) * m)
            total = dot_nt(act_ref[own, :HC], w[0])
            for j in range(1, hid // HC):
                total = total + dot_nt(act_ref[own, j * HC : (j + 1) * HC], w[j])
            if i == 0:
                mine_ref[...] = total
            else:
                theirs_ref[...] = total.astype(BF)

    return run(
        kernel,
        [shape((m, D), F32), shape((m, D), BF)],
        [act],
        pieces,
        [pltpu.VMEM((hid // HC, D, HC), BF), pltpu.SemaphoreType.DMA((hid // HC, 1))],
        flops=2 * rows * D * hid,
    )


GC = 384


def full_grads(xs, ys):
    cols = ys[0].shape[1]
    most = sum(x.shape[0] for x in xs)

    def kernel(*refs):
        x_refs, y_refs, (out_ref, turned) = refs[: len(xs)], refs[len(xs) : -2], refs[-2:]
        row = 0
        for x_ref in x_refs:
            m = x_ref.shape[0]
            turned[:, row : row + m] = jnp.transpose(x_ref[...])
            row += m
        for c in range(0, cols, HC):
            lanes = slice(c, c + HC)
            for k in range(0, D, 512):
                row = 0
                total = None
                for y_ref in y_refs:
                    m = y_ref.shape[0]
                    term = dot_nn(turned[k : k + 512, row : row + m], y_ref[:, lanes])
                    total = term if total is None else total + term
                    row += m
                out_ref[k : k + 512, lanes] = total.astype(BF)

    return run(
        kernel,
        [shape((D, cols), BF)],
        [*xs, *ys],
        (),
        [pltpu.VMEM((D, most), BF)],
        flops=2 * most * D * cols,
        limit=60,
    )[0]


def weight_grads(pairs, n, after=()):
    widths = [ys[0].shape[1] for _, ys in pairs]
    cols = sum(widths)
    r = D // n
    flat = [a for xs, ys in pairs for a in (*xs, *ys)]
    out = shape((n // 2, r, cols), BF)
    most = max(sum(x.shape[0] for x in xs) for xs, _ in pairs)

    def kernel(*refs):
        ins, refs = refs[: len(flat)], refs[len(flat) + len(after) :]
        theirs_ref, mine_ref, total_ref, turned, sems = refs
        minor = lax.axis_index("dp") % 2
        at = 0
        col = 0
        copies = []
        for p, (xs, ys) in enumerate(pairs):
            x_refs, y_refs = ins[at : at + len(xs)], ins[at + len(xs) : at + len(xs) + len(ys)]
            at += len(xs) + len(ys)
            row = 0
            for x_ref in x_refs:
                m = x_ref.shape[0]
                turned[:, row : row + m] = jnp.transpose(x_ref[...])
                row += m
            for c in range(0, widths[p], GC):
                lanes = slice(c, c + GC)
                for k in range(0, D, 512):
                    row = 0
                    total = None
                    for y_ref in y_refs:
                        m = y_ref.shape[0]
                        term = dot_nn(turned[k : k + 512, row : row + m], y_ref[:, lanes])
                        total = term if total is None else total + term
                        row += m
                    total_ref[k : k + 512, col + c : col + c + GC] = total.astype(BF)
                for j in range(n // 2):
                    for flip, ref in ((1, theirs_ref), (0, mine_ref)):
                        block = 2 * j + (1 - minor if flip else minor)
                        copy = pltpu.make_async_copy(
                            total_ref.at[
                                pl.ds(pl.multiple_of(block * r, 16), r), pl.ds(col + c, GC)
                            ],
                            ref.at[j, :, pl.ds(col + c, GC)],
                            sems.at[(col + c) // GC, 2 * j + flip],
                        )
                        copy.start()
                        copies.append(copy)
            col += widths[p]
        wait(copies)

    moved = sum(math.prod(v.shape) * 2 for v in flat) + 2 * D * cols
    return pl.pallas_call(
        kernel,
        out_shape=(out, out),
        in_specs=[pl.BlockSpec(memory_space=pltpu.VMEM)] * len(flat)
        + [pl.BlockSpec(memory_space=pl.ANY)] * len(after),
        out_specs=(pl.BlockSpec(memory_space=pl.ANY),) * 2,
        scratch_shapes=[
            pltpu.VMEM((D, cols), BF),
            pltpu.VMEM((D, most), BF),
            pltpu.SemaphoreType.DMA((cols // GC, n)),
        ],
        compiler_params=pltpu.CompilerParams(vmem_limit_bytes=60 * 2**20),
        cost_estimate=pl.CostEstimate(
            flops=int(2 * most * D * cols), bytes_accessed=moved, transcendentals=0
        ),
    )(*flat, *after)


def run_remote(kernel, outs, far_outs, blocks, far, scratch, cid, flops):
    moved = sum(math.prod(v.shape) * v.dtype.itemsize for v in (*blocks, *outs))
    vmem, hbm = pl.BlockSpec(memory_space=pltpu.VMEM), pl.BlockSpec(memory_space=pl.ANY)
    return pl.pallas_call(
        kernel,
        out_shape=(*outs, *far_outs),
        in_specs=[vmem] * len(blocks) + [hbm] * len(far),
        out_specs=(vmem,) * len(outs) + (hbm,) * len(far_outs),
        scratch_shapes=list(scratch),
        compiler_params=pltpu.CompilerParams(
            vmem_limit_bytes=60 * 2**20, collective_id=cid, has_side_effects=True
        ),
        cost_estimate=pl.CostEstimate(flops=int(flops), bytes_accessed=moved, transcendentals=0),
    )(*blocks, *far)


def tensor_peers():
    t = lax.axis_index("tensor")
    core = t + 1 - 2 * lax.rem(t, 2)
    across = lax.rem(t + 2, 4)
    return t, core, across, 3 - t


def greet(n_dp):
    d = lax.axis_index("dp")
    barrier = pltpu.get_barrier_semaphore()
    for k in range(1, n_dp):
        pl.semaphore_signal(
            barrier, inc=1, device_id={"dp": lax.rem(d + k, n_dp)}, device_id_type=MESH
        )
    for peer in tensor_peers()[1:]:
        pl.semaphore_signal(barrier, inc=1, device_id={"tensor": peer}, device_id_type=MESH)
    pl.semaphore_wait(barrier, n_dp + 2)


def remote(src, dst, send, recv, **place):
    return pltpu.make_async_remote_copy(
        src_ref=src, dst_ref=dst, send_sem=send, recv_sem=recv, device_id=place, device_id_type=MESH
    )


class Gather:
    def __init__(self, ref, sems, n):
        d = lax.axis_index("dp")
        self.z, self.y = d // 2, lax.rem(d, 2)
        self.ref, self.sems, self.n, self.r = ref, sems, n, ref.shape[0] // (2 * n)

    def block(self, o, y):
        return self.ref.at[pl.ds(pl.multiple_of((2 * o + y) * self.r, 16), self.r)]

    def copy(self, o, kind, index, z, y, own=True):
        block = self.block(o, self.y if own else 1 - self.y)
        sems = self.sems
        return remote(
            block, block, sems.at[2 * kind, index], sems.at[2 * kind + 1, index], dp=2 * z + y
        )

    def up(self, s):
        return self.copy(self.z - s, 0, s, self.z + 1, self.y)

    def down(self, s):
        return self.copy(self.z + s, 1, s, self.z - 1, self.y)

    def over(self, o):
        return self.copy(o, 2, o, self.z, 1 - self.y)

    def start(self, own, sem):
        copy = pltpu.make_async_copy(own, self.block(self.z, self.y), sem)
        copy.start()
        copy.wait()
        pl.when(self.z < self.n - 1)(lambda: self.up(0).start())
        pl.when(self.z > 0)(lambda: self.down(0).start())
        self.over(self.z).start()

    def step(self, s):
        z, n = self.z, self.n

        @pl.when(z - 1 - s >= 0)
        def _():
            self.copy(z - 1 - s, 0, s, z - 1, self.y).wait_recv()
            pl.when(z < n - 1)(lambda: self.up(s + 1).start())
            self.over(z - 1 - s).start()

        @pl.when(z + 1 + s <= n - 1)
        def _():
            self.copy(z + 1 + s, 1, s, z + 1, self.y).wait_recv()
            pl.when(z > 0)(lambda: self.down(s + 1).start())
            self.over(z + 1 + s).start()

    def finish(self):
        for o in range(self.n):
            self.copy(o, 2, o, self.z, 1 - self.y, own=False).wait_recv()

    def drain(self):
        z, n = self.z, self.n
        for s in range(n - 1):
            pl.when((z - s >= 0) & (z < n - 1))(lambda: self.up(s).wait_send())
            pl.when((z + s <= n - 1) & (z > 0))(lambda: self.down(s).wait_send())
        for o in range(n):
            self.over(o).wait_send()


class Swap:
    def __init__(self, sems):
        self.sems, self.used, self.sent = sems, 0, []

    def start(self, src, dst, peer):
        k = self.used
        self.used += 1
        copy = remote(src, dst, self.sems.at[0, k], self.sems.at[1, k], tensor=peer)
        copy.start()
        self.sent.append(copy)
        return copy

    def settle(self):
        for copy in self.sent:
            copy.wait_send()
        self.sent = []


class Sums:
    def __init__(self, landed, sems, peers):
        self.landed, self.peers, self.used = landed, peers, 0
        self.swap = Swap(sems)

    def start(self, ref):
        k, c = self.used, ref.shape[1]
        self.used += 1
        copies = [
            self.swap.start(ref, self.landed.at[k, p, :, pl.ds(0, c)], peer)
            for p, peer in enumerate(self.peers)
        ]

        def collect():
            for copy in copies:
                copy.wait()
            stat_sum(ref, [self.landed[k, p, :, :c] for p in range(3)])

        return collect


def project_body(x_refs, w, first, out_ref, low_ref, stat_ref, squares, lows, wide):
    at = 0
    for x_ref in x_refs:
        m = x_ref.shape[0]
        value = dot_nn(x_ref[...], w[:, first : first + (squares + lows) * wide])
        columns = []
        for i in range(squares):
            part = value[:, i * wide : (i + 1) * wide]
            columns.append(jnp.sum(part * part, axis=1, keepdims=True))
        out_ref[at : at + m] = value[:, : squares * wide]
        stat_ref[:, at : at + m] = to_rows(columns, m)
        if lows:
            low_ref[at : at + m] = value[:, squares * wide :].astype(BF)
        at += m


def normalize_body(raw_ref, stat_ref, gains, cos, sin, out_refs, wide):
    scale = lax.rsqrt(to_columns(stat_ref[...]) / D + EPS)
    for i, out_ref in enumerate(out_refs):
        for h in range(wide // HEAD):
            lanes = slice(i * wide + h * HEAD, i * wide + (h + 1) * HEAD)
            value = raw_ref[:, lanes] * scale[:, i : i + 1] * gains[i][h]
            if cos is not None:
                value = turn(value, cos, sin)
            out_ref[:, h * HEAD : (h + 1) * HEAD] = value.astype(BF)


def attend_body(q_ref, k_refs, v_refs, bias_ref, out_ref, lse_ref):
    rows, wide = q_ref.shape
    lse_ref[...] = jnp.zeros_like(lse_ref)
    for h in range(wide // HEAD):
        lanes = slice(h * HEAD, (h + 1) * HEAD)
        k = jnp.concatenate([r[:, lanes] for r in k_refs]) if len(k_refs) > 1 else k_refs[0][:, lanes]
        v = jnp.concatenate([r[:, lanes] for r in v_refs]) if len(v_refs) > 1 else v_refs[0][:, lanes]
        for b in range(rows // QB):
            block = slice(b * QB, (b + 1) * QB)
            s = dot_nt(k, q_ref[block, lanes]) * FACTOR
            if bias_ref is not None:
                s = s + bias_ref[...]
            top = jnp.max(s, axis=0, keepdims=True)
            e = jnp.exp(s - top)
            total = jnp.sum(e, axis=0, keepdims=True)
            lse_ref[h : h + 1, block] = top + jnp.log(total)
            o = dot_tn(v, e.astype(BF)) * (1.0 / total)
            out_ref[block, lanes] = jnp.transpose(o).astype(BF)


def stat_sum(stat_ref, landed):
    h = stat_ref.shape[1] // 2
    other = landed[0] + landed[2]
    total = stat_ref[...] + landed[1]
    stat_ref[:, :h] = total[:, :h] + other[:, h:]
    stat_ref[:, h:] = total[:, h:] + other[:, :h]


def join_body(mine, got, chip):
    def body(i):
        chip[i] = (mine[i] + got[i].astype(F32)).astype(BF)

    over_rows(mine.shape[0], body)


def stream_body(base, chip, far, s, m, t, out_ref, rows_ref):
    def body(i):
        out = base(i) + (chip[i].astype(F32) + far[i].astype(F32)) * s
        out_ref[i] = out
        n, _ = norm_of(out)
        rows_ref[i] = (n * m + t).astype(BF)

    over_rows(rows_ref.shape[0], body)


def self_forward(hidden, context, cotangent, time_rows, tables, small, own_self, own_cross, own_first, n_dp, heads):
    quarter, texts = hidden.shape[0], context.shape[0]
    half, wide = 2 * quarter, heads * HEAD
    n = n_dp // 2
    r = D // n_dp
    g_cols = HEAD // n_dp
    rows = shape((quarter, D), BF)
    outs = dict(
        w_self=shape((D, 4 * wide), BF), w_cross=shape((D, 4 * wide), BF), got=rows,
        c0=shape((texts, D), BF), c1=shape((texts, D), BF), c2=shape((texts, D), BF), c3=shape((texts, D), BF),
        shifts=shape((8, D), F32), gains=shape((16, HEAD), F32),
        x0=rows, x1=rows, x2=rows, x3=rows,
        qk0=shape((half, 2 * wide), F32), qk1=shape((half, 2 * wide), F32),
        v0=shape((half, wide), BF), v1=shape((half, wide), BF),
        stat0=shape((8, half), F32), stat1=shape((8, half), F32),
        q0=shape((half, wide), BF), q1=shape((half, wide), BF),
        k0=shape((half, wide), BF), k1=shape((half, wide), BF),
        attn0=shape((half, wide), BF), attn1=shape((half, wide), BF),
        lse0=shape((8, half), F32), lse1=shape((8, half), F32),
        chip0=rows, chip1=rows, far0=rows, far1=rows,
        after0=shape((quarter, D), F32), after1=shape((quarter, D), F32),
        y0=rows, y1=rows, y2=rows, y3=rows,
        ck_raw=shape((4 * texts, wide), F32), cv=shape((4 * texts, wide), BF),
        ck_stat=shape((8, 4 * texts), F32), ck=shape((4 * texts, wide), BF),
    )
    far_outs = dict(f0=shape((D, own_first.shape[1]), BF), g_got=rows)
    blocks = [hidden, context, time_rows, tables[0], tables[1], small]
    far = [own_self, own_cross, own_first, cotangent]
    names = [*outs, *far_outs]

    def kernel(*refs):
        hid, ctx, times, cos, sin, small_ref = refs[:6]
        own1, own2, own3, cot = refs[6:10]
        o = dict(zip(names, refs[10 : 10 + len(names)]))
        all_small, ctx_got, theirs, landed, mine, stats_in, ring, near, cross_x, near_sums, small_sems, local = refs[
            10 + len(names) :
        ]
        t, core, across, diagonal = tensor_peers()
        first = t < 2
        d = lax.axis_index("dp")
        cores, xs = Swap(near), Swap(cross_x)
        greet(n_dp)

        g1 = Gather(o["w_self"], ring.at[0], n)
        g2 = Gather(o["w_cross"], ring.at[1], n)
        g3 = Gather(o["f0"], ring.at[2], n)
        g1.start(own1, local.at[0])
        own_small = all_small.at[pl.ds(pl.multiple_of(d * r, 16), r)]
        own_small[...] = small_ref[...]
        small_copies = []
        for k in range(1, n_dp):
            copy = remote(
                own_small, own_small, small_sems.at[0, k], small_sems.at[1, k], dp=lax.rem(d + k, n_dp)
            )
            copy.start()
            small_copies.append(copy)
        hid_copy = xs.start(hid, o["got"], across)
        ctx_copy = xs.start(ctx, ctx_got, across)
        g_copy = xs.start(cot, o["g_got"], across)

        for k in range(1, n_dp):
            source = lax.rem(d - k + n_dp, n_dp)
            block = all_small.at[pl.ds(pl.multiple_of(source * r, 16), r)]
            remote(block, block, small_sems.at[0, k], small_sems.at[1, k], dp=source).wait_recv()
        turned = jnp.transpose(all_small[...].astype(F32))
        o["shifts"][:6] = turned[:6] + times[...]
        o["shifts"][6:] = turned[6:8]
        at = lax.broadcasted_iota(jnp.int32, (D, HEAD), 0)
        to = lax.broadcasted_iota(jnp.int32, (D, HEAD), 1)
        pick = (at == (to // g_cols) * r + lax.rem(to, g_cols)).astype(F32)
        o["gains"][...] = dot_nn(turned[8:24].astype(BF), pick.astype(BF))
        g1.step(0)

        hid_copy.wait_recv()
        m_row, t_row = 1.0 + o["shifts"][1:2], o["shifts"][0:1]
        slots = [o["x0"], o["x1"], o["x2"], o["x3"]]

        def base(j):
            def pick_rows(i):
                own, other = hid[i].astype(F32), o["got"][i].astype(F32)
                return jnp.where(first, own, other) if j == 0 else jnp.where(first, other, own)

            return pick_rows

        arrivals = []
        for j in range(2):

            def body(i, j=j):
                v, _ = norm_of(base(j)(i))
                slots[2 * j][i] = (v * m_row + t_row).astype(BF)

            over_rows(quarter, body)
            arrivals.append(cores.start(slots[2 * j], slots[2 * j + 1], core))
        g1.step(1)
        ctx_copy.wait_recv()
        c_slots = [o["c0"], o["c1"], o["c2"], o["c3"]]
        a, b = ctx[...].astype(F32), ctx_got[...].astype(F32)
        c_slots[0][...] = jnp.where(first, a, b).astype(BF)
        c_slots[2][...] = jnp.where(first, b, a).astype(BF)
        c_arrivals = [cores.start(c_slots[2 * j], c_slots[2 * j + 1], core) for j in range(2)]
        for s in range(2, n - 1):
            g1.step(s)
        g2.start(own2, local.at[0])
        g1.finish()
        g2.step(0)

        qk, v = [o["qk0"], o["qk1"]], [o["v0"], o["v1"]]
        stat = [o["stat0"], o["stat1"]]
        w_self, w_cross = o["w_self"], o["w_cross"]

        sums = Sums(stats_in, near_sums, (core, across, diagonal))
        shared = []
        for j in range(2):
            arrivals[j].wait_recv()
            project_body(slots[2 * j : 2 * j + 2], w_self, 0, qk[j], v[j], stat[j], 2, 1, wide)
            shared.append(sums.start(stat[j]))
            if j == 0 and n > 2:
                g2.step(1)
        q, k = [o["q0"], o["q1"]], [o["k0"], o["k1"]]
        gain = [[o["gains"][i * heads + h : i * heads + h + 1] for h in range(heads)] for i in range(4)]
        for s in range(2, n - 1):
            g2.step(s)
        g3.start(own3, local.at[0])
        for j in range(2):
            shared[j]()
            own = slice(j * half, (j + 1) * half)
            normalize_body(qk[j], stat[j], gain[:2], cos[own], sin[own], [q[j], k[j]], wide)

        attn, lse = [o["attn0"], o["attn1"]], [o["lse0"], o["lse1"]]
        sent = []
        for j in range(2):
            attend_body(q[j], k, v, None, attn[j], lse[j])
            w_out = w_self[:, 3 * wide :]
            theirs[j] = dot_nt(attn[j][quarter:], w_out).astype(BF)
            sent.append(cores.start(theirs.at[j], landed.at[j], core))
            mine[j] = dot_nt(attn[j][:quarter], w_out)
            if j == 0:
                g3.step(0)
        chip, far_refs = [o["chip0"], o["chip1"]], [o["far0"], o["far1"]]
        crossed = []
        for j in range(2):
            sent[j].wait_recv()
            join_body(mine.at[j], landed.at[j], chip[j])
            crossed.append(xs.start(chip[j], far_refs[j], across))
        if n > 2:
            g3.step(1)

        g2.finish()
        for copy in c_arrivals:
            copy.wait_recv()
        project_body(c_slots, w_cross, wide, o["ck_raw"], o["cv"], o["ck_stat"], 1, 1, wide)
        halves = 2 * texts
        for j in range(2):
            part = o["ck_stat"].at[:, pl.ds(j * halves, halves)]
            sums.start(part)()
        normalize_body(o["ck_raw"], o["ck_stat"], gain[3:], None, None, [o["ck"]], wide)

        after = [o["after0"], o["after1"]]
        y_slots = [o["y0"], o["y1"], o["y2"], o["y3"]]
        shifts = o["shifts"]
        passed = []
        for j in range(2):
            crossed[j].wait_recv()
            stream_body(
                base(j), chip[j], far_refs[j], shifts[2:3], shifts[6:7], shifts[7:8], after[j], y_slots[2 * j]
            )
            passed.append(cores.start(y_slots[2 * j], y_slots[2 * j + 1], core))
            if j == 0:
                for s in range(2, n - 1):
                    g3.step(s)
        for copy in passed:
            copy.wait_recv()
        g_copy.wait_recv()
        g3.finish()
        for g in (g1, g2, g3):
            g.drain()
        for copy in small_copies:
            copy.wait_send()
        cores.settle()
        xs.settle()

    scratch = [
        pltpu.VMEM((D, HEAD), BF),
        pltpu.VMEM((texts, D), BF),
        pltpu.VMEM((2, quarter, D), BF),
        pltpu.VMEM((2, quarter, D), BF),
        pltpu.VMEM((2, quarter, D), F32),
        pltpu.VMEM((4, 3, 8, half), F32),
        pltpu.SemaphoreType.DMA((3, 6, n)),
        pltpu.SemaphoreType.DMA((2, 8)),
        pltpu.SemaphoreType.DMA((2, 8)),
        pltpu.SemaphoreType.DMA((2, 12)),
        pltpu.SemaphoreType.DMA((2, n_dp)),
        pltpu.SemaphoreType.DMA((1,)),
    ]
    got = run_remote(
        kernel, list(outs.values()), list(far_outs.values()), blocks, far, scratch, 1, 2e10
    )
    return dict(zip(names, got))


def cross_forward(state, bias, own_second, own_third, n_dp, heads):
    quarter = state["y0"].shape[0]
    half, wide = 2 * quarter, heads * HEAD
    n = n_dp // 2
    rows = shape((quarter, D), BF)
    outs = dict(
        cq_raw0=shape((half, wide), F32), cq_raw1=shape((half, wide), F32),
        cq_stat0=shape((8, half), F32), cq_stat1=shape((8, half), F32),
        cq0=shape((half, wide), BF), cq1=shape((half, wide), BF),
        cattn0=shape((half, wide), BF), cattn1=shape((half, wide), BF),
        clse0=shape((8, half), F32), clse1=shape((8, half), F32),
        after_c0=shape((quarter, D), F32), after_c1=shape((quarter, D), F32),
        z0=rows, z1=rows, z2=rows, z3=rows,
    )
    far_outs = dict(f1=shape((D, own_second.shape[1]), BF), f2=shape((D, own_third.shape[1]), BF))
    given = ("w_cross", "after0", "after1", "y0", "y1", "y2", "y3", "ck", "cv", "shifts", "gains")
    blocks = [state[name] for name in given] + [bias]
    far = [own_second, own_third]
    names = [*outs, *far_outs]

    def kernel(*refs):
        i = dict(zip(given, refs))
        bias_ref, own1, own2 = refs[len(given) : len(given) + 3]
        refs = refs[len(given) + 3 :]
        o = dict(zip(names, refs))
        theirs, landed, mine, chips, fars, stats_in, ring, near, cross_x, near_sums, local = refs[len(names) :]
        t, core, across, diagonal = tensor_peers()
        cores, xs = Swap(near), Swap(cross_x)
        sums = Sums(stats_in, near_sums, (core, across, diagonal))
        greet(n_dp)
        g1 = Gather(o["f1"], ring.at[0], n)
        g2 = Gather(o["f2"], ring.at[1], n)
        g1.start(own1, local.at[0])
        w = i["w_cross"]
        slots = [i["y0"], i["y1"], i["y2"], i["y3"]]
        raw, stat = [o["cq_raw0"], o["cq_raw1"]], [o["cq_stat0"], o["cq_stat1"]]
        q = [o["cq0"], o["cq1"]]
        attn, lse = [o["cattn0"], o["cattn1"]], [o["clse0"], o["clse1"]]
        gain = [i["gains"][2 * heads + h : 2 * heads + h + 1] for h in range(heads)]
        shared = []
        for j in range(2):
            project_body(slots[2 * j : 2 * j + 2], w, 0, raw[j], None, stat[j], 1, 0, wide)
            shared.append(sums.start(stat[j]))
        sent = []
        for j in range(2):
            shared[j]()
            normalize_body(raw[j], stat[j], [gain], None, None, [q[j]], wide)
            attend_body(q[j], [i["ck"]], [i["cv"]], bias_ref, attn[j], lse[j])
            w_out = w[:, 3 * wide :]
            theirs[j] = dot_nt(attn[j][quarter:], w_out).astype(BF)
            sent.append(cores.start(theirs.at[j], landed.at[j], core))
            mine[j] = dot_nt(attn[j][:quarter], w_out)
            if j == 0:
                g1.step(0)
        crossed = []
        for j in range(2):
            sent[j].wait_recv()
            join_body(mine.at[j], landed.at[j], chips.at[j])
            crossed.append(xs.start(chips.at[j], fars.at[j], across))
        for s in range(1, n - 1):
            g1.step(s)
        g2.start(own2, local.at[0])
        base = [i["after0"], i["after1"]]
        after = [o["after_c0"], o["after_c1"]]
        z_slots = [o["z0"], o["z1"], o["z2"], o["z3"]]
        m_row, t_row = 1.0 + i["shifts"][4:5], i["shifts"][3:4]
        passed = []
        for j in range(2):
            crossed[j].wait_recv()
            stream_body(
                lambda rows, j=j: base[j][rows], chips.at[j], fars.at[j], 1.0, m_row, t_row, after[j], z_slots[2 * j]
            )
            passed.append(cores.start(z_slots[2 * j], z_slots[2 * j + 1], core))
        for s in range(n - 1):
            g2.step(s)
        for copy in passed:
            copy.wait_recv()
        for g in (g1, g2):
            g.finish()
        for g in (g1, g2):
            g.drain()
        cores.settle()
        xs.settle()

    scratch = [
        pltpu.VMEM((2, quarter, D), BF),
        pltpu.VMEM((2, quarter, D), BF),
        pltpu.VMEM((2, quarter, D), F32),
        pltpu.VMEM((2, quarter, D), BF),
        pltpu.VMEM((2, quarter, D), BF),
        pltpu.VMEM((2, 3, 8, half), F32),
        pltpu.SemaphoreType.DMA((2, 6, n)),
        pltpu.SemaphoreType.DMA((2, 8)),
        pltpu.SemaphoreType.DMA((2, 8)),
        pltpu.SemaphoreType.DMA((2, 6)),
        pltpu.SemaphoreType.DMA((1,)),
    ]
    got = run_remote(
        kernel, list(outs.values()), list(far_outs.values()), blocks, far, scratch, 2, 1e10
    )
    return dict(zip(names, got))


def rotary_tables(positions, head_dim):
    pair_count = head_dim // 2
    side_pairs = pair_count // 3
    frame_pairs = pair_count - 2 * side_pairs
    pair_index = jnp.arange(pair_count)
    frame_mask = pair_index < frame_pairs
    height_mask = (pair_index >= frame_pairs) & (pair_index < frame_pairs + side_pairs)
    within = jnp.where(
        frame_mask,
        pair_index,
        jnp.where(height_mask, pair_index - frame_pairs, pair_index - frame_pairs - side_pairs),
    )
    extent = jnp.where(frame_mask, frame_pairs, side_pairs)
    frequency = jnp.power(10000.0, -within.astype(F32) / extent.astype(F32))
    coords = positions.astype(F32)
    coordinate = jnp.where(
        frame_mask[None, :],
        coords[0][:, None],
        jnp.where(height_mask[None, :], coords[1][:, None], coords[2][:, None]),
    )
    angles = jnp.repeat(coordinate * frequency[None, :], 2, axis=1)
    parity = jnp.arange(head_dim) % 2
    sign_pattern = jnp.where(parity == 0, -1.0, 1.0)
    return (jnp.cos(angles), jnp.sin(angles) * sign_pattern)


def solution(mesh):
    n_dp = mesh.shape["dp"]
    n_major = n_dp // 2
    pair_perm = [(i, i ^ 1) for i in range(n_dp)]
    ring_perm = {
        t: [((((i // 2) + t) % n_major) * 2 + i % 2, i) for i in range(n_dp)]
        for t in range(1, n_major)
    }
    back_perm = {t: [(b, a) for a, b in ring_perm[t]] for t in ring_perm}
    core_perm = [(i, i ^ 1) for i in range(4)]
    x_perm = [(i, i ^ 2) for i in range(4)]

    def core_swap(v):
        return lax.ppermute(v, "tensor", core_perm)

    def x_swap(v):
        return lax.ppermute(v, "tensor", x_perm)

    def gather_dp(block):
        pieces = []
        for t in range(n_major):
            piece = block if t == 0 else lax.ppermute(block, "dp", ring_perm[t])
            pieces += [piece, lax.ppermute(piece, "dp", pair_perm)]
        return pieces

    def scatter_dp(theirs, mine):
        major = lax.axis_index("dp") // 2
        got = lax.ppermute(theirs, "dp", pair_perm)

        def block(t):
            at = (major + t) % n_major
            a = lax.dynamic_slice_in_dim(mine, at, 1, axis=0)[0].astype(F32)
            return a + lax.dynamic_slice_in_dim(got, at, 1, axis=0)[0].astype(F32)

        arrived = [
            lax.ppermute(block(t).astype(BF), "dp", back_perm[t]) for t in range(1, n_major)
        ]
        total = block(0)
        for piece in arrived:
            total = total + piece.astype(F32)
        return total

    def join(mine, theirs):
        return (mine + core_swap(theirs).astype(F32)).astype(BF)

    def own_half(pair):
        first = lax.axis_index("tensor") < 2
        return jnp.where(first, pair[0], pair[1])

    def other_half(pair):
        first = lax.axis_index("tensor") < 2
        return jnp.where(first, pair[1], pair[0])

    def two_halves(own):
        got = x_swap(own)
        first = lax.axis_index("tensor") < 2
        return jnp.where(first, own, got), jnp.where(first, got, own)

    def sum_all(v):
        v = v + core_swap(v)
        return v + x_swap(v)

    def sum_vectors(v):
        h = v.shape[-1] // 2
        other = core_swap(v)
        v = v + jnp.concatenate([other[..., h:], other[..., :h]], -1)
        return v + x_swap(v)

    def sum_halves(pair):
        both = sum_vectors(jnp.stack(pair))
        return both[0], both[1]

    def quarters(values, axis):
        core = lax.axis_index("tensor") % 2
        step = values.shape[axis] // 4
        return jnp.concatenate(
            [
                lax.dynamic_slice_in_dim(values, at * step, step, axis)
                for at in (core, 1 - core, 2 + core, 3 - core)
            ],
            axis,
        )

    def on_device(
        hidden_in, context, time_emb, text_lengths, positions, modulation,
        self_query, self_key, self_value, self_output, self_query_gain, self_key_gain,
        cross_query, cross_key, cross_value, cross_output, cross_query_gain, cross_key_gain,
        norm_weight, norm_bias, ffn_up, ffn_down, out_cotangent,
    ):
        heads = self_query_gain.shape[0]
        half = positions.shape[1] // 2
        wide = heads * HEAD
        r_dp = self_query.shape[0]
        hid = ffn_up.shape[1]
        spare = -hid % HC

        texts = context.shape[1]
        quarter = half // 2
        g_cols = self_query_gain.shape[1]
        gains = [self_query_gain, self_key_gain, cross_query_gain, cross_key_gain]
        flat = jnp.concatenate([modulation, norm_weight[None], norm_bias[None]])
        side = jnp.pad(jnp.concatenate(gains), ((0, 0), (0, r_dp - g_cols)))
        small = jnp.concatenate([flat, side])
        small = jnp.pad(small, ((0, HEAD - small.shape[0]), (0, 0))).T.astype(BF)
        own_self = jnp.concatenate([self_query, self_key, self_value, self_output.T], axis=1).astype(BF)
        own_cross = jnp.concatenate([cross_query, cross_key, cross_value, cross_output.T], axis=1).astype(BF)
        padded = [jnp.pad(w, ((0, 0), (0, spare))) for w in (ffn_up.astype(BF), ffn_down.T.astype(BF))]
        hid_low = hid + spare
        own_ffn = [
            jnp.concatenate([w[:, j * HC : (j + 1) * HC] for w in padded], axis=1) for j in range(hid_low // HC)
        ]
        tables = rotary_tables(quarters(positions, 1), HEAD)
        text_bias = jnp.where(quarters(jnp.arange(4 * texts), 0) < text_lengths[0], 0.0, -1e30)
        text_bias = text_bias.astype(F32)[:, None]

        st = self_forward(
            hidden_in, context[0], out_cotangent, time_emb[0], tables, small,
            own_self, own_cross, own_ffn[0], n_dp, heads,
        )
        st |= cross_forward(st, text_bias, own_ffn[1], own_ffn[2], n_dp, heads)
        d = lax.axis_index("dp")
        cosine, sine = ((t[:half], t[half:]) for t in tables)
        s0, s1, s2, s3, s4, s5, norm_gain, norm_shift = (st["shifts"][i : i + 1] for i in range(8))
        sq_gain, sk_gain, cq_gain, ck_gain = (
            st["gains"][i * heads : (i + 1) * heads].reshape(1, wide) for i in range(4)
        )
        ones = jnp.ones((1, D), F32)
        w_self, w_cross = [st["w_self"]], [st["w_cross"]]
        w_ffn = [st["f0"], st["f1"], st["f2"]]
        at_o, at_cq, at_ck, at_co = 3 * wide, 0, wide, 3 * wide

        def both(name):
            return [st[name + "0"], st[name + "1"]]

        def four(name):
            return [[st[name + "0"], st[name + "1"]], [st[name + "2"], st[name + "3"]]]

        first = lax.axis_index("tensor") < 2
        g = [jnp.where(first, out_cotangent, st["g_got"]), jnp.where(first, st["g_got"], out_cotangent)]
        ctx = [st[f"c{i}"] for i in range(4)]
        self_rows, cross_rows, ffn_rows = four("x"), four("y"), four("z")
        qk, v, stat, q, k, attn, lse = (both(name) for name in ("qk", "v", "stat", "q", "k", "attn", "lse"))
        self_chip, self_far, after_self = both("chip"), both("far"), both("after")
        ck_raw, cv, ck_stat, ck = st["ck_raw"], st["cv"], st["ck_stat"], st["ck"]
        cq_raw, cq_stat, cq, cattn, clse = (both(name) for name in ("cq_raw", "cq_stat", "cq", "cattn", "clse"))
        after_cross = both("after_c")

        def with_peer(rows):
            return [rows, core_swap(rows)]

        dffn = [with_peer((a.astype(F32) * s5).astype(BF)) for a in g]
        dact = [expand(a, w_ffn, HC, hid_low) for a in dffn]
        act, dpre, mine, theirs = zip(*(feed(ffn_rows[i], dact[i], w_ffn, 0) for i in range(2)))
        ffn_chip = [join(a, b) for a, b in zip(mine, theirs)]
        ffn_far = [x_swap(a) for a in ffn_chip]
        g_c, rows, sums_f = zip(
            *(norm_backward(g[i], after_cross[i], ffn_chip[i], ffn_far[i], 1.0 + s4, ones) for i in range(2))
        )
        down_grad = full_grads(dffn[0] + dffn[1], act)
        down_grad = lax.psum_scatter(down_grad, "dp", scatter_dimension=0, tiled=True).astype(F32)
        up_grad = full_grads(ffn_rows[0] + ffn_rows[1], dpre)
        up_grad = lax.psum_scatter(up_grad, "dp", scatter_dimension=0, tiled=True).astype(F32)

        dcross = [with_peer(a) for a in rows]
        sofar = ()
        dcq = []
        for i in range(2):
            a, *sofar = attend_back(dcross[i], w_cross, at_co, cq[i], [ck], [cv], text_bias, clse[i], sofar)
            dcq.append(a)
        dck, dcv = sofar
        dcq_low, mine, theirs, cq_gain_grad = [], [], [], 0.0
        for i in range(2):
            raws = [(cq_raw[i], 0, 0)]
            dots, grad = root_dots([dcq[i]], raws, [cq_stat[i]], [cq_gain], None, wide)
            cq_gain_grad = cq_gain_grad + grad[0]
            low, a, b = root_back(
                [dcq[i]], raws, [cq_stat[i]], [sum_vectors(dots)], [cq_gain], None, w_cross, at_cq, wide, 1
            )
            dcq_low.append(low)
            mine.append(a)
            theirs.append(b)
        cross_in_chip = [join(a, b) for a, b in zip(mine, theirs)]
        cross_in_far = [x_swap(a) for a in cross_in_chip]
        g_s, rows, sums_c = zip(
            *(norm_backward(g_c[i], after_self[i], cross_in_chip[i], cross_in_far[i], norm_gain, s2) for i in range(2))
        )
        raws = [(ck_raw, 0, 0)]
        dots, grad = root_dots([dck], raws, [ck_stat], [ck_gain], None, wide)
        ck_gain_grad = grad[0]
        dots = jnp.concatenate(sum_halves((dots[:, : 2 * texts], dots[:, 2 * texts :])), -1)
        dckv, mine0, mine1, theirs0, theirs1 = root_back(
            [dck], raws, [ck_stat], [dots], [ck_gain], dcv, w_cross, at_ck, wide, 2
        )
        chip = [join(mine0, theirs0), join(mine1, theirs1)]
        context_grad = (own_half(chip).astype(F32) + x_swap(other_half(chip)).astype(F32)).astype(BF)
        cross_grad = scatter_dp(
            *weight_grads(
                [(cross_rows[0] + cross_rows[1], dcq_low), (ctx, [dckv]), (dcross[0] + dcross[1], cattn)], n_dp
            )
        )

        dself = [with_peer(a) for a in rows]
        oT_grad = scatter_dp(*weight_grads([(dself[0] + dself[1], attn)], n_dp))
        sofar = ()
        dq = []
        for i in range(2):
            a, *sofar = attend_back(dself[i], w_self, at_o, q[i], k, v, None, lse[i], sofar)
            dq.append(a)
        dk, dv = sofar
        dk, dv = (dk[:half], dk[half:]), (dv[:half], dv[half:])
        dqkv, mine, theirs = [], [], []
        turned, dots, self_gain_grad = [], [], 0.0
        for i in range(2):
            raws = [(qk[i], 0, 0), (qk[i], wide, 1)]
            tq, tk, dot_q, dot_k, grad = root_dots(
                [dq[i], dk[i]], raws, [stat[i]] * 2, [sq_gain, sk_gain], (cosine[i], sine[i]), wide
            )
            self_gain_grad = self_gain_grad + grad[:2]
            turned.append((tq, tk))
            dots.append(jnp.stack([dot_q, dot_k]))
        dots = sum_halves(dots)
        for i in range(2):
            raws = [(qk[i], 0, 0), (qk[i], wide, 1)]
            low, a, b = root_back(
                list(turned[i]), raws, [stat[i]] * 2, [dots[i][0], dots[i][1]],
                [sq_gain, sk_gain], dv[i], w_self, 0, wide, 1,
            )
            dqkv.append(low)
            mine.append(a)
            theirs.append(b)
        qkv_grad = scatter_dp(*weight_grads([(self_rows[0] + self_rows[1], dqkv)], n_dp))
        chip = [join(a, b) for a, b in zip(mine, theirs)]
        ones_row = jnp.ones((1, D), F32)
        hidden_grad, _, sums_s = norm_backward(
            own_half(g_s), hidden_in, own_half(chip), x_swap(other_half(chip)), 1.0 + s1, ones_row
        )
        hidden_grad = hidden_grad.astype(BF)

        mine, theirs = zip(*(contract(a, w_ffn, HC) for a in act))
        chip = [join(a, b) for a, b in zip(mine, theirs)]
        ffn_branch = own_half(chip).astype(F32) + x_swap(other_half(chip)).astype(F32)
        block_out = (own_half(after_cross) + ffn_branch * s5).astype(BF)

        self_branch = own_half(self_chip).astype(F32) + own_half(self_far).astype(F32)
        sums_f = own_half(sums_f)
        sums_c = own_half(sums_c)
        sums_own = jnp.stack(
            [
                jnp.sum(sums_s[:8], 0),
                jnp.sum(sums_s[8:], 0),
                jnp.sum(own_half(g_s) * self_branch, 0),
                jnp.sum(sums_f[:8], 0),
                jnp.sum(sums_f[8:], 0),
                jnp.sum(out_cotangent.astype(F32) * ffn_branch, 0),
                jnp.sum(sums_c[8:], 0),
                jnp.sum(sums_c[:8], 0),
            ]
        )
        sums_clip = sum_all(sums_own)
        time_grad = sums_clip[:6]
        low_sums = sums_clip.reshape(8, n_dp, r_dp).transpose(1, 0, 2).reshape(n_dp, -1)
        gain_grads = jnp.stack([self_gain_grad[0], self_gain_grad[1], cq_gain_grad, ck_gain_grad])
        low_gains = gain_grads.reshape(4 * heads, n_dp, g_cols).transpose(1, 0, 2).reshape(n_dp, -1)
        packed = jnp.concatenate([low_sums, low_gains], axis=1).astype(BF)
        packed = jnp.pad(packed, ((0, 0), (0, -packed.shape[1] % 1024))).reshape(n_major, 2, 8, -1)
        minor = d % 2
        tiny = scatter_dp(
            lax.dynamic_slice_in_dim(packed, 1 - minor, 1, 1)[:, 0],
            lax.dynamic_slice_in_dim(packed, minor, 1, 1)[:, 0],
        ).reshape(-1)
        eight = tiny[: 8 * r_dp].reshape(8, r_dp)
        gains_out = tiny[8 * r_dp : 8 * r_dp + 4 * heads * g_cols].reshape(4, heads, g_cols)

        return (
            block_out,
            hidden_grad,
            context_grad[None],
            time_grad[None],
            eight[:6],
            qkv_grad[:, :wide],
            qkv_grad[:, wide : 2 * wide],
            qkv_grad[:, 2 * wide :],
            oT_grad.T,
            gains_out[0],
            gains_out[1],
            cross_grad[:, :wide],
            cross_grad[:, wide : 2 * wide],
            cross_grad[:, 2 * wide : 3 * wide],
            cross_grad[:, 3 * wide :].T,
            gains_out[2],
            gains_out[3],
            eight[6],
            eight[7],
            up_grad[:, :hid],
            down_grad[:, :hid].T,
        )

    rows = P(("dp", "tensor"), None)
    col = P("dp", "tensor")
    row = P("tensor", "dp")
    text = P("dp", "tensor", None)
    time = P("dp", None, None)
    one = P("dp")
    ins = (
        rows, text, time, one, P(None, "dp"), P(None, "dp"),
        col, col, col, row, row, row,
        col, col, col, row, row, row,
        one, one, col, row, rows,
    )
    outs = (
        rows, rows, text, time, P(None, "dp"),
        col, col, col, row, row, row,
        col, col, col, row, row, row,
        one, one, col, row,
    )
    return jax.shard_map(on_device, mesh=mesh, in_specs=ins, out_specs=outs, check_vma=False)
```

```python
import math

import jax
import jax.numpy as jnp
from jax import lax
from jax.experimental import pallas as pl
from jax.experimental.pallas import tpu as pltpu
from jax.sharding import PartitionSpec as P

D = 1536
HEAD = 128
EPS = 1e-6
BF = jnp.bfloat16
F32 = jnp.float32
FACTOR = 1.0 / math.sqrt(HEAD)
GELU = math.sqrt(2.0 / math.pi)
CUBE = 0.044715
MESH = pl.DeviceIdType.MESH


def dot_nn(a, b):
    return lax.dot_general(a, b, (((1,), (0,)), ((), ())), preferred_element_type=F32)


def dot_nt(a, b):
    return lax.dot_general(a, b, (((1,), (1,)), ((), ())), preferred_element_type=F32)


def dot_tn(a, b):
    return lax.dot_general(a, b, (((0,), (0,)), ((), ())), preferred_element_type=F32)


def shape(dims, dtype):
    return jax.ShapeDtypeStruct(dims, dtype)


def run(kernel, outs, blocks, far=(), scratch=(), flops=0, exps=0, limit=60):
    moved = sum(math.prod(v.shape) * v.dtype.itemsize for v in (*blocks, *far, *outs))
    return pl.pallas_call(
        kernel,
        out_shape=tuple(outs),
        in_specs=[pl.BlockSpec(memory_space=pltpu.VMEM)] * len(blocks)
        + [pl.BlockSpec(memory_space=pl.ANY)] * len(far),
        out_specs=tuple(pl.BlockSpec(memory_space=pltpu.VMEM) for _ in outs),
        scratch_shapes=list(scratch),
        compiler_params=pltpu.CompilerParams(vmem_limit_bytes=limit * 2**20),
        cost_estimate=pl.CostEstimate(flops=int(flops), bytes_accessed=moved, transcendentals=int(exps)),
    )(*blocks, *far)


def load(pieces, w, sems, first=0):
    n = len(pieces)
    r, c = w.shape[0] // n, w.shape[1]
    if n == 1:
        copy = pltpu.make_async_copy(pieces[0].at[:, pl.ds(first, c)], w, sems.at[0])
        copy.start()
        return [copy]
    d = lax.axis_index("dp")
    major, minor = d // 2, d % 2
    copies = []
    for i, piece in enumerate(pieces):
        t, flip = i // 2, i % 2
        block = 2 * lax.rem(major + t, n // 2) + (1 - minor if flip else minor)
        rows = pl.ds(pl.multiple_of(block * r, 16), r)
        copy = pltpu.make_async_copy(piece.at[:, pl.ds(first, c)], w.at[rows], sems.at[i])
        copy.start()
        copies.append(copy)
    return copies


def wait(copies):
    for copy in copies:
        copy.wait()


def weight(n, c):
    return [pltpu.VMEM((D, c), BF), pltpu.SemaphoreType.DMA((n,))]


def to_rows(columns, count):
    lane = lax.broadcasted_iota(jnp.int32, (count, 128), 1)
    out = jnp.zeros((count, 128), F32)
    for i, column in enumerate(columns):
        out = jnp.where(lane == i, column, out)
    return jnp.transpose(out)[:8]


def to_columns(rows):
    return jnp.transpose(jnp.concatenate([rows] * 16, axis=0))


def turn(values, cosine, sine):
    even = lax.broadcasted_iota(jnp.int32, values.shape, 1) % 2 == 0
    partner = jnp.where(even, pltpu.roll(values, HEAD - 1, 1), pltpu.roll(values, 1, 1))
    return values * cosine + partner * sine


def norm_of(v):
    center = v - jnp.mean(v, axis=-1, keepdims=True)
    r = lax.rsqrt(jnp.mean(center * center, axis=-1, keepdims=True) + EPS)
    return center * r, r


STEP = 32


def over_rows(count, body):
    def one(i, carry):
        body(pl.ds(pl.multiple_of(i * STEP, STEP), STEP))
        return carry

    lax.fori_loop(0, count // STEP, one, 0)


def norm_first(v, m, t):
    def kernel(v_ref, m_ref, t_ref, rows_ref):
        def body(s):
            n, _ = norm_of(v_ref[s].astype(F32))
            rows_ref[s] = (n * m_ref[...] + t_ref[...]).astype(BF)

        over_rows(v_ref.shape[0], body)

    return run(kernel, [shape(v.shape, BF)], [v, m, t], flops=1e9)[0]


def norm_forward(v, chip, far_chip, s, m, t):
    def kernel(v_ref, a_ref, b_ref, s_ref, m_ref, t_ref, out_ref, rows_ref):
        def body(i):
            branch = a_ref[i].astype(F32) + b_ref[i].astype(F32)
            out = v_ref[i].astype(F32) + branch * s_ref[...]
            out_ref[i] = out
            n, _ = norm_of(out)
            rows_ref[i] = (n * m_ref[...] + t_ref[...]).astype(BF)

        over_rows(v_ref.shape[0], body)

    return run(
        kernel, [shape(v.shape, F32), shape(v.shape, BF)], [v, chip, far_chip, s, m, t], flops=1e9
    )


def norm_backward(g, v, chip, far_chip, m, s):
    def kernel(g_ref, v_ref, a_ref, b_ref, m_ref, s_ref, out_ref, rows_ref, sum_ref):
        sum_ref[...] = jnp.zeros_like(sum_ref)

        def body(i):
            da = a_ref[i].astype(F32) + b_ref[i].astype(F32)
            n, r = norm_of(v_ref[i].astype(F32))
            dn = da * m_ref[...]
            mean = jnp.mean(dn, axis=-1, keepdims=True)
            along = jnp.mean(dn * n, axis=-1, keepdims=True)
            out = g_ref[i].astype(F32) + r * (dn - mean - n * along)
            out_ref[i] = out
            rows_ref[i] = (out * s_ref[...]).astype(BF)
            dan = da * n
            for k in range(STEP // 8):
                sum_ref[:8] += da[k * 8 : k * 8 + 8]
                sum_ref[8:] += dan[k * 8 : k * 8 + 8]

        over_rows(g_ref.shape[0], body)

    return run(
        kernel,
        [shape(g.shape, F32), shape(g.shape, BF), shape((16, D), F32)],
        [g, v, chip, far_chip, m, s],
        flops=1e9,
    )


def hold(v, after):
    def kernel(v_ref, *refs):
        refs[-1][...] = v_ref[...]

    return run(kernel, [shape(v.shape, v.dtype)], [v], after)[0]


def project(xs, pieces, first, squares, lows, wide):
    total = sum(x.shape[0] for x in xs)
    cols = (squares + lows) * wide
    n = len(pieces)
    outs = [shape((total, squares * wide), F32)] * (squares > 0)
    outs += [shape((total, lows * wide), BF)] * (lows > 0)
    outs += [shape((8, total), F32)] * (squares > 0)

    def kernel(*refs):
        x_refs, refs = refs[: len(xs)], refs[len(xs) :]
        piece_refs, refs = refs[:n], refs[n:]
        out_refs, (w, sems) = list(refs[:-2]), refs[-2:]
        wait(load(piece_refs, w, sems, first))
        at = 0
        for x_ref in x_refs:
            m = x_ref.shape[0]
            value = dot_nn(x_ref[...], w[...])
            columns = []
            for i in range(squares):
                part = value[:, i * wide : (i + 1) * wide]
                columns.append(jnp.sum(part * part, axis=1, keepdims=True))
            if squares:
                out_refs[0][at : at + m] = value[:, : squares * wide]
                out_refs[-1][:, at : at + m] = to_rows(columns, m)
            if lows:
                out_refs[1 if squares else 0][at : at + m] = value[:, squares * wide :].astype(BF)
            at += m

    return run(kernel, outs, xs, pieces, weight(n, cols), flops=2 * total * D * cols)


def normalize(raws, stats, gains, tables, wide):
    count = len(gains)
    parts = len(raws)
    outs = [shape((r.shape[0], wide), BF) for r in raws for _ in range(count)]

    def kernel(*refs):
        raw_refs, refs = refs[:parts], refs[parts:]
        stat_refs, refs = refs[:parts], refs[parts:]
        gain_refs, refs = refs[:count], refs[count:]
        if tables:
            cos_refs, sin_refs, refs = refs[:parts], refs[parts : 2 * parts], refs[2 * parts :]
        for p in range(parts):
            scale = lax.rsqrt(to_columns(stat_refs[p][...]) / D + EPS)
            for i in range(count):
                for h in range(wide // HEAD):
                    lanes = slice(i * wide + h * HEAD, i * wide + (h + 1) * HEAD)
                    own = slice(h * HEAD, (h + 1) * HEAD)
                    value = raw_refs[p][:, lanes] * scale[:, i : i + 1] * gain_refs[i][:, own]
                    if tables:
                        value = turn(value, cos_refs[p][...], sin_refs[p][...])
                    refs[p * count + i][:, own] = value.astype(BF)

    args = [*raws, *stats, *gains]
    if tables:
        args += [*tables[0], *tables[1]]
    return run(kernel, outs, args, flops=1e9)


QB = 256


def attend(q, ks, vs, bias, pieces, first):
    rows, wide = q.shape
    heads = wide // HEAD
    nk = sum(k.shape[0] for k in ks)
    n = len(pieces)
    parts = len(ks)
    half = rows // 2
    biases = [] if bias is None else [bias]

    def kernel(*refs):
        q_ref, k_refs, v_refs = refs[0], refs[1 : 1 + parts], refs[1 + parts : 1 + 2 * parts]
        refs = refs[1 + 2 * parts :]
        b_refs, refs = refs[: len(biases)], refs[len(biases) :]
        piece_refs, (out_ref, lse_ref, mine_ref, theirs_ref, w, sems) = refs[:n], refs[n:]
        copies = load(piece_refs, w, sems, first)
        lse_ref[...] = jnp.zeros_like(lse_ref)
        for h in range(heads):
            lanes = slice(h * HEAD, (h + 1) * HEAD)
            k = jnp.concatenate([r[:, lanes] for r in k_refs]) if parts > 1 else k_refs[0][:, lanes]
            v = jnp.concatenate([r[:, lanes] for r in v_refs]) if parts > 1 else v_refs[0][:, lanes]
            for b in range(rows // QB):
                block = slice(b * QB, (b + 1) * QB)
                s = dot_nt(k, q_ref[block, lanes]) * FACTOR
                if biases:
                    s = s + b_refs[0][...]
                top = jnp.max(s, axis=0, keepdims=True)
                e = jnp.exp(s - top)
                total = jnp.sum(e, axis=0, keepdims=True)
                lse_ref[h : h + 1, block] = top + jnp.log(total)
                o = dot_tn(v, e.astype(BF)) * (1.0 / total)
                out_ref[block, lanes] = jnp.transpose(o).astype(BF)
        wait(copies)
        mine_ref[...] = dot_nt(out_ref[:half], w[...])
        theirs_ref[...] = dot_nt(out_ref[half:], w[...]).astype(BF)

    return run(
        kernel,
        [shape((rows, wide), BF), shape((8, rows), F32), shape((half, D), F32), shape((half, D), BF)],
        [q, *ks, *vs, *biases],
        pieces,
        weight(n, wide),
        flops=2 * rows * wide * (2 * nk + D),
        exps=rows * nk * heads,
    )


def attend_back(xs, pieces, first, q, ks, vs, bias, lse, sofar):
    rows, wide = q.shape
    heads = wide // HEAD
    nk = sum(k.shape[0] for k in ks)
    n = len(pieces)
    parts = len(ks)
    biases = [] if bias is None else [bias]

    def kernel(*refs):
        x_refs, q_ref, refs = refs[:2], refs[2], refs[3:]
        k_refs, v_refs, lse_ref, refs = refs[:parts], refs[parts : 2 * parts], refs[2 * parts], refs[2 * parts + 1 :]
        b_refs, refs = refs[: len(biases)], refs[len(biases) :]
        old_refs, refs = refs[: len(sofar)], refs[len(sofar) :]
        piece_refs, (dq_ref, dk_ref, dv_ref, w, sems, do_ref) = refs[:n], refs[n:]
        wait(load(piece_refs, w, sems, first))
        for i in range(2):
            m = x_refs[i].shape[0]
            do_ref[i * m : (i + 1) * m] = dot_nn(x_refs[i][...], w[...]).astype(BF)
        for h in range(heads):
            lanes = slice(h * HEAD, (h + 1) * HEAD)
            k = jnp.concatenate([r[:, lanes] for r in k_refs]) if parts > 1 else k_refs[0][:, lanes]
            v = jnp.concatenate([r[:, lanes] for r in v_refs]) if parts > 1 else v_refs[0][:, lanes]
            for b in range(rows // QB):
                block = slice(b * QB, (b + 1) * QB)
                qb = q_ref[block, lanes]
                do = do_ref[block, lanes]
                s = dot_nt(k, qb) * FACTOR
                if biases:
                    s = s + b_refs[0][...]
                p = jnp.exp(s - lse_ref[h : h + 1, block])
                dp = dot_nt(v, do)
                center = jnp.sum(p * dp, axis=0, keepdims=True)
                ds = (p * (dp - center)).astype(BF)
                dq_ref[block, lanes] = dot_tn(ds, k) * FACTOR
                dk = dot_nn(ds, qb) * FACTOR
                dv = dot_nn(p.astype(BF), do)
                if b == 0 and not sofar:
                    dk_ref[:, lanes] = dk
                    dv_ref[:, lanes] = dv
                elif b == 0:
                    dk_ref[:, lanes] = old_refs[0][:, lanes] + dk
                    dv_ref[:, lanes] = old_refs[1][:, lanes] + dv
                else:
                    dk_ref[:, lanes] += dk
                    dv_ref[:, lanes] += dv

    return run(
        kernel,
        [shape((rows, wide), F32), shape((nk, wide), F32), shape((nk, wide), F32)],
        [*xs, q, *ks, *vs, lse, *biases, *sofar],
        pieces,
        weight(n, wide) + [pltpu.VMEM((rows, wide), BF)],
        flops=2 * rows * wide * (5 * nk + D),
        exps=rows * nk * heads,
    )


def root_dots(dys, raws, stats, gains, tables, wide):
    count = len(gains)
    outs = [shape(dy.shape, F32) for dy in dys] if tables else []
    outs += [shape((8, dy.shape[0]), F32) for dy in dys]
    outs += [shape((8, wide), F32)]

    def kernel(*refs):
        dy_refs, refs = refs[:count], refs[count:]
        raw_refs, refs = refs[:count], refs[count:]
        stat_refs, refs = refs[:count], refs[count:]
        gain_refs, refs = refs[:count], refs[count:]
        if tables:
            cos_ref, sin_ref, refs = refs[0], refs[1], refs[2:]
            turned, refs = refs[:count], refs[count:]
        dot_refs, grad_ref = refs[:count], refs[count]
        grad_ref[...] = jnp.zeros_like(grad_ref)
        for i in range(count):
            row = raws[i][2]
            m = dy_refs[i].shape[0]
            scale = lax.rsqrt(to_columns(stat_refs[i][...]) / D + EPS)[:, row : row + 1]
            dots = jnp.zeros((m, 1), F32)
            for h in range(wide // HEAD):
                own = slice(h * HEAD, (h + 1) * HEAD)
                dy = dy_refs[i][:, own]
                if tables:
                    dy = turn(dy, cos_ref[...], -sin_ref[...])
                    turned[i][:, own] = dy
                c = raws[i][1] + h * HEAD
                both = raw_refs[i][:, c : c + HEAD] * dy
                dots = dots + jnp.sum(both * gain_refs[i][:, own], axis=1, keepdims=True)
                grad_ref[i : i + 1, own] = jnp.sum(both * scale, axis=0, keepdims=True)
            dot_refs[i][...] = to_rows([dots], m)

    args = [*dys, *(r[0] for r in raws), *stats, *gains]
    if tables:
        args += [*tables]
    return run(kernel, outs, args, flops=1e9)


def root_back(dys, raws, stats, dots, gains, dv, pieces, first, wide, halves):
    count = len(gains)
    extra = 0 if dv is None else 1
    rows = dys[0].shape[0]
    cols = (count + extra) * wide
    n = len(pieces)
    part = rows // (2 * halves)
    vs = [] if dv is None else [dv]

    def kernel(*refs):
        dy_refs, refs = refs[:count], refs[count:]
        raw_refs, refs = refs[:count], refs[count:]
        stat_refs, refs = refs[:count], refs[count:]
        dot_refs, refs = refs[:count], refs[count:]
        gain_refs, refs = refs[:count], refs[count:]
        v_refs, refs = refs[:extra], refs[extra:]
        piece_refs, refs = refs[:n], refs[n:]
        low_ref, refs = refs[0], refs[1:]
        mine_refs, their_refs, (w, sems) = refs[:halves], refs[halves : 2 * halves], refs[2 * halves :]
        copies = load(piece_refs, w, sems, first)
        for i in range(count):
            row = raws[i][2]
            scale = lax.rsqrt(to_columns(stat_refs[i][...]) / D + EPS)[:, row : row + 1]
            along = scale * scale * scale * to_columns(dot_refs[i][...])[:, 0:1] / D
            for h in range(wide // HEAD):
                own = slice(h * HEAD, (h + 1) * HEAD)
                c = raws[i][1] + h * HEAD
                dx = scale * gain_refs[i][:, own] * dy_refs[i][:, own] - raw_refs[i][:, c : c + HEAD] * along
                low_ref[:, i * wide + h * HEAD : i * wide + (h + 1) * HEAD] = dx.astype(BF)
        if extra:
            low_ref[:, count * wide :] = v_refs[0][...].astype(BF)
        wait(copies)
        for j in range(halves):
            at = 2 * part * j
            mine_refs[j][...] = dot_nt(low_ref[at : at + part], w[...])
            their_refs[j][...] = dot_nt(low_ref[at + part : at + 2 * part], w[...]).astype(BF)

    return run(
        kernel,
        [shape((rows, cols), BF)]
        + [shape((part, D), F32)] * halves
        + [shape((part, D), BF)] * halves,
        [*dys, *(r[0] for r in raws), *stats, *dots, *gains, *vs],
        pieces,
        weight(n, cols),
        flops=2 * rows * cols * D,
    )


HC = 768


def expand(xs, pieces, first, hid):
    rows = sum(x.shape[0] for x in xs)
    n = len(pieces)

    def kernel(*refs):
        x_refs, piece_refs, (out_ref, w, sems) = refs[: len(xs)], refs[len(xs) : len(xs) + n], refs[len(xs) + n :]
        chunks = [load(piece_refs[j : j + 1], w.at[j], sems.at[j], first) for j in range(hid // HC)]
        for j in range(hid // HC):
            wait(chunks[j])
            at = 0
            for x_ref in x_refs:
                m = x_ref.shape[0]
                out_ref[at : at + m, j * HC : (j + 1) * HC] = dot_nn(x_ref[...], w[j]).astype(BF)
                at += m

    return run(
        kernel,
        [shape((rows, hid), BF)],
        xs,
        pieces,
        [pltpu.VMEM((hid // HC, D, HC), BF), pltpu.SemaphoreType.DMA((hid // HC, 1))],
        flops=2 * rows * D * hid,
    )[0]


def feed(xs, dact, pieces, first):
    rows, hid = dact.shape
    n = len(pieces)
    m = rows // 2

    def kernel(*refs):
        x_refs, dact_ref, piece_refs = refs[:2], refs[2], refs[3 : 3 + n]
        act_ref, dpre_ref, mine_ref, theirs_ref, w, sems = refs[3 + n :]
        chunks = [load(piece_refs[j : j + 1], w.at[j], sems.at[j], first) for j in range(hid // HC)]
        for j in range(hid // HC):
            cols = slice(j * HC, (j + 1) * HC)
            wait(chunks[j])
            for i in range(2):
                own = slice(i * m, (i + 1) * m)
                u = dot_nn(x_refs[i][...], w[j])
                sq = u * u
                th = jnp.tanh(u * (GELU + GELU * CUBE * sq))
                near = 0.5 + 0.5 * th
                act_ref[own, cols] = (u * near).astype(BF)
                slope = near + u * near * (1.0 - th) * (GELU + 3 * GELU * CUBE * sq)
                dpre_ref[own, cols] = (dact_ref[own, cols].astype(F32) * slope).astype(BF)
        for i in range(2):
            own = slice(i * m, (i + 1) * m)
            total = dot_nt(dpre_ref[own, :HC], w[0])
            for j in range(1, hid // HC):
                total = total + dot_nt(dpre_ref[own, j * HC : (j + 1) * HC], w[j])
            if i == 0:
                mine_ref[...] = total
            else:
                theirs_ref[...] = total.astype(BF)

    return run(
        kernel,
        [shape((rows, hid), BF), shape((rows, hid), BF), shape((m, D), F32), shape((m, D), BF)],
        [*xs, dact],
        pieces,
        [pltpu.VMEM((hid // HC, D, HC), BF), pltpu.SemaphoreType.DMA((hid // HC, 1))],
        flops=4 * rows * D * hid,
        exps=rows * hid,
        limit=60,
    )


def contract(act, pieces, first):
    rows, hid = act.shape
    n = len(pieces)
    m = rows // 2

    def kernel(*refs):
        act_ref, piece_refs, (mine_ref, theirs_ref, w, sems) = refs[0], refs[1 : 1 + n], refs[1 + n :]
        chunks = [load(piece_refs[j : j + 1], w.at[j], sems.at[j], first) for j in range(hid // HC)]
        for chunk in chunks:
            wait(chunk)
        for i in range(2):
            own = slice(i * m, (i + 1) * m)
            total = dot_nt(act_ref[own, :HC], w[0])
            for j in range(1, hid // HC):
                total = total + dot_nt(act_ref[own, j * HC : (j + 1) * HC], w[j])
            if i == 0:
                mine_ref[...] = total
            else:
                theirs_ref[...] = total.astype(BF)

    return run(
        kernel,
        [shape((m, D), F32), shape((m, D), BF)],
        [act],
        pieces,
        [pltpu.VMEM((hid // HC, D, HC), BF), pltpu.SemaphoreType.DMA((hid // HC, 1))],
        flops=2 * rows * D * hid,
    )


GC = 384


def full_grads(xs, ys):
    cols = ys[0].shape[1]
    most = sum(x.shape[0] for x in xs)

    def kernel(*refs):
        x_refs, y_refs, (out_ref, turned) = refs[: len(xs)], refs[len(xs) : -2], refs[-2:]
        row = 0
        for x_ref in x_refs:
            m = x_ref.shape[0]
            turned[:, row : row + m] = jnp.transpose(x_ref[...])
            row += m
        for c in range(0, cols, HC):
            lanes = slice(c, c + HC)
            for k in range(0, D, 512):
                row = 0
                total = None
                for y_ref in y_refs:
                    m = y_ref.shape[0]
                    term = dot_nn(turned[k : k + 512, row : row + m], y_ref[:, lanes])
                    total = term if total is None else total + term
                    row += m
                out_ref[k : k + 512, lanes] = total.astype(BF)

    return run(
        kernel,
        [shape((D, cols), BF)],
        [*xs, *ys],
        (),
        [pltpu.VMEM((D, most), BF)],
        flops=2 * most * D * cols,
        limit=60,
    )[0]


def weight_grads(pairs, n, after=()):
    widths = [ys[0].shape[1] for _, ys in pairs]
    cols = sum(widths)
    r = D // n
    flat = [a for xs, ys in pairs for a in (*xs, *ys)]
    out = shape((n // 2, r, cols), BF)
    most = max(sum(x.shape[0] for x in xs) for xs, _ in pairs)

    def kernel(*refs):
        ins, refs = refs[: len(flat)], refs[len(flat) + len(after) :]
        theirs_ref, mine_ref, total_ref, turned, sems = refs
        minor = lax.axis_index("dp") % 2
        at = 0
        col = 0
        copies = []
        for p, (xs, ys) in enumerate(pairs):
            x_refs, y_refs = ins[at : at + len(xs)], ins[at + len(xs) : at + len(xs) + len(ys)]
            at += len(xs) + len(ys)
            row = 0
            for x_ref in x_refs:
                m = x_ref.shape[0]
                turned[:, row : row + m] = jnp.transpose(x_ref[...])
                row += m
            for c in range(0, widths[p], GC):
                lanes = slice(c, c + GC)
                for k in range(0, D, 512):
                    row = 0
                    total = None
                    for y_ref in y_refs:
                        m = y_ref.shape[0]
                        term = dot_nn(turned[k : k + 512, row : row + m], y_ref[:, lanes])
                        total = term if total is None else total + term
                        row += m
                    total_ref[k : k + 512, col + c : col + c + GC] = total.astype(BF)
                for j in range(n // 2):
                    for flip, ref in ((1, theirs_ref), (0, mine_ref)):
                        block = 2 * j + (1 - minor if flip else minor)
                        copy = pltpu.make_async_copy(
                            total_ref.at[
                                pl.ds(pl.multiple_of(block * r, 16), r), pl.ds(col + c, GC)
                            ],
                            ref.at[j, :, pl.ds(col + c, GC)],
                            sems.at[(col + c) // GC, 2 * j + flip],
                        )
                        copy.start()
                        copies.append(copy)
            col += widths[p]
        wait(copies)

    moved = sum(math.prod(v.shape) * 2 for v in flat) + 2 * D * cols
    return pl.pallas_call(
        kernel,
        out_shape=(out, out),
        in_specs=[pl.BlockSpec(memory_space=pltpu.VMEM)] * len(flat)
        + [pl.BlockSpec(memory_space=pl.ANY)] * len(after),
        out_specs=(pl.BlockSpec(memory_space=pl.ANY),) * 2,
        scratch_shapes=[
            pltpu.VMEM((D, cols), BF),
            pltpu.VMEM((D, most), BF),
            pltpu.SemaphoreType.DMA((cols // GC, n)),
        ],
        compiler_params=pltpu.CompilerParams(vmem_limit_bytes=60 * 2**20),
        cost_estimate=pl.CostEstimate(
            flops=int(2 * most * D * cols), bytes_accessed=moved, transcendentals=0
        ),
    )(*flat, *after)


def run_remote(kernel, outs, far_outs, blocks, far, scratch, cid, flops):
    moved = sum(math.prod(v.shape) * v.dtype.itemsize for v in (*blocks, *outs))
    vmem, hbm = pl.BlockSpec(memory_space=pltpu.VMEM), pl.BlockSpec(memory_space=pl.ANY)
    return pl.pallas_call(
        kernel,
        out_shape=(*outs, *far_outs),
        in_specs=[vmem] * len(blocks) + [hbm] * len(far),
        out_specs=(vmem,) * len(outs) + (hbm,) * len(far_outs),
        scratch_shapes=list(scratch),
        compiler_params=pltpu.CompilerParams(
            vmem_limit_bytes=61 * 2**20, collective_id=cid, has_side_effects=True
        ),
        cost_estimate=pl.CostEstimate(flops=int(flops), bytes_accessed=moved, transcendentals=0),
    )(*blocks, *far)


def tensor_peers():
    t = lax.axis_index("tensor")
    core = t + 1 - 2 * lax.rem(t, 2)
    across = lax.rem(t + 2, 4)
    return t, core, across, 3 - t


def greet(n_dp):
    d = lax.axis_index("dp")
    barrier = pltpu.get_barrier_semaphore()
    for k in range(1, n_dp):
        pl.semaphore_signal(
            barrier, inc=1, device_id={"dp": lax.rem(d + k, n_dp)}, device_id_type=MESH
        )
    for peer in tensor_peers()[1:]:
        pl.semaphore_signal(barrier, inc=1, device_id={"tensor": peer}, device_id_type=MESH)
    pl.semaphore_wait(barrier, n_dp + 2)


def remote(src, dst, send, recv, **place):
    return pltpu.make_async_remote_copy(
        src_ref=src, dst_ref=dst, send_sem=send, recv_sem=recv, device_id=place, device_id_type=MESH
    )


class Gather:
    def __init__(self, ref, sems, n):
        d = lax.axis_index("dp")
        self.z, self.y = d // 2, lax.rem(d, 2)
        self.ref, self.sems, self.n, self.r = ref, sems, n, ref.shape[0] // (2 * n)
        self.cols = (0, ref.shape[1])
        self.near = (0, ref.shape[1] - 256)
        self.last = (ref.shape[1] - 256, ref.shape[1])

    def copy(self, o, kind, index, z, y, own, cols):
        start = (2 * o + (self.y if own else 1 - self.y)) * self.r
        block = self.ref.at[pl.ds(pl.multiple_of(start, 16), self.r), pl.ds(cols[0], cols[1] - cols[0])]
        sems = self.sems
        return remote(block, block, sems.at[2 * kind, index], sems.at[2 * kind + 1, index], dp=2 * z + y)

    def along(self, way, s, own=True):
        kind = (0 if way > 0 else 1) + (0 if own else 3)
        cols = self.cols if own else self.last
        return self.copy(self.z - way * s, kind, s, self.z + way, self.y, own, cols)

    def came(self, way, s, own=True):
        kind = (0 if way > 0 else 1) + (0 if own else 3)
        cols = self.cols if own else self.last
        return self.copy(self.z - way * (s + 1), kind, s, self.z - way, self.y, own, cols)

    def over(self, o, cols):
        return self.copy(o, 2, o, self.z, 1 - self.y, True, cols)

    def inside(self, o):
        return (o >= 0) & (o <= self.n - 1)

    def start(self, own, sem):
        start = (2 * self.z + self.y) * self.r
        copy = pltpu.make_async_copy(own, self.ref.at[pl.ds(pl.multiple_of(start, 16), self.r)], sem)
        copy.start()
        copy.wait()
        for way in (1, -1):
            pl.when(self.inside(self.z + way))(lambda way=way: self.along(way, 0).start())
        self.over(self.z, self.cols).start()

    def step(self, s):
        for way in (1, -1):

            @pl.when(self.inside(self.z - way * (s + 1)))
            def _(way=way):
                self.came(way, s).wait_recv()
                pl.when(self.inside(self.z + way))(lambda: self.along(way, s + 1).start())
                self.over(self.z - way * (s + 1), self.near).start()

        self.rest(s)

    def rest(self, s):
        if s == 0:
            self.copy(self.z, 2, self.z, self.z, 1 - self.y, False, self.cols).wait_recv()
        for way in (1, -1):
            if s == 0:
                pl.when(self.inside(self.z + way))(lambda way=way: self.along(way, 0, False).start())
            else:

                @pl.when(self.inside(self.z - way * s))
                def _(way=way):
                    self.came(way, s - 1, False).wait_recv()
                    if s < self.n - 1:
                        pl.when(self.inside(self.z + way))(lambda: self.along(way, s, False).start())

    def finish(self):
        self.rest(self.n - 1)
        for o in range(self.n):
            pl.when(self.z != o)(
                lambda o=o: self.copy(o, 2, o, self.z, 1 - self.y, False, self.near).wait_recv()
            )

    def drain(self):
        for own in (True, False):
            for s in range(self.n - 1):
                for way in (1, -1):
                    pl.when(self.inside(self.z - way * s) & self.inside(self.z + way))(
                        lambda s=s, way=way, own=own: self.along(way, s, own).wait_send()
                    )
        for o in range(self.n):
            pl.when(self.z == o)(lambda: self.over(self.z, self.cols).wait_send())
            pl.when(self.z != o)(lambda o=o: self.over(o, self.near).wait_send())


class Swap:
    def __init__(self, sems):
        self.sems, self.used, self.sent = sems, 0, []

    def start(self, src, dst, peer):
        k = self.used
        self.used += 1
        copy = remote(src, dst, self.sems.at[0, k], self.sems.at[1, k], tensor=peer)
        copy.start()
        self.sent.append(copy)
        return copy

    def settle(self):
        for copy in self.sent:
            copy.wait_send()
        self.sent = []


class Sums:
    def __init__(self, landed, sems, peers):
        self.landed, self.peers, self.used = landed, peers, 0
        self.swap = Swap(sems)

    def start(self, ref):
        k, c = self.used, ref.shape[1]
        self.used += 1
        copies = [
            self.swap.start(ref, self.landed.at[k, p, :, pl.ds(0, c)], peer)
            for p, peer in enumerate(self.peers)
        ]

        def collect():
            for copy in copies:
                copy.wait()
            stat_sum(ref, [self.landed[k, p, :, :c] for p in range(3)])

        return collect


def project_body(x_refs, w, first, out_ref, low_ref, stat_ref, squares, lows, wide):
    at = 0
    for x_ref in x_refs:
        m = x_ref.shape[0]
        value = dot_nn(x_ref[...], w[:, first : first + (squares + lows) * wide])
        columns = []
        for i in range(squares):
            part = value[:, i * wide : (i + 1) * wide]
            columns.append(jnp.sum(part * part, axis=1, keepdims=True))
        out_ref[at : at + m] = value[:, : squares * wide]
        stat_ref[:, at : at + m] = to_rows(columns, m)
        if lows:
            low_ref[at : at + m] = value[:, squares * wide :].astype(BF)
        at += m


def normalize_body(raw_ref, stat_ref, gains, cos, sin, out_refs, wide):
    scale = lax.rsqrt(to_columns(stat_ref[...]) / D + EPS)
    for i, out_ref in enumerate(out_refs):
        for h in range(wide // HEAD):
            lanes = slice(i * wide + h * HEAD, i * wide + (h + 1) * HEAD)
            value = raw_ref[:, lanes] * scale[:, i : i + 1] * gains[i][h]
            if cos is not None:
                value = turn(value, cos, sin)
            out_ref[:, h * HEAD : (h + 1) * HEAD] = value.astype(BF)


def attend_body(q_ref, k_refs, v_refs, bias_ref, out_ref, lse_ref):
    rows, wide = q_ref.shape
    lse_ref[...] = jnp.zeros_like(lse_ref)
    for h in range(wide // HEAD):
        lanes = slice(h * HEAD, (h + 1) * HEAD)
        k = jnp.concatenate([r[:, lanes] for r in k_refs]) if len(k_refs) > 1 else k_refs[0][:, lanes]
        v = jnp.concatenate([r[:, lanes] for r in v_refs]) if len(v_refs) > 1 else v_refs[0][:, lanes]
        for b in range(rows // QB):
            block = slice(b * QB, (b + 1) * QB)
            s = dot_nt(k, q_ref[block, lanes]) * FACTOR
            if bias_ref is not None:
                s = s + bias_ref[...]
            top = jnp.max(s, axis=0, keepdims=True)
            e = jnp.exp(s - top)
            total = jnp.sum(e, axis=0, keepdims=True)
            lse_ref[h : h + 1, block] = top + jnp.log(total)
            o = dot_tn(v, e.astype(BF)) * (1.0 / total)
            out_ref[block, lanes] = jnp.transpose(o).astype(BF)


def stat_sum(stat_ref, landed):
    h = stat_ref.shape[1] // 2
    other = landed[0] + landed[2]
    total = stat_ref[...] + landed[1]
    stat_ref[:, :h] = total[:, :h] + other[:, h:]
    stat_ref[:, h:] = total[:, h:] + other[:, :h]


def join_body(mine, got, chip):
    def body(i):
        chip[i] = (mine[i] + got[i].astype(F32)).astype(BF)

    over_rows(mine.shape[0], body)


def stream_body(base, chip, far, s, m, t, out_ref, rows_ref):
    def body(i):
        out = base(i) + (chip[i].astype(F32) + far[i].astype(F32)) * s
        out_ref[i] = out
        n, _ = norm_of(out)
        rows_ref[i] = (n * m + t).astype(BF)

    over_rows(rows_ref.shape[0], body)


def self_forward(hidden, context, cotangent, time_rows, tables, small, own_self, own_cross, own_first, n_dp, heads):
    quarter, texts = hidden.shape[0], context.shape[0]
    half, wide = 2 * quarter, heads * HEAD
    n = n_dp // 2
    r = D // n_dp
    g_cols = HEAD // n_dp
    rows = shape((quarter, D), BF)
    outs = dict(
        w_self=shape((D, 4 * wide), BF), w_cross=shape((D, 4 * wide), BF), got=rows,
        c0=shape((texts, D), BF), c1=shape((texts, D), BF), c2=shape((texts, D), BF), c3=shape((texts, D), BF),
        shifts=shape((8, D), F32), gains=shape((16, HEAD), F32),
        x0=rows, x1=rows, x2=rows, x3=rows,
        qk0=shape((half, 2 * wide), F32), qk1=shape((half, 2 * wide), F32),
        v0=shape((half, wide), BF), v1=shape((half, wide), BF),
        stat0=shape((8, half), F32), stat1=shape((8, half), F32),
        q0=shape((half, wide), BF), q1=shape((half, wide), BF),
        k0=shape((half, wide), BF), k1=shape((half, wide), BF),
        attn0=shape((half, wide), BF), attn1=shape((half, wide), BF),
        lse0=shape((8, half), F32), lse1=shape((8, half), F32),
        chip0=rows, chip1=rows, far0=rows, far1=rows,
        after0=shape((quarter, D), F32), after1=shape((quarter, D), F32),
        y0=rows, y1=rows, y2=rows, y3=rows,
        ck_raw=shape((4 * texts, wide), F32), cv=shape((4 * texts, wide), BF),
        ck_stat=shape((8, 4 * texts), F32), ck=shape((4 * texts, wide), BF),
        f0=shape((D, own_first.shape[1]), BF),
    )
    far_outs = dict(g_got=rows)
    blocks = [hidden, context, time_rows, tables[0], tables[1], small]
    far = [own_self, own_cross, own_first, cotangent]
    names = [*outs, *far_outs]

    def kernel(*refs):
        hid, ctx, times, cos, sin, small_ref = refs[:6]
        own1, own2, own3, cot = refs[6:10]
        o = dict(zip(names, refs[10 : 10 + len(names)]))
        all_small, ctx_got, theirs, landed, mine, stats_in, ring, near, cross_x, near_sums, small_sems, local = refs[
            10 + len(names) :
        ]
        t, core, across, diagonal = tensor_peers()
        first = t < 2
        d = lax.axis_index("dp")
        cores, xs = Swap(near), Swap(cross_x)
        greet(n_dp)

        g1 = Gather(o["w_self"], ring.at[0], n)
        g2 = Gather(o["w_cross"], ring.at[1], n)
        g3 = Gather(o["f0"], ring.at[2], n)
        g1.start(own1, local.at[0])
        own_small = all_small.at[pl.ds(pl.multiple_of(d * r, 16), r)]
        own_small[...] = small_ref[...]
        small_copies = []
        for k in range(1, n_dp):
            copy = remote(
                own_small, own_small, small_sems.at[0, k], small_sems.at[1, k], dp=lax.rem(d + k, n_dp)
            )
            copy.start()
            small_copies.append(copy)
        hid_copy = xs.start(hid, o["got"], across)
        ctx_copy = xs.start(ctx, ctx_got, across)
        g_copy = xs.start(cot, o["g_got"], across)

        for k in range(1, n_dp):
            source = lax.rem(d - k + n_dp, n_dp)
            block = all_small.at[pl.ds(pl.multiple_of(source * r, 16), r)]
            remote(block, block, small_sems.at[0, k], small_sems.at[1, k], dp=source).wait_recv()
        turned = jnp.transpose(all_small[...].astype(F32))
        o["shifts"][:6] = turned[:6] + times[...]
        o["shifts"][6:] = turned[6:8]
        at = lax.broadcasted_iota(jnp.int32, (D, HEAD), 0)
        to = lax.broadcasted_iota(jnp.int32, (D, HEAD), 1)
        pick = (at == (to // g_cols) * r + lax.rem(to, g_cols)).astype(F32)
        o["gains"][...] = dot_nn(turned[8:24].astype(BF), pick.astype(BF))
        g1.step(0)

        hid_copy.wait_recv()
        m_row, t_row = 1.0 + o["shifts"][1:2], o["shifts"][0:1]
        slots = [o["x0"], o["x1"], o["x2"], o["x3"]]

        def base(j):
            def pick_rows(i):
                own, other = hid[i].astype(F32), o["got"][i].astype(F32)
                return jnp.where(first, own, other) if j == 0 else jnp.where(first, other, own)

            return pick_rows

        arrivals = []
        for j in range(2):

            def body(i, j=j):
                v, _ = norm_of(base(j)(i))
                slots[2 * j][i] = (v * m_row + t_row).astype(BF)

            over_rows(quarter, body)
            arrivals.append(cores.start(slots[2 * j], slots[2 * j + 1], core))
        g1.step(1)
        ctx_copy.wait_recv()
        c_slots = [o["c0"], o["c1"], o["c2"], o["c3"]]
        a, b = ctx[...].astype(F32), ctx_got[...].astype(F32)
        c_slots[0][...] = jnp.where(first, a, b).astype(BF)
        c_slots[2][...] = jnp.where(first, b, a).astype(BF)
        c_arrivals = [cores.start(c_slots[2 * j], c_slots[2 * j + 1], core) for j in range(2)]
        for s in range(2, n - 1):
            g1.step(s)
        g2.start(own2, local.at[0])
        g1.finish()
        g2.step(0)

        qk, v = [o["qk0"], o["qk1"]], [o["v0"], o["v1"]]
        stat = [o["stat0"], o["stat1"]]
        w_self, w_cross = o["w_self"], o["w_cross"]

        sums = Sums(stats_in, near_sums, (core, across, diagonal))
        shared = []
        for j in range(2):
            arrivals[j].wait_recv()
            project_body(slots[2 * j : 2 * j + 2], w_self, 0, qk[j], v[j], stat[j], 2, 1, wide)
            shared.append(sums.start(stat[j]))
            if j == 0 and n > 2:
                g2.step(1)
        q, k = [o["q0"], o["q1"]], [o["k0"], o["k1"]]
        gain = [[o["gains"][i * heads + h : i * heads + h + 1] for h in range(heads)] for i in range(4)]
        for s in range(2, n - 1):
            g2.step(s)
        g3.start(own3, local.at[0])
        for j in range(2):
            shared[j]()
            own = slice(j * half, (j + 1) * half)
            normalize_body(qk[j], stat[j], gain[:2], cos[own], sin[own], [q[j], k[j]], wide)

        attn, lse = [o["attn0"], o["attn1"]], [o["lse0"], o["lse1"]]
        sent = []
        for j in range(2):
            attend_body(q[j], k, v, None, attn[j], lse[j])
            w_out = w_self[:, 3 * wide :]
            theirs[j] = dot_nt(attn[j][quarter:], w_out).astype(BF)
            sent.append(cores.start(theirs.at[j], landed.at[j], core))
            mine[j] = dot_nt(attn[j][:quarter], w_out)
            if j == 0:
                g3.step(0)
        chip, far_refs = [o["chip0"], o["chip1"]], [o["far0"], o["far1"]]
        crossed = []
        for j in range(2):
            sent[j].wait_recv()
            join_body(mine.at[j], landed.at[j], chip[j])
            crossed.append(xs.start(chip[j], far_refs[j], across))
        if n > 2:
            g3.step(1)

        g2.finish()
        for copy in c_arrivals:
            copy.wait_recv()
        project_body(c_slots, w_cross, wide, o["ck_raw"], o["cv"], o["ck_stat"], 1, 1, wide)
        halves = 2 * texts
        for j in range(2):
            part = o["ck_stat"].at[:, pl.ds(j * halves, halves)]
            sums.start(part)()
        normalize_body(o["ck_raw"], o["ck_stat"], gain[3:], None, None, [o["ck"]], wide)

        after = [o["after0"], o["after1"]]
        y_slots = [o["y0"], o["y1"], o["y2"], o["y3"]]
        shifts = o["shifts"]
        passed = []
        for j in range(2):
            crossed[j].wait_recv()
            stream_body(
                base(j), chip[j], far_refs[j], shifts[2:3], shifts[6:7], shifts[7:8], after[j], y_slots[2 * j]
            )
            passed.append(cores.start(y_slots[2 * j], y_slots[2 * j + 1], core))
            if j == 0:
                for s in range(2, n - 1):
                    g3.step(s)
        for copy in passed:
            copy.wait_recv()
        g_copy.wait_recv()
        g3.finish()
        for g in (g1, g2, g3):
            g.drain()
        for copy in small_copies:
            copy.wait_send()
        cores.settle()
        xs.settle()

    scratch = [
        pltpu.VMEM((D, HEAD), BF),
        pltpu.VMEM((texts, D), BF),
        pltpu.VMEM((2, quarter, D), BF),
        pltpu.VMEM((2, quarter, D), BF),
        pltpu.VMEM((2, quarter, D), F32),
        pltpu.VMEM((4, 3, 8, half), F32),
        pltpu.SemaphoreType.DMA((3, 10, n)),
        pltpu.SemaphoreType.DMA((2, 8)),
        pltpu.SemaphoreType.DMA((2, 8)),
        pltpu.SemaphoreType.DMA((2, 12)),
        pltpu.SemaphoreType.DMA((2, n_dp)),
        pltpu.SemaphoreType.DMA((1,)),
    ]
    got = run_remote(
        kernel, list(outs.values()), list(far_outs.values()), blocks, far, scratch, 1, 2e10
    )
    return dict(zip(names, got))


def cross_forward(state, cotangent, bias, own_second, own_third, n_dp, heads):
    quarter = state["y0"].shape[0]
    half, wide = 2 * quarter, heads * HEAD
    n = n_dp // 2
    rows = shape((quarter, D), BF)
    outs = dict(
        cq_raw0=shape((half, wide), F32), cq_raw1=shape((half, wide), F32),
        cq_stat0=shape((8, half), F32), cq_stat1=shape((8, half), F32),
        cq0=shape((half, wide), BF), cq1=shape((half, wide), BF),
        cattn0=shape((half, wide), BF), cattn1=shape((half, wide), BF),
        clse0=shape((8, half), F32), clse1=shape((8, half), F32),
        after_c0=shape((quarter, D), F32), after_c1=shape((quarter, D), F32),
        z0=rows, z1=rows, z2=rows, z3=rows, d0=rows, d1=rows, d2=rows, d3=rows,
        dact0=shape((2 * half, HC), BF), dact1=shape((2 * half, HC), BF),
        f1=shape((D, own_second.shape[1]), BF), f2=shape((D, own_third.shape[1]), BF),
    )
    far_outs = {}
    given = ("w_cross", "after0", "after1", "y0", "y1", "y2", "y3", "ck", "cv", "shifts", "gains", "g_got")
    blocks = [state[name] for name in given] + [bias, cotangent]
    far = [own_second, own_third, state["f0"]]
    names = [*outs, *far_outs]

    def kernel(*refs):
        i = dict(zip(given, refs))
        bias_ref, cot, own1, own2, f0 = refs[len(given) : len(given) + 5]
        refs = refs[len(given) + 5 :]
        o = dict(zip(names, refs))
        theirs, landed, mine, chips, fars, stats_in, w_down, ring, near, cross_x, near_sums, local = refs[len(names) :]
        t, core, across, diagonal = tensor_peers()
        cores, xs = Swap(near), Swap(cross_x)
        sums = Sums(stats_in, near_sums, (core, across, diagonal))
        greet(n_dp)
        g1 = Gather(o["f1"], ring.at[0], n)
        g2 = Gather(o["f2"], ring.at[1], n)
        g1.start(own1, local.at[0])
        first_down = pltpu.make_async_copy(f0.at[:, pl.ds(HC, HC)], w_down, local.at[1])
        first_down.start()
        d_slots = [o["d0"], o["d1"], o["d2"], o["d3"]]
        s_five = i["shifts"][5:6]
        first = t < 2
        sent_d = []

        def act_grad(part):
            down = o["f1"][:, HC:] if part else w_down[...]
            for p, slot in enumerate(d_slots):
                o[f"dact{part}"][p * quarter : (p + 1) * quarter] = dot_nn(slot[...], down).astype(BF)

        w = i["w_cross"]
        slots = [i["y0"], i["y1"], i["y2"], i["y3"]]
        raw, stat = [o["cq_raw0"], o["cq_raw1"]], [o["cq_stat0"], o["cq_stat1"]]
        q = [o["cq0"], o["cq1"]]
        attn, lse = [o["cattn0"], o["cattn1"]], [o["clse0"], o["clse1"]]
        gain = [i["gains"][2 * heads + h : 2 * heads + h + 1] for h in range(heads)]
        shared = []
        for j in range(2):
            project_body(slots[2 * j : 2 * j + 2], w, 0, raw[j], None, stat[j], 1, 0, wide)
            shared.append(sums.start(stat[j]))

            def scaled(rows, j=j):
                own, other = cot[rows].astype(F32), i["g_got"][rows].astype(F32)
                g = jnp.where(first, own, other) if j == 0 else jnp.where(first, other, own)
                d_slots[2 * j][rows] = (g * s_five).astype(BF)

            over_rows(quarter, scaled)
            sent_d.append(cores.start(d_slots[2 * j], d_slots[2 * j + 1], core))
        sent = []
        for j in range(2):
            shared[j]()
            normalize_body(raw[j], stat[j], [gain], None, None, [q[j]], wide)
            attend_body(q[j], [i["ck"]], [i["cv"]], bias_ref, attn[j], lse[j])
            w_out = w[:, 3 * wide :]
            theirs[j] = dot_nt(attn[j][quarter:], w_out).astype(BF)
            sent.append(cores.start(theirs.at[j], landed.at[j], core))
            mine[j] = dot_nt(attn[j][:quarter], w_out)
            if j == 0:
                g1.step(0)
        crossed = []
        for j in range(2):
            sent[j].wait_recv()
            join_body(mine.at[j], landed.at[j], chips.at[j])
            crossed.append(xs.start(chips.at[j], fars.at[j], across))
        for s in range(1, n - 2):
            g1.step(s)
        for copy in sent_d:
            copy.wait_recv()
        first_down.wait()
        act_grad(0)
        g1.step(n - 2)
        g2.start(own2, local.at[0])
        base = [i["after0"], i["after1"]]
        after = [o["after_c0"], o["after_c1"]]
        z_slots = [o["z0"], o["z1"], o["z2"], o["z3"]]
        m_row, t_row = 1.0 + i["shifts"][4:5], i["shifts"][3:4]
        passed = []
        for j in range(2):
            crossed[j].wait_recv()
            stream_body(
                lambda rows, j=j: base[j][rows], chips.at[j], fars.at[j], 1.0, m_row, t_row, after[j], z_slots[2 * j]
            )
            passed.append(cores.start(z_slots[2 * j], z_slots[2 * j + 1], core))
        g2.step(0)
        g1.finish()
        if n > 2:
            g2.step(1)
        act_grad(1)
        for s in range(2, n - 1):
            g2.step(s)
        for copy in passed:
            copy.wait_recv()
        g2.finish()
        for g in (g1, g2):
            g.drain()
        cores.settle()
        xs.settle()

    scratch = [
        pltpu.VMEM((2, quarter, D), BF),
        pltpu.VMEM((2, quarter, D), BF),
        pltpu.VMEM((2, quarter, D), F32),
        pltpu.VMEM((2, quarter, D), BF),
        pltpu.VMEM((2, quarter, D), BF),
        pltpu.VMEM((2, 3, 8, half), F32),
        pltpu.VMEM((D, HC), BF),
        pltpu.SemaphoreType.DMA((2, 10, n)),
        pltpu.SemaphoreType.DMA((2, 8)),
        pltpu.SemaphoreType.DMA((2, 8)),
        pltpu.SemaphoreType.DMA((2, 6)),
        pltpu.SemaphoreType.DMA((3,)),
    ]
    got = run_remote(
        kernel, list(outs.values()), list(far_outs.values()), blocks, far, scratch, 2, 1e10
    )
    return dict(zip(names, got))


def back_body(g, v, chip, far, m, s, out_ref, rows_ref, sum_ref):
    sum_ref[...] = jnp.zeros_like(sum_ref)

    def body(i):
        da = chip[i].astype(F32) + far[i].astype(F32)
        n, r = norm_of(v[i].astype(F32))
        dn = da * m
        mean = jnp.mean(dn, axis=-1, keepdims=True)
        along = jnp.mean(dn * n, axis=-1, keepdims=True)
        out = g(i) + r * (dn - mean - n * along)
        out_ref[i] = out
        rows_ref[i] = (out * s).astype(BF)
        dan = da * n
        for k in range(STEP // 8):
            sum_ref[:8] += da[k * 8 : k * 8 + 8]
            sum_ref[8:] += dan[k * 8 : k * 8 + 8]

    over_rows(v.shape[0], body)


def feed_forward(state, cotangent, n_dp):
    quarter = state["z0"].shape[0]
    half = 2 * quarter
    rows = shape((quarter, D), BF)
    whole = shape((quarter, D), F32)
    outs = dict(
        gc0=whole, gc1=whole, e0=rows, e1=rows, e2=rows, e3=rows,
        sf0=shape((16, D), F32), sf1=shape((16, D), F32), branch=whole,
    )
    far_outs = {f"t{j}": shape((D, 2 * HC), BF) for j in range(3)}
    given = ("z0", "z1", "z2", "z3", "d0", "d1", "d2", "d3", "after_c0", "after_c1", "shifts", "g_got")
    blocks = [state[name] for name in given] + [cotangent]
    far = [state["f0"], state["f1"], state["f2"], state["dact0"], state["dact1"]]
    names = [*outs, *far_outs]

    def kernel(*refs):
        i = dict(zip(given, refs))
        cot, f, dact, refs = refs[len(given)], refs[len(given) + 1 :][:3], refs[len(given) + 4 :][:2], refs[len(given) + 6 :]
        o = dict(zip(names, refs))
        (
            w, act, dpre, theirs, landed, mine, chips, fars, turned, near, cross_x, local,
        ) = refs[len(names) :]
        t, core, across, diagonal = tensor_peers()
        first = t < 2
        cores, xs = Swap(near), Swap(cross_x)
        loads = [pltpu.make_async_copy(f[j], w.at[j], local.at[j]) for j in range(3)]
        loads += [pltpu.make_async_copy(dact[j], dpre.at[j], local.at[3 + j]) for j in range(2)]
        for copy in loads:
            copy.start()
        greet(n_dp)
        z = [i["z0"], i["z1"], i["z2"], i["z3"]]
        ds = [i["d0"], i["d1"], i["d2"], i["d3"]]
        loads[2].wait()
        for p in range(4):
            dpre[2, p * quarter : (p + 1) * quarter] = dot_nn(ds[p][...], w[2, :, HC:]).astype(BF)

        def pre_part(h, j):
            for p in (2 * h, 2 * h + 1):
                own = slice(p * quarter, (p + 1) * quarter)
                u = dot_nn(z[p][...], w[j, :, :HC])
                sq = u * u
                th = jnp.tanh(u * (GELU + GELU * CUBE * sq))
                near_half = 0.5 + 0.5 * th
                act[j, own] = (u * near_half).astype(BF)
                slope = near_half + u * near_half * (1.0 - th) * (GELU + 3 * GELU * CUBE * sq)
                dpre[j, own] = (dpre[j, own].astype(F32) * slope).astype(BF)

        def contracted(a, p, side):
            own = slice(p * quarter, (p + 1) * quarter)
            total = None
            for j in range(3):
                term = dot_nt(a[j, own], w[j, :, side * HC : (side + 1) * HC])
                total = term if total is None else total + term
            return total

        def back_half(h):
            theirs[h] = contracted(dpre, 2 * h + 1, 0).astype(BF)
            copy = cores.start(theirs.at[h], landed.at[h], core)
            mine[h] = contracted(dpre, 2 * h, 0)
            return copy

        def forward_half(h):
            theirs[2 + h] = contracted(act, 2 * h + 1, 1).astype(BF)
            copy = cores.start(theirs.at[2 + h], landed.at[2 + h], core)
            mine[h] = contracted(act, 2 * h, 1)
            return copy

        def join(k, copy):
            copy.wait_recv()
            join_body(mine.at[k % 2], landed.at[k], chips.at[k])

        loads[0].wait()
        loads[3].wait()
        pre_part(0, 0)
        loads[1].wait()
        loads[4].wait()
        pre_part(0, 1)
        pre_part(0, 2)
        sent = back_half(0)
        pre_part(1, 0)
        join(0, sent)
        crossed = [xs.start(chips.at[0], fars.at[0], across)]
        pre_part(1, 1)
        pre_part(1, 2)
        sent = back_half(1)
        sent_f = forward_half(0)
        join(1, sent)
        crossed.append(xs.start(chips.at[1], fars.at[1], across))
        join(2, sent_f)
        sent_f = forward_half(1)
        join(3, sent_f)
        own_half = jnp.where(first, 0, 1)
        last = xs.start(chips.at[3 - own_half], fars.at[2], across)

        def turn_rows(slots):
            for p in range(4):
                turned[:, p * quarter : (p + 1) * quarter] = jnp.transpose(slots[p][...])

        def weight_grad(j, side, right):
            for k in range(0, D, 512):
                w[j, k : k + 512, side * HC : (side + 1) * HC] = dot_nn(turned[k : k + 512], right[j]).astype(BF)

        def g_of(h):
            def rows_of(r):
                own, other = cot[r].astype(F32), i["g_got"][r].astype(F32)
                return jnp.where(first, own, other) if h == 0 else jnp.where(first, other, own)

            return rows_of

        e = [o["e0"], o["e1"], o["e2"], o["e3"]]
        passed = []

        def norm_half(h):
            crossed[h].wait_recv()
            back_body(
                g_of(h), i[f"after_c{h}"], chips.at[h], fars.at[h], 1.0 + i["shifts"][4:5], 1.0,
                o[f"gc{h}"], e[2 * h], o[f"sf{h}"],
            )
            passed.append(cores.start(e[2 * h], e[2 * h + 1], core))

        turn_rows(z)
        weight_grad(0, 0, dpre)
        norm_half(0)
        weight_grad(1, 0, dpre)
        weight_grad(2, 0, dpre)
        turn_rows(ds)
        stores = []
        for j in range(3):
            weight_grad(j, 1, act)
            store = pltpu.make_async_copy(w.at[j], o[f"t{j}"], local.at[j])
            store.start()
            stores.append(store)
            if j == 0:
                norm_half(1)
        last.wait_recv()
        o["branch"][...] = chips[2 + own_half].astype(F32) + fars[2].astype(F32)
        for copy in passed:
            copy.wait_recv()
        for store in stores:
            store.wait()
        cores.settle()
        xs.settle()

    scratch = [
        pltpu.VMEM((3, D, 2 * HC), BF),
        pltpu.VMEM((3, 2 * half, HC), BF),
        pltpu.VMEM((3, 2 * half, HC), BF),
        pltpu.VMEM((4, quarter, D), BF),
        pltpu.VMEM((4, quarter, D), BF),
        pltpu.VMEM((2, quarter, D), F32),
        pltpu.VMEM((4, quarter, D), BF),
        pltpu.VMEM((3, quarter, D), BF),
        pltpu.VMEM((D, 2 * half), BF),
        pltpu.SemaphoreType.DMA((2, 8)),
        pltpu.SemaphoreType.DMA((2, 4)),
        pltpu.SemaphoreType.DMA((5,)),
    ]
    got = run_remote(
        kernel, list(outs.values()), list(far_outs.values()), blocks, far, scratch, 3, 6e10
    )
    return dict(zip(names, got))


class Scatter:
    def __init__(self, got, arrived, over, along, n):
        d = lax.axis_index("dp")
        self.z, self.y = d // 2, lax.rem(d, 2)
        self.got, self.arrived, self.sems_y, self.sems_z, self.n = got, arrived, over, along, n
        self.r = arrived.shape[1]

    def block(self, full, o, own):
        start = (2 * o + (self.y if own else 1 - self.y)) * self.r
        return full.at[pl.ds(pl.multiple_of(start, 16), self.r)]

    def begin(self, full):
        self.full = full
        self.sent = []
        for o in range(self.n):
            copy = remote(
                self.block(full, o, False), self.got.at[o], self.sems_y.at[0, o], self.sems_y.at[1, o],
                dp=2 * self.z + 1 - self.y,
            )
            copy.start()
            self.sent.append(copy)

    def pair(self, a, b, local):
        loads = []
        for o in range(self.n):
            copy = pltpu.make_async_copy(self.block(self.full, o, True), a.at[o], local.at[0, o])
            copy.start()
            loads.append(copy)
        for o in range(self.n):
            self.sent[o].wait()
            copy = pltpu.make_async_copy(self.got.at[o], b.at[o], local.at[1, o])
            copy.start()
            loads.append(copy)
        for o in range(self.n):
            loads[o].wait()
            loads[self.n + o].wait()
            a[o] = (a[o].astype(F32) + b[o].astype(F32)).astype(BF)

    def spread(self, a):
        self.out = []
        for k in range(1, self.n):
            at = lax.rem(self.z + k, self.n)
            copy = remote(
                a.at[at], self.arrived.at[k - 1], self.sems_z.at[0, k], self.sems_z.at[1, k], dp=2 * at + self.y
            )
            copy.start()
            self.out.append(copy)

    def total(self, a, stage, result, sem):
        for copy in self.out:
            copy.wait()
        total = a[self.z].astype(F32)
        for k in range(self.n - 1):
            total = total + self.arrived[k].astype(F32)
        stage[...] = total
        copy = pltpu.make_async_copy(stage, result, sem)
        copy.start()
        copy.wait()


def attend_back_body(do_ref, q_ref, k_refs, v_refs, lse_ref, bias_ref, dq_ref, dk_ref, dv_ref, fresh):
    rows, wide = q_ref.shape
    for h in range(wide // HEAD):
        lanes = slice(h * HEAD, (h + 1) * HEAD)
        k = jnp.concatenate([r[:, lanes] for r in k_refs]) if len(k_refs) > 1 else k_refs[0][:, lanes]
        v = jnp.concatenate([r[:, lanes] for r in v_refs]) if len(v_refs) > 1 else v_refs[0][:, lanes]
        for b in range(rows // QB):
            block = slice(b * QB, (b + 1) * QB)
            qb = q_ref[block, lanes]
            do = do_ref[block, lanes]
            s = dot_nt(k, qb) * FACTOR
            if bias_ref is not None:
                s = s + bias_ref[...]
            p = jnp.exp(s - lse_ref[h : h + 1, block])
            dp = dot_nt(v, do)
            center = jnp.sum(p * dp, axis=0, keepdims=True)
            ds = (p * (dp - center)).astype(BF)
            dq_ref[block, lanes] = dot_tn(ds, k) * FACTOR
            dk = dot_nn(ds, qb) * FACTOR
            dv = dot_nn(p.astype(BF), do)
            if b == 0 and fresh:
                dk_ref[:, lanes] = dk
                dv_ref[:, lanes] = dv
            else:
                dk_ref[:, lanes] += dk
                dv_ref[:, lanes] += dv


def dots_body(dy_ref, raw_ref, col, stat_ref, row, gain, tables, grad_ref, grad_row, wide):
    scale = lax.rsqrt(to_columns(stat_ref[...]) / D + EPS)[:, row : row + 1]
    dots = jnp.zeros((dy_ref.shape[0], 1), F32)
    for h in range(wide // HEAD):
        own = slice(h * HEAD, (h + 1) * HEAD)
        dy = dy_ref[:, own]
        if tables is not None:
            dy = turn(dy, tables[0], -tables[1])
            dy_ref[:, own] = dy
        both = raw_ref[:, col + h * HEAD : col + (h + 1) * HEAD] * dy
        dots = dots + jnp.sum(both * gain[h], axis=1, keepdims=True)
        grad_ref[grad_row : grad_row + 1, own] += jnp.sum(both * scale, axis=0, keepdims=True)
    return dots


def root_back_body(dy_ref, raw_ref, col, stat_ref, row, dots_ref, dots_row, gain, low_ref, at, wide):
    scale = lax.rsqrt(to_columns(stat_ref[...]) / D + EPS)[:, row : row + 1]
    along = scale * scale * scale * to_columns(dots_ref[...])[:, dots_row : dots_row + 1] / D
    for h in range(wide // HEAD):
        own = slice(h * HEAD, (h + 1) * HEAD)
        raw = raw_ref[:, col + h * HEAD : col + (h + 1) * HEAD]
        dx = scale * gain[h] * dy_ref[:, own] - raw * along
        low_ref[:, at + h * HEAD : at + (h + 1) * HEAD] = dx.astype(BF)


class Grads:
    def __init__(self, turned, stage, sems):
        self.turned, self.stage, self.sems = turned, stage, sems
        self.stores = [None, None]
        self.used = 0

    def turn(self, slots):
        at = 0
        for slot in slots:
            m = slot.shape[0]
            self.turned[:, at : at + m] = jnp.transpose(slot[...])
            at += m

    def put(self, ys, full, col):
        i = self.used % 2
        self.used += 1
        if self.stores[i] is not None:
            self.stores[i].wait()
        for k in range(0, D, 512):
            total, at = None, 0
            for y in ys:
                m = y.shape[0]
                term = dot_nn(self.turned[k : k + 512, at : at + m], y)
                total = term if total is None else total + term
                at += m
            self.stage[i, k : k + 512] = total.astype(BF)
        store = pltpu.make_async_copy(self.stage.at[i], full.at[:, pl.ds(col, GC)], self.sems.at[i])
        store.start()
        self.stores[i] = store

    def finish(self):
        for i in range(2):
            if self.stores[i] is not None:
                self.stores[i].wait()
                self.stores[i] = None


def cross_backward(state, bias, n_dp, heads):
    quarter, texts = state["e0"].shape[0], state["c0"].shape[0]
    half, wide = 2 * quarter, heads * HEAD
    n, r = n_dp // 2, D // n_dp
    W = state["t0"].shape[1]
    rows = shape((quarter, D), BF)
    whole = shape((quarter, D), F32)
    sums_shape = shape((16, D), F32)
    outs = dict(
        gs0=whole, gs1=whole, h0=rows, h1=rows, h2=rows, h3=rows, sc0=sums_shape, sc1=sums_shape,
        cross_gain=shape((8, wide), F32), ctx_grad=shape((texts, D), BF),
    )
    far_outs = dict(
        tc=shape((D, 4 * wide), BF), p1=shape((n, r, W), BF), s0=shape((r, W), F32),
        got0=shape((n, r, W), BF), got1=shape((n, r, W), BF),
    )
    given = (
        "e0", "e1", "e2", "e3", "cq0", "cq1", "ck", "cv", "clse0", "clse1", "cq_raw0", "cq_raw1", "ck_raw",
        "cq_stat0", "cq_stat1", "ck_stat", "gains", "shifts", "gc0", "gc1", "after0", "after1", "w_cross",
        "cattn0", "cattn1", "y0", "y1", "y2", "y3", "c0", "c1", "c2", "c3",
    )
    blocks = [state[name] for name in given] + [bias]
    far = [state["t0"], state["t1"]]
    names = [*outs, *far_outs]

    def kernel(*refs):
        i = dict(zip(given, refs))
        bias_ref, t0, t1 = refs[len(given) : len(given) + 3]
        refs = refs[len(given) + 3 :]
        o = dict(zip(names, refs))
        (
            do, dq, dk, dv, low, dckv, theirs, landed, mine, chips, fars, c_theirs, c_landed, c_chips, c_far,
            dots, ck_dots, stats_in, turned, stage, a, b, arrived, result,
            near, cross_x, near_sums, over, along, local, stores,
        ) = refs[len(names) :]
        t, core, across, diagonal = tensor_peers()
        first = t < 2
        cores, xs = Swap(near), Swap(cross_x)
        sums = Sums(stats_in, near_sums, (core, across, diagonal))
        greet(n_dp)
        f0 = Scatter(o["got0"], arrived, over.at[0], along.at[0], n)
        f1 = Scatter(o["got1"], arrived, over.at[1], along.at[0], n)
        f0.begin(t0)
        w = i["w_cross"]
        e = [i["e0"], i["e1"], i["e2"], i["e3"]]
        gain_q = [i["gains"][2 * heads + h : 2 * heads + h + 1] for h in range(heads)]
        gain_k = [i["gains"][3 * heads + h : 3 * heads + h + 1] for h in range(heads)]
        o["cross_gain"][...] = jnp.zeros_like(o["cross_gain"])

        def back(h):
            for p in range(2):
                do[p * quarter : (p + 1) * quarter] = dot_nn(e[2 * h + p][...], w[:, 3 * wide :]).astype(BF)
            attend_back_body(
                do, i[f"cq{h}"], [i["ck"]], [i["cv"]], i[f"clse{h}"], bias_ref, dq, dk, dv, h == 0
            )
            column = dots_body(
                dq, i[f"cq_raw{h}"], 0, i[f"cq_stat{h}"], 0, gain_q, None, o["cross_gain"], 0, wide
            )
            dots[h] = to_rows([column], half)
            return sums.start(dots.at[h])

        def send(h):
            root_back_body(
                dq, i[f"cq_raw{h}"], 0, i[f"cq_stat{h}"], 0, dots.at[h], 0, gain_q, low.at[h], 0, wide
            )
            theirs[h] = dot_nt(low[h, quarter:], w[:, :wide]).astype(BF)
            copy = cores.start(theirs.at[h], landed.at[h], core)
            mine[...] = dot_nt(low[h, :quarter], w[:, :wide])
            return copy

        def join(h, copy):
            copy.wait_recv()
            join_body(mine, landed.at[h], chips.at[h])
            return xs.start(chips.at[h], fars.at[h], across)

        collect = back(0)
        collect()
        sent0 = send(0)
        collect = back(1)
        crossed = [join(0, sent0)]
        column = dots_body(dk, i["ck_raw"], 0, i["ck_stat"], 0, gain_k, None, o["cross_gain"], 1, wide)
        ck_dots[...] = to_rows([column], 4 * texts)
        collect_k = [sums.start(ck_dots.at[:, pl.ds(j * 2 * texts, 2 * texts)]) for j in range(2)]
        collect()
        sent1 = send(1)
        crossed.append(join(1, sent1))
        f1.begin(t1)
        for part in collect_k:
            part()
        f0.pair(a, b, local)
        f0.spread(a)

        root_back_body(dk, i["ck_raw"], 0, i["ck_stat"], 0, ck_dots, 0, gain_k, dckv, 0, wide)
        dckv[:, wide:] = dv[...].astype(BF)
        c_sent = []
        for j in range(2):
            at = 2 * texts * j
            c_theirs[j] = dot_nt(dckv[at + texts : at + 2 * texts], w[:, wide : 3 * wide]).astype(BF)
            c_sent.append(cores.start(c_theirs.at[j], c_landed.at[j], core))
        for j in range(2):
            at = 2 * texts * j
            part = dot_nt(dckv[at : at + texts], w[:, wide : 3 * wide])
            c_sent[j].wait_recv()
            c_chips[j] = (part + c_landed[j].astype(F32)).astype(BF)
        own_half = jnp.where(first, 0, 1)
        c_last = xs.start(c_chips.at[1 - own_half], c_far, across)

        h_slots = [o["h0"], o["h1"], o["h2"], o["h3"]]
        passed = []

        def norm_half(h):
            crossed[h].wait_recv()
            back_body(
                lambda rows: i[f"gc{h}"][rows], i[f"after{h}"], chips.at[h], fars.at[h], i["shifts"][6:7],
                i["shifts"][2:3], o[f"gs{h}"], h_slots[2 * h], o[f"sc{h}"],
            )
            passed.append(cores.start(h_slots[2 * h], h_slots[2 * h + 1], core))

        norm_half(0)
        grads = Grads(turned, stage, stores)
        grads.turn([i["y0"], i["y1"], i["y2"], i["y3"]])
        grads.put([low[0], low[1]], o["tc"], 0)
        norm_half(1)
        grads.turn([i["c0"], i["c1"], i["c2"], i["c3"]])
        for c in range(2):
            grads.put([dckv[:, c * wide : (c + 1) * wide]], o["tc"], (1 + c) * wide)
        grads.turn(e)
        grads.put([i["cattn0"][...], i["cattn1"][...]], o["tc"], 3 * wide)
        c_last.wait_recv()
        o["ctx_grad"][...] = (c_chips[own_half].astype(F32) + c_far[...].astype(F32)).astype(BF)
        grads.finish()
        f0.total(a, result, o["s0"], stores.at[0])
        f1.pair(a, b, local)
        copy = pltpu.make_async_copy(a, o["p1"], stores.at[0])
        copy.start()
        copy.wait()
        for copy in passed:
            copy.wait_recv()
        cores.settle()
        xs.settle()

    scratch = [
        pltpu.VMEM((half, wide), BF),
        pltpu.VMEM((half, wide), F32),
        pltpu.VMEM((4 * texts, wide), F32),
        pltpu.VMEM((4 * texts, wide), F32),
        pltpu.VMEM((2, half, wide), BF),
        pltpu.VMEM((4 * texts, 2 * wide), BF),
        pltpu.VMEM((2, quarter, D), BF),
        pltpu.VMEM((2, quarter, D), BF),
        pltpu.VMEM((quarter, D), F32),
        pltpu.VMEM((2, quarter, D), BF),
        pltpu.VMEM((2, quarter, D), BF),
        pltpu.VMEM((2, texts, D), BF),
        pltpu.VMEM((2, texts, D), BF),
        pltpu.VMEM((2, texts, D), BF),
        pltpu.VMEM((texts, D), BF),
        pltpu.VMEM((2, 8, half), F32),
        pltpu.VMEM((8, 4 * texts), F32),
        pltpu.VMEM((4, 3, 8, half), F32),
        pltpu.VMEM((D, 2 * half), BF),
        pltpu.VMEM((2, D, GC), BF),
        pltpu.VMEM((n, r, W), BF),
        pltpu.VMEM((n, r, W), BF),
        pltpu.VMEM((n - 1, r, W), BF),
        pltpu.VMEM((r, W), F32),
        pltpu.SemaphoreType.DMA((2, 8)),
        pltpu.SemaphoreType.DMA((2, 4)),
        pltpu.SemaphoreType.DMA((2, 12)),
        pltpu.SemaphoreType.DMA((2, 2, n)),
        pltpu.SemaphoreType.DMA((1, 2, n)),
        pltpu.SemaphoreType.DMA((2, n)),
        pltpu.SemaphoreType.DMA((2,)),
    ]
    got = run_remote(
        kernel, list(outs.values()), list(far_outs.values()), blocks, far, scratch, 4, 4e10
    )
    return dict(zip(names, got))


def self_backward(state, hidden, tables, n_dp, heads):
    quarter = hidden.shape[0]
    half, wide = 2 * quarter, heads * HEAD
    n, r = n_dp // 2, D // n_dp
    W, V = state["t2"].shape[1], 2 * wide
    outs = dict(hidden_grad=shape((quarter, D), BF), ss=shape((16, D), F32), self_gain=shape((8, wide), F32))
    far_outs = dict(
        s1=shape((r, W), F32), s2=shape((r, W), F32), s3=shape((r, W), F32), s4=shape((r, V), F32), s5=shape((r, V), F32),
        tv=shape((D, V), BF), tq=shape((D, V), BF),
        got2=shape((n, r, W), BF), got3=shape((n, r, W), BF), got4=shape((n, r, V), BF), got5=shape((n, r, V), BF),
    )
    given = (
        "h0", "h1", "h2", "h3", "q0", "q1", "k0", "k1", "v0", "v1", "lse0", "lse1", "qk0", "qk1", "stat0", "stat1",
        "gains", "shifts", "gs0", "gs1", "attn0", "attn1", "w_self",
    )
    blocks = [state[name] for name in given] + [hidden, *tables]
    far = [state["p1"], state["t2"], state["tc"], *(state[f"x{p}"] for p in range(4))]
    names = [*outs, *far_outs]

    def kernel(*refs):
        i = dict(zip(given, refs))
        hid, cos, sin, p1, t2, tc = refs[len(given) : len(given) + 6]
        xs_far = refs[len(given) + 6 : len(given) + 10]
        refs = refs[len(given) + 10 :]
        o = dict(zip(names, refs))
        (
            do, dq, dk, dv, low, theirs, landed, mine, chips, far_chip,
            dots, stats_in, turned, stage, a, b, arrived, arrived_v, result,
            near, cross_x, near_sums, over, along, local, stores, slots,
        ) = refs[len(names) :]
        t, core, across, diagonal = tensor_peers()
        first = t < 2
        cores, xs = Swap(near), Swap(cross_x)
        sums = Sums(stats_in, near_sums, (core, across, diagonal))
        held = pltpu.make_async_copy(p1, a.at[0], stores.at[0])
        held.start()
        x_copies = [pltpu.make_async_copy(xs_far[p], theirs.at[p % 2], slots.at[p]) for p in range(4)]
        for p in range(2):
            x_copies[p].start()
        greet(n_dp)
        f1 = Scatter(None, arrived.at[0], None, along.at[0], n)
        f2 = Scatter(o["got2"], arrived.at[1], over.at[0], along.at[1], n)
        fc = Scatter(o["got3"], arrived.at[2], over.at[1], along.at[2], n)
        fv = Scatter(o["got4"], arrived_v.at[0], over.at[2], along.at[3], n)
        fq = Scatter(o["got5"], arrived_v.at[1], over.at[3], along.at[4], n)
        f2.begin(t2)
        held.wait()
        f1.spread(a.at[0])
        w = i["w_self"]
        hs = [i["h0"], i["h1"], i["h2"], i["h3"]]
        ks, vs = [i["k0"], i["k1"]], [i["v0"], i["v1"]]
        gain = [[i["gains"][g * heads + h : g * heads + h + 1] for h in range(heads)] for g in range(2)]
        o["self_gain"][...] = jnp.zeros_like(o["self_gain"])
        for h in range(2):
            for p in range(2):
                do[p * quarter : (p + 1) * quarter] = dot_nn(hs[2 * h + p][...], w[:, 3 * wide :]).astype(BF)
            attend_back_body(do, i[f"q{h}"], ks, vs, i[f"lse{h}"], None, dq.at[h], dk, dv, h == 0)
        collects = []
        for h in range(2):
            own = slice(h * half, (h + 1) * half)
            turns = (cos[own], sin[own])
            dk_half = dk.at[pl.ds(h * half, half)]
            columns = [
                dots_body(dq.at[h], i[f"qk{h}"], 0, i[f"stat{h}"], 0, gain[0], turns, o["self_gain"], 0, wide),
                dots_body(dk_half, i[f"qk{h}"], wide, i[f"stat{h}"], 1, gain[1], turns, o["self_gain"], 1, wide),
            ]
            dots[h] = to_rows(columns, half)
            collects.append(sums.start(dots.at[h]))
            low[h, :, 2 * wide :] = dv[own].astype(BF)

        grads = Grads(turned, stage, stores)
        for p in range(4):
            x_copies[p].wait()
            turned[:, p * quarter : (p + 1) * quarter] = jnp.transpose(theirs[p % 2])
            if p < 2:
                x_copies[p + 2].start()
        grads.put([low[0, :, 2 * wide :], low[1, :, 2 * wide :]], o["tv"], 0)
        fc.begin(tc)
        f2.pair(a.at[1], b, local)
        f2.spread(a.at[1])
        sent = []

        def join(h):
            sent[h].wait_recv()
            join_body(mine, landed.at[h], chips.at[h])

        for h in range(2):
            collects[h]()
            dk_half = dk.at[pl.ds(h * half, half)]
            root_back_body(dq.at[h], i[f"qk{h}"], 0, i[f"stat{h}"], 0, dots.at[h], 0, gain[0], low.at[h], 0, wide)
            root_back_body(
                dk_half, i[f"qk{h}"], wide, i[f"stat{h}"], 1, dots.at[h], 1, gain[1], low.at[h], wide, wide
            )
            theirs[h] = dot_nt(low[h, quarter:], w[:, : 3 * wide]).astype(BF)
            sent.append(cores.start(theirs.at[h], landed.at[h], core))
            if h == 1:
                join(0)
            mine[...] = dot_nt(low[h, :quarter], w[:, : 3 * wide])
        join(1)
        own_half = jnp.where(first, 0, 1)
        last = xs.start(chips.at[1 - own_half], far_chip, across)
        for c in range(2):
            lanes = slice(c * wide, (c + 1) * wide)
            grads.put([low[0, :, lanes], low[1, :, lanes]], o["tq"], c * wide)
        grads.turn(hs)
        grads.put([i["attn0"][...], i["attn1"][...]], o["tv"], wide)
        grads.finish()
        f1.total(a.at[0], result, o["s1"], stores.at[0])
        fv.begin(o["tv"])

        last.wait_recv()
        m_row = 1.0 + i["shifts"][1:2]
        sum_ref = o["ss"]
        sum_ref[...] = jnp.zeros_like(sum_ref)

        def body(rows):
            da = chips[own_half, rows].astype(F32) + far_chip[rows].astype(F32)
            nv, rv = norm_of(hid[rows].astype(F32))
            dn = da * m_row
            mean = jnp.mean(dn, axis=-1, keepdims=True)
            proj = jnp.mean(dn * nv, axis=-1, keepdims=True)
            g = jnp.where(first, i["gs0"][rows], i["gs1"][rows])
            o["hidden_grad"][rows] = (g + rv * (dn - mean - nv * proj)).astype(BF)
            dan = da * nv
            for k in range(STEP // 8):
                sum_ref[:8] += da[k * 8 : k * 8 + 8]
                sum_ref[8:] += dan[k * 8 : k * 8 + 8]

        over_rows(quarter, body)
        fc.pair(a.at[0], b, local)
        fc.spread(a.at[0])
        fq.begin(o["tq"])
        f2.total(a.at[1], result, o["s2"], stores.at[0])
        a_v, b_v = a.at[1, :, :, pl.ds(0, V)], b.at[:, :, pl.ds(0, V)]
        fv.pair(a_v, b_v, local)
        fv.spread(a_v)
        fc.total(a.at[0], result, o["s3"], stores.at[0])
        a_q = a.at[0, :, :, pl.ds(0, V)]
        fq.pair(a_q, b_v, local)
        fq.spread(a_q)
        fv.total(a_v, result.at[:, pl.ds(0, V)], o["s4"], stores.at[0])
        fq.total(a_q, result.at[:, pl.ds(0, V)], o["s5"], stores.at[0])
        cores.settle()
        xs.settle()

    scratch = [
        pltpu.VMEM((half, wide), BF),
        pltpu.VMEM((2, half, wide), F32),
        pltpu.VMEM((2 * half, wide), F32),
        pltpu.VMEM((2 * half, wide), F32),
        pltpu.VMEM((2, half, 3 * wide), BF),
        pltpu.VMEM((2, quarter, D), BF),
        pltpu.VMEM((2, quarter, D), BF),
        pltpu.VMEM((quarter, D), F32),
        pltpu.VMEM((2, quarter, D), BF),
        pltpu.VMEM((quarter, D), BF),
        pltpu.VMEM((2, 8, half), F32),
        pltpu.VMEM((2, 3, 8, half), F32),
        pltpu.VMEM((D, 2 * half), BF),
        pltpu.VMEM((2, D, GC), BF),
        pltpu.VMEM((2, n, r, W), BF),
        pltpu.VMEM((n, r, W), BF),
        pltpu.VMEM((3, n - 1, r, W), BF),
        pltpu.VMEM((2, n - 1, r, V), BF),
        pltpu.VMEM((r, W), F32),
        pltpu.SemaphoreType.DMA((2, 4)),
        pltpu.SemaphoreType.DMA((2, 4)),
        pltpu.SemaphoreType.DMA((2, 6)),
        pltpu.SemaphoreType.DMA((4, 2, n)),
        pltpu.SemaphoreType.DMA((5, 2, n)),
        pltpu.SemaphoreType.DMA((2, n)),
        pltpu.SemaphoreType.DMA((2,)),
        pltpu.SemaphoreType.DMA((4,)),
    ]
    got = run_remote(
        kernel, list(outs.values()), list(far_outs.values()), blocks, far, scratch, 5, 5e10
    )
    return dict(zip(names, got))


def rotary_tables(positions, head_dim):
    pair_count = head_dim // 2
    side_pairs = pair_count // 3
    frame_pairs = pair_count - 2 * side_pairs
    pair_index = jnp.arange(pair_count)
    frame_mask = pair_index < frame_pairs
    height_mask = (pair_index >= frame_pairs) & (pair_index < frame_pairs + side_pairs)
    within = jnp.where(
        frame_mask,
        pair_index,
        jnp.where(height_mask, pair_index - frame_pairs, pair_index - frame_pairs - side_pairs),
    )
    extent = jnp.where(frame_mask, frame_pairs, side_pairs)
    frequency = jnp.power(10000.0, -within.astype(F32) / extent.astype(F32))
    coords = positions.astype(F32)
    coordinate = jnp.where(
        frame_mask[None, :],
        coords[0][:, None],
        jnp.where(height_mask[None, :], coords[1][:, None], coords[2][:, None]),
    )
    angles = jnp.repeat(coordinate * frequency[None, :], 2, axis=1)
    parity = jnp.arange(head_dim) % 2
    sign_pattern = jnp.where(parity == 0, -1.0, 1.0)
    return (jnp.cos(angles), jnp.sin(angles) * sign_pattern)


def solution(mesh):
    n_dp = mesh.shape["dp"]
    n_major = n_dp // 2
    pair_perm = [(i, i ^ 1) for i in range(n_dp)]
    ring_perm = {
        t: [((((i // 2) + t) % n_major) * 2 + i % 2, i) for i in range(n_dp)]
        for t in range(1, n_major)
    }
    back_perm = {t: [(b, a) for a, b in ring_perm[t]] for t in ring_perm}
    core_perm = [(i, i ^ 1) for i in range(4)]
    x_perm = [(i, i ^ 2) for i in range(4)]

    def core_swap(v):
        return lax.ppermute(v, "tensor", core_perm)

    def x_swap(v):
        return lax.ppermute(v, "tensor", x_perm)

    def gather_dp(block):
        pieces = []
        for t in range(n_major):
            piece = block if t == 0 else lax.ppermute(block, "dp", ring_perm[t])
            pieces += [piece, lax.ppermute(piece, "dp", pair_perm)]
        return pieces

    def scatter_dp(theirs, mine):
        major = lax.axis_index("dp") // 2
        got = lax.ppermute(theirs, "dp", pair_perm)

        def block(t):
            at = (major + t) % n_major
            a = lax.dynamic_slice_in_dim(mine, at, 1, axis=0)[0].astype(F32)
            return a + lax.dynamic_slice_in_dim(got, at, 1, axis=0)[0].astype(F32)

        arrived = [
            lax.ppermute(block(t).astype(BF), "dp", back_perm[t]) for t in range(1, n_major)
        ]
        total = block(0)
        for piece in arrived:
            total = total + piece.astype(F32)
        return total

    def join(mine, theirs):
        return (mine + core_swap(theirs).astype(F32)).astype(BF)

    def own_half(pair):
        first = lax.axis_index("tensor") < 2
        return jnp.where(first, pair[0], pair[1])

    def other_half(pair):
        first = lax.axis_index("tensor") < 2
        return jnp.where(first, pair[1], pair[0])

    def two_halves(own):
        got = x_swap(own)
        first = lax.axis_index("tensor") < 2
        return jnp.where(first, own, got), jnp.where(first, got, own)

    def sum_all(v):
        v = v + core_swap(v)
        return v + x_swap(v)

    def sum_vectors(v):
        h = v.shape[-1] // 2
        other = core_swap(v)
        v = v + jnp.concatenate([other[..., h:], other[..., :h]], -1)
        return v + x_swap(v)

    def sum_halves(pair):
        both = sum_vectors(jnp.stack(pair))
        return both[0], both[1]

    def quarters(values, axis):
        core = lax.axis_index("tensor") % 2
        step = values.shape[axis] // 4
        return jnp.concatenate(
            [
                lax.dynamic_slice_in_dim(values, at * step, step, axis)
                for at in (core, 1 - core, 2 + core, 3 - core)
            ],
            axis,
        )

    def on_device(
        hidden_in, context, time_emb, text_lengths, positions, modulation,
        self_query, self_key, self_value, self_output, self_query_gain, self_key_gain,
        cross_query, cross_key, cross_value, cross_output, cross_query_gain, cross_key_gain,
        norm_weight, norm_bias, ffn_up, ffn_down, out_cotangent,
    ):
        heads = self_query_gain.shape[0]
        half = positions.shape[1] // 2
        wide = heads * HEAD
        r_dp = self_query.shape[0]
        hid = ffn_up.shape[1]
        spare = -hid % HC

        texts = context.shape[1]
        quarter = half // 2
        g_cols = self_query_gain.shape[1]
        gains = [self_query_gain, self_key_gain, cross_query_gain, cross_key_gain]
        flat = jnp.concatenate([modulation, norm_weight[None], norm_bias[None]])
        side = jnp.pad(jnp.concatenate(gains), ((0, 0), (0, r_dp - g_cols)))
        small = jnp.concatenate([flat, side])
        small = jnp.pad(small, ((0, HEAD - small.shape[0]), (0, 0))).T.astype(BF)
        own_self = jnp.concatenate([self_query, self_key, self_value, self_output.T], axis=1).astype(BF)
        own_cross = jnp.concatenate([cross_query, cross_key, cross_value, cross_output.T], axis=1).astype(BF)
        padded = [jnp.pad(w, ((0, 0), (0, spare))) for w in (ffn_up.astype(BF), ffn_down.T.astype(BF))]
        hid_low = hid + spare
        own_ffn = [
            jnp.concatenate([w[:, j * HC : (j + 1) * HC] for w in padded], axis=1) for j in range(hid_low // HC)
        ]
        tables = rotary_tables(quarters(positions, 1), HEAD)
        text_bias = jnp.where(quarters(jnp.arange(4 * texts), 0) < text_lengths[0], 0.0, -1e30)
        text_bias = text_bias.astype(F32)[:, None]

        st = self_forward(
            hidden_in, context[0], out_cotangent, time_emb[0], tables, small,
            own_self, own_cross, own_ffn[0], n_dp, heads,
        )
        st |= cross_forward(st, out_cotangent, text_bias, own_ffn[1], own_ffn[2], n_dp, heads)
        d = lax.axis_index("dp")
        cosine, sine = ((t[:half], t[half:]) for t in tables)
        s0, s1, s2, s3, s4, s5, norm_gain, norm_shift = (st["shifts"][i : i + 1] for i in range(8))
        sq_gain, sk_gain, cq_gain, ck_gain = (
            st["gains"][i * heads : (i + 1) * heads].reshape(1, wide) for i in range(4)
        )
        ones = jnp.ones((1, D), F32)
        w_self, w_cross = [st["w_self"]], [st["w_cross"]]
        w_ffn = [st["f0"], st["f1"], st["f2"]]
        at_o, at_cq, at_ck, at_co = 3 * wide, 0, wide, 3 * wide

        def both(name):
            return [st[name + "0"], st[name + "1"]]

        def four(name):
            return [[st[name + "0"], st[name + "1"]], [st[name + "2"], st[name + "3"]]]

        first = lax.axis_index("tensor") < 2
        g = [jnp.where(first, out_cotangent, st["g_got"]), jnp.where(first, st["g_got"], out_cotangent)]
        ctx = [st[f"c{i}"] for i in range(4)]
        self_rows, cross_rows, ffn_rows = four("x"), four("y"), four("z")
        qk, v, stat, q, k, attn, lse = (both(name) for name in ("qk", "v", "stat", "q", "k", "attn", "lse"))
        self_chip, self_far, after_self = both("chip"), both("far"), both("after")
        ck_raw, cv, ck_stat, ck = st["ck_raw"], st["cv"], st["ck_stat"], st["ck"]
        cq_raw, cq_stat, cq, cattn, clse = (both(name) for name in ("cq_raw", "cq_stat", "cq", "cattn", "clse"))
        after_cross = both("after_c")

        def with_peer(rows):
            return [rows, core_swap(rows)]

        st |= feed_forward(st, out_cotangent, n_dp)
        g_c, sums_f = both("gc"), both("sf")

        st |= cross_backward(st, text_bias, n_dp, heads)
        st |= self_backward(st, hidden_in, tables, n_dp, heads)
        hid_grads = [st["s0"], st["s1"], st["s2"]]
        up_grad = jnp.concatenate([a[:, :HC] for a in hid_grads], axis=1)
        down_grad = jnp.concatenate([a[:, HC:] for a in hid_grads], axis=1)
        cross_grad = st["s3"]
        qkv_grad = [st["s5"][:, :wide], st["s5"][:, wide:], st["s4"][:, :wide]]
        oT_grad = st["s4"][:, wide:]
        g_s, sums_c, sums_s = both("gs"), both("sc"), st["ss"]
        hidden_grad, context_grad = st["hidden_grad"], st["ctx_grad"]

        ffn_branch = st["branch"]
        block_out = (own_half(after_cross) + ffn_branch * s5).astype(BF)

        self_branch = own_half(self_chip).astype(F32) + own_half(self_far).astype(F32)
        sums_f = own_half(sums_f)
        sums_c = own_half(sums_c)
        sums_own = jnp.stack(
            [
                jnp.sum(sums_s[:8], 0),
                jnp.sum(sums_s[8:], 0),
                jnp.sum(own_half(g_s) * self_branch, 0),
                jnp.sum(sums_f[:8], 0),
                jnp.sum(sums_f[8:], 0),
                jnp.sum(out_cotangent.astype(F32) * ffn_branch, 0),
                jnp.sum(sums_c[8:], 0),
                jnp.sum(sums_c[:8], 0),
            ]
        )
        sums_clip = sum_all(sums_own)
        time_grad = sums_clip[:6]
        low_sums = sums_clip.reshape(8, n_dp, r_dp).transpose(1, 0, 2).reshape(n_dp, -1)
        gain_grads = jnp.concatenate([st["self_gain"][:2], st["cross_gain"][:2]])
        low_gains = gain_grads.reshape(4 * heads, n_dp, g_cols).transpose(1, 0, 2).reshape(n_dp, -1)
        packed = jnp.concatenate([low_sums, low_gains], axis=1).astype(BF)
        packed = jnp.pad(packed, ((0, 0), (0, -packed.shape[1] % 1024))).reshape(n_major, 2, 8, -1)
        minor = d % 2
        tiny = scatter_dp(
            lax.dynamic_slice_in_dim(packed, 1 - minor, 1, 1)[:, 0],
            lax.dynamic_slice_in_dim(packed, minor, 1, 1)[:, 0],
        ).reshape(-1)
        eight = tiny[: 8 * r_dp].reshape(8, r_dp)
        gains_out = tiny[8 * r_dp : 8 * r_dp + 4 * heads * g_cols].reshape(4, heads, g_cols)

        return (
            block_out,
            hidden_grad,
            context_grad[None],
            time_grad[None],
            eight[:6],
            qkv_grad[0],
            qkv_grad[1],
            qkv_grad[2],
            oT_grad.T,
            gains_out[0],
            gains_out[1],
            cross_grad[:, :wide],
            cross_grad[:, wide : 2 * wide],
            cross_grad[:, 2 * wide : 3 * wide],
            cross_grad[:, 3 * wide :].T,
            gains_out[2],
            gains_out[3],
            eight[6],
            eight[7],
            up_grad[:, :hid],
            down_grad[:, :hid].T,
        )

    rows = P(("dp", "tensor"), None)
    col = P("dp", "tensor")
    row = P("tensor", "dp")
    text = P("dp", "tensor", None)
    time = P("dp", None, None)
    one = P("dp")
    ins = (
        rows, text, time, one, P(None, "dp"), P(None, "dp"),
        col, col, col, row, row, row,
        col, col, col, row, row, row,
        one, one, col, row, rows,
    )
    outs = (
        rows, rows, text, time, P(None, "dp"),
        col, col, col, row, row, row,
        col, col, col, row, row, row,
        one, one, col, row,
    )
    return jax.shard_map(on_device, mesh=mesh, in_specs=ins, out_specs=outs, check_vma=False)
```

```python
import math

import jax
import jax.numpy as jnp
from jax import lax
from jax.experimental import pallas as pl
from jax.experimental.pallas import tpu as pltpu
from jax.sharding import PartitionSpec as P

D = 1536
HEAD = 128
EPS = 1e-6
BF = jnp.bfloat16
F32 = jnp.float32
FACTOR = 1.0 / math.sqrt(HEAD)
GELU = math.sqrt(2.0 / math.pi)
CUBE = 0.044715
MESH = pl.DeviceIdType.MESH


def dot_nn(a, b):
    return lax.dot_general(a, b, (((1,), (0,)), ((), ())), preferred_element_type=F32)


def dot_nt(a, b):
    return lax.dot_general(a, b, (((1,), (1,)), ((), ())), preferred_element_type=F32)


def dot_tn(a, b):
    return lax.dot_general(a, b, (((0,), (0,)), ((), ())), preferred_element_type=F32)


def shape(dims, dtype):
    return jax.ShapeDtypeStruct(dims, dtype)


def run(kernel, outs, blocks, far=(), scratch=(), flops=0, exps=0, limit=60):
    moved = sum(math.prod(v.shape) * v.dtype.itemsize for v in (*blocks, *far, *outs))
    return pl.pallas_call(
        kernel,
        out_shape=tuple(outs),
        in_specs=[pl.BlockSpec(memory_space=pltpu.VMEM)] * len(blocks)
        + [pl.BlockSpec(memory_space=pl.ANY)] * len(far),
        out_specs=tuple(pl.BlockSpec(memory_space=pltpu.VMEM) for _ in outs),
        scratch_shapes=list(scratch),
        compiler_params=pltpu.CompilerParams(vmem_limit_bytes=limit * 2**20),
        cost_estimate=pl.CostEstimate(flops=int(flops), bytes_accessed=moved, transcendentals=int(exps)),
    )(*blocks, *far)


def load(pieces, w, sems, first=0):
    n = len(pieces)
    r, c = w.shape[0] // n, w.shape[1]
    if n == 1:
        copy = pltpu.make_async_copy(pieces[0].at[:, pl.ds(first, c)], w, sems.at[0])
        copy.start()
        return [copy]
    d = lax.axis_index("dp")
    major, minor = d // 2, d % 2
    copies = []
    for i, piece in enumerate(pieces):
        t, flip = i // 2, i % 2
        block = 2 * lax.rem(major + t, n // 2) + (1 - minor if flip else minor)
        rows = pl.ds(pl.multiple_of(block * r, 16), r)
        copy = pltpu.make_async_copy(piece.at[:, pl.ds(first, c)], w.at[rows], sems.at[i])
        copy.start()
        copies.append(copy)
    return copies


def wait(copies):
    for copy in copies:
        copy.wait()


def weight(n, c):
    return [pltpu.VMEM((D, c), BF), pltpu.SemaphoreType.DMA((n,))]


def to_rows(columns, count):
    lane = lax.broadcasted_iota(jnp.int32, (count, 128), 1)
    out = jnp.zeros((count, 128), F32)
    for i, column in enumerate(columns):
        out = jnp.where(lane == i, column, out)
    return jnp.transpose(out)[:8]


def to_columns(rows):
    return jnp.transpose(jnp.concatenate([rows] * 16, axis=0))


def turn(values, cosine, sine):
    even = lax.broadcasted_iota(jnp.int32, values.shape, 1) % 2 == 0
    partner = jnp.where(even, pltpu.roll(values, HEAD - 1, 1), pltpu.roll(values, 1, 1))
    return values * cosine + partner * sine


def norm_of(v):
    center = v - jnp.mean(v, axis=-1, keepdims=True)
    r = lax.rsqrt(jnp.mean(center * center, axis=-1, keepdims=True) + EPS)
    return center * r, r


STEP = 32


def over_rows(count, body):
    def one(i, carry):
        body(pl.ds(pl.multiple_of(i * STEP, STEP), STEP))
        return carry

    lax.fori_loop(0, count // STEP, one, 0)


def norm_first(v, m, t):
    def kernel(v_ref, m_ref, t_ref, rows_ref):
        def body(s):
            n, _ = norm_of(v_ref[s].astype(F32))
            rows_ref[s] = (n * m_ref[...] + t_ref[...]).astype(BF)

        over_rows(v_ref.shape[0], body)

    return run(kernel, [shape(v.shape, BF)], [v, m, t], flops=1e9)[0]


def norm_forward(v, chip, far_chip, s, m, t):
    def kernel(v_ref, a_ref, b_ref, s_ref, m_ref, t_ref, out_ref, rows_ref):
        def body(i):
            branch = a_ref[i].astype(F32) + b_ref[i].astype(F32)
            out = v_ref[i].astype(F32) + branch * s_ref[...]
            out_ref[i] = out
            n, _ = norm_of(out)
            rows_ref[i] = (n * m_ref[...] + t_ref[...]).astype(BF)

        over_rows(v_ref.shape[0], body)

    return run(
        kernel, [shape(v.shape, F32), shape(v.shape, BF)], [v, chip, far_chip, s, m, t], flops=1e9
    )


def norm_backward(g, v, chip, far_chip, m, s):
    def kernel(g_ref, v_ref, a_ref, b_ref, m_ref, s_ref, out_ref, rows_ref, sum_ref):
        sum_ref[...] = jnp.zeros_like(sum_ref)

        def body(i):
            da = a_ref[i].astype(F32) + b_ref[i].astype(F32)
            n, r = norm_of(v_ref[i].astype(F32))
            dn = da * m_ref[...]
            mean = jnp.mean(dn, axis=-1, keepdims=True)
            along = jnp.mean(dn * n, axis=-1, keepdims=True)
            out = g_ref[i].astype(F32) + r * (dn - mean - n * along)
            out_ref[i] = out
            rows_ref[i] = (out * s_ref[...]).astype(BF)
            dan = da * n
            for k in range(STEP // 8):
                sum_ref[:8] += da[k * 8 : k * 8 + 8]
                sum_ref[8:] += dan[k * 8 : k * 8 + 8]

        over_rows(g_ref.shape[0], body)

    return run(
        kernel,
        [shape(g.shape, F32), shape(g.shape, BF), shape((16, D), F32)],
        [g, v, chip, far_chip, m, s],
        flops=1e9,
    )


def hold(v, after):
    def kernel(v_ref, *refs):
        refs[-1][...] = v_ref[...]

    return run(kernel, [shape(v.shape, v.dtype)], [v], after)[0]


def project(xs, pieces, first, squares, lows, wide):
    total = sum(x.shape[0] for x in xs)
    cols = (squares + lows) * wide
    n = len(pieces)
    outs = [shape((total, squares * wide), F32)] * (squares > 0)
    outs += [shape((total, lows * wide), BF)] * (lows > 0)
    outs += [shape((8, total), F32)] * (squares > 0)

    def kernel(*refs):
        x_refs, refs = refs[: len(xs)], refs[len(xs) :]
        piece_refs, refs = refs[:n], refs[n:]
        out_refs, (w, sems) = list(refs[:-2]), refs[-2:]
        wait(load(piece_refs, w, sems, first))
        at = 0
        for x_ref in x_refs:
            m = x_ref.shape[0]
            value = dot_nn(x_ref[...], w[...])
            columns = []
            for i in range(squares):
                part = value[:, i * wide : (i + 1) * wide]
                columns.append(jnp.sum(part * part, axis=1, keepdims=True))
            if squares:
                out_refs[0][at : at + m] = value[:, : squares * wide]
                out_refs[-1][:, at : at + m] = to_rows(columns, m)
            if lows:
                out_refs[1 if squares else 0][at : at + m] = value[:, squares * wide :].astype(BF)
            at += m

    return run(kernel, outs, xs, pieces, weight(n, cols), flops=2 * total * D * cols)


def normalize(raws, stats, gains, tables, wide):
    count = len(gains)
    parts = len(raws)
    outs = [shape((r.shape[0], wide), BF) for r in raws for _ in range(count)]

    def kernel(*refs):
        raw_refs, refs = refs[:parts], refs[parts:]
        stat_refs, refs = refs[:parts], refs[parts:]
        gain_refs, refs = refs[:count], refs[count:]
        if tables:
            cos_refs, sin_refs, refs = refs[:parts], refs[parts : 2 * parts], refs[2 * parts :]
        for p in range(parts):
            scale = lax.rsqrt(to_columns(stat_refs[p][...]) / D + EPS)
            for i in range(count):
                for h in range(wide // HEAD):
                    lanes = slice(i * wide + h * HEAD, i * wide + (h + 1) * HEAD)
                    own = slice(h * HEAD, (h + 1) * HEAD)
                    value = raw_refs[p][:, lanes] * scale[:, i : i + 1] * gain_refs[i][:, own]
                    if tables:
                        value = turn(value, cos_refs[p][...], sin_refs[p][...])
                    refs[p * count + i][:, own] = value.astype(BF)

    args = [*raws, *stats, *gains]
    if tables:
        args += [*tables[0], *tables[1]]
    return run(kernel, outs, args, flops=1e9)


QB = 256


def attend(q, ks, vs, bias, pieces, first):
    rows, wide = q.shape
    heads = wide // HEAD
    nk = sum(k.shape[0] for k in ks)
    n = len(pieces)
    parts = len(ks)
    half = rows // 2
    biases = [] if bias is None else [bias]

    def kernel(*refs):
        q_ref, k_refs, v_refs = refs[0], refs[1 : 1 + parts], refs[1 + parts : 1 + 2 * parts]
        refs = refs[1 + 2 * parts :]
        b_refs, refs = refs[: len(biases)], refs[len(biases) :]
        piece_refs, (out_ref, lse_ref, mine_ref, theirs_ref, w, sems) = refs[:n], refs[n:]
        copies = load(piece_refs, w, sems, first)
        lse_ref[...] = jnp.zeros_like(lse_ref)
        for h in range(heads):
            lanes = slice(h * HEAD, (h + 1) * HEAD)
            k = jnp.concatenate([r[:, lanes] for r in k_refs]) if parts > 1 else k_refs[0][:, lanes]
            v = jnp.concatenate([r[:, lanes] for r in v_refs]) if parts > 1 else v_refs[0][:, lanes]
            for b in range(rows // QB):
                block = slice(b * QB, (b + 1) * QB)
                s = dot_nt(k, q_ref[block, lanes]) * FACTOR
                if biases:
                    s = s + b_refs[0][...]
                top = jnp.max(s, axis=0, keepdims=True)
                e = jnp.exp(s - top)
                total = jnp.sum(e, axis=0, keepdims=True)
                lse_ref[h : h + 1, block] = top + jnp.log(total)
                o = dot_tn(v, e.astype(BF)) * (1.0 / total)
                out_ref[block, lanes] = jnp.transpose(o).astype(BF)
        wait(copies)
        mine_ref[...] = dot_nt(out_ref[:half], w[...])
        theirs_ref[...] = dot_nt(out_ref[half:], w[...]).astype(BF)

    return run(
        kernel,
        [shape((rows, wide), BF), shape((8, rows), F32), shape((half, D), F32), shape((half, D), BF)],
        [q, *ks, *vs, *biases],
        pieces,
        weight(n, wide),
        flops=2 * rows * wide * (2 * nk + D),
        exps=rows * nk * heads,
    )


def attend_back(xs, pieces, first, q, ks, vs, bias, lse, sofar):
    rows, wide = q.shape
    heads = wide // HEAD
    nk = sum(k.shape[0] for k in ks)
    n = len(pieces)
    parts = len(ks)
    biases = [] if bias is None else [bias]

    def kernel(*refs):
        x_refs, q_ref, refs = refs[:2], refs[2], refs[3:]
        k_refs, v_refs, lse_ref, refs = refs[:parts], refs[parts : 2 * parts], refs[2 * parts], refs[2 * parts + 1 :]
        b_refs, refs = refs[: len(biases)], refs[len(biases) :]
        old_refs, refs = refs[: len(sofar)], refs[len(sofar) :]
        piece_refs, (dq_ref, dk_ref, dv_ref, w, sems, do_ref) = refs[:n], refs[n:]
        wait(load(piece_refs, w, sems, first))
        for i in range(2):
            m = x_refs[i].shape[0]
            do_ref[i * m : (i + 1) * m] = dot_nn(x_refs[i][...], w[...]).astype(BF)
        for h in range(heads):
            lanes = slice(h * HEAD, (h + 1) * HEAD)
            k = jnp.concatenate([r[:, lanes] for r in k_refs]) if parts > 1 else k_refs[0][:, lanes]
            v = jnp.concatenate([r[:, lanes] for r in v_refs]) if parts > 1 else v_refs[0][:, lanes]
            for b in range(rows // QB):
                block = slice(b * QB, (b + 1) * QB)
                qb = q_ref[block, lanes]
                do = do_ref[block, lanes]
                s = dot_nt(k, qb) * FACTOR
                if biases:
                    s = s + b_refs[0][...]
                p = jnp.exp(s - lse_ref[h : h + 1, block])
                dp = dot_nt(v, do)
                center = jnp.sum(p * dp, axis=0, keepdims=True)
                ds = (p * (dp - center)).astype(BF)
                dq_ref[block, lanes] = dot_tn(ds, k) * FACTOR
                dk = dot_nn(ds, qb) * FACTOR
                dv = dot_nn(p.astype(BF), do)
                if b == 0 and not sofar:
                    dk_ref[:, lanes] = dk
                    dv_ref[:, lanes] = dv
                elif b == 0:
                    dk_ref[:, lanes] = old_refs[0][:, lanes] + dk
                    dv_ref[:, lanes] = old_refs[1][:, lanes] + dv
                else:
                    dk_ref[:, lanes] += dk
                    dv_ref[:, lanes] += dv

    return run(
        kernel,
        [shape((rows, wide), F32), shape((nk, wide), F32), shape((nk, wide), F32)],
        [*xs, q, *ks, *vs, lse, *biases, *sofar],
        pieces,
        weight(n, wide) + [pltpu.VMEM((rows, wide), BF)],
        flops=2 * rows * wide * (5 * nk + D),
        exps=rows * nk * heads,
    )


def root_dots(dys, raws, stats, gains, tables, wide):
    count = len(gains)
    outs = [shape(dy.shape, F32) for dy in dys] if tables else []
    outs += [shape((8, dy.shape[0]), F32) for dy in dys]
    outs += [shape((8, wide), F32)]

    def kernel(*refs):
        dy_refs, refs = refs[:count], refs[count:]
        raw_refs, refs = refs[:count], refs[count:]
        stat_refs, refs = refs[:count], refs[count:]
        gain_refs, refs = refs[:count], refs[count:]
        if tables:
            cos_ref, sin_ref, refs = refs[0], refs[1], refs[2:]
            turned, refs = refs[:count], refs[count:]
        dot_refs, grad_ref = refs[:count], refs[count]
        grad_ref[...] = jnp.zeros_like(grad_ref)
        for i in range(count):
            row = raws[i][2]
            m = dy_refs[i].shape[0]
            scale = lax.rsqrt(to_columns(stat_refs[i][...]) / D + EPS)[:, row : row + 1]
            dots = jnp.zeros((m, 1), F32)
            for h in range(wide // HEAD):
                own = slice(h * HEAD, (h + 1) * HEAD)
                dy = dy_refs[i][:, own]
                if tables:
                    dy = turn(dy, cos_ref[...], -sin_ref[...])
                    turned[i][:, own] = dy
                c = raws[i][1] + h * HEAD
                both = raw_refs[i][:, c : c + HEAD] * dy
                dots = dots + jnp.sum(both * gain_refs[i][:, own], axis=1, keepdims=True)
                grad_ref[i : i + 1, own] = jnp.sum(both * scale, axis=0, keepdims=True)
            dot_refs[i][...] = to_rows([dots], m)

    args = [*dys, *(r[0] for r in raws), *stats, *gains]
    if tables:
        args += [*tables]
    return run(kernel, outs, args, flops=1e9)


def root_back(dys, raws, stats, dots, gains, dv, pieces, first, wide, halves):
    count = len(gains)
    extra = 0 if dv is None else 1
    rows = dys[0].shape[0]
    cols = (count + extra) * wide
    n = len(pieces)
    part = rows // (2 * halves)
    vs = [] if dv is None else [dv]

    def kernel(*refs):
        dy_refs, refs = refs[:count], refs[count:]
        raw_refs, refs = refs[:count], refs[count:]
        stat_refs, refs = refs[:count], refs[count:]
        dot_refs, refs = refs[:count], refs[count:]
        gain_refs, refs = refs[:count], refs[count:]
        v_refs, refs = refs[:extra], refs[extra:]
        piece_refs, refs = refs[:n], refs[n:]
        low_ref, refs = refs[0], refs[1:]
        mine_refs, their_refs, (w, sems) = refs[:halves], refs[halves : 2 * halves], refs[2 * halves :]
        copies = load(piece_refs, w, sems, first)
        for i in range(count):
            row = raws[i][2]
            scale = lax.rsqrt(to_columns(stat_refs[i][...]) / D + EPS)[:, row : row + 1]
            along = scale * scale * scale * to_columns(dot_refs[i][...])[:, 0:1] / D
            for h in range(wide // HEAD):
                own = slice(h * HEAD, (h + 1) * HEAD)
                c = raws[i][1] + h * HEAD
                dx = scale * gain_refs[i][:, own] * dy_refs[i][:, own] - raw_refs[i][:, c : c + HEAD] * along
                low_ref[:, i * wide + h * HEAD : i * wide + (h + 1) * HEAD] = dx.astype(BF)
        if extra:
            low_ref[:, count * wide :] = v_refs[0][...].astype(BF)
        wait(copies)
        for j in range(halves):
            at = 2 * part * j
            mine_refs[j][...] = dot_nt(low_ref[at : at + part], w[...])
            their_refs[j][...] = dot_nt(low_ref[at + part : at + 2 * part], w[...]).astype(BF)

    return run(
        kernel,
        [shape((rows, cols), BF)]
        + [shape((part, D), F32)] * halves
        + [shape((part, D), BF)] * halves,
        [*dys, *(r[0] for r in raws), *stats, *dots, *gains, *vs],
        pieces,
        weight(n, cols),
        flops=2 * rows * cols * D,
    )


HC = 768


def expand(xs, pieces, first, hid):
    rows = sum(x.shape[0] for x in xs)
    n = len(pieces)

    def kernel(*refs):
        x_refs, piece_refs, (out_ref, w, sems) = refs[: len(xs)], refs[len(xs) : len(xs) + n], refs[len(xs) + n :]
        chunks = [load(piece_refs[j : j + 1], w.at[j], sems.at[j], first) for j in range(hid // HC)]
        for j in range(hid // HC):
            wait(chunks[j])
            at = 0
            for x_ref in x_refs:
                m = x_ref.shape[0]
                out_ref[at : at + m, j * HC : (j + 1) * HC] = dot_nn(x_ref[...], w[j]).astype(BF)
                at += m

    return run(
        kernel,
        [shape((rows, hid), BF)],
        xs,
        pieces,
        [pltpu.VMEM((hid // HC, D, HC), BF), pltpu.SemaphoreType.DMA((hid // HC, 1))],
        flops=2 * rows * D * hid,
    )[0]


def feed(xs, dact, pieces, first):
    rows, hid = dact.shape
    n = len(pieces)
    m = rows // 2

    def kernel(*refs):
        x_refs, dact_ref, piece_refs = refs[:2], refs[2], refs[3 : 3 + n]
        act_ref, dpre_ref, mine_ref, theirs_ref, w, sems = refs[3 + n :]
        chunks = [load(piece_refs[j : j + 1], w.at[j], sems.at[j], first) for j in range(hid // HC)]
        for j in range(hid // HC):
            cols = slice(j * HC, (j + 1) * HC)
            wait(chunks[j])
            for i in range(2):
                own = slice(i * m, (i + 1) * m)
                u = dot_nn(x_refs[i][...], w[j])
                sq = u * u
                th = jnp.tanh(u * (GELU + GELU * CUBE * sq))
                near = 0.5 + 0.5 * th
                act_ref[own, cols] = (u * near).astype(BF)
                slope = near + u * near * (1.0 - th) * (GELU + 3 * GELU * CUBE * sq)
                dpre_ref[own, cols] = (dact_ref[own, cols].astype(F32) * slope).astype(BF)
        for i in range(2):
            own = slice(i * m, (i + 1) * m)
            total = dot_nt(dpre_ref[own, :HC], w[0])
            for j in range(1, hid // HC):
                total = total + dot_nt(dpre_ref[own, j * HC : (j + 1) * HC], w[j])
            if i == 0:
                mine_ref[...] = total
            else:
                theirs_ref[...] = total.astype(BF)

    return run(
        kernel,
        [shape((rows, hid), BF), shape((rows, hid), BF), shape((m, D), F32), shape((m, D), BF)],
        [*xs, dact],
        pieces,
        [pltpu.VMEM((hid // HC, D, HC), BF), pltpu.SemaphoreType.DMA((hid // HC, 1))],
        flops=4 * rows * D * hid,
        exps=rows * hid,
        limit=60,
    )


def contract(act, pieces, first):
    rows, hid = act.shape
    n = len(pieces)
    m = rows // 2

    def kernel(*refs):
        act_ref, piece_refs, (mine_ref, theirs_ref, w, sems) = refs[0], refs[1 : 1 + n], refs[1 + n :]
        chunks = [load(piece_refs[j : j + 1], w.at[j], sems.at[j], first) for j in range(hid // HC)]
        for chunk in chunks:
            wait(chunk)
        for i in range(2):
            own = slice(i * m, (i + 1) * m)
            total = dot_nt(act_ref[own, :HC], w[0])
            for j in range(1, hid // HC):
                total = total + dot_nt(act_ref[own, j * HC : (j + 1) * HC], w[j])
            if i == 0:
                mine_ref[...] = total
            else:
                theirs_ref[...] = total.astype(BF)

    return run(
        kernel,
        [shape((m, D), F32), shape((m, D), BF)],
        [act],
        pieces,
        [pltpu.VMEM((hid // HC, D, HC), BF), pltpu.SemaphoreType.DMA((hid // HC, 1))],
        flops=2 * rows * D * hid,
    )


GC = 384


def full_grads(xs, ys):
    cols = ys[0].shape[1]
    most = sum(x.shape[0] for x in xs)

    def kernel(*refs):
        x_refs, y_refs, (out_ref, turned) = refs[: len(xs)], refs[len(xs) : -2], refs[-2:]
        row = 0
        for x_ref in x_refs:
            m = x_ref.shape[0]
            turned[:, row : row + m] = jnp.transpose(x_ref[...])
            row += m
        for c in range(0, cols, HC):
            lanes = slice(c, c + HC)
            for k in range(0, D, 512):
                row = 0
                total = None
                for y_ref in y_refs:
                    m = y_ref.shape[0]
                    term = dot_nn(turned[k : k + 512, row : row + m], y_ref[:, lanes])
                    total = term if total is None else total + term
                    row += m
                out_ref[k : k + 512, lanes] = total.astype(BF)

    return run(
        kernel,
        [shape((D, cols), BF)],
        [*xs, *ys],
        (),
        [pltpu.VMEM((D, most), BF)],
        flops=2 * most * D * cols,
        limit=60,
    )[0]


def weight_grads(pairs, n, after=()):
    widths = [ys[0].shape[1] for _, ys in pairs]
    cols = sum(widths)
    r = D // n
    flat = [a for xs, ys in pairs for a in (*xs, *ys)]
    out = shape((n // 2, r, cols), BF)
    most = max(sum(x.shape[0] for x in xs) for xs, _ in pairs)

    def kernel(*refs):
        ins, refs = refs[: len(flat)], refs[len(flat) + len(after) :]
        theirs_ref, mine_ref, total_ref, turned, sems = refs
        minor = lax.axis_index("dp") % 2
        at = 0
        col = 0
        copies = []
        for p, (xs, ys) in enumerate(pairs):
            x_refs, y_refs = ins[at : at + len(xs)], ins[at + len(xs) : at + len(xs) + len(ys)]
            at += len(xs) + len(ys)
            row = 0
            for x_ref in x_refs:
                m = x_ref.shape[0]
                turned[:, row : row + m] = jnp.transpose(x_ref[...])
                row += m
            for c in range(0, widths[p], GC):
                lanes = slice(c, c + GC)
                for k in range(0, D, 512):
                    row = 0
                    total = None
                    for y_ref in y_refs:
                        m = y_ref.shape[0]
                        term = dot_nn(turned[k : k + 512, row : row + m], y_ref[:, lanes])
                        total = term if total is None else total + term
                        row += m
                    total_ref[k : k + 512, col + c : col + c + GC] = total.astype(BF)
                for j in range(n // 2):
                    for flip, ref in ((1, theirs_ref), (0, mine_ref)):
                        block = 2 * j + (1 - minor if flip else minor)
                        copy = pltpu.make_async_copy(
                            total_ref.at[
                                pl.ds(pl.multiple_of(block * r, 16), r), pl.ds(col + c, GC)
                            ],
                            ref.at[j, :, pl.ds(col + c, GC)],
                            sems.at[(col + c) // GC, 2 * j + flip],
                        )
                        copy.start()
                        copies.append(copy)
            col += widths[p]
        wait(copies)

    moved = sum(math.prod(v.shape) * 2 for v in flat) + 2 * D * cols
    return pl.pallas_call(
        kernel,
        out_shape=(out, out),
        in_specs=[pl.BlockSpec(memory_space=pltpu.VMEM)] * len(flat)
        + [pl.BlockSpec(memory_space=pl.ANY)] * len(after),
        out_specs=(pl.BlockSpec(memory_space=pl.ANY),) * 2,
        scratch_shapes=[
            pltpu.VMEM((D, cols), BF),
            pltpu.VMEM((D, most), BF),
            pltpu.SemaphoreType.DMA((cols // GC, n)),
        ],
        compiler_params=pltpu.CompilerParams(vmem_limit_bytes=60 * 2**20),
        cost_estimate=pl.CostEstimate(
            flops=int(2 * most * D * cols), bytes_accessed=moved, transcendentals=0
        ),
    )(*flat, *after)


class Flush:
    def __init__(self, names, held, outs, sems):
        self.copies = {
            name: pltpu.make_async_copy(held[j], outs[j], sems.at[j]) for j, name in enumerate(names)
        }
        self.gone = []

    def __call__(self, *names):
        for name in names:
            self.copies[name].start()
            self.gone.append(name)

    def finish(self):
        self(*[name for name in self.copies if name not in self.gone])
        for copy in self.copies.values():
            copy.wait()


def run_remote(kernel, outs, far_outs, blocks, far, scratch, cid, flops):
    moved = sum(math.prod(v.shape) * v.dtype.itemsize for v in (*blocks, *outs.values()))
    vmem, hbm = pl.BlockSpec(memory_space=pltpu.VMEM), pl.BlockSpec(memory_space=pl.ANY)
    n_in, n_out, n_far = len(blocks) + len(far), len(outs), len(far_outs)

    def body(*refs):
        given, refs = refs[:n_in], refs[n_in:]
        results, refs = refs[:n_out], refs[n_out:]
        beyond, refs = refs[:n_far], refs[n_far:]
        held, sems, rest = refs[:n_out], refs[n_out], refs[n_out + 1 :]
        flush = Flush(list(outs), held, results, sems)
        kernel(*given, *held, *beyond, *rest, flush=flush)
        flush.finish()

    got = pl.pallas_call(
        body,
        out_shape=(*outs.values(), *far_outs.values()),
        in_specs=[vmem] * len(blocks) + [hbm] * len(far),
        out_specs=(hbm,) * (n_out + n_far),
        scratch_shapes=[
            *(pltpu.VMEM(v.shape, v.dtype) for v in outs.values()),
            pltpu.SemaphoreType.DMA((n_out,)),
            *scratch,
        ],
        compiler_params=pltpu.CompilerParams(
            vmem_limit_bytes=61 * 2**20, collective_id=cid, has_side_effects=True
        ),
        cost_estimate=pl.CostEstimate(flops=int(flops), bytes_accessed=moved, transcendentals=0),
    )(*blocks, *far)
    return dict(zip([*outs, *far_outs], got))


def tensor_peers():
    t = lax.axis_index("tensor")
    core = t + 1 - 2 * lax.rem(t, 2)
    across = lax.rem(t + 2, 4)
    return t, core, across, 3 - t


def greet(n_dp):
    d = lax.axis_index("dp")
    barrier = pltpu.get_barrier_semaphore()
    for k in range(1, n_dp):
        pl.semaphore_signal(
            barrier, inc=1, device_id={"dp": lax.rem(d + k, n_dp)}, device_id_type=MESH
        )
    for peer in tensor_peers()[1:]:
        pl.semaphore_signal(barrier, inc=1, device_id={"tensor": peer}, device_id_type=MESH)
    pl.semaphore_wait(barrier, n_dp + 2)


def remote(src, dst, send, recv, **place):
    return pltpu.make_async_remote_copy(
        src_ref=src, dst_ref=dst, send_sem=send, recv_sem=recv, device_id=place, device_id_type=MESH
    )


class Gather:
    def __init__(self, ref, sems, n):
        d = lax.axis_index("dp")
        self.z, self.y = d // 2, lax.rem(d, 2)
        self.ref, self.sems, self.n, self.r = ref, sems, n, ref.shape[0] // (2 * n)
        self.cols = (0, ref.shape[1])
        self.near = (0, ref.shape[1] - 256)
        self.last = (ref.shape[1] - 256, ref.shape[1])

    def copy(self, o, kind, index, z, y, own, cols):
        start = (2 * o + (self.y if own else 1 - self.y)) * self.r
        block = self.ref.at[pl.ds(pl.multiple_of(start, 16), self.r), pl.ds(cols[0], cols[1] - cols[0])]
        sems = self.sems
        return remote(block, block, sems.at[2 * kind, index], sems.at[2 * kind + 1, index], dp=2 * z + y)

    def along(self, way, s, own=True):
        kind = (0 if way > 0 else 1) + (0 if own else 3)
        cols = self.cols if own else self.last
        return self.copy(self.z - way * s, kind, s, self.z + way, self.y, own, cols)

    def came(self, way, s, own=True):
        kind = (0 if way > 0 else 1) + (0 if own else 3)
        cols = self.cols if own else self.last
        return self.copy(self.z - way * (s + 1), kind, s, self.z - way, self.y, own, cols)

    def over(self, o, cols):
        return self.copy(o, 2, o, self.z, 1 - self.y, True, cols)

    def inside(self, o):
        return (o >= 0) & (o <= self.n - 1)

    def start(self, own, sem):
        start = (2 * self.z + self.y) * self.r
        copy = pltpu.make_async_copy(own, self.ref.at[pl.ds(pl.multiple_of(start, 16), self.r)], sem)
        copy.start()
        copy.wait()
        for way in (1, -1):
            pl.when(self.inside(self.z + way))(lambda way=way: self.along(way, 0).start())
        self.over(self.z, self.cols).start()

    def step(self, s):
        for way in (1, -1):

            @pl.when(self.inside(self.z - way * (s + 1)))
            def _(way=way):
                self.came(way, s).wait_recv()
                pl.when(self.inside(self.z + way))(lambda: self.along(way, s + 1).start())
                self.over(self.z - way * (s + 1), self.near).start()

        self.rest(s)

    def rest(self, s):
        if s == 0:
            self.copy(self.z, 2, self.z, self.z, 1 - self.y, False, self.cols).wait_recv()
        for way in (1, -1):
            if s == 0:
                pl.when(self.inside(self.z + way))(lambda way=way: self.along(way, 0, False).start())
            else:

                @pl.when(self.inside(self.z - way * s))
                def _(way=way):
                    self.came(way, s - 1, False).wait_recv()
                    if s < self.n - 1:
                        pl.when(self.inside(self.z + way))(lambda: self.along(way, s, False).start())

    def finish(self):
        self.rest(self.n - 1)
        for o in range(self.n):
            pl.when(self.z != o)(
                lambda o=o: self.copy(o, 2, o, self.z, 1 - self.y, False, self.near).wait_recv()
            )

    def drain(self):
        for own in (True, False):
            for s in range(self.n - 1):
                for way in (1, -1):
                    pl.when(self.inside(self.z - way * s) & self.inside(self.z + way))(
                        lambda s=s, way=way, own=own: self.along(way, s, own).wait_send()
                    )
        for o in range(self.n):
            pl.when(self.z == o)(lambda: self.over(self.z, self.cols).wait_send())
            pl.when(self.z != o)(lambda o=o: self.over(o, self.near).wait_send())


class Swap:
    def __init__(self, sems):
        self.sems, self.used, self.sent = sems, 0, []

    def start(self, src, dst, peer):
        k = self.used
        self.used += 1
        copy = remote(src, dst, self.sems.at[0, k], self.sems.at[1, k], tensor=peer)
        copy.start()
        self.sent.append(copy)
        return copy

    def settle(self):
        for copy in self.sent:
            copy.wait_send()
        self.sent = []


class Sums:
    def __init__(self, landed, sems, peers):
        self.landed, self.peers, self.used = landed, peers, 0
        self.swap = Swap(sems)

    def start(self, ref):
        k, c = self.used, ref.shape[1]
        self.used += 1
        copies = [
            self.swap.start(ref, self.landed.at[k, p, :, pl.ds(0, c)], peer)
            for p, peer in enumerate(self.peers)
        ]

        def collect():
            for copy in copies:
                copy.wait()
            stat_sum(ref, [self.landed[k, p, :, :c] for p in range(3)])

        return collect


def project_body(x_refs, w, first, out_ref, low_ref, stat_ref, squares, lows, wide):
    at = 0
    for x_ref in x_refs:
        m = x_ref.shape[0]
        value = dot_nn(x_ref[...], w[:, first : first + (squares + lows) * wide])
        columns = []
        for i in range(squares):
            part = value[:, i * wide : (i + 1) * wide]
            columns.append(jnp.sum(part * part, axis=1, keepdims=True))
        out_ref[at : at + m] = value[:, : squares * wide]
        stat_ref[:, at : at + m] = to_rows(columns, m)
        if lows:
            low_ref[at : at + m] = value[:, squares * wide :].astype(BF)
        at += m


def normalize_body(raw_ref, stat_ref, gains, cos, sin, out_refs, wide):
    scale = lax.rsqrt(to_columns(stat_ref[...]) / D + EPS)
    for i, out_ref in enumerate(out_refs):
        for h in range(wide // HEAD):
            lanes = slice(i * wide + h * HEAD, i * wide + (h + 1) * HEAD)
            value = raw_ref[:, lanes] * scale[:, i : i + 1] * gains[i][h]
            if cos is not None:
                value = turn(value, cos, sin)
            out_ref[:, h * HEAD : (h + 1) * HEAD] = value.astype(BF)


def attend_body(q_ref, k_refs, v_refs, bias_ref, out_ref, lse_ref):
    rows, wide = q_ref.shape
    lse_ref[...] = jnp.zeros_like(lse_ref)
    for h in range(wide // HEAD):
        lanes = slice(h * HEAD, (h + 1) * HEAD)
        k = jnp.concatenate([r[:, lanes] for r in k_refs]) if len(k_refs) > 1 else k_refs[0][:, lanes]
        v = jnp.concatenate([r[:, lanes] for r in v_refs]) if len(v_refs) > 1 else v_refs[0][:, lanes]
        for b in range(rows // QB):
            block = slice(b * QB, (b + 1) * QB)
            s = dot_nt(k, q_ref[block, lanes]) * FACTOR
            if bias_ref is not None:
                s = s + bias_ref[...]
            top = jnp.max(s, axis=0, keepdims=True)
            e = jnp.exp(s - top)
            total = jnp.sum(e, axis=0, keepdims=True)
            lse_ref[h : h + 1, block] = top + jnp.log(total)
            o = dot_tn(v, e.astype(BF)) * (1.0 / total)
            out_ref[block, lanes] = jnp.transpose(o).astype(BF)


def stat_sum(stat_ref, landed):
    h = stat_ref.shape[1] // 2
    other = landed[0] + landed[2]
    total = stat_ref[...] + landed[1]
    stat_ref[:, :h] = total[:, :h] + other[:, h:]
    stat_ref[:, h:] = total[:, h:] + other[:, :h]


def join_body(mine, got, chip):
    def body(i):
        chip[i] = (mine[i] + got[i].astype(F32)).astype(BF)

    over_rows(mine.shape[0], body)


def stream_body(base, chip, far, s, m, t, out_ref, rows_ref):
    def body(i):
        out = base(i) + (chip[i].astype(F32) + far[i].astype(F32)) * s
        out_ref[i] = out
        n, _ = norm_of(out)
        rows_ref[i] = (n * m + t).astype(BF)

    over_rows(rows_ref.shape[0], body)


def self_forward(hidden, context, cotangent, time_rows, tables, small, own_self, own_cross, own_first, n_dp, heads):
    quarter, texts = hidden.shape[0], context.shape[0]
    half, wide = 2 * quarter, heads * HEAD
    n = n_dp // 2
    r = D // n_dp
    g_cols = HEAD // n_dp
    rows = shape((quarter, D), BF)
    outs = dict(
        w_self=shape((D, 4 * wide), BF), w_cross=shape((D, 4 * wide), BF), got=rows,
        c0=shape((texts, D), BF), c1=shape((texts, D), BF), c2=shape((texts, D), BF), c3=shape((texts, D), BF),
        shifts=shape((8, D), F32), gains=shape((16, HEAD), F32),
        x0=rows, x1=rows, x2=rows, x3=rows,
        qk0=shape((half, 2 * wide), F32), qk1=shape((half, 2 * wide), F32),
        v0=shape((half, wide), BF), v1=shape((half, wide), BF),
        stat0=shape((8, half), F32), stat1=shape((8, half), F32),
        q0=shape((half, wide), BF), q1=shape((half, wide), BF),
        k0=shape((half, wide), BF), k1=shape((half, wide), BF),
        attn0=shape((half, wide), BF), attn1=shape((half, wide), BF),
        lse0=shape((8, half), F32), lse1=shape((8, half), F32),
        chip0=rows, chip1=rows, far0=rows, far1=rows,
        after0=shape((quarter, D), F32), after1=shape((quarter, D), F32),
        y0=rows, y1=rows, y2=rows, y3=rows,
        ck_raw=shape((4 * texts, wide), F32), cv=shape((4 * texts, wide), BF),
        ck_stat=shape((8, 4 * texts), F32), ck=shape((4 * texts, wide), BF),
        f0=shape((D, own_first.shape[1]), BF),
    )
    far_outs = dict(g_got=rows)
    blocks = [hidden, context, time_rows, tables[0], tables[1], small]
    far = [own_self, own_cross, own_first, cotangent]
    names = [*outs, *far_outs]

    def kernel(*refs, flush):
        hid, ctx, times, cos, sin, small_ref = refs[:6]
        own1, own2, own3, cot = refs[6:10]
        o = dict(zip(names, refs[10 : 10 + len(names)]))
        all_small, ctx_got, theirs, landed, mine, stats_in, ring, near, cross_x, near_sums, small_sems, local = refs[
            10 + len(names) :
        ]
        t, core, across, diagonal = tensor_peers()
        first = t < 2
        d = lax.axis_index("dp")
        cores, xs = Swap(near), Swap(cross_x)
        greet(n_dp)

        g1 = Gather(o["w_self"], ring.at[0], n)
        g2 = Gather(o["w_cross"], ring.at[1], n)
        g3 = Gather(o["f0"], ring.at[2], n)
        g1.start(own1, local.at[0])
        own_small = all_small.at[pl.ds(pl.multiple_of(d * r, 16), r)]
        own_small[...] = small_ref[...]
        small_copies = []
        for k in range(1, n_dp):
            copy = remote(
                own_small, own_small, small_sems.at[0, k], small_sems.at[1, k], dp=lax.rem(d + k, n_dp)
            )
            copy.start()
            small_copies.append(copy)
        hid_copy = xs.start(hid, o["got"], across)
        ctx_copy = xs.start(ctx, ctx_got, across)
        g_copy = xs.start(cot, o["g_got"], across)

        for k in range(1, n_dp):
            source = lax.rem(d - k + n_dp, n_dp)
            block = all_small.at[pl.ds(pl.multiple_of(source * r, 16), r)]
            remote(block, block, small_sems.at[0, k], small_sems.at[1, k], dp=source).wait_recv()
        turned = jnp.transpose(all_small[...].astype(F32))
        o["shifts"][:6] = turned[:6] + times[...]
        o["shifts"][6:] = turned[6:8]
        at = lax.broadcasted_iota(jnp.int32, (D, HEAD), 0)
        to = lax.broadcasted_iota(jnp.int32, (D, HEAD), 1)
        pick = (at == (to // g_cols) * r + lax.rem(to, g_cols)).astype(F32)
        o["gains"][...] = dot_nn(turned[8:24].astype(BF), pick.astype(BF))
        g1.step(0)

        hid_copy.wait_recv()
        m_row, t_row = 1.0 + o["shifts"][1:2], o["shifts"][0:1]
        slots = [o["x0"], o["x1"], o["x2"], o["x3"]]

        def base(j):
            def pick_rows(i):
                own, other = hid[i].astype(F32), o["got"][i].astype(F32)
                return jnp.where(first, own, other) if j == 0 else jnp.where(first, other, own)

            return pick_rows

        arrivals = []
        for j in range(2):

            def body(i, j=j):
                v, _ = norm_of(base(j)(i))
                slots[2 * j][i] = (v * m_row + t_row).astype(BF)

            over_rows(quarter, body)
            arrivals.append(cores.start(slots[2 * j], slots[2 * j + 1], core))
        g1.step(1)
        ctx_copy.wait_recv()
        c_slots = [o["c0"], o["c1"], o["c2"], o["c3"]]
        a, b = ctx[...].astype(F32), ctx_got[...].astype(F32)
        c_slots[0][...] = jnp.where(first, a, b).astype(BF)
        c_slots[2][...] = jnp.where(first, b, a).astype(BF)
        c_arrivals = [cores.start(c_slots[2 * j], c_slots[2 * j + 1], core) for j in range(2)]
        for s in range(2, n - 1):
            g1.step(s)
        g2.start(own2, local.at[0])
        g1.finish()
        g2.step(0)

        qk, v = [o["qk0"], o["qk1"]], [o["v0"], o["v1"]]
        stat = [o["stat0"], o["stat1"]]
        w_self, w_cross = o["w_self"], o["w_cross"]

        sums = Sums(stats_in, near_sums, (core, across, diagonal))
        shared = []
        for j in range(2):
            arrivals[j].wait_recv()
            project_body(slots[2 * j : 2 * j + 2], w_self, 0, qk[j], v[j], stat[j], 2, 1, wide)
            shared.append(sums.start(stat[j]))
            if j == 0 and n > 2:
                g2.step(1)
        flush("shifts", "gains", "got", "x0", "x1", "x2", "x3", "qk0", "qk1", "v0", "v1")
        q, k = [o["q0"], o["q1"]], [o["k0"], o["k1"]]
        gain = [[o["gains"][i * heads + h : i * heads + h + 1] for h in range(heads)] for i in range(4)]
        for s in range(2, n - 1):
            g2.step(s)
        g3.start(own3, local.at[0])
        for j in range(2):
            shared[j]()
            own = slice(j * half, (j + 1) * half)
            normalize_body(qk[j], stat[j], gain[:2], cos[own], sin[own], [q[j], k[j]], wide)

        flush("stat0", "stat1", "q0", "q1", "k0", "k1")

        attn, lse = [o["attn0"], o["attn1"]], [o["lse0"], o["lse1"]]
        sent = []
        for j in range(2):
            attend_body(q[j], k, v, None, attn[j], lse[j])
            w_out = w_self[:, 3 * wide :]
            theirs[j] = dot_nt(attn[j][quarter:], w_out).astype(BF)
            sent.append(cores.start(theirs.at[j], landed.at[j], core))
            mine[j] = dot_nt(attn[j][:quarter], w_out)
            if j == 0:
                g3.step(0)
        chip, far_refs = [o["chip0"], o["chip1"]], [o["far0"], o["far1"]]
        crossed = []
        for j in range(2):
            sent[j].wait_recv()
            join_body(mine.at[j], landed.at[j], chip[j])
            crossed.append(xs.start(chip[j], far_refs[j], across))
        flush("attn0", "attn1", "lse0", "lse1", "w_self", "chip0", "chip1")
        if n > 2:
            g3.step(1)

        g2.finish()
        for copy in c_arrivals:
            copy.wait_recv()
        project_body(c_slots, w_cross, wide, o["ck_raw"], o["cv"], o["ck_stat"], 1, 1, wide)
        halves = 2 * texts
        for j in range(2):
            part = o["ck_stat"].at[:, pl.ds(j * halves, halves)]
            sums.start(part)()
        normalize_body(o["ck_raw"], o["ck_stat"], gain[3:], None, None, [o["ck"]], wide)

        flush("w_cross", "c0", "c1", "c2", "c3", "ck_raw", "cv", "ck_stat", "ck")

        after = [o["after0"], o["after1"]]
        y_slots = [o["y0"], o["y1"], o["y2"], o["y3"]]
        shifts = o["shifts"]
        passed = []
        for j in range(2):
            crossed[j].wait_recv()
            stream_body(
                base(j), chip[j], far_refs[j], shifts[2:3], shifts[6:7], shifts[7:8], after[j], y_slots[2 * j]
            )
            passed.append(cores.start(y_slots[2 * j], y_slots[2 * j + 1], core))
            flush(f"far{j}", f"after{j}", f"y{2 * j}")
            if j == 0:
                for s in range(2, n - 1):
                    g3.step(s)
        for copy in passed:
            copy.wait_recv()
        flush("y1", "y3")
        g_copy.wait_recv()
        g3.finish()
        for g in (g1, g2, g3):
            g.drain()
        for copy in small_copies:
            copy.wait_send()
        cores.settle()
        xs.settle()

    scratch = [
        pltpu.VMEM((D, HEAD), BF),
        pltpu.VMEM((texts, D), BF),
        pltpu.VMEM((2, quarter, D), BF),
        pltpu.VMEM((2, quarter, D), BF),
        pltpu.VMEM((2, quarter, D), F32),
        pltpu.VMEM((4, 3, 8, half), F32),
        pltpu.SemaphoreType.DMA((3, 10, n)),
        pltpu.SemaphoreType.DMA((2, 8)),
        pltpu.SemaphoreType.DMA((2, 8)),
        pltpu.SemaphoreType.DMA((2, 12)),
        pltpu.SemaphoreType.DMA((2, n_dp)),
        pltpu.SemaphoreType.DMA((1,)),
    ]
    return run_remote(kernel, outs, far_outs, blocks, far, scratch, 1, 2e10)


def cross_forward(state, cotangent, bias, own_second, own_third, n_dp, heads):
    quarter = state["y0"].shape[0]
    half, wide = 2 * quarter, heads * HEAD
    n = n_dp // 2
    rows = shape((quarter, D), BF)
    outs = dict(
        cq_raw0=shape((half, wide), F32), cq_raw1=shape((half, wide), F32),
        cq_stat0=shape((8, half), F32), cq_stat1=shape((8, half), F32),
        cq0=shape((half, wide), BF), cq1=shape((half, wide), BF),
        cattn0=shape((half, wide), BF), cattn1=shape((half, wide), BF),
        clse0=shape((8, half), F32), clse1=shape((8, half), F32),
        after_c0=shape((quarter, D), F32), after_c1=shape((quarter, D), F32),
        z0=rows, z1=rows, z2=rows, z3=rows, d0=rows, d1=rows, d2=rows, d3=rows,
        dact0=shape((2 * half, HC), BF), dact1=shape((2 * half, HC), BF),
        f1=shape((D, own_second.shape[1]), BF), f2=shape((D, own_third.shape[1]), BF),
    )
    far_outs = {}
    given = ("w_cross", "after0", "after1", "y0", "y1", "y2", "y3", "ck", "cv", "shifts", "gains", "g_got")
    blocks = [state[name] for name in given] + [bias, cotangent]
    far = [own_second, own_third, state["f0"]]
    names = [*outs, *far_outs]

    def kernel(*refs, flush):
        i = dict(zip(given, refs))
        bias_ref, cot, own1, own2, f0 = refs[len(given) : len(given) + 5]
        refs = refs[len(given) + 5 :]
        o = dict(zip(names, refs))
        theirs, landed, mine, chips, fars, stats_in, w_down, ring, near, cross_x, near_sums, local = refs[len(names) :]
        t, core, across, diagonal = tensor_peers()
        cores, xs = Swap(near), Swap(cross_x)
        sums = Sums(stats_in, near_sums, (core, across, diagonal))
        greet(n_dp)
        g1 = Gather(o["f1"], ring.at[0], n)
        g2 = Gather(o["f2"], ring.at[1], n)
        g1.start(own1, local.at[0])
        first_down = pltpu.make_async_copy(f0.at[:, pl.ds(HC, HC)], w_down, local.at[1])
        first_down.start()
        d_slots = [o["d0"], o["d1"], o["d2"], o["d3"]]
        s_five = i["shifts"][5:6]
        first = t < 2
        sent_d = []

        def act_grad(part):
            down = o["f1"][:, HC:] if part else w_down[...]
            for p, slot in enumerate(d_slots):
                o[f"dact{part}"][p * quarter : (p + 1) * quarter] = dot_nn(slot[...], down).astype(BF)

        w = i["w_cross"]
        slots = [i["y0"], i["y1"], i["y2"], i["y3"]]
        raw, stat = [o["cq_raw0"], o["cq_raw1"]], [o["cq_stat0"], o["cq_stat1"]]
        q = [o["cq0"], o["cq1"]]
        attn, lse = [o["cattn0"], o["cattn1"]], [o["clse0"], o["clse1"]]
        gain = [i["gains"][2 * heads + h : 2 * heads + h + 1] for h in range(heads)]
        shared = []
        for j in range(2):
            project_body(slots[2 * j : 2 * j + 2], w, 0, raw[j], None, stat[j], 1, 0, wide)
            shared.append(sums.start(stat[j]))

            def scaled(rows, j=j):
                own, other = cot[rows].astype(F32), i["g_got"][rows].astype(F32)
                g = jnp.where(first, own, other) if j == 0 else jnp.where(first, other, own)
                d_slots[2 * j][rows] = (g * s_five).astype(BF)

            over_rows(quarter, scaled)
            sent_d.append(cores.start(d_slots[2 * j], d_slots[2 * j + 1], core))
        sent = []
        for j in range(2):
            shared[j]()
            normalize_body(raw[j], stat[j], [gain], None, None, [q[j]], wide)
            attend_body(q[j], [i["ck"]], [i["cv"]], bias_ref, attn[j], lse[j])
            w_out = w[:, 3 * wide :]
            theirs[j] = dot_nt(attn[j][quarter:], w_out).astype(BF)
            sent.append(cores.start(theirs.at[j], landed.at[j], core))
            mine[j] = dot_nt(attn[j][:quarter], w_out)
            if j == 0:
                g1.step(0)
        crossed = []
        for j in range(2):
            sent[j].wait_recv()
            join_body(mine.at[j], landed.at[j], chips.at[j])
            crossed.append(xs.start(chips.at[j], fars.at[j], across))
        for s in range(1, n - 2):
            g1.step(s)
        for copy in sent_d:
            copy.wait_recv()
        flush("cq_raw0", "cq_raw1", "cq_stat0", "cq_stat1", "cq0", "cq1", "cattn0", "cattn1", "clse0", "clse1")
        first_down.wait()
        act_grad(0)
        flush("d0", "d1", "d2", "d3", "dact0")
        g1.step(n - 2)
        g2.start(own2, local.at[0])
        base = [i["after0"], i["after1"]]
        after = [o["after_c0"], o["after_c1"]]
        z_slots = [o["z0"], o["z1"], o["z2"], o["z3"]]
        m_row, t_row = 1.0 + i["shifts"][4:5], i["shifts"][3:4]
        passed = []
        for j in range(2):
            crossed[j].wait_recv()
            stream_body(
                lambda rows, j=j: base[j][rows], chips.at[j], fars.at[j], 1.0, m_row, t_row, after[j], z_slots[2 * j]
            )
            passed.append(cores.start(z_slots[2 * j], z_slots[2 * j + 1], core))
            flush(f"after_c{j}", f"z{2 * j}")
        g2.step(0)
        g1.finish()
        if n > 2:
            g2.step(1)
        act_grad(1)
        flush("dact1", "f1")
        for s in range(2, n - 1):
            g2.step(s)
        for copy in passed:
            copy.wait_recv()
        flush("z1", "z3")
        g2.finish()
        for g in (g1, g2):
            g.drain()
        cores.settle()
        xs.settle()

    scratch = [
        pltpu.VMEM((2, quarter, D), BF),
        pltpu.VMEM((2, quarter, D), BF),
        pltpu.VMEM((2, quarter, D), F32),
        pltpu.VMEM((2, quarter, D), BF),
        pltpu.VMEM((2, quarter, D), BF),
        pltpu.VMEM((2, 3, 8, half), F32),
        pltpu.VMEM((D, HC), BF),
        pltpu.SemaphoreType.DMA((2, 10, n)),
        pltpu.SemaphoreType.DMA((2, 8)),
        pltpu.SemaphoreType.DMA((2, 8)),
        pltpu.SemaphoreType.DMA((2, 6)),
        pltpu.SemaphoreType.DMA((3,)),
    ]
    return run_remote(kernel, outs, far_outs, blocks, far, scratch, 2, 1e10)


def back_body(g, v, chip, far, m, s, out_ref, rows_ref, sum_ref):
    sum_ref[...] = jnp.zeros_like(sum_ref)

    def body(i):
        da = chip[i].astype(F32) + far[i].astype(F32)
        n, r = norm_of(v[i].astype(F32))
        dn = da * m
        mean = jnp.mean(dn, axis=-1, keepdims=True)
        along = jnp.mean(dn * n, axis=-1, keepdims=True)
        out = g(i) + r * (dn - mean - n * along)
        out_ref[i] = out
        rows_ref[i] = (out * s).astype(BF)
        dan = da * n
        for k in range(STEP // 8):
            sum_ref[:8] += da[k * 8 : k * 8 + 8]
            sum_ref[8:] += dan[k * 8 : k * 8 + 8]

    over_rows(v.shape[0], body)


def feed_forward(state, cotangent, n_dp):
    quarter = state["z0"].shape[0]
    half = 2 * quarter
    rows = shape((quarter, D), BF)
    whole = shape((quarter, D), F32)
    outs = dict(
        gc0=whole, gc1=whole, e0=rows, e1=rows, e2=rows, e3=rows,
        sf0=shape((16, D), F32), sf1=shape((16, D), F32), branch=whole,
    )
    far_outs = {f"t{j}": shape((D, 2 * HC), BF) for j in range(3)}
    given = ("z0", "z1", "z2", "z3", "d0", "d1", "d2", "d3", "after_c0", "after_c1", "shifts", "g_got")
    blocks = [state[name] for name in given] + [cotangent]
    far = [state["f0"], state["f1"], state["f2"], state["dact0"], state["dact1"]]
    names = [*outs, *far_outs]

    def kernel(*refs, flush):
        i = dict(zip(given, refs))
        cot, f, dact, refs = refs[len(given)], refs[len(given) + 1 :][:3], refs[len(given) + 4 :][:2], refs[len(given) + 6 :]
        o = dict(zip(names, refs))
        (
            w, act, dpre, theirs, landed, mine, chips, fars, turned, near, cross_x, local,
        ) = refs[len(names) :]
        t, core, across, diagonal = tensor_peers()
        first = t < 2
        cores, xs = Swap(near), Swap(cross_x)
        loads = [pltpu.make_async_copy(f[j], w.at[j], local.at[j]) for j in range(3)]
        loads += [pltpu.make_async_copy(dact[j], dpre.at[j], local.at[3 + j]) for j in range(2)]
        for copy in loads:
            copy.start()
        greet(n_dp)
        z = [i["z0"], i["z1"], i["z2"], i["z3"]]
        ds = [i["d0"], i["d1"], i["d2"], i["d3"]]
        loads[2].wait()
        for p in range(4):
            dpre[2, p * quarter : (p + 1) * quarter] = dot_nn(ds[p][...], w[2, :, HC:]).astype(BF)

        def pre_part(h, j):
            for p in (2 * h, 2 * h + 1):
                own = slice(p * quarter, (p + 1) * quarter)
                u = dot_nn(z[p][...], w[j, :, :HC])
                sq = u * u
                th = jnp.tanh(u * (GELU + GELU * CUBE * sq))
                near_half = 0.5 + 0.5 * th
                act[j, own] = (u * near_half).astype(BF)
                slope = near_half + u * near_half * (1.0 - th) * (GELU + 3 * GELU * CUBE * sq)
                dpre[j, own] = (dpre[j, own].astype(F32) * slope).astype(BF)

        def contracted(a, p, side):
            own = slice(p * quarter, (p + 1) * quarter)
            total = None
            for j in range(3):
                term = dot_nt(a[j, own], w[j, :, side * HC : (side + 1) * HC])
                total = term if total is None else total + term
            return total

        def back_half(h):
            theirs[h] = contracted(dpre, 2 * h + 1, 0).astype(BF)
            copy = cores.start(theirs.at[h], landed.at[h], core)
            mine[h] = contracted(dpre, 2 * h, 0)
            return copy

        def forward_half(h):
            theirs[2 + h] = contracted(act, 2 * h + 1, 1).astype(BF)
            copy = cores.start(theirs.at[2 + h], landed.at[2 + h], core)
            mine[h] = contracted(act, 2 * h, 1)
            return copy

        def join(k, copy):
            copy.wait_recv()
            join_body(mine.at[k % 2], landed.at[k], chips.at[k])

        loads[0].wait()
        loads[3].wait()
        pre_part(0, 0)
        loads[1].wait()
        loads[4].wait()
        pre_part(0, 1)
        pre_part(0, 2)
        sent = back_half(0)
        pre_part(1, 0)
        join(0, sent)
        crossed = [xs.start(chips.at[0], fars.at[0], across)]
        pre_part(1, 1)
        pre_part(1, 2)
        sent = back_half(1)
        sent_f = forward_half(0)
        join(1, sent)
        crossed.append(xs.start(chips.at[1], fars.at[1], across))
        join(2, sent_f)
        sent_f = forward_half(1)
        join(3, sent_f)
        own_half = jnp.where(first, 0, 1)
        last = xs.start(chips.at[3 - own_half], fars.at[2], across)

        def turn_rows(slots):
            for p in range(4):
                turned[:, p * quarter : (p + 1) * quarter] = jnp.transpose(slots[p][...])

        def weight_grad(j, side, right):
            for k in range(0, D, 512):
                w[j, k : k + 512, side * HC : (side + 1) * HC] = dot_nn(turned[k : k + 512], right[j]).astype(BF)

        def g_of(h):
            def rows_of(r):
                own, other = cot[r].astype(F32), i["g_got"][r].astype(F32)
                return jnp.where(first, own, other) if h == 0 else jnp.where(first, other, own)

            return rows_of

        e = [o["e0"], o["e1"], o["e2"], o["e3"]]
        passed = []

        def norm_half(h):
            crossed[h].wait_recv()
            back_body(
                g_of(h), i[f"after_c{h}"], chips.at[h], fars.at[h], 1.0 + i["shifts"][4:5], 1.0,
                o[f"gc{h}"], e[2 * h], o[f"sf{h}"],
            )
            passed.append(cores.start(e[2 * h], e[2 * h + 1], core))
            flush(f"gc{h}", f"sf{h}", f"e{2 * h}")

        turn_rows(z)
        weight_grad(0, 0, dpre)
        norm_half(0)
        weight_grad(1, 0, dpre)
        weight_grad(2, 0, dpre)
        turn_rows(ds)
        stores = []
        for j in range(3):
            weight_grad(j, 1, act)
            store = pltpu.make_async_copy(w.at[j], o[f"t{j}"], local.at[j])
            store.start()
            stores.append(store)
            if j == 0:
                norm_half(1)
        last.wait_recv()
        o["branch"][...] = chips[2 + own_half].astype(F32) + fars[2].astype(F32)
        for copy in passed:
            copy.wait_recv()
        for store in stores:
            store.wait()
        cores.settle()
        xs.settle()

    scratch = [
        pltpu.VMEM((3, D, 2 * HC), BF),
        pltpu.VMEM((3, 2 * half, HC), BF),
        pltpu.VMEM((3, 2 * half, HC), BF),
        pltpu.VMEM((4, quarter, D), BF),
        pltpu.VMEM((4, quarter, D), BF),
        pltpu.VMEM((2, quarter, D), F32),
        pltpu.VMEM((4, quarter, D), BF),
        pltpu.VMEM((3, quarter, D), BF),
        pltpu.VMEM((D, 2 * half), BF),
        pltpu.SemaphoreType.DMA((2, 8)),
        pltpu.SemaphoreType.DMA((2, 4)),
        pltpu.SemaphoreType.DMA((5,)),
    ]
    return run_remote(kernel, outs, far_outs, blocks, far, scratch, 3, 6e10)


class Scatter:
    def __init__(self, got, arrived, over, along, n):
        d = lax.axis_index("dp")
        self.z, self.y = d // 2, lax.rem(d, 2)
        self.got, self.arrived, self.sems_y, self.sems_z, self.n = got, arrived, over, along, n
        self.r = D // (2 * n)

    def block(self, full, o, own):
        start = (2 * o + (self.y if own else 1 - self.y)) * self.r
        return full.at[pl.ds(pl.multiple_of(start, 16), self.r)]

    def begin(self, full):
        self.full = full
        self.sent = []
        for o in range(self.n):
            copy = remote(
                self.block(full, o, False), self.got.at[o], self.sems_y.at[0, o], self.sems_y.at[1, o],
                dp=2 * self.z + 1 - self.y,
            )
            copy.start()
            self.sent.append(copy)

    def pair(self, a, b, local):
        loads = []
        for o in range(self.n):
            copy = pltpu.make_async_copy(self.block(self.full, o, True), a.at[o], local.at[0, o])
            copy.start()
            loads.append(copy)
        for o in range(self.n):
            self.sent[o].wait()
            copy = pltpu.make_async_copy(self.got.at[o], b.at[o], local.at[1, o])
            copy.start()
            loads.append(copy)
        for o in range(self.n):
            loads[o].wait()
            loads[self.n + o].wait()
            a[o] = (a[o].astype(F32) + b[o].astype(F32)).astype(BF)

    def spread(self, a, relay=None):
        self.a, self.relay = a, relay if self.n == 4 else None
        if self.relay is None:
            self.out = []
            for k in range(1, self.n):
                at = lax.rem(self.z + k, self.n)
                copy = self.send(at, at, self.arrived.at[k - 1], k, k)
                copy.start()
                self.out.append(copy)
            return
        z = self.z
        self.end = (z == 0) | (z == 3)
        self.inner = jnp.where(z < 2, 1, 2)
        self.edge = jnp.where(z < 2, 0, 3)

        @pl.when(self.end)
        def _():
            self.send(3 - z, self.inner, relay.at[0], 1, 1).start()
            self.send(3 - self.inner, self.inner, relay.at[1], 2, 2).start()
            self.send(self.inner, self.inner, self.arrived.at[0], 0, 0).start()

        @pl.when(jnp.logical_not(self.end))
        def _():
            self.send(self.edge, self.edge, self.arrived.at[0], 0, 0).start()

    def send(self, block, to, place, k, j):
        return remote(
            self.a.at[block], place, self.sems_z.at[0, k], self.sems_z.at[1, j], dp=2 * to + self.y
        )

    def forward(self, b, local):
        if self.relay is None:
            return

        @pl.when(jnp.logical_not(self.end))
        def _():
            loads = []
            for k in range(2):
                self.send(self.edge, self.edge, self.relay.at[k], 1 + k, 1 + k).wait_recv()
                copy = pltpu.make_async_copy(self.relay.at[k], b.at[k], local.at[0, k])
                copy.start()
                loads.append(copy)
            for k, to in enumerate((3 - self.edge, 3 - self.inner)):
                loads[k].wait()
                self.a[to] = (self.a[to].astype(F32) + b[k].astype(F32)).astype(BF)
                self.send(to, to, self.arrived.at[1], 1 + k, 3).start()

    def total(self, a, stage, result, sem, b, local):
        count = self.n - 1
        if self.relay is None:
            for copy in self.out:
                copy.wait()
        else:
            count = 2
            for slot, j in ((0, 0), (1, 3)):
                self.send(self.edge, self.edge, self.arrived.at[slot], j, j).wait_recv()
            for k in range(3):
                self.send(self.edge, self.edge, self.arrived.at[0], k, k).wait_send()
        arrived = self.arrived
        if self.n != 4:
            loads = [pltpu.make_async_copy(arrived.at[k], b.at[k], local.at[0, k]) for k in range(count)]
            for copy in loads:
                copy.start()
            wait(loads)
            arrived = b
        total = a[self.z].astype(F32)
        for k in range(count):
            total = total + arrived[k].astype(F32)
        stage[...] = total
        copy = pltpu.make_async_copy(stage, result, sem)
        copy.start()
        copy.wait()


def attend_back_body(do_ref, q_ref, k_refs, v_refs, lse_ref, bias_ref, dq_ref, dk_ref, dv_ref, fresh):
    rows, wide = q_ref.shape
    for h in range(wide // HEAD):
        lanes = slice(h * HEAD, (h + 1) * HEAD)
        k = jnp.concatenate([r[:, lanes] for r in k_refs]) if len(k_refs) > 1 else k_refs[0][:, lanes]
        v = jnp.concatenate([r[:, lanes] for r in v_refs]) if len(v_refs) > 1 else v_refs[0][:, lanes]
        for b in range(rows // QB):
            block = slice(b * QB, (b + 1) * QB)
            qb = q_ref[block, lanes]
            do = do_ref[block, lanes]
            s = dot_nt(k, qb) * FACTOR
            if bias_ref is not None:
                s = s + bias_ref[...]
            p = jnp.exp(s - lse_ref[h : h + 1, block])
            dp = dot_nt(v, do)
            center = jnp.sum(p * dp, axis=0, keepdims=True)
            ds = (p * (dp - center)).astype(BF)
            dq_ref[block, lanes] = dot_tn(ds, k) * FACTOR
            dk = dot_nn(ds, qb) * FACTOR
            dv = dot_nn(p.astype(BF), do)
            if b == 0 and fresh:
                dk_ref[:, lanes] = dk
                dv_ref[:, lanes] = dv
            else:
                dk_ref[:, lanes] += dk
                dv_ref[:, lanes] += dv


def dots_body(dy_ref, raw_ref, col, stat_ref, row, gain, tables, grad_ref, grad_row, wide):
    scale = lax.rsqrt(to_columns(stat_ref[...]) / D + EPS)[:, row : row + 1]
    dots = jnp.zeros((dy_ref.shape[0], 1), F32)
    for h in range(wide // HEAD):
        own = slice(h * HEAD, (h + 1) * HEAD)
        dy = dy_ref[:, own]
        if tables is not None:
            dy = turn(dy, tables[0], -tables[1])
            dy_ref[:, own] = dy
        both = raw_ref[:, col + h * HEAD : col + (h + 1) * HEAD] * dy
        dots = dots + jnp.sum(both * gain[h], axis=1, keepdims=True)
        grad_ref[grad_row : grad_row + 1, own] += jnp.sum(both * scale, axis=0, keepdims=True)
    return dots


def root_back_body(dy_ref, raw_ref, col, stat_ref, row, dots_ref, dots_row, gain, low_ref, at, wide):
    scale = lax.rsqrt(to_columns(stat_ref[...]) / D + EPS)[:, row : row + 1]
    along = scale * scale * scale * to_columns(dots_ref[...])[:, dots_row : dots_row + 1] / D
    for h in range(wide // HEAD):
        own = slice(h * HEAD, (h + 1) * HEAD)
        raw = raw_ref[:, col + h * HEAD : col + (h + 1) * HEAD]
        dx = scale * gain[h] * dy_ref[:, own] - raw * along
        low_ref[:, at + h * HEAD : at + (h + 1) * HEAD] = dx.astype(BF)


class Grads:
    def __init__(self, turned, stage, sems):
        self.turned, self.stage, self.sems = turned, stage, sems
        self.stores = [None, None]
        self.used = 0

    def turn(self, slots):
        at = 0
        for slot in slots:
            m = slot.shape[0]
            self.turned[:, at : at + m] = jnp.transpose(slot[...])
            at += m

    def put(self, ys, full, col):
        i = self.used % 2
        self.used += 1
        if self.stores[i] is not None:
            self.stores[i].wait()
        for k in range(0, D, 512):
            total, at = None, 0
            for y in ys:
                m = y.shape[0]
                term = dot_nn(self.turned[k : k + 512, at : at + m], y)
                total = term if total is None else total + term
                at += m
            self.stage[i, k : k + 512] = total.astype(BF)
        store = pltpu.make_async_copy(self.stage.at[i], full.at[:, pl.ds(col, GC)], self.sems.at[i])
        store.start()
        self.stores[i] = store

    def finish(self):
        for i in range(2):
            if self.stores[i] is not None:
                self.stores[i].wait()
                self.stores[i] = None


def cross_backward(state, bias, n_dp, heads):
    quarter, texts = state["e0"].shape[0], state["c0"].shape[0]
    half, wide = 2 * quarter, heads * HEAD
    n, r = n_dp // 2, D // n_dp
    W = state["t0"].shape[1]
    rows = shape((quarter, D), BF)
    whole = shape((quarter, D), F32)
    sums_shape = shape((16, D), F32)
    outs = dict(
        gs0=whole, gs1=whole, h0=rows, h1=rows, h2=rows, h3=rows, sc0=sums_shape, sc1=sums_shape,
        cross_gain=shape((8, wide), F32), ctx_grad=shape((texts, D), BF),
    )
    far_outs = dict(
        tc=shape((D, 4 * wide), BF), p1=shape((n, r, W), BF), s0=shape((r, W), F32), relay0=shape((2, r, W), BF),
        got0=shape((n, r, W), BF), got1=shape((n, r, W), BF),
    )
    if n != 4:
        far_outs["arrived"] = shape((n - 1, r, W), BF)
    given = (
        "e0", "e1", "e2", "e3", "cq0", "cq1", "ck", "cv", "clse0", "clse1", "cq_raw0", "cq_raw1", "ck_raw",
        "cq_stat0", "cq_stat1", "ck_stat", "gains", "shifts", "gc0", "gc1", "after0", "after1", "w_cross",
        "cattn0", "cattn1", "y0", "y1", "y2", "y3", "c0", "c1", "c2", "c3",
    )
    blocks = [state[name] for name in given] + [bias]
    far = [state["t0"], state["t1"]]
    names = [*outs, *far_outs]

    def kernel(*refs, flush):
        i = dict(zip(given, refs))
        bias_ref, t0, t1 = refs[len(given) : len(given) + 3]
        refs = refs[len(given) + 3 :]
        o = dict(zip(names, refs))
        (
            do, dq, dk, dv, low, dckv, theirs, landed, mine, chips, fars, c_theirs, c_landed, c_chips, c_far,
            dots, ck_dots, stats_in, turned, stage, a, b, arrived, result,
            near, cross_x, near_sums, over, along, local, stores,
        ) = refs[len(names) :]
        t, core, across, diagonal = tensor_peers()
        first = t < 2
        cores, xs = Swap(near), Swap(cross_x)
        sums = Sums(stats_in, near_sums, (core, across, diagonal))
        greet(n_dp)
        arrived = o.get("arrived", arrived)
        f0 = Scatter(o["got0"], arrived, over.at[0], along.at[0], n)
        f1 = Scatter(o["got1"], arrived, over.at[1], along.at[0], n)
        f0.begin(t0)
        w = i["w_cross"]
        e = [i["e0"], i["e1"], i["e2"], i["e3"]]
        gain_q = [i["gains"][2 * heads + h : 2 * heads + h + 1] for h in range(heads)]
        gain_k = [i["gains"][3 * heads + h : 3 * heads + h + 1] for h in range(heads)]
        o["cross_gain"][...] = jnp.zeros_like(o["cross_gain"])

        def back(h):
            for p in range(2):
                do[p * quarter : (p + 1) * quarter] = dot_nn(e[2 * h + p][...], w[:, 3 * wide :]).astype(BF)
            attend_back_body(
                do, i[f"cq{h}"], [i["ck"]], [i["cv"]], i[f"clse{h}"], bias_ref, dq, dk, dv, h == 0
            )
            column = dots_body(
                dq, i[f"cq_raw{h}"], 0, i[f"cq_stat{h}"], 0, gain_q, None, o["cross_gain"], 0, wide
            )
            dots[h] = to_rows([column], half)
            return sums.start(dots.at[h])

        def send(h):
            root_back_body(
                dq, i[f"cq_raw{h}"], 0, i[f"cq_stat{h}"], 0, dots.at[h], 0, gain_q, low.at[h], 0, wide
            )
            theirs[h] = dot_nt(low[h, quarter:], w[:, :wide]).astype(BF)
            copy = cores.start(theirs.at[h], landed.at[h], core)
            mine[...] = dot_nt(low[h, :quarter], w[:, :wide])
            return copy

        def join(h, copy):
            copy.wait_recv()
            join_body(mine, landed.at[h], chips.at[h])
            return xs.start(chips.at[h], fars.at[h], across)

        collect = back(0)
        collect()
        sent0 = send(0)
        collect = back(1)
        crossed = [join(0, sent0)]
        column = dots_body(dk, i["ck_raw"], 0, i["ck_stat"], 0, gain_k, None, o["cross_gain"], 1, wide)
        ck_dots[...] = to_rows([column], 4 * texts)
        collect_k = [sums.start(ck_dots.at[:, pl.ds(j * 2 * texts, 2 * texts)]) for j in range(2)]
        collect()
        sent1 = send(1)
        crossed.append(join(1, sent1))
        f1.begin(t1)
        for part in collect_k:
            part()
        f0.pair(a, b, local)
        f0.spread(a, o["relay0"])

        root_back_body(dk, i["ck_raw"], 0, i["ck_stat"], 0, ck_dots, 0, gain_k, dckv, 0, wide)
        dckv[:, wide:] = dv[...].astype(BF)
        c_sent = []
        for j in range(2):
            at = 2 * texts * j
            c_theirs[j] = dot_nt(dckv[at + texts : at + 2 * texts], w[:, wide : 3 * wide]).astype(BF)
            c_sent.append(cores.start(c_theirs.at[j], c_landed.at[j], core))
        for j in range(2):
            at = 2 * texts * j
            part = dot_nt(dckv[at : at + texts], w[:, wide : 3 * wide])
            c_sent[j].wait_recv()
            c_chips[j] = (part + c_landed[j].astype(F32)).astype(BF)
        own_half = jnp.where(first, 0, 1)
        c_last = xs.start(c_chips.at[1 - own_half], c_far, across)

        h_slots = [o["h0"], o["h1"], o["h2"], o["h3"]]
        passed = []

        def norm_half(h):
            crossed[h].wait_recv()
            back_body(
                lambda rows: i[f"gc{h}"][rows], i[f"after{h}"], chips.at[h], fars.at[h], i["shifts"][6:7],
                i["shifts"][2:3], o[f"gs{h}"], h_slots[2 * h], o[f"sc{h}"],
            )
            passed.append(cores.start(h_slots[2 * h], h_slots[2 * h + 1], core))
            flush(f"gs{h}", f"sc{h}", f"h{2 * h}")

        norm_half(0)
        grads = Grads(turned, stage, stores)
        grads.turn([i["y0"], i["y1"], i["y2"], i["y3"]])
        grads.put([low[0], low[1]], o["tc"], 0)
        norm_half(1)
        f0.forward(b, local)
        grads.turn([i["c0"], i["c1"], i["c2"], i["c3"]])
        for c in range(2):
            grads.put([dckv[:, c * wide : (c + 1) * wide]], o["tc"], (1 + c) * wide)
        grads.turn(e)
        grads.put([i["cattn0"][...], i["cattn1"][...]], o["tc"], 3 * wide)
        c_last.wait_recv()
        o["ctx_grad"][...] = (c_chips[own_half].astype(F32) + c_far[...].astype(F32)).astype(BF)
        grads.finish()
        f0.total(a, result, o["s0"], stores.at[0], b, local)
        f1.pair(a, b, local)
        copy = pltpu.make_async_copy(a, o["p1"], stores.at[0])
        copy.start()
        copy.wait()
        for copy in passed:
            copy.wait_recv()
        cores.settle()
        xs.settle()

    scratch = [
        pltpu.VMEM((half, wide), BF),
        pltpu.VMEM((half, wide), F32),
        pltpu.VMEM((4 * texts, wide), F32),
        pltpu.VMEM((4 * texts, wide), F32),
        pltpu.VMEM((2, half, wide), BF),
        pltpu.VMEM((4 * texts, 2 * wide), BF),
        pltpu.VMEM((2, quarter, D), BF),
        pltpu.VMEM((2, quarter, D), BF),
        pltpu.VMEM((quarter, D), F32),
        pltpu.VMEM((2, quarter, D), BF),
        pltpu.VMEM((2, quarter, D), BF),
        pltpu.VMEM((2, texts, D), BF),
        pltpu.VMEM((2, texts, D), BF),
        pltpu.VMEM((2, texts, D), BF),
        pltpu.VMEM((texts, D), BF),
        pltpu.VMEM((2, 8, half), F32),
        pltpu.VMEM((8, 4 * texts), F32),
        pltpu.VMEM((4, 3, 8, half), F32),
        pltpu.VMEM((D, 2 * half), BF),
        pltpu.VMEM((2, D, GC), BF),
        pltpu.VMEM((n, r, W), BF),
        pltpu.VMEM((n, r, W), BF),
        pltpu.VMEM((n - 1, r, W) if n == 4 else (8, HEAD), BF),
        pltpu.VMEM((r, W), F32),
        pltpu.SemaphoreType.DMA((2, 8)),
        pltpu.SemaphoreType.DMA((2, 4)),
        pltpu.SemaphoreType.DMA((2, 12)),
        pltpu.SemaphoreType.DMA((2, 2, n)),
        pltpu.SemaphoreType.DMA((1, 2, n)),
        pltpu.SemaphoreType.DMA((2, n)),
        pltpu.SemaphoreType.DMA((2,)),
    ]
    return run_remote(kernel, outs, far_outs, blocks, far, scratch, 4, 4e10)


def self_backward(state, hidden, tables, sums_two, sums_five, n_dp, heads):
    quarter = hidden.shape[0]
    half, wide = 2 * quarter, heads * HEAD
    n, r = n_dp // 2, D // n_dp
    W, V = state["t2"].shape[1], 2 * wide
    g_cols = HEAD // n_dp
    outs = dict(
        hidden_grad=shape((quarter, D), BF), ss=shape((16, D), F32), self_gain=shape((8, wide), F32),
        time=shape((8, D), F32), tiny=shape((r, HEAD), F32),
    )
    far_outs = dict(
        s1=shape((r, W), F32), s2=shape((r, W), F32), s3=shape((r, W), F32), s4=shape((r, V), F32), s5=shape((r, V), F32),
        tv=shape((D, V), BF), tq=shape((D, V), BF),
        relay1=shape((2, r, W), BF), relay2=shape((2, r, W), BF), relay3=shape((2, r, W), BF), relay4=shape((2, r, V), BF),
        got2=shape((n, r, W), BF), got3=shape((n, r, W), BF), got4=shape((n, r, V), BF), got5=shape((n, r, V), BF),
    )
    if n != 4:
        far_outs["arrived"] = shape((3, n - 1, r, W), BF)
        far_outs["arrived_v"] = shape((2, n - 1, r, V), BF)
    given = (
        "h0", "h1", "h2", "h3", "q0", "q1", "k0", "k1", "v0", "v1", "lse0", "lse1", "qk0", "qk1", "stat0", "stat1",
        "gains", "shifts", "gs0", "gs1", "attn0", "attn1", "w_self", "sf0", "sf1", "sc0", "sc1", "cross_gain",
    )
    blocks = [state[name] for name in given] + [hidden, *tables, sums_two, sums_five]
    far = [state["p1"], state["t2"], state["tc"], *(state[f"x{p}"] for p in range(4))]
    names = [*outs, *far_outs]

    def kernel(*refs, flush):
        i = dict(zip(given, refs))
        hid, cos, sin, two, five, p1, t2, tc = refs[len(given) : len(given) + 8]
        xs_far = refs[len(given) + 8 : len(given) + 12]
        refs = refs[len(given) + 12 :]
        o = dict(zip(names, refs))
        (
            do, dq, dk, dv, low, theirs, landed, mine, chips, far_chip,
            dots, stats_in, turned, stage, a, b, arrived, arrived_v, result, four_sums, side, side_in,
            near, cross_x, near_sums, over, along, local, stores, slots, side_sems,
        ) = refs[len(names) :]
        t, core, across, diagonal = tensor_peers()
        first = t < 2
        cores, xs = Swap(near), Swap(cross_x)
        sums = Sums(stats_in, near_sums, (core, across, diagonal))
        held = pltpu.make_async_copy(p1, a.at[0], stores.at[0])
        held.start()
        x_copies = [pltpu.make_async_copy(xs_far[p], theirs.at[p % 2], slots.at[p]) for p in range(4)]
        for p in range(2):
            x_copies[p].start()
        greet(n_dp)
        arrived, arrived_v = o.get("arrived", arrived), o.get("arrived_v", arrived_v)
        f1 = Scatter(None, arrived.at[0], None, along.at[0], n)
        f2 = Scatter(o["got2"], arrived.at[1], over.at[0], along.at[1], n)
        fc = Scatter(o["got3"], arrived.at[2], over.at[1], along.at[2], n)
        fv = Scatter(o["got4"], arrived_v.at[0], over.at[2], along.at[3], n)
        fq = Scatter(o["got5"], arrived_v.at[1], over.at[3], along.at[4], n)
        f2.begin(t2)
        held.wait()
        f1.spread(a.at[0], o["relay1"])
        w = i["w_self"]
        hs = [i["h0"], i["h1"], i["h2"], i["h3"]]
        ks, vs = [i["k0"], i["k1"]], [i["v0"], i["v1"]]
        gain = [[i["gains"][g * heads + h : g * heads + h + 1] for h in range(heads)] for g in range(2)]
        o["self_gain"][...] = jnp.zeros_like(o["self_gain"])
        for h in range(2):
            for p in range(2):
                do[p * quarter : (p + 1) * quarter] = dot_nn(hs[2 * h + p][...], w[:, 3 * wide :]).astype(BF)
            attend_back_body(do, i[f"q{h}"], ks, vs, i[f"lse{h}"], None, dq.at[h], dk, dv, h == 0)
        collects = []
        for h in range(2):
            own = slice(h * half, (h + 1) * half)
            turns = (cos[own], sin[own])
            dk_half = dk.at[pl.ds(h * half, half)]
            columns = [
                dots_body(dq.at[h], i[f"qk{h}"], 0, i[f"stat{h}"], 0, gain[0], turns, o["self_gain"], 0, wide),
                dots_body(dk_half, i[f"qk{h}"], wide, i[f"stat{h}"], 1, gain[1], turns, o["self_gain"], 1, wide),
            ]
            dots[h] = to_rows(columns, half)
            collects.append(sums.start(dots.at[h]))
            low[h, :, 2 * wide :] = dv[own].astype(BF)

        grads = Grads(turned, stage, stores)
        for p in range(4):
            x_copies[p].wait()
            turned[:, p * quarter : (p + 1) * quarter] = jnp.transpose(theirs[p % 2])
            if p < 2:
                x_copies[p + 2].start()
        grads.put([low[0, :, 2 * wide :], low[1, :, 2 * wide :]], o["tv"], 0)
        fc.begin(tc)
        f1.forward(b, local)
        f2.pair(a.at[1], b, local)
        f2.spread(a.at[1], o["relay2"])
        sent = []

        def join(h):
            sent[h].wait_recv()
            join_body(mine, landed.at[h], chips.at[h])

        for h in range(2):
            collects[h]()
            dk_half = dk.at[pl.ds(h * half, half)]
            root_back_body(dq.at[h], i[f"qk{h}"], 0, i[f"stat{h}"], 0, dots.at[h], 0, gain[0], low.at[h], 0, wide)
            root_back_body(
                dk_half, i[f"qk{h}"], wide, i[f"stat{h}"], 1, dots.at[h], 1, gain[1], low.at[h], wide, wide
            )
            theirs[h] = dot_nt(low[h, quarter:], w[:, : 3 * wide]).astype(BF)
            sent.append(cores.start(theirs.at[h], landed.at[h], core))
            if h == 1:
                join(0)
            mine[...] = dot_nt(low[h, :quarter], w[:, : 3 * wide])
        join(1)
        own_half = jnp.where(first, 0, 1)
        last = xs.start(chips.at[1 - own_half], far_chip, across)
        for c in range(2):
            lanes = slice(c * wide, (c + 1) * wide)
            grads.put([low[0, :, lanes], low[1, :, lanes]], o["tq"], c * wide)
        grads.turn(hs)
        grads.put([i["attn0"][...], i["attn1"][...]], o["tv"], wide)
        grads.finish()
        f1.total(a.at[0], result, o["s1"], stores.at[0], b, local)
        fv.begin(o["tv"])

        last.wait_recv()
        m_row = 1.0 + i["shifts"][1:2]
        sum_ref = o["ss"]
        sum_ref[...] = jnp.zeros_like(sum_ref)

        def body(rows):
            da = chips[own_half, rows].astype(F32) + far_chip[rows].astype(F32)
            nv, rv = norm_of(hid[rows].astype(F32))
            dn = da * m_row
            mean = jnp.mean(dn, axis=-1, keepdims=True)
            proj = jnp.mean(dn * nv, axis=-1, keepdims=True)
            g = jnp.where(first, i["gs0"][rows], i["gs1"][rows])
            o["hidden_grad"][rows] = (g + rv * (dn - mean - nv * proj)).astype(BF)
            dan = da * nv
            for k in range(STEP // 8):
                sum_ref[:8] += da[k * 8 : k * 8 + 8]
                sum_ref[8:] += dan[k * 8 : k * 8 + 8]

        over_rows(quarter, body)
        flush("hidden_grad")

        def summed(ref, at):
            return jnp.sum(ref[at : at + 8], axis=0, keepdims=True)

        def own(name, at):
            return jnp.where(first, summed(i[name + "0"], at), summed(i[name + "1"], at))

        four_sums[0] = jnp.concatenate(
            [
                summed(sum_ref, 0), summed(sum_ref, 8), two[...], own("sf", 0), own("sf", 8), five[...],
                own("sc", 8), own("sc", 0),
            ]
        )
        cores.start(four_sums.at[0], four_sums.at[1], core).wait_recv()
        four_sums[2] = four_sums[0] + four_sums[1]
        xs.start(four_sums.at[2], four_sums.at[3], across).wait_recv()
        o["time"][...] = four_sums[2] + four_sums[3]
        flush("time", "ss", "self_gain")
        head_rows = [
            ref[g : g + 1, h * HEAD : (h + 1) * HEAD]
            for ref in (o["self_gain"], i["cross_gain"])
            for g in range(2)
            for h in range(heads)
        ]
        head_rows = jnp.concatenate([*head_rows, jnp.zeros((16 - 4 * heads, HEAD), F32)])
        at = lax.broadcasted_iota(jnp.int32, (D, HEAD), 0)
        to = lax.broadcasted_iota(jnp.int32, (D, HEAD), 1)
        pick = (at == (to // g_cols) * r + lax.rem(to, g_cols)).astype(F32)
        spread = dot_nt(head_rows.astype(BF), pick.astype(BF))
        both = jnp.concatenate([o["time"][...], spread, jnp.zeros((HEAD - 24, D), F32)])
        side[...] = jnp.transpose(both).astype(BF)
        d = lax.axis_index("dp")

        def side_block(k):
            return side.at[pl.ds(pl.multiple_of(lax.rem(d + k, n_dp) * r, 16), r)]

        side_copies = []
        for k in range(1, n_dp):
            copy = remote(
                side_block(k), side_in.at[k - 1], side_sems.at[0, k], side_sems.at[1, k], dp=lax.rem(d + k, n_dp)
            )
            copy.start()
            side_copies.append(copy)
        f2.forward(b, local)
        fq.begin(o["tq"])
        fc.pair(a.at[0], b, local)
        fc.spread(a.at[0], o["relay3"])
        f2.total(a.at[1], result, o["s2"], stores.at[0], b, local)
        a_v, a_q = (a.at[1, :, :, pl.ds(c * V, V)] for c in range(2))
        b_v = b.at[:, :, pl.ds(0, V)]
        fv.pair(a_v, b_v, local)
        fv.spread(a_v, o["relay4"])
        fc.forward(b, local)
        fv.forward(b_v, local)
        fq.pair(a_q, b_v, local)
        fq.spread(a_q)
        fc.total(a.at[0], result, o["s3"], stores.at[0], b, local)
        fv.total(a_v, result.at[:, pl.ds(0, V)], o["s4"], stores.at[0], b_v, local)
        small = side_block(0)[...].astype(F32)
        for k in range(1, n_dp):
            side_copies[k - 1].wait()
            small = small + side_in[k - 1].astype(F32)
        o["tiny"][...] = small
        flush("tiny")
        fq.total(a_q, result.at[:, pl.ds(0, V)], o["s5"], stores.at[0], b_v, local)
        cores.settle()
        xs.settle()

    scratch = [
        pltpu.VMEM((half, wide), BF),
        pltpu.VMEM((2, half, wide), F32),
        pltpu.VMEM((2 * half, wide), F32),
        pltpu.VMEM((2 * half, wide), F32),
        pltpu.VMEM((2, half, 3 * wide), BF),
        pltpu.VMEM((2, quarter, D), BF),
        pltpu.VMEM((2, quarter, D), BF),
        pltpu.VMEM((quarter, D), F32),
        pltpu.VMEM((2, quarter, D), BF),
        pltpu.VMEM((quarter, D), BF),
        pltpu.VMEM((2, 8, half), F32),
        pltpu.VMEM((2, 3, 8, half), F32),
        pltpu.VMEM((D, 2 * half), BF),
        pltpu.VMEM((2, D, GC), BF),
        pltpu.VMEM((2, n, r, W), BF),
        pltpu.VMEM((n, r, W), BF),
        pltpu.VMEM((3, n - 1, r, W) if n == 4 else (8, HEAD), BF),
        pltpu.VMEM((2, n - 1, r, V) if n == 4 else (8, HEAD), BF),
        pltpu.VMEM((r, W), F32),
        pltpu.VMEM((4, 8, D), F32),
        pltpu.VMEM((D, HEAD), BF),
        pltpu.VMEM((n_dp - 1, r, HEAD), BF),
        pltpu.SemaphoreType.DMA((2, 4)),
        pltpu.SemaphoreType.DMA((2, 4)),
        pltpu.SemaphoreType.DMA((2, 6)),
        pltpu.SemaphoreType.DMA((4, 2, n)),
        pltpu.SemaphoreType.DMA((5, 2, n)),
        pltpu.SemaphoreType.DMA((2, n)),
        pltpu.SemaphoreType.DMA((2,)),
        pltpu.SemaphoreType.DMA((4,)),
        pltpu.SemaphoreType.DMA((2, n_dp)),
    ]
    return run_remote(kernel, outs, far_outs, blocks, far, scratch, 5, 5e10)


def rotary_tables(positions, head_dim):
    pair_count = head_dim // 2
    side_pairs = pair_count // 3
    frame_pairs = pair_count - 2 * side_pairs
    pair_index = jnp.arange(pair_count)
    frame_mask = pair_index < frame_pairs
    height_mask = (pair_index >= frame_pairs) & (pair_index < frame_pairs + side_pairs)
    within = jnp.where(
        frame_mask,
        pair_index,
        jnp.where(height_mask, pair_index - frame_pairs, pair_index - frame_pairs - side_pairs),
    )
    extent = jnp.where(frame_mask, frame_pairs, side_pairs)
    frequency = jnp.power(10000.0, -within.astype(F32) / extent.astype(F32))
    coords = positions.astype(F32)
    coordinate = jnp.where(
        frame_mask[None, :],
        coords[0][:, None],
        jnp.where(height_mask[None, :], coords[1][:, None], coords[2][:, None]),
    )
    angles = jnp.repeat(coordinate * frequency[None, :], 2, axis=1)
    parity = jnp.arange(head_dim) % 2
    sign_pattern = jnp.where(parity == 0, -1.0, 1.0)
    return (jnp.cos(angles), jnp.sin(angles) * sign_pattern)


def solution(mesh):
    n_dp = mesh.shape["dp"]
    n_major = n_dp // 2
    pair_perm = [(i, i ^ 1) for i in range(n_dp)]
    ring_perm = {
        t: [((((i // 2) + t) % n_major) * 2 + i % 2, i) for i in range(n_dp)]
        for t in range(1, n_major)
    }
    back_perm = {t: [(b, a) for a, b in ring_perm[t]] for t in ring_perm}
    core_perm = [(i, i ^ 1) for i in range(4)]
    x_perm = [(i, i ^ 2) for i in range(4)]

    def core_swap(v):
        return lax.ppermute(v, "tensor", core_perm)

    def x_swap(v):
        return lax.ppermute(v, "tensor", x_perm)

    def gather_dp(block):
        pieces = []
        for t in range(n_major):
            piece = block if t == 0 else lax.ppermute(block, "dp", ring_perm[t])
            pieces += [piece, lax.ppermute(piece, "dp", pair_perm)]
        return pieces

    def scatter_dp(theirs, mine):
        major = lax.axis_index("dp") // 2
        got = lax.ppermute(theirs, "dp", pair_perm)

        def block(t):
            at = (major + t) % n_major
            a = lax.dynamic_slice_in_dim(mine, at, 1, axis=0)[0].astype(F32)
            return a + lax.dynamic_slice_in_dim(got, at, 1, axis=0)[0].astype(F32)

        arrived = [
            lax.ppermute(block(t).astype(BF), "dp", back_perm[t]) for t in range(1, n_major)
        ]
        total = block(0)
        for piece in arrived:
            total = total + piece.astype(F32)
        return total

    def join(mine, theirs):
        return (mine + core_swap(theirs).astype(F32)).astype(BF)

    def own_half(pair):
        first = lax.axis_index("tensor") < 2
        return jnp.where(first, pair[0], pair[1])

    def other_half(pair):
        first = lax.axis_index("tensor") < 2
        return jnp.where(first, pair[1], pair[0])

    def two_halves(own):
        got = x_swap(own)
        first = lax.axis_index("tensor") < 2
        return jnp.where(first, own, got), jnp.where(first, got, own)

    def sum_all(v):
        v = v + core_swap(v)
        return v + x_swap(v)

    def sum_vectors(v):
        h = v.shape[-1] // 2
        other = core_swap(v)
        v = v + jnp.concatenate([other[..., h:], other[..., :h]], -1)
        return v + x_swap(v)

    def sum_halves(pair):
        both = sum_vectors(jnp.stack(pair))
        return both[0], both[1]

    def quarters(values, axis):
        core = lax.axis_index("tensor") % 2
        step = values.shape[axis] // 4
        return jnp.concatenate(
            [
                lax.dynamic_slice_in_dim(values, at * step, step, axis)
                for at in (core, 1 - core, 2 + core, 3 - core)
            ],
            axis,
        )

    def on_device(
        hidden_in, context, time_emb, text_lengths, positions, modulation,
        self_query, self_key, self_value, self_output, self_query_gain, self_key_gain,
        cross_query, cross_key, cross_value, cross_output, cross_query_gain, cross_key_gain,
        norm_weight, norm_bias, ffn_up, ffn_down, out_cotangent,
    ):
        heads = self_query_gain.shape[0]
        half = positions.shape[1] // 2
        wide = heads * HEAD
        r_dp = self_query.shape[0]
        hid = ffn_up.shape[1]
        spare = -hid % HC

        texts = context.shape[1]
        quarter = half // 2
        g_cols = self_query_gain.shape[1]
        gains = [self_query_gain, self_key_gain, cross_query_gain, cross_key_gain]
        flat = jnp.concatenate([modulation, norm_weight[None], norm_bias[None]])
        side = jnp.pad(jnp.concatenate(gains), ((0, 0), (0, r_dp - g_cols)))
        small = jnp.concatenate([flat, side])
        small = jnp.pad(small, ((0, HEAD - small.shape[0]), (0, 0))).T.astype(BF)
        own_self = jnp.concatenate([self_query, self_key, self_value, self_output.T], axis=1).astype(BF)
        own_cross = jnp.concatenate([cross_query, cross_key, cross_value, cross_output.T], axis=1).astype(BF)
        padded = [jnp.pad(w, ((0, 0), (0, spare))) for w in (ffn_up.astype(BF), ffn_down.T.astype(BF))]
        hid_low = hid + spare
        own_ffn = [
            jnp.concatenate([w[:, j * HC : (j + 1) * HC] for w in padded], axis=1) for j in range(hid_low // HC)
        ]
        tables = rotary_tables(quarters(positions, 1), HEAD)
        text_bias = jnp.where(quarters(jnp.arange(4 * texts), 0) < text_lengths[0], 0.0, -1e30)
        text_bias = text_bias.astype(F32)[:, None]

        st = self_forward(
            hidden_in, context[0], out_cotangent, time_emb[0], tables, small,
            own_self, own_cross, own_ffn[0], n_dp, heads,
        )
        st |= cross_forward(st, out_cotangent, text_bias, own_ffn[1], own_ffn[2], n_dp, heads)
        d = lax.axis_index("dp")
        cosine, sine = ((t[:half], t[half:]) for t in tables)
        s0, s1, s2, s3, s4, s5, norm_gain, norm_shift = (st["shifts"][i : i + 1] for i in range(8))
        sq_gain, sk_gain, cq_gain, ck_gain = (
            st["gains"][i * heads : (i + 1) * heads].reshape(1, wide) for i in range(4)
        )
        ones = jnp.ones((1, D), F32)
        w_self, w_cross = [st["w_self"]], [st["w_cross"]]
        w_ffn = [st["f0"], st["f1"], st["f2"]]
        at_o, at_cq, at_ck, at_co = 3 * wide, 0, wide, 3 * wide

        def both(name):
            return [st[name + "0"], st[name + "1"]]

        def four(name):
            return [[st[name + "0"], st[name + "1"]], [st[name + "2"], st[name + "3"]]]

        first = lax.axis_index("tensor") < 2
        g = [jnp.where(first, out_cotangent, st["g_got"]), jnp.where(first, st["g_got"], out_cotangent)]
        ctx = [st[f"c{i}"] for i in range(4)]
        self_rows, cross_rows, ffn_rows = four("x"), four("y"), four("z")
        qk, v, stat, q, k, attn, lse = (both(name) for name in ("qk", "v", "stat", "q", "k", "attn", "lse"))
        self_chip, self_far, after_self = both("chip"), both("far"), both("after")
        ck_raw, cv, ck_stat, ck = st["ck_raw"], st["cv"], st["ck_stat"], st["ck"]
        cq_raw, cq_stat, cq, cattn, clse = (both(name) for name in ("cq_raw", "cq_stat", "cq", "cattn", "clse"))
        after_cross = both("after_c")

        def with_peer(rows):
            return [rows, core_swap(rows)]

        st |= feed_forward(st, out_cotangent, n_dp)
        g_c, sums_f = both("gc"), both("sf")

        st |= cross_backward(st, text_bias, n_dp, heads)
        g_own = own_half(both("gs"))
        self_branch = own_half(self_chip).astype(F32) + own_half(self_far).astype(F32)
        ffn_branch = st["branch"]
        sums_two = jnp.sum(g_own * self_branch, 0, keepdims=True)
        sums_five = jnp.sum(out_cotangent.astype(F32) * ffn_branch, 0, keepdims=True)
        st |= self_backward(st, hidden_in, tables, sums_two, sums_five, n_dp, heads)
        hid_grads = [st["s0"], st["s1"], st["s2"]]
        up_grad = jnp.concatenate([a[:, :HC] for a in hid_grads], axis=1)
        down_grad = jnp.concatenate([a[:, HC:] for a in hid_grads], axis=1)
        cross_grad = st["s3"]
        qkv_grad = [st["s5"][:, :wide], st["s5"][:, wide:], st["s4"][:, :wide]]
        oT_grad = st["s4"][:, wide:]
        hidden_grad, context_grad = st["hidden_grad"], st["ctx_grad"]

        block_out = (own_half(after_cross) + ffn_branch * s5).astype(BF)

        time_grad = st["time"][:6]
        eight = st["tiny"][:, :8].T
        gains_out = st["tiny"][:g_cols, 8 : 8 + 4 * heads].T.reshape(4, heads, g_cols)

        return (
            block_out,
            hidden_grad,
            context_grad[None],
            time_grad[None],
            eight[:6],
            qkv_grad[0],
            qkv_grad[1],
            qkv_grad[2],
            oT_grad.T,
            gains_out[0],
            gains_out[1],
            cross_grad[:, :wide],
            cross_grad[:, wide : 2 * wide],
            cross_grad[:, 2 * wide : 3 * wide],
            cross_grad[:, 3 * wide :].T,
            gains_out[2],
            gains_out[3],
            eight[6],
            eight[7],
            up_grad[:, :hid],
            down_grad[:, :hid].T,
        )

    rows = P(("dp", "tensor"), None)
    col = P("dp", "tensor")
    row = P("tensor", "dp")
    text = P("dp", "tensor", None)
    time = P("dp", None, None)
    one = P("dp")
    ins = (
        rows, text, time, one, P(None, "dp"), P(None, "dp"),
        col, col, col, row, row, row,
        col, col, col, row, row, row,
        one, one, col, row, rows,
    )
    outs = (
        rows, rows, text, time, P(None, "dp"),
        col, col, col, row, row, row,
        col, col, col, row, row, row,
        one, one, col, row,
    )
    return jax.shard_map(on_device, mesh=mesh, in_specs=ins, out_specs=outs, check_vma=False)
```

```python
import math

import jax
import jax.numpy as jnp
from jax import lax
from jax.experimental import pallas as pl
from jax.experimental.pallas import tpu as pltpu
from jax.sharding import PartitionSpec as P

D = 1536
HEAD = 128
EPS = 1e-6
BF = jnp.bfloat16
F32 = jnp.float32
FACTOR = 1.0 / math.sqrt(HEAD)
GELU = math.sqrt(2.0 / math.pi)
CUBE = 0.044715
MESH = pl.DeviceIdType.MESH


def dot_nn(a, b):
    return lax.dot_general(a, b, (((1,), (0,)), ((), ())), preferred_element_type=F32)


def dot_nt(a, b):
    return lax.dot_general(a, b, (((1,), (1,)), ((), ())), preferred_element_type=F32)


def dot_tn(a, b):
    return lax.dot_general(a, b, (((0,), (0,)), ((), ())), preferred_element_type=F32)


def shape(dims, dtype):
    return jax.ShapeDtypeStruct(dims, dtype)


def run(kernel, outs, blocks, far=(), scratch=(), flops=0, exps=0, limit=60):
    moved = sum(math.prod(v.shape) * v.dtype.itemsize for v in (*blocks, *far, *outs))
    return pl.pallas_call(
        kernel,
        out_shape=tuple(outs),
        in_specs=[pl.BlockSpec(memory_space=pltpu.VMEM)] * len(blocks)
        + [pl.BlockSpec(memory_space=pl.ANY)] * len(far),
        out_specs=tuple(pl.BlockSpec(memory_space=pltpu.VMEM) for _ in outs),
        scratch_shapes=list(scratch),
        compiler_params=pltpu.CompilerParams(vmem_limit_bytes=limit * 2**20),
        cost_estimate=pl.CostEstimate(flops=int(flops), bytes_accessed=moved, transcendentals=int(exps)),
    )(*blocks, *far)


def load(pieces, w, sems, first=0):
    n = len(pieces)
    r, c = w.shape[0] // n, w.shape[1]
    if n == 1:
        copy = pltpu.make_async_copy(pieces[0].at[:, pl.ds(first, c)], w, sems.at[0])
        copy.start()
        return [copy]
    d = lax.axis_index("dp")
    major, minor = d // 2, d % 2
    copies = []
    for i, piece in enumerate(pieces):
        t, flip = i // 2, i % 2
        block = 2 * lax.rem(major + t, n // 2) + (1 - minor if flip else minor)
        rows = pl.ds(pl.multiple_of(block * r, 16), r)
        copy = pltpu.make_async_copy(piece.at[:, pl.ds(first, c)], w.at[rows], sems.at[i])
        copy.start()
        copies.append(copy)
    return copies


def wait(copies):
    for copy in copies:
        copy.wait()


def weight(n, c):
    return [pltpu.VMEM((D, c), BF), pltpu.SemaphoreType.DMA((n,))]


def to_rows(columns, count):
    lane = lax.broadcasted_iota(jnp.int32, (count, 128), 1)
    out = jnp.zeros((count, 128), F32)
    for i, column in enumerate(columns):
        out = jnp.where(lane == i, column, out)
    return jnp.transpose(out)[:8]


def to_columns(rows):
    return jnp.transpose(jnp.concatenate([rows] * 16, axis=0))


def turn(values, cosine, sine):
    even = lax.broadcasted_iota(jnp.int32, values.shape, 1) % 2 == 0
    partner = jnp.where(even, pltpu.roll(values, HEAD - 1, 1), pltpu.roll(values, 1, 1))
    return values * cosine + partner * sine


def norm_of(v):
    center = v - jnp.mean(v, axis=-1, keepdims=True)
    r = lax.rsqrt(jnp.mean(center * center, axis=-1, keepdims=True) + EPS)
    return center * r, r


STEP = 32


def over_rows(count, body):
    def one(i, carry):
        body(pl.ds(pl.multiple_of(i * STEP, STEP), STEP))
        return carry

    lax.fori_loop(0, count // STEP, one, 0)


def norm_first(v, m, t):
    def kernel(v_ref, m_ref, t_ref, rows_ref):
        def body(s):
            n, _ = norm_of(v_ref[s].astype(F32))
            rows_ref[s] = (n * m_ref[...] + t_ref[...]).astype(BF)

        over_rows(v_ref.shape[0], body)

    return run(kernel, [shape(v.shape, BF)], [v, m, t], flops=1e9)[0]


def norm_forward(v, chip, far_chip, s, m, t):
    def kernel(v_ref, a_ref, b_ref, s_ref, m_ref, t_ref, out_ref, rows_ref):
        def body(i):
            branch = a_ref[i].astype(F32) + b_ref[i].astype(F32)
            out = v_ref[i].astype(F32) + branch * s_ref[...]
            out_ref[i] = out
            n, _ = norm_of(out)
            rows_ref[i] = (n * m_ref[...] + t_ref[...]).astype(BF)

        over_rows(v_ref.shape[0], body)

    return run(
        kernel, [shape(v.shape, F32), shape(v.shape, BF)], [v, chip, far_chip, s, m, t], flops=1e9
    )


def norm_backward(g, v, chip, far_chip, m, s):
    def kernel(g_ref, v_ref, a_ref, b_ref, m_ref, s_ref, out_ref, rows_ref, sum_ref):
        sum_ref[...] = jnp.zeros_like(sum_ref)

        def body(i):
            da = a_ref[i].astype(F32) + b_ref[i].astype(F32)
            n, r = norm_of(v_ref[i].astype(F32))
            dn = da * m_ref[...]
            mean = jnp.mean(dn, axis=-1, keepdims=True)
            along = jnp.mean(dn * n, axis=-1, keepdims=True)
            out = g_ref[i].astype(F32) + r * (dn - mean - n * along)
            out_ref[i] = out
            rows_ref[i] = (out * s_ref[...]).astype(BF)
            dan = da * n
            for k in range(STEP // 8):
                sum_ref[:8] += da[k * 8 : k * 8 + 8]
                sum_ref[8:] += dan[k * 8 : k * 8 + 8]

        over_rows(g_ref.shape[0], body)

    return run(
        kernel,
        [shape(g.shape, F32), shape(g.shape, BF), shape((16, D), F32)],
        [g, v, chip, far_chip, m, s],
        flops=1e9,
    )


def hold(v, after):
    def kernel(v_ref, *refs):
        refs[-1][...] = v_ref[...]

    return run(kernel, [shape(v.shape, v.dtype)], [v], after)[0]


def project(xs, pieces, first, squares, lows, wide):
    total = sum(x.shape[0] for x in xs)
    cols = (squares + lows) * wide
    n = len(pieces)
    outs = [shape((total, squares * wide), F32)] * (squares > 0)
    outs += [shape((total, lows * wide), BF)] * (lows > 0)
    outs += [shape((8, total), F32)] * (squares > 0)

    def kernel(*refs):
        x_refs, refs = refs[: len(xs)], refs[len(xs) :]
        piece_refs, refs = refs[:n], refs[n:]
        out_refs, (w, sems) = list(refs[:-2]), refs[-2:]
        wait(load(piece_refs, w, sems, first))
        at = 0
        for x_ref in x_refs:
            m = x_ref.shape[0]
            value = dot_nn(x_ref[...], w[...])
            columns = []
            for i in range(squares):
                part = value[:, i * wide : (i + 1) * wide]
                columns.append(jnp.sum(part * part, axis=1, keepdims=True))
            if squares:
                out_refs[0][at : at + m] = value[:, : squares * wide]
                out_refs[-1][:, at : at + m] = to_rows(columns, m)
            if lows:
                out_refs[1 if squares else 0][at : at + m] = value[:, squares * wide :].astype(BF)
            at += m

    return run(kernel, outs, xs, pieces, weight(n, cols), flops=2 * total * D * cols)


def normalize(raws, stats, gains, tables, wide):
    count = len(gains)
    parts = len(raws)
    outs = [shape((r.shape[0], wide), BF) for r in raws for _ in range(count)]

    def kernel(*refs):
        raw_refs, refs = refs[:parts], refs[parts:]
        stat_refs, refs = refs[:parts], refs[parts:]
        gain_refs, refs = refs[:count], refs[count:]
        if tables:
            cos_refs, sin_refs, refs = refs[:parts], refs[parts : 2 * parts], refs[2 * parts :]
        for p in range(parts):
            scale = lax.rsqrt(to_columns(stat_refs[p][...]) / D + EPS)
            for i in range(count):
                for h in range(wide // HEAD):
                    lanes = slice(i * wide + h * HEAD, i * wide + (h + 1) * HEAD)
                    own = slice(h * HEAD, (h + 1) * HEAD)
                    value = raw_refs[p][:, lanes] * scale[:, i : i + 1] * gain_refs[i][:, own]
                    if tables:
                        value = turn(value, cos_refs[p][...], sin_refs[p][...])
                    refs[p * count + i][:, own] = value.astype(BF)

    args = [*raws, *stats, *gains]
    if tables:
        args += [*tables[0], *tables[1]]
    return run(kernel, outs, args, flops=1e9)


QB = 256


def attend(q, ks, vs, bias, pieces, first):
    rows, wide = q.shape
    heads = wide // HEAD
    nk = sum(k.shape[0] for k in ks)
    n = len(pieces)
    parts = len(ks)
    half = rows // 2
    biases = [] if bias is None else [bias]

    def kernel(*refs):
        q_ref, k_refs, v_refs = refs[0], refs[1 : 1 + parts], refs[1 + parts : 1 + 2 * parts]
        refs = refs[1 + 2 * parts :]
        b_refs, refs = refs[: len(biases)], refs[len(biases) :]
        piece_refs, (out_ref, lse_ref, mine_ref, theirs_ref, w, sems) = refs[:n], refs[n:]
        copies = load(piece_refs, w, sems, first)
        lse_ref[...] = jnp.zeros_like(lse_ref)
        for h in range(heads):
            lanes = slice(h * HEAD, (h + 1) * HEAD)
            k = jnp.concatenate([r[:, lanes] for r in k_refs]) if parts > 1 else k_refs[0][:, lanes]
            v = jnp.concatenate([r[:, lanes] for r in v_refs]) if parts > 1 else v_refs[0][:, lanes]
            for b in range(rows // QB):
                block = slice(b * QB, (b + 1) * QB)
                s = dot_nt(k, q_ref[block, lanes]) * FACTOR
                if biases:
                    s = s + b_refs[0][...]
                top = jnp.max(s, axis=0, keepdims=True)
                e = jnp.exp(s - top)
                total = jnp.sum(e, axis=0, keepdims=True)
                lse_ref[h : h + 1, block] = top + jnp.log(total)
                o = dot_tn(v, e.astype(BF)) * (1.0 / total)
                out_ref[block, lanes] = jnp.transpose(o).astype(BF)
        wait(copies)
        mine_ref[...] = dot_nt(out_ref[:half], w[...])
        theirs_ref[...] = dot_nt(out_ref[half:], w[...]).astype(BF)

    return run(
        kernel,
        [shape((rows, wide), BF), shape((8, rows), F32), shape((half, D), F32), shape((half, D), BF)],
        [q, *ks, *vs, *biases],
        pieces,
        weight(n, wide),
        flops=2 * rows * wide * (2 * nk + D),
        exps=rows * nk * heads,
    )


def attend_back(xs, pieces, first, q, ks, vs, bias, lse, sofar):
    rows, wide = q.shape
    heads = wide // HEAD
    nk = sum(k.shape[0] for k in ks)
    n = len(pieces)
    parts = len(ks)
    biases = [] if bias is None else [bias]

    def kernel(*refs):
        x_refs, q_ref, refs = refs[:2], refs[2], refs[3:]
        k_refs, v_refs, lse_ref, refs = refs[:parts], refs[parts : 2 * parts], refs[2 * parts], refs[2 * parts + 1 :]
        b_refs, refs = refs[: len(biases)], refs[len(biases) :]
        old_refs, refs = refs[: len(sofar)], refs[len(sofar) :]
        piece_refs, (dq_ref, dk_ref, dv_ref, w, sems, do_ref) = refs[:n], refs[n:]
        wait(load(piece_refs, w, sems, first))
        for i in range(2):
            m = x_refs[i].shape[0]
            do_ref[i * m : (i + 1) * m] = dot_nn(x_refs[i][...], w[...]).astype(BF)
        for h in range(heads):
            lanes = slice(h * HEAD, (h + 1) * HEAD)
            k = jnp.concatenate([r[:, lanes] for r in k_refs]) if parts > 1 else k_refs[0][:, lanes]
            v = jnp.concatenate([r[:, lanes] for r in v_refs]) if parts > 1 else v_refs[0][:, lanes]
            for b in range(rows // QB):
                block = slice(b * QB, (b + 1) * QB)
                qb = q_ref[block, lanes]
                do = do_ref[block, lanes]
                s = dot_nt(k, qb) * FACTOR
                if biases:
                    s = s + b_refs[0][...]
                p = jnp.exp(s - lse_ref[h : h + 1, block])
                dp = dot_nt(v, do)
                center = jnp.sum(p * dp, axis=0, keepdims=True)
                ds = (p * (dp - center)).astype(BF)
                dq_ref[block, lanes] = dot_tn(ds, k) * FACTOR
                dk = dot_nn(ds, qb) * FACTOR
                dv = dot_nn(p.astype(BF), do)
                if b == 0 and not sofar:
                    dk_ref[:, lanes] = dk
                    dv_ref[:, lanes] = dv
                elif b == 0:
                    dk_ref[:, lanes] = old_refs[0][:, lanes] + dk
                    dv_ref[:, lanes] = old_refs[1][:, lanes] + dv
                else:
                    dk_ref[:, lanes] += dk
                    dv_ref[:, lanes] += dv

    return run(
        kernel,
        [shape((rows, wide), F32), shape((nk, wide), F32), shape((nk, wide), F32)],
        [*xs, q, *ks, *vs, lse, *biases, *sofar],
        pieces,
        weight(n, wide) + [pltpu.VMEM((rows, wide), BF)],
        flops=2 * rows * wide * (5 * nk + D),
        exps=rows * nk * heads,
    )


def root_dots(dys, raws, stats, gains, tables, wide):
    count = len(gains)
    outs = [shape(dy.shape, F32) for dy in dys] if tables else []
    outs += [shape((8, dy.shape[0]), F32) for dy in dys]
    outs += [shape((8, wide), F32)]

    def kernel(*refs):
        dy_refs, refs = refs[:count], refs[count:]
        raw_refs, refs = refs[:count], refs[count:]
        stat_refs, refs = refs[:count], refs[count:]
        gain_refs, refs = refs[:count], refs[count:]
        if tables:
            cos_ref, sin_ref, refs = refs[0], refs[1], refs[2:]
            turned, refs = refs[:count], refs[count:]
        dot_refs, grad_ref = refs[:count], refs[count]
        grad_ref[...] = jnp.zeros_like(grad_ref)
        for i in range(count):
            row = raws[i][2]
            m = dy_refs[i].shape[0]
            scale = lax.rsqrt(to_columns(stat_refs[i][...]) / D + EPS)[:, row : row + 1]
            dots = jnp.zeros((m, 1), F32)
            for h in range(wide // HEAD):
                own = slice(h * HEAD, (h + 1) * HEAD)
                dy = dy_refs[i][:, own]
                if tables:
                    dy = turn(dy, cos_ref[...], -sin_ref[...])
                    turned[i][:, own] = dy
                c = raws[i][1] + h * HEAD
                both = raw_refs[i][:, c : c + HEAD] * dy
                dots = dots + jnp.sum(both * gain_refs[i][:, own], axis=1, keepdims=True)
                grad_ref[i : i + 1, own] = jnp.sum(both * scale, axis=0, keepdims=True)
            dot_refs[i][...] = to_rows([dots], m)

    args = [*dys, *(r[0] for r in raws), *stats, *gains]
    if tables:
        args += [*tables]
    return run(kernel, outs, args, flops=1e9)


def root_back(dys, raws, stats, dots, gains, dv, pieces, first, wide, halves):
    count = len(gains)
    extra = 0 if dv is None else 1
    rows = dys[0].shape[0]
    cols = (count + extra) * wide
    n = len(pieces)
    part = rows // (2 * halves)
    vs = [] if dv is None else [dv]

    def kernel(*refs):
        dy_refs, refs = refs[:count], refs[count:]
        raw_refs, refs = refs[:count], refs[count:]
        stat_refs, refs = refs[:count], refs[count:]
        dot_refs, refs = refs[:count], refs[count:]
        gain_refs, refs = refs[:count], refs[count:]
        v_refs, refs = refs[:extra], refs[extra:]
        piece_refs, refs = refs[:n], refs[n:]
        low_ref, refs = refs[0], refs[1:]
        mine_refs, their_refs, (w, sems) = refs[:halves], refs[halves : 2 * halves], refs[2 * halves :]
        copies = load(piece_refs, w, sems, first)
        for i in range(count):
            row = raws[i][2]
            scale = lax.rsqrt(to_columns(stat_refs[i][...]) / D + EPS)[:, row : row + 1]
            along = scale * scale * scale * to_columns(dot_refs[i][...])[:, 0:1] / D
            for h in range(wide // HEAD):
                own = slice(h * HEAD, (h + 1) * HEAD)
                c = raws[i][1] + h * HEAD
                dx = scale * gain_refs[i][:, own] * dy_refs[i][:, own] - raw_refs[i][:, c : c + HEAD] * along
                low_ref[:, i * wide + h * HEAD : i * wide + (h + 1) * HEAD] = dx.astype(BF)
        if extra:
            low_ref[:, count * wide :] = v_refs[0][...].astype(BF)
        wait(copies)
        for j in range(halves):
            at = 2 * part * j
            mine_refs[j][...] = dot_nt(low_ref[at : at + part], w[...])
            their_refs[j][...] = dot_nt(low_ref[at + part : at + 2 * part], w[...]).astype(BF)

    return run(
        kernel,
        [shape((rows, cols), BF)]
        + [shape((part, D), F32)] * halves
        + [shape((part, D), BF)] * halves,
        [*dys, *(r[0] for r in raws), *stats, *dots, *gains, *vs],
        pieces,
        weight(n, cols),
        flops=2 * rows * cols * D,
    )


HC = 768


def expand(xs, pieces, first, hid):
    rows = sum(x.shape[0] for x in xs)
    n = len(pieces)

    def kernel(*refs):
        x_refs, piece_refs, (out_ref, w, sems) = refs[: len(xs)], refs[len(xs) : len(xs) + n], refs[len(xs) + n :]
        chunks = [load(piece_refs[j : j + 1], w.at[j], sems.at[j], first) for j in range(hid // HC)]
        for j in range(hid // HC):
            wait(chunks[j])
            at = 0
            for x_ref in x_refs:
                m = x_ref.shape[0]
                out_ref[at : at + m, j * HC : (j + 1) * HC] = dot_nn(x_ref[...], w[j]).astype(BF)
                at += m

    return run(
        kernel,
        [shape((rows, hid), BF)],
        xs,
        pieces,
        [pltpu.VMEM((hid // HC, D, HC), BF), pltpu.SemaphoreType.DMA((hid // HC, 1))],
        flops=2 * rows * D * hid,
    )[0]


def feed(xs, dact, pieces, first):
    rows, hid = dact.shape
    n = len(pieces)
    m = rows // 2

    def kernel(*refs):
        x_refs, dact_ref, piece_refs = refs[:2], refs[2], refs[3 : 3 + n]
        act_ref, dpre_ref, mine_ref, theirs_ref, w, sems = refs[3 + n :]
        chunks = [load(piece_refs[j : j + 1], w.at[j], sems.at[j], first) for j in range(hid // HC)]
        for j in range(hid // HC):
            cols = slice(j * HC, (j + 1) * HC)
            wait(chunks[j])
            for i in range(2):
                own = slice(i * m, (i + 1) * m)
                u = dot_nn(x_refs[i][...], w[j])
                sq = u * u
                th = jnp.tanh(u * (GELU + GELU * CUBE * sq))
                near = 0.5 + 0.5 * th
                act_ref[own, cols] = (u * near).astype(BF)
                slope = near + u * near * (1.0 - th) * (GELU + 3 * GELU * CUBE * sq)
                dpre_ref[own, cols] = (dact_ref[own, cols].astype(F32) * slope).astype(BF)
        for i in range(2):
            own = slice(i * m, (i + 1) * m)
            total = dot_nt(dpre_ref[own, :HC], w[0])
            for j in range(1, hid // HC):
                total = total + dot_nt(dpre_ref[own, j * HC : (j + 1) * HC], w[j])
            if i == 0:
                mine_ref[...] = total
            else:
                theirs_ref[...] = total.astype(BF)

    return run(
        kernel,
        [shape((rows, hid), BF), shape((rows, hid), BF), shape((m, D), F32), shape((m, D), BF)],
        [*xs, dact],
        pieces,
        [pltpu.VMEM((hid // HC, D, HC), BF), pltpu.SemaphoreType.DMA((hid // HC, 1))],
        flops=4 * rows * D * hid,
        exps=rows * hid,
        limit=60,
    )


def contract(act, pieces, first):
    rows, hid = act.shape
    n = len(pieces)
    m = rows // 2

    def kernel(*refs):
        act_ref, piece_refs, (mine_ref, theirs_ref, w, sems) = refs[0], refs[1 : 1 + n], refs[1 + n :]
        chunks = [load(piece_refs[j : j + 1], w.at[j], sems.at[j], first) for j in range(hid // HC)]
        for chunk in chunks:
            wait(chunk)
        for i in range(2):
            own = slice(i * m, (i + 1) * m)
            total = dot_nt(act_ref[own, :HC], w[0])
            for j in range(1, hid // HC):
                total = total + dot_nt(act_ref[own, j * HC : (j + 1) * HC], w[j])
            if i == 0:
                mine_ref[...] = total
            else:
                theirs_ref[...] = total.astype(BF)

    return run(
        kernel,
        [shape((m, D), F32), shape((m, D), BF)],
        [act],
        pieces,
        [pltpu.VMEM((hid // HC, D, HC), BF), pltpu.SemaphoreType.DMA((hid // HC, 1))],
        flops=2 * rows * D * hid,
    )


GC = 384


def full_grads(xs, ys):
    cols = ys[0].shape[1]
    most = sum(x.shape[0] for x in xs)

    def kernel(*refs):
        x_refs, y_refs, (out_ref, turned) = refs[: len(xs)], refs[len(xs) : -2], refs[-2:]
        row = 0
        for x_ref in x_refs:
            m = x_ref.shape[0]
            turned[:, row : row + m] = jnp.transpose(x_ref[...])
            row += m
        for c in range(0, cols, HC):
            lanes = slice(c, c + HC)
            for k in range(0, D, 512):
                row = 0
                total = None
                for y_ref in y_refs:
                    m = y_ref.shape[0]
                    term = dot_nn(turned[k : k + 512, row : row + m], y_ref[:, lanes])
                    total = term if total is None else total + term
                    row += m
                out_ref[k : k + 512, lanes] = total.astype(BF)

    return run(
        kernel,
        [shape((D, cols), BF)],
        [*xs, *ys],
        (),
        [pltpu.VMEM((D, most), BF)],
        flops=2 * most * D * cols,
        limit=60,
    )[0]


def weight_grads(pairs, n, after=()):
    widths = [ys[0].shape[1] for _, ys in pairs]
    cols = sum(widths)
    r = D // n
    flat = [a for xs, ys in pairs for a in (*xs, *ys)]
    out = shape((n // 2, r, cols), BF)
    most = max(sum(x.shape[0] for x in xs) for xs, _ in pairs)

    def kernel(*refs):
        ins, refs = refs[: len(flat)], refs[len(flat) + len(after) :]
        theirs_ref, mine_ref, total_ref, turned, sems = refs
        minor = lax.axis_index("dp") % 2
        at = 0
        col = 0
        copies = []
        for p, (xs, ys) in enumerate(pairs):
            x_refs, y_refs = ins[at : at + len(xs)], ins[at + len(xs) : at + len(xs) + len(ys)]
            at += len(xs) + len(ys)
            row = 0
            for x_ref in x_refs:
                m = x_ref.shape[0]
                turned[:, row : row + m] = jnp.transpose(x_ref[...])
                row += m
            for c in range(0, widths[p], GC):
                lanes = slice(c, c + GC)
                for k in range(0, D, 512):
                    row = 0
                    total = None
                    for y_ref in y_refs:
                        m = y_ref.shape[0]
                        term = dot_nn(turned[k : k + 512, row : row + m], y_ref[:, lanes])
                        total = term if total is None else total + term
                        row += m
                    total_ref[k : k + 512, col + c : col + c + GC] = total.astype(BF)
                for j in range(n // 2):
                    for flip, ref in ((1, theirs_ref), (0, mine_ref)):
                        block = 2 * j + (1 - minor if flip else minor)
                        copy = pltpu.make_async_copy(
                            total_ref.at[
                                pl.ds(pl.multiple_of(block * r, 16), r), pl.ds(col + c, GC)
                            ],
                            ref.at[j, :, pl.ds(col + c, GC)],
                            sems.at[(col + c) // GC, 2 * j + flip],
                        )
                        copy.start()
                        copies.append(copy)
            col += widths[p]
        wait(copies)

    moved = sum(math.prod(v.shape) * 2 for v in flat) + 2 * D * cols
    return pl.pallas_call(
        kernel,
        out_shape=(out, out),
        in_specs=[pl.BlockSpec(memory_space=pltpu.VMEM)] * len(flat)
        + [pl.BlockSpec(memory_space=pl.ANY)] * len(after),
        out_specs=(pl.BlockSpec(memory_space=pl.ANY),) * 2,
        scratch_shapes=[
            pltpu.VMEM((D, cols), BF),
            pltpu.VMEM((D, most), BF),
            pltpu.SemaphoreType.DMA((cols // GC, n)),
        ],
        compiler_params=pltpu.CompilerParams(vmem_limit_bytes=60 * 2**20),
        cost_estimate=pl.CostEstimate(
            flops=int(2 * most * D * cols), bytes_accessed=moved, transcendentals=0
        ),
    )(*flat, *after)


class Flush:
    def __init__(self, names, held, outs, sems):
        self.copies = {
            name: pltpu.make_async_copy(held[j], outs[j], sems.at[j]) for j, name in enumerate(names)
        }
        self.gone = []

    def __call__(self, *names):
        for name in names:
            self.copies[name].start()
            self.gone.append(name)

    def finish(self):
        self(*[name for name in self.copies if name not in self.gone])
        for copy in self.copies.values():
            copy.wait()


def run_remote(kernel, outs, far_outs, blocks, far, scratch, cid, flops):
    moved = sum(math.prod(v.shape) * v.dtype.itemsize for v in (*blocks, *outs.values()))
    vmem, hbm = pl.BlockSpec(memory_space=pltpu.VMEM), pl.BlockSpec(memory_space=pl.ANY)
    n_in, n_out, n_far = len(blocks) + len(far), len(outs), len(far_outs)

    def body(*refs):
        given, refs = refs[:n_in], refs[n_in:]
        results, refs = refs[:n_out], refs[n_out:]
        beyond, refs = refs[:n_far], refs[n_far:]
        held, sems, rest = refs[:n_out], refs[n_out], refs[n_out + 1 :]
        flush = Flush(list(outs), held, results, sems)
        kernel(*given, *held, *beyond, *rest, flush=flush)
        flush.finish()

    got = pl.pallas_call(
        body,
        out_shape=(*outs.values(), *far_outs.values()),
        in_specs=[vmem] * len(blocks) + [hbm] * len(far),
        out_specs=(hbm,) * (n_out + n_far),
        scratch_shapes=[
            *(pltpu.VMEM(v.shape, v.dtype) for v in outs.values()),
            pltpu.SemaphoreType.DMA((n_out,)),
            *scratch,
        ],
        compiler_params=pltpu.CompilerParams(
            vmem_limit_bytes=61 * 2**20, collective_id=cid, has_side_effects=True
        ),
        cost_estimate=pl.CostEstimate(flops=int(flops), bytes_accessed=moved, transcendentals=0),
    )(*blocks, *far)
    return dict(zip([*outs, *far_outs], got))


def tensor_peers():
    t = lax.axis_index("tensor")
    core = t + 1 - 2 * lax.rem(t, 2)
    across = lax.rem(t + 2, 4)
    return t, core, across, 3 - t


def greet(n_dp):
    d = lax.axis_index("dp")
    barrier = pltpu.get_barrier_semaphore()
    for k in range(1, n_dp):
        pl.semaphore_signal(
            barrier, inc=1, device_id={"dp": lax.rem(d + k, n_dp)}, device_id_type=MESH
        )
    for peer in tensor_peers()[1:]:
        pl.semaphore_signal(barrier, inc=1, device_id={"tensor": peer}, device_id_type=MESH)
    pl.semaphore_wait(barrier, n_dp + 2)


def remote(src, dst, send, recv, **place):
    return pltpu.make_async_remote_copy(
        src_ref=src, dst_ref=dst, send_sem=send, recv_sem=recv, device_id=place, device_id_type=MESH
    )


class Gather:
    def __init__(self, ref, sems, n):
        d = lax.axis_index("dp")
        self.z, self.y = d // 2, lax.rem(d, 2)
        self.ref, self.sems, self.n, self.r = ref, sems, n, ref.shape[0] // (2 * n)
        self.cols = (0, ref.shape[1])
        self.near = (0, ref.shape[1] - 256)
        self.last = (ref.shape[1] - 256, ref.shape[1])

    def copy(self, o, kind, index, z, y, own, cols):
        start = (2 * o + (self.y if own else 1 - self.y)) * self.r
        block = self.ref.at[pl.ds(pl.multiple_of(start, 16), self.r), pl.ds(cols[0], cols[1] - cols[0])]
        sems = self.sems
        return remote(block, block, sems.at[2 * kind, index], sems.at[2 * kind + 1, index], dp=2 * z + y)

    def along(self, way, s, own=True):
        kind = (0 if way > 0 else 1) + (0 if own else 3)
        cols = self.cols if own else self.last
        return self.copy(self.z - way * s, kind, s, self.z + way, self.y, own, cols)

    def came(self, way, s, own=True):
        kind = (0 if way > 0 else 1) + (0 if own else 3)
        cols = self.cols if own else self.last
        return self.copy(self.z - way * (s + 1), kind, s, self.z - way, self.y, own, cols)

    def over(self, o, cols):
        return self.copy(o, 2, o, self.z, 1 - self.y, True, cols)

    def inside(self, o):
        return (o >= 0) & (o <= self.n - 1)

    def start(self, own, sem):
        start = (2 * self.z + self.y) * self.r
        copy = pltpu.make_async_copy(own, self.ref.at[pl.ds(pl.multiple_of(start, 16), self.r)], sem)
        copy.start()
        copy.wait()
        for way in (1, -1):
            pl.when(self.inside(self.z + way))(lambda way=way: self.along(way, 0).start())
        self.over(self.z, self.cols).start()

    def step(self, s):
        for way in (1, -1):

            @pl.when(self.inside(self.z - way * (s + 1)))
            def _(way=way):
                self.came(way, s).wait_recv()
                pl.when(self.inside(self.z + way))(lambda: self.along(way, s + 1).start())
                self.over(self.z - way * (s + 1), self.near).start()

        self.rest(s)

    def rest(self, s):
        if s == 0:
            self.copy(self.z, 2, self.z, self.z, 1 - self.y, False, self.cols).wait_recv()
        for way in (1, -1):
            if s == 0:
                pl.when(self.inside(self.z + way))(lambda way=way: self.along(way, 0, False).start())
            else:

                @pl.when(self.inside(self.z - way * s))
                def _(way=way):
                    self.came(way, s - 1, False).wait_recv()
                    if s < self.n - 1:
                        pl.when(self.inside(self.z + way))(lambda: self.along(way, s, False).start())

    def finish(self):
        self.rest(self.n - 1)
        for o in range(self.n):
            pl.when(self.z != o)(
                lambda o=o: self.copy(o, 2, o, self.z, 1 - self.y, False, self.near).wait_recv()
            )

    def drain(self):
        for own in (True, False):
            for s in range(self.n - 1):
                for way in (1, -1):
                    pl.when(self.inside(self.z - way * s) & self.inside(self.z + way))(
                        lambda s=s, way=way, own=own: self.along(way, s, own).wait_send()
                    )
        for o in range(self.n):
            pl.when(self.z == o)(lambda: self.over(self.z, self.cols).wait_send())
            pl.when(self.z != o)(lambda o=o: self.over(o, self.near).wait_send())


class Swap:
    def __init__(self, sems):
        self.sems, self.used, self.sent = sems, 0, []

    def start(self, src, dst, peer):
        k = self.used
        self.used += 1
        copy = remote(src, dst, self.sems.at[0, k], self.sems.at[1, k], tensor=peer)
        copy.start()
        self.sent.append(copy)
        return copy

    def settle(self):
        for copy in self.sent:
            copy.wait_send()
        self.sent = []


class Sums:
    def __init__(self, landed, sems, peers):
        self.landed, self.peers, self.used = landed, peers, 0
        self.swap = Swap(sems)

    def start(self, ref):
        k, c = self.used, ref.shape[1]
        self.used += 1
        copies = [
            self.swap.start(ref, self.landed.at[k, p, :, pl.ds(0, c)], peer)
            for p, peer in enumerate(self.peers)
        ]

        def collect():
            for copy in copies:
                copy.wait()
            stat_sum(ref, [self.landed[k, p, :, :c] for p in range(3)])

        return collect


def project_body(x_refs, w, first, out_ref, low_ref, stat_ref, squares, lows, wide):
    at = 0
    for x_ref in x_refs:
        m = x_ref.shape[0]
        value = dot_nn(x_ref[...], w[:, first : first + (squares + lows) * wide])
        columns = []
        for i in range(squares):
            part = value[:, i * wide : (i + 1) * wide]
            columns.append(jnp.sum(part * part, axis=1, keepdims=True))
        out_ref[at : at + m] = value[:, : squares * wide]
        stat_ref[:, at : at + m] = to_rows(columns, m)
        if lows:
            low_ref[at : at + m] = value[:, squares * wide :].astype(BF)
        at += m


def normalize_body(raw_ref, stat_ref, gains, cos, sin, out_refs, wide):
    scale = lax.rsqrt(to_columns(stat_ref[...]) / D + EPS)
    for i, out_ref in enumerate(out_refs):
        for h in range(wide // HEAD):
            lanes = slice(i * wide + h * HEAD, i * wide + (h + 1) * HEAD)
            value = raw_ref[:, lanes] * scale[:, i : i + 1] * gains[i][h]
            if cos is not None:
                value = turn(value, cos, sin)
            out_ref[:, h * HEAD : (h + 1) * HEAD] = value.astype(BF)


def attend_body(q_ref, k_refs, v_refs, bias_ref, out_ref, lse_ref):
    rows, wide = q_ref.shape
    lse_ref[...] = jnp.zeros_like(lse_ref)
    for h in range(wide // HEAD):
        lanes = slice(h * HEAD, (h + 1) * HEAD)
        k = jnp.concatenate([r[:, lanes] for r in k_refs]) if len(k_refs) > 1 else k_refs[0][:, lanes]
        v = jnp.concatenate([r[:, lanes] for r in v_refs]) if len(v_refs) > 1 else v_refs[0][:, lanes]
        for b in range(rows // QB):
            block = slice(b * QB, (b + 1) * QB)
            s = dot_nt(k, q_ref[block, lanes]) * FACTOR
            if bias_ref is not None:
                s = s + bias_ref[...]
            top = jnp.max(s, axis=0, keepdims=True)
            e = jnp.exp(s - top)
            total = jnp.sum(e, axis=0, keepdims=True)
            lse_ref[h : h + 1, block] = top + jnp.log(total)
            o = dot_tn(v, e.astype(BF)) * (1.0 / total)
            out_ref[block, lanes] = jnp.transpose(o).astype(BF)


def stat_sum(stat_ref, landed):
    h = stat_ref.shape[1] // 2
    other = landed[0] + landed[2]
    total = stat_ref[...] + landed[1]
    stat_ref[:, :h] = total[:, :h] + other[:, h:]
    stat_ref[:, h:] = total[:, h:] + other[:, :h]


def join_body(mine, got, chip):
    def body(i):
        chip[i] = (mine[i] + got[i].astype(F32)).astype(BF)

    over_rows(mine.shape[0], body)


def stream_body(base, chip, far, s, m, t, out_ref, rows_ref):
    def body(i):
        out = base(i) + (chip[i].astype(F32) + far[i].astype(F32)) * s
        out_ref[i] = out
        n, _ = norm_of(out)
        rows_ref[i] = (n * m + t).astype(BF)

    over_rows(rows_ref.shape[0], body)


def self_forward(hidden, context, cotangent, time_rows, tables, small, own_self, own_cross, own_first, n_dp, heads):
    quarter, texts = hidden.shape[0], context.shape[0]
    half, wide = 2 * quarter, heads * HEAD
    n = n_dp // 2
    r = D // n_dp
    g_cols = HEAD // n_dp
    rows = shape((quarter, D), BF)
    outs = dict(
        w_self=shape((D, 4 * wide), BF), w_cross=shape((D, 4 * wide), BF), got=rows,
        c0=shape((texts, D), BF), c1=shape((texts, D), BF), c2=shape((texts, D), BF), c3=shape((texts, D), BF),
        shifts=shape((8, D), F32), gains=shape((16, HEAD), F32),
        x0=rows, x1=rows, x2=rows, x3=rows,
        qk0=shape((half, 2 * wide), F32), qk1=shape((half, 2 * wide), F32),
        v0=shape((half, wide), BF), v1=shape((half, wide), BF),
        stat0=shape((8, half), F32), stat1=shape((8, half), F32),
        q0=shape((half, wide), BF), q1=shape((half, wide), BF),
        k0=shape((half, wide), BF), k1=shape((half, wide), BF),
        attn0=shape((half, wide), BF), attn1=shape((half, wide), BF),
        lse0=shape((8, half), F32), lse1=shape((8, half), F32),
        chip0=rows, chip1=rows, far0=rows, far1=rows,
        after0=shape((quarter, D), F32), after1=shape((quarter, D), F32),
        y0=rows, y1=rows, y2=rows, y3=rows,
        ck_raw=shape((4 * texts, wide), F32), cv=shape((4 * texts, wide), BF),
        ck_stat=shape((8, 4 * texts), F32), ck=shape((4 * texts, wide), BF),
        f0=shape((D, own_first.shape[1]), BF),
    )
    far_outs = dict(g_got=rows)
    blocks = [hidden, context, time_rows, tables[0], tables[1], small]
    far = [own_self, own_cross, own_first, cotangent]
    names = [*outs, *far_outs]

    def kernel(*refs, flush):
        hid, ctx, times, cos, sin, small_ref = refs[:6]
        own1, own2, own3, cot = refs[6:10]
        o = dict(zip(names, refs[10 : 10 + len(names)]))
        all_small, ctx_got, theirs, landed, mine, stats_in, ring, near, cross_x, near_sums, small_sems, local = refs[
            10 + len(names) :
        ]
        t, core, across, diagonal = tensor_peers()
        first = t < 2
        d = lax.axis_index("dp")
        cores, xs = Swap(near), Swap(cross_x)
        greet(n_dp)

        g1 = Gather(o["w_self"], ring.at[0], n)
        g2 = Gather(o["w_cross"], ring.at[1], n)
        g3 = Gather(o["f0"], ring.at[2], n)
        g1.start(own1, local.at[0])
        own_small = all_small.at[pl.ds(pl.multiple_of(d * r, 16), r)]
        own_small[...] = small_ref[...]
        small_copies = []
        for k in range(1, n_dp):
            copy = remote(
                own_small, own_small, small_sems.at[0, k], small_sems.at[1, k], dp=lax.rem(d + k, n_dp)
            )
            copy.start()
            small_copies.append(copy)
        hid_copy = xs.start(hid, o["got"], across)
        ctx_copy = xs.start(ctx, ctx_got, across)
        g_copy = xs.start(cot, o["g_got"], across)

        for k in range(1, n_dp):
            source = lax.rem(d - k + n_dp, n_dp)
            block = all_small.at[pl.ds(pl.multiple_of(source * r, 16), r)]
            remote(block, block, small_sems.at[0, k], small_sems.at[1, k], dp=source).wait_recv()
        turned = jnp.transpose(all_small[...].astype(F32))
        o["shifts"][:6] = turned[:6] + times[...]
        o["shifts"][6:] = turned[6:8]
        at = lax.broadcasted_iota(jnp.int32, (D, HEAD), 0)
        to = lax.broadcasted_iota(jnp.int32, (D, HEAD), 1)
        pick = (at == (to // g_cols) * r + lax.rem(to, g_cols)).astype(F32)
        o["gains"][...] = dot_nn(turned[8:24].astype(BF), pick.astype(BF))
        g1.step(0)

        hid_copy.wait_recv()
        m_row, t_row = 1.0 + o["shifts"][1:2], o["shifts"][0:1]
        slots = [o["x0"], o["x1"], o["x2"], o["x3"]]

        def base(j):
            def pick_rows(i):
                own, other = hid[i].astype(F32), o["got"][i].astype(F32)
                return jnp.where(first, own, other) if j == 0 else jnp.where(first, other, own)

            return pick_rows

        arrivals = []
        for j in range(2):

            def body(i, j=j):
                v, _ = norm_of(base(j)(i))
                slots[2 * j][i] = (v * m_row + t_row).astype(BF)

            over_rows(quarter, body)
            arrivals.append(cores.start(slots[2 * j], slots[2 * j + 1], core))
        g1.step(1)
        ctx_copy.wait_recv()
        c_slots = [o["c0"], o["c1"], o["c2"], o["c3"]]
        a, b = ctx[...].astype(F32), ctx_got[...].astype(F32)
        c_slots[0][...] = jnp.where(first, a, b).astype(BF)
        c_slots[2][...] = jnp.where(first, b, a).astype(BF)
        c_arrivals = [cores.start(c_slots[2 * j], c_slots[2 * j + 1], core) for j in range(2)]
        for s in range(2, n - 1):
            g1.step(s)
        g2.start(own2, local.at[0])
        g1.finish()
        g2.step(0)

        qk, v = [o["qk0"], o["qk1"]], [o["v0"], o["v1"]]
        stat = [o["stat0"], o["stat1"]]
        w_self, w_cross = o["w_self"], o["w_cross"]

        sums = Sums(stats_in, near_sums, (core, across, diagonal))
        shared = []
        for j in range(2):
            arrivals[j].wait_recv()
            project_body(slots[2 * j : 2 * j + 2], w_self, 0, qk[j], v[j], stat[j], 2, 1, wide)
            shared.append(sums.start(stat[j]))
            if j == 0 and n > 2:
                g2.step(1)
        flush("shifts", "gains", "got", "x0", "x1", "x2", "x3", "qk0", "qk1", "v0", "v1")
        q, k = [o["q0"], o["q1"]], [o["k0"], o["k1"]]
        gain = [[o["gains"][i * heads + h : i * heads + h + 1] for h in range(heads)] for i in range(4)]
        for s in range(2, n - 1):
            g2.step(s)
        g3.start(own3, local.at[0])
        for j in range(2):
            shared[j]()
            own = slice(j * half, (j + 1) * half)
            normalize_body(qk[j], stat[j], gain[:2], cos[own], sin[own], [q[j], k[j]], wide)

        flush("stat0", "stat1", "q0", "q1", "k0", "k1")

        attn, lse = [o["attn0"], o["attn1"]], [o["lse0"], o["lse1"]]
        sent = []
        for j in range(2):
            attend_body(q[j], k, v, None, attn[j], lse[j])
            w_out = w_self[:, 3 * wide :]
            theirs[j] = dot_nt(attn[j][quarter:], w_out).astype(BF)
            sent.append(cores.start(theirs.at[j], landed.at[j], core))
            mine[j] = dot_nt(attn[j][:quarter], w_out)
            if j == 0:
                g3.step(0)
        chip, far_refs = [o["chip0"], o["chip1"]], [o["far0"], o["far1"]]
        crossed = []
        for j in range(2):
            sent[j].wait_recv()
            join_body(mine.at[j], landed.at[j], chip[j])
            crossed.append(xs.start(chip[j], far_refs[j], across))
        flush("attn0", "attn1", "lse0", "lse1", "w_self", "chip0", "chip1")
        if n > 2:
            g3.step(1)

        g2.finish()
        for copy in c_arrivals:
            copy.wait_recv()
        project_body(c_slots, w_cross, wide, o["ck_raw"], o["cv"], o["ck_stat"], 1, 1, wide)
        halves = 2 * texts
        for j in range(2):
            part = o["ck_stat"].at[:, pl.ds(j * halves, halves)]
            sums.start(part)()
        normalize_body(o["ck_raw"], o["ck_stat"], gain[3:], None, None, [o["ck"]], wide)

        flush("w_cross", "c0", "c1", "c2", "c3", "ck_raw", "cv", "ck_stat", "ck")

        after = [o["after0"], o["after1"]]
        y_slots = [o["y0"], o["y1"], o["y2"], o["y3"]]
        shifts = o["shifts"]
        passed = []
        for j in range(2):
            crossed[j].wait_recv()
            stream_body(
                base(j), chip[j], far_refs[j], shifts[2:3], shifts[6:7], shifts[7:8], after[j], y_slots[2 * j]
            )
            passed.append(cores.start(y_slots[2 * j], y_slots[2 * j + 1], core))
            flush(f"far{j}", f"after{j}", f"y{2 * j}")
            if j == 0:
                for s in range(2, n - 1):
                    g3.step(s)
        for copy in passed:
            copy.wait_recv()
        flush("y1", "y3")
        g_copy.wait_recv()
        g3.finish()
        for g in (g1, g2, g3):
            g.drain()
        for copy in small_copies:
            copy.wait_send()
        cores.settle()
        xs.settle()

    scratch = [
        pltpu.VMEM((D, HEAD), BF),
        pltpu.VMEM((texts, D), BF),
        pltpu.VMEM((2, quarter, D), BF),
        pltpu.VMEM((2, quarter, D), BF),
        pltpu.VMEM((2, quarter, D), F32),
        pltpu.VMEM((4, 3, 8, half), F32),
        pltpu.SemaphoreType.DMA((3, 10, n)),
        pltpu.SemaphoreType.DMA((2, 8)),
        pltpu.SemaphoreType.DMA((2, 8)),
        pltpu.SemaphoreType.DMA((2, 12)),
        pltpu.SemaphoreType.DMA((2, n_dp)),
        pltpu.SemaphoreType.DMA((1,)),
    ]
    return run_remote(kernel, outs, far_outs, blocks, far, scratch, 1, 2e10)


def cross_forward(state, cotangent, bias, own_second, own_third, n_dp, heads):
    quarter = state["y0"].shape[0]
    half, wide = 2 * quarter, heads * HEAD
    n = n_dp // 2
    rows = shape((quarter, D), BF)
    outs = dict(
        cq_raw0=shape((half, wide), F32), cq_raw1=shape((half, wide), F32),
        cq_stat0=shape((8, half), F32), cq_stat1=shape((8, half), F32),
        cq0=shape((half, wide), BF), cq1=shape((half, wide), BF),
        cattn0=shape((half, wide), BF), cattn1=shape((half, wide), BF),
        clse0=shape((8, half), F32), clse1=shape((8, half), F32),
        after_c0=shape((quarter, D), F32), after_c1=shape((quarter, D), F32),
        z0=rows, z1=rows, z2=rows, z3=rows, d0=rows, d1=rows, d2=rows, d3=rows,
        dpre0=shape((2 * half, HC), BF), dpre1=shape((2 * half, HC), BF),
        act0=shape((2 * half, HC), BF), act1=shape((2 * half, HC), BF),
        f1=shape((D, own_second.shape[1]), BF), f2=shape((D, own_third.shape[1]), BF),
    )
    far_outs = {}
    given = ("w_cross", "after0", "after1", "y0", "y1", "y2", "y3", "ck", "cv", "shifts", "gains", "g_got")
    blocks = [state[name] for name in given] + [bias, cotangent]
    far = [own_second, own_third, state["f0"]]
    names = [*outs, *far_outs]

    def kernel(*refs, flush):
        i = dict(zip(given, refs))
        bias_ref, cot, own1, own2, f0 = refs[len(given) : len(given) + 5]
        refs = refs[len(given) + 5 :]
        o = dict(zip(names, refs))
        theirs, landed, mine, chips, fars, stats_in, w_down, ring, near, cross_x, near_sums, local = refs[len(names) :]
        t, core, across, diagonal = tensor_peers()
        cores, xs = Swap(near), Swap(cross_x)
        sums = Sums(stats_in, near_sums, (core, across, diagonal))
        greet(n_dp)
        g1 = Gather(o["f1"], ring.at[0], n)
        g2 = Gather(o["f2"], ring.at[1], n)
        g1.start(own1, local.at[0])
        first_down = pltpu.make_async_copy(f0.at[:, pl.ds(HC, HC)], w_down, local.at[1])
        first_down.start()
        d_slots = [o["d0"], o["d1"], o["d2"], o["d3"]]
        s_five = i["shifts"][5:6]
        first = t < 2
        sent_d = []

        def act_grad(part):
            down = o["f1"][:, HC:] if part else w_down[...]
            for p, slot in enumerate(d_slots):
                o[f"dpre{part}"][p * quarter : (p + 1) * quarter] = dot_nn(slot[...], down).astype(BF)

        def activate(part, h):
            up = o["f1"][:, :HC] if part else w_down[...]
            act_ref, dpre_ref = o[f"act{part}"], o[f"dpre{part}"]
            for p in (2 * h, 2 * h + 1):
                own = slice(p * quarter, (p + 1) * quarter)
                u = dot_nn(z_slots[p][...], up)
                act_ref[own], slope = gelu_of(u)
                dpre_ref[own] = (dpre_ref[own].astype(F32) * slope).astype(BF)

        w = i["w_cross"]
        slots = [i["y0"], i["y1"], i["y2"], i["y3"]]
        raw, stat = [o["cq_raw0"], o["cq_raw1"]], [o["cq_stat0"], o["cq_stat1"]]
        q = [o["cq0"], o["cq1"]]
        attn, lse = [o["cattn0"], o["cattn1"]], [o["clse0"], o["clse1"]]
        gain = [i["gains"][2 * heads + h : 2 * heads + h + 1] for h in range(heads)]
        shared = []
        for j in range(2):
            project_body(slots[2 * j : 2 * j + 2], w, 0, raw[j], None, stat[j], 1, 0, wide)
            shared.append(sums.start(stat[j]))

            def scaled(rows, j=j):
                own, other = cot[rows].astype(F32), i["g_got"][rows].astype(F32)
                g = jnp.where(first, own, other) if j == 0 else jnp.where(first, other, own)
                d_slots[2 * j][rows] = (g * s_five).astype(BF)

            over_rows(quarter, scaled)
            sent_d.append(cores.start(d_slots[2 * j], d_slots[2 * j + 1], core))
        sent = []
        for j in range(2):
            shared[j]()
            normalize_body(raw[j], stat[j], [gain], None, None, [q[j]], wide)
            attend_body(q[j], [i["ck"]], [i["cv"]], bias_ref, attn[j], lse[j])
            w_out = w[:, 3 * wide :]
            theirs[j] = dot_nt(attn[j][quarter:], w_out).astype(BF)
            sent.append(cores.start(theirs.at[j], landed.at[j], core))
            mine[j] = dot_nt(attn[j][:quarter], w_out)
            if j == 0:
                g1.step(0)
        crossed = []
        for j in range(2):
            sent[j].wait_recv()
            join_body(mine.at[j], landed.at[j], chips.at[j])
            crossed.append(xs.start(chips.at[j], fars.at[j], across))
        for s in range(1, n - 2):
            g1.step(s)
        for copy in sent_d:
            copy.wait_recv()
        flush("cq_raw0", "cq_raw1", "cq_stat0", "cq_stat1", "cq0", "cq1", "cattn0", "cattn1", "clse0", "clse1")
        first_down.wait()
        act_grad(0)
        first_up = pltpu.make_async_copy(f0.at[:, pl.ds(0, HC)], w_down, local.at[2])
        first_up.start()
        flush("d0", "d1", "d2", "d3")
        g1.step(n - 2)
        g2.start(own2, local.at[0])
        base = [i["after0"], i["after1"]]
        after = [o["after_c0"], o["after_c1"]]
        z_slots = [o["z0"], o["z1"], o["z2"], o["z3"]]
        m_row, t_row = 1.0 + i["shifts"][4:5], i["shifts"][3:4]
        passed = []
        for j in range(2):
            crossed[j].wait_recv()
            stream_body(
                lambda rows, j=j: base[j][rows], chips.at[j], fars.at[j], 1.0, m_row, t_row, after[j], z_slots[2 * j]
            )
            passed.append(cores.start(z_slots[2 * j], z_slots[2 * j + 1], core))
            flush(f"after_c{j}", f"z{2 * j}")
            if j == 0:
                g2.step(0)
        g1.finish()
        act_grad(1)
        flush("f1")
        if n > 2:
            g2.step(1)
        first_up.wait()
        for j in range(2):
            passed[j].wait_recv()
            activate(0, j)
        flush("z1", "z3", "act0", "dpre0")
        activate(1, 0)
        for s in range(2, n - 1):
            g2.step(s)
        activate(1, 1)
        flush("act1", "dpre1")
        g2.finish()
        for g in (g1, g2):
            g.drain()
        cores.settle()
        xs.settle()

    scratch = [
        pltpu.VMEM((2, quarter, D), BF),
        pltpu.VMEM((2, quarter, D), BF),
        pltpu.VMEM((2, quarter, D), F32),
        pltpu.VMEM((2, quarter, D), BF),
        pltpu.VMEM((2, quarter, D), BF),
        pltpu.VMEM((2, 3, 8, half), F32),
        pltpu.VMEM((D, HC), BF),
        pltpu.SemaphoreType.DMA((2, 10, n)),
        pltpu.SemaphoreType.DMA((2, 8)),
        pltpu.SemaphoreType.DMA((2, 8)),
        pltpu.SemaphoreType.DMA((2, 6)),
        pltpu.SemaphoreType.DMA((3,)),
    ]
    return run_remote(kernel, outs, far_outs, blocks, far, scratch, 2, 1e10)


def gelu_of(u):
    sq = u * u
    th = jnp.tanh(u * (GELU + GELU * CUBE * sq))
    near = 0.5 + 0.5 * th
    slope = near + u * near * (1.0 - th) * (GELU + 3 * GELU * CUBE * sq)
    return (u * near).astype(BF), slope


def back_body(g, v, chip, far, m, s, out_ref, rows_ref, sum_ref):
    sum_ref[...] = jnp.zeros_like(sum_ref)

    def body(i):
        da = chip[i].astype(F32) + far[i].astype(F32)
        n, r = norm_of(v[i].astype(F32))
        dn = da * m
        mean = jnp.mean(dn, axis=-1, keepdims=True)
        along = jnp.mean(dn * n, axis=-1, keepdims=True)
        out = g(i) + r * (dn - mean - n * along)
        out_ref[i] = out
        rows_ref[i] = (out * s).astype(BF)
        dan = da * n
        for k in range(STEP // 8):
            sum_ref[:8] += da[k * 8 : k * 8 + 8]
            sum_ref[8:] += dan[k * 8 : k * 8 + 8]

    over_rows(v.shape[0], body)


def feed_forward(state, cotangent, n_dp):
    quarter = state["z0"].shape[0]
    half = 2 * quarter
    rows = shape((quarter, D), BF)
    whole = shape((quarter, D), F32)
    outs = dict(
        gc0=whole, gc1=whole, e0=rows, e1=rows, e2=rows, e3=rows,
        sf0=shape((16, D), F32), sf1=shape((16, D), F32), branch=whole,
    )
    far_outs = {f"t{j}": shape((D, 2 * HC), BF) for j in range(3)}
    given = ("z0", "z1", "z2", "z3", "d0", "d1", "d2", "d3", "after_c0", "after_c1", "shifts", "g_got")
    blocks = [state[name] for name in given] + [cotangent]
    far = [state[name] for name in ("f0", "f1", "f2", "dpre0", "dpre1", "act0", "act1")]
    names = [*outs, *far_outs]

    def kernel(*refs, flush):
        i = dict(zip(given, refs))
        cot, f, early, refs = refs[len(given)], refs[len(given) + 1 :][:3], refs[len(given) + 4 :][:4], refs[len(given) + 8 :]
        o = dict(zip(names, refs))
        (
            w, act, dpre, theirs, landed, mine, chips, fars, turned, near, cross_x, local,
        ) = refs[len(names) :]
        t, core, across, diagonal = tensor_peers()
        first = t < 2
        cores, xs = Swap(near), Swap(cross_x)
        loads = [pltpu.make_async_copy(f[j], w.at[j], local.at[j]) for j in range(3)]
        places = (dpre.at[0], dpre.at[1], act.at[0], act.at[1])
        loads += [pltpu.make_async_copy(early[j], places[j], local.at[3 + j]) for j in range(4)]
        for copy in loads:
            copy.start()
        greet(n_dp)
        z = [i["z0"], i["z1"], i["z2"], i["z3"]]
        ds = [i["d0"], i["d1"], i["d2"], i["d3"]]
        loads[2].wait()
        for p in range(4):
            dpre[2, p * quarter : (p + 1) * quarter] = dot_nn(ds[p][...], w[2, :, HC:]).astype(BF)

        def pre_part(h, j):
            for p in (2 * h, 2 * h + 1):
                own = slice(p * quarter, (p + 1) * quarter)
                u = dot_nn(z[p][...], w[j, :, :HC])
                act[j, own], slope = gelu_of(u)
                dpre[j, own] = (dpre[j, own].astype(F32) * slope).astype(BF)

        def contracted(a, p, side):
            own = slice(p * quarter, (p + 1) * quarter)
            total = None
            for j in range(3):
                term = dot_nt(a[j, own], w[j, :, side * HC : (side + 1) * HC])
                total = term if total is None else total + term
            return total

        def back_half(h):
            theirs[h] = contracted(dpre, 2 * h + 1, 0).astype(BF)
            copy = cores.start(theirs.at[h], landed.at[h], core)
            mine[h] = contracted(dpre, 2 * h, 0)
            return copy

        def forward_half(h):
            theirs[2 + h] = contracted(act, 2 * h + 1, 1).astype(BF)
            copy = cores.start(theirs.at[2 + h], landed.at[2 + h], core)
            mine[h] = contracted(act, 2 * h, 1)
            return copy

        def join(k, copy):
            copy.wait_recv()
            join_body(mine.at[k % 2], landed.at[k], chips.at[k])

        pre_part(0, 2)
        for copy in (*loads[:2], *loads[3:]):
            copy.wait()
        sent = back_half(0)
        pre_part(1, 2)
        join(0, sent)
        crossed = [xs.start(chips.at[0], fars.at[0], across)]
        sent = back_half(1)
        sent_f = forward_half(0)
        join(1, sent)
        crossed.append(xs.start(chips.at[1], fars.at[1], across))
        join(2, sent_f)
        sent_f = forward_half(1)
        join(3, sent_f)
        own_half = jnp.where(first, 0, 1)
        last = xs.start(chips.at[3 - own_half], fars.at[2], across)

        def turn_rows(slots):
            for p in range(4):
                turned[:, p * quarter : (p + 1) * quarter] = jnp.transpose(slots[p][...])

        def weight_grad(j, side, right):
            for k in range(0, D, 512):
                w[j, k : k + 512, side * HC : (side + 1) * HC] = dot_nn(turned[k : k + 512], right[j]).astype(BF)

        def g_of(h):
            def rows_of(r):
                own, other = cot[r].astype(F32), i["g_got"][r].astype(F32)
                return jnp.where(first, own, other) if h == 0 else jnp.where(first, other, own)

            return rows_of

        e = [o["e0"], o["e1"], o["e2"], o["e3"]]
        passed = []

        def norm_half(h):
            crossed[h].wait_recv()
            back_body(
                g_of(h), i[f"after_c{h}"], chips.at[h], fars.at[h], 1.0 + i["shifts"][4:5], 1.0,
                o[f"gc{h}"], e[2 * h], o[f"sf{h}"],
            )
            passed.append(cores.start(e[2 * h], e[2 * h + 1], core))
            flush(f"gc{h}", f"sf{h}", f"e{2 * h}")

        turn_rows(z)
        weight_grad(0, 0, dpre)
        norm_half(0)
        weight_grad(1, 0, dpre)
        weight_grad(2, 0, dpre)
        turn_rows(ds)
        stores = []
        for j in range(3):
            weight_grad(j, 1, act)
            store = pltpu.make_async_copy(w.at[j], o[f"t{j}"], local.at[j])
            store.start()
            stores.append(store)
            if j == 0:
                norm_half(1)
        last.wait_recv()
        o["branch"][...] = chips[2 + own_half].astype(F32) + fars[2].astype(F32)
        for copy in passed:
            copy.wait_recv()
        for store in stores:
            store.wait()
        cores.settle()
        xs.settle()

    scratch = [
        pltpu.VMEM((3, D, 2 * HC), BF),
        pltpu.VMEM((3, 2 * half, HC), BF),
        pltpu.VMEM((3, 2 * half, HC), BF),
        pltpu.VMEM((4, quarter, D), BF),
        pltpu.VMEM((4, quarter, D), BF),
        pltpu.VMEM((2, quarter, D), F32),
        pltpu.VMEM((4, quarter, D), BF),
        pltpu.VMEM((3, quarter, D), BF),
        pltpu.VMEM((D, 2 * half), BF),
        pltpu.SemaphoreType.DMA((2, 8)),
        pltpu.SemaphoreType.DMA((2, 4)),
        pltpu.SemaphoreType.DMA((7,)),
    ]
    return run_remote(kernel, outs, far_outs, blocks, far, scratch, 3, 6e10)


class Scatter:
    def __init__(self, got, arrived, over, along, n):
        d = lax.axis_index("dp")
        self.z, self.y = d // 2, lax.rem(d, 2)
        self.got, self.arrived, self.sems_y, self.sems_z, self.n = got, arrived, over, along, n
        self.r = D // (2 * n)

    def block(self, full, o, own):
        start = (2 * o + (self.y if own else 1 - self.y)) * self.r
        return full.at[pl.ds(pl.multiple_of(start, 16), self.r)]

    def begin(self, full):
        self.full = full
        self.sent = []
        for o in range(self.n):
            copy = remote(
                self.block(full, o, False), self.got.at[o], self.sems_y.at[0, o], self.sems_y.at[1, o],
                dp=2 * self.z + 1 - self.y,
            )
            copy.start()
            self.sent.append(copy)

    def pair(self, a, b, local):
        loads = []
        for o in range(self.n):
            copy = pltpu.make_async_copy(self.block(self.full, o, True), a.at[o], local.at[0, o])
            copy.start()
            loads.append(copy)
        for o in range(self.n):
            self.sent[o].wait()
            copy = pltpu.make_async_copy(self.got.at[o], b.at[o], local.at[1, o])
            copy.start()
            loads.append(copy)
        for o in range(self.n):
            loads[o].wait()
            loads[self.n + o].wait()
            a[o] = (a[o].astype(F32) + b[o].astype(F32)).astype(BF)

    def spread(self, a, relay=None):
        self.a, self.relay = a, relay if self.n == 4 else None
        if self.relay is None:
            self.out = []
            for k in range(1, self.n):
                at = lax.rem(self.z + k, self.n)
                copy = self.send(at, at, self.arrived.at[k - 1], k, k)
                copy.start()
                self.out.append(copy)
            return
        z = self.z
        self.end = (z == 0) | (z == 3)
        self.inner = jnp.where(z < 2, 1, 2)
        self.edge = jnp.where(z < 2, 0, 3)

        @pl.when(self.end)
        def _():
            self.send(3 - z, self.inner, relay.at[0], 1, 1).start()
            self.send(3 - self.inner, self.inner, relay.at[1], 2, 2).start()
            self.send(self.inner, self.inner, self.arrived.at[0], 0, 0).start()

        @pl.when(jnp.logical_not(self.end))
        def _():
            self.send(self.edge, self.edge, self.arrived.at[0], 0, 0).start()

    def send(self, block, to, place, k, j):
        return remote(
            self.a.at[block], place, self.sems_z.at[0, k], self.sems_z.at[1, j], dp=2 * to + self.y
        )

    def forward(self, b, local):
        if self.relay is None:
            return

        @pl.when(jnp.logical_not(self.end))
        def _():
            loads = []
            for k in range(2):
                self.send(self.edge, self.edge, self.relay.at[k], 1 + k, 1 + k).wait_recv()
                copy = pltpu.make_async_copy(self.relay.at[k], b.at[k], local.at[0, k])
                copy.start()
                loads.append(copy)
            for k, to in enumerate((3 - self.edge, 3 - self.inner)):
                loads[k].wait()
                self.a[to] = (self.a[to].astype(F32) + b[k].astype(F32)).astype(BF)
                self.send(to, to, self.arrived.at[1], 1 + k, 3).start()

    def total(self, a, stage, result, sem, b, local):
        count = self.n - 1
        if self.relay is None:
            for copy in self.out:
                copy.wait()
        else:
            count = 2
            for slot, j in ((0, 0), (1, 3)):
                self.send(self.edge, self.edge, self.arrived.at[slot], j, j).wait_recv()
            for k in range(3):
                self.send(self.edge, self.edge, self.arrived.at[0], k, k).wait_send()
        arrived = self.arrived
        if self.n != 4:
            loads = [pltpu.make_async_copy(arrived.at[k], b.at[k], local.at[0, k]) for k in range(count)]
            for copy in loads:
                copy.start()
            wait(loads)
            arrived = b
        total = a[self.z].astype(F32)
        for k in range(count):
            total = total + arrived[k].astype(F32)
        stage[...] = total
        copy = pltpu.make_async_copy(stage, result, sem)
        copy.start()
        copy.wait()


def attend_back_body(do_ref, q_ref, k_refs, v_refs, lse_ref, bias_ref, dq_ref, dk_ref, dv_ref, fresh):
    rows, wide = q_ref.shape
    for h in range(wide // HEAD):
        lanes = slice(h * HEAD, (h + 1) * HEAD)
        k = jnp.concatenate([r[:, lanes] for r in k_refs]) if len(k_refs) > 1 else k_refs[0][:, lanes]
        v = jnp.concatenate([r[:, lanes] for r in v_refs]) if len(v_refs) > 1 else v_refs[0][:, lanes]
        for b in range(rows // QB):
            block = slice(b * QB, (b + 1) * QB)
            qb = q_ref[block, lanes]
            do = do_ref[block, lanes]
            s = dot_nt(k, qb) * FACTOR
            if bias_ref is not None:
                s = s + bias_ref[...]
            p = jnp.exp(s - lse_ref[h : h + 1, block])
            dp = dot_nt(v, do)
            center = jnp.sum(p * dp, axis=0, keepdims=True)
            ds = (p * (dp - center)).astype(BF)
            dq_ref[block, lanes] = dot_tn(ds, k) * FACTOR
            dk = dot_nn(ds, qb) * FACTOR
            dv = dot_nn(p.astype(BF), do)
            if b == 0 and fresh:
                dk_ref[:, lanes] = dk
                dv_ref[:, lanes] = dv
            else:
                dk_ref[:, lanes] += dk
                dv_ref[:, lanes] += dv


def dots_body(dy_ref, raw_ref, col, stat_ref, row, gain, tables, grad_ref, grad_row, wide):
    scale = lax.rsqrt(to_columns(stat_ref[...]) / D + EPS)[:, row : row + 1]
    dots = jnp.zeros((dy_ref.shape[0], 1), F32)
    for h in range(wide // HEAD):
        own = slice(h * HEAD, (h + 1) * HEAD)
        dy = dy_ref[:, own]
        if tables is not None:
            dy = turn(dy, tables[0], -tables[1])
            dy_ref[:, own] = dy
        both = raw_ref[:, col + h * HEAD : col + (h + 1) * HEAD] * dy
        dots = dots + jnp.sum(both * gain[h], axis=1, keepdims=True)
        grad_ref[grad_row : grad_row + 1, own] += jnp.sum(both * scale, axis=0, keepdims=True)
    return dots


def root_back_body(dy_ref, raw_ref, col, stat_ref, row, dots_ref, dots_row, gain, low_ref, at, wide):
    scale = lax.rsqrt(to_columns(stat_ref[...]) / D + EPS)[:, row : row + 1]
    along = scale * scale * scale * to_columns(dots_ref[...])[:, dots_row : dots_row + 1] / D
    for h in range(wide // HEAD):
        own = slice(h * HEAD, (h + 1) * HEAD)
        raw = raw_ref[:, col + h * HEAD : col + (h + 1) * HEAD]
        dx = scale * gain[h] * dy_ref[:, own] - raw * along
        low_ref[:, at + h * HEAD : at + (h + 1) * HEAD] = dx.astype(BF)


class Grads:
    def __init__(self, turned, stage, sems):
        self.turned, self.stage, self.sems = turned, stage, sems
        self.stores = [None, None]
        self.used = 0

    def turn(self, slots):
        at = 0
        for slot in slots:
            m = slot.shape[0]
            self.turned[:, at : at + m] = jnp.transpose(slot[...])
            at += m

    def put(self, ys, full, col):
        i = self.used % 2
        self.used += 1
        if self.stores[i] is not None:
            self.stores[i].wait()
        for k in range(0, D, 512):
            total, at = None, 0
            for y in ys:
                m = y.shape[0]
                term = dot_nn(self.turned[k : k + 512, at : at + m], y)
                total = term if total is None else total + term
                at += m
            self.stage[i, k : k + 512] = total.astype(BF)
        store = pltpu.make_async_copy(self.stage.at[i], full.at[:, pl.ds(col, GC)], self.sems.at[i])
        store.start()
        self.stores[i] = store

    def finish(self):
        for i in range(2):
            if self.stores[i] is not None:
                self.stores[i].wait()
                self.stores[i] = None


def cross_backward(state, bias, n_dp, heads):
    quarter, texts = state["e0"].shape[0], state["c0"].shape[0]
    half, wide = 2 * quarter, heads * HEAD
    n, r = n_dp // 2, D // n_dp
    W = state["t0"].shape[1]
    rows = shape((quarter, D), BF)
    whole = shape((quarter, D), F32)
    sums_shape = shape((16, D), F32)
    outs = dict(
        gs0=whole, gs1=whole, h0=rows, h1=rows, h2=rows, h3=rows, sc0=sums_shape, sc1=sums_shape,
        cross_gain=shape((8, wide), F32), ctx_grad=shape((texts, D), BF),
    )
    far_outs = dict(
        tc=shape((D, 4 * wide), BF), p1=shape((n, r, W), BF), s0=shape((r, W), F32), relay0=shape((2, r, W), BF),
        got0=shape((n, r, W), BF), got1=shape((n, r, W), BF),
    )
    if n != 4:
        far_outs["arrived"] = shape((n - 1, r, W), BF)
    given = (
        "e0", "e1", "e2", "e3", "cq0", "cq1", "ck", "cv", "clse0", "clse1", "cq_raw0", "cq_raw1", "ck_raw",
        "cq_stat0", "cq_stat1", "ck_stat", "gains", "shifts", "gc0", "gc1", "after0", "after1", "w_cross",
        "cattn0", "cattn1", "y0", "y1", "y2", "y3", "c0", "c1", "c2", "c3",
    )
    blocks = [state[name] for name in given] + [bias]
    far = [state["t0"], state["t1"]]
    names = [*outs, *far_outs]

    def kernel(*refs, flush):
        i = dict(zip(given, refs))
        bias_ref, t0, t1 = refs[len(given) : len(given) + 3]
        refs = refs[len(given) + 3 :]
        o = dict(zip(names, refs))
        (
            do, dq, dk, dv, low, dckv, theirs, landed, mine, chips, fars, c_theirs, c_landed, c_chips, c_far,
            dots, ck_dots, stats_in, turned, stage, a, b, arrived, result,
            near, cross_x, near_sums, over, along, local, stores,
        ) = refs[len(names) :]
        t, core, across, diagonal = tensor_peers()
        first = t < 2
        cores, xs = Swap(near), Swap(cross_x)
        sums = Sums(stats_in, near_sums, (core, across, diagonal))
        greet(n_dp)
        arrived = o.get("arrived", arrived)
        f0 = Scatter(o["got0"], arrived, over.at[0], along.at[0], n)
        f1 = Scatter(o["got1"], arrived, over.at[1], along.at[0], n)
        f0.begin(t0)
        w = i["w_cross"]
        e = [i["e0"], i["e1"], i["e2"], i["e3"]]
        gain_q = [i["gains"][2 * heads + h : 2 * heads + h + 1] for h in range(heads)]
        gain_k = [i["gains"][3 * heads + h : 3 * heads + h + 1] for h in range(heads)]
        o["cross_gain"][...] = jnp.zeros_like(o["cross_gain"])

        def back(h):
            for p in range(2):
                do[p * quarter : (p + 1) * quarter] = dot_nn(e[2 * h + p][...], w[:, 3 * wide :]).astype(BF)
            attend_back_body(
                do, i[f"cq{h}"], [i["ck"]], [i["cv"]], i[f"clse{h}"], bias_ref, dq, dk, dv, h == 0
            )
            column = dots_body(
                dq, i[f"cq_raw{h}"], 0, i[f"cq_stat{h}"], 0, gain_q, None, o["cross_gain"], 0, wide
            )
            dots[h] = to_rows([column], half)
            return sums.start(dots.at[h])

        def send(h):
            root_back_body(
                dq, i[f"cq_raw{h}"], 0, i[f"cq_stat{h}"], 0, dots.at[h], 0, gain_q, low.at[h], 0, wide
            )
            theirs[h] = dot_nt(low[h, quarter:], w[:, :wide]).astype(BF)
            copy = cores.start(theirs.at[h], landed.at[h], core)
            mine[...] = dot_nt(low[h, :quarter], w[:, :wide])
            return copy

        def join(h, copy):
            copy.wait_recv()
            join_body(mine, landed.at[h], chips.at[h])
            return xs.start(chips.at[h], fars.at[h], across)

        collect = back(0)
        collect()
        sent0 = send(0)
        collect = back(1)
        crossed = [join(0, sent0)]
        column = dots_body(dk, i["ck_raw"], 0, i["ck_stat"], 0, gain_k, None, o["cross_gain"], 1, wide)
        ck_dots[...] = to_rows([column], 4 * texts)
        collect_k = [sums.start(ck_dots.at[:, pl.ds(j * 2 * texts, 2 * texts)]) for j in range(2)]
        collect()
        sent1 = send(1)
        crossed.append(join(1, sent1))
        f1.begin(t1)
        for part in collect_k:
            part()
        f0.pair(a, b, local)
        f0.spread(a, o["relay0"])

        root_back_body(dk, i["ck_raw"], 0, i["ck_stat"], 0, ck_dots, 0, gain_k, dckv, 0, wide)
        dckv[:, wide:] = dv[...].astype(BF)
        c_sent = []
        for j in range(2):
            at = 2 * texts * j
            c_theirs[j] = dot_nt(dckv[at + texts : at + 2 * texts], w[:, wide : 3 * wide]).astype(BF)
            c_sent.append(cores.start(c_theirs.at[j], c_landed.at[j], core))
        for j in range(2):
            at = 2 * texts * j
            part = dot_nt(dckv[at : at + texts], w[:, wide : 3 * wide])
            c_sent[j].wait_recv()
            c_chips[j] = (part + c_landed[j].astype(F32)).astype(BF)
        own_half = jnp.where(first, 0, 1)
        c_last = xs.start(c_chips.at[1 - own_half], c_far, across)

        h_slots = [o["h0"], o["h1"], o["h2"], o["h3"]]
        passed = []

        def norm_half(h):
            crossed[h].wait_recv()
            back_body(
                lambda rows: i[f"gc{h}"][rows], i[f"after{h}"], chips.at[h], fars.at[h], i["shifts"][6:7],
                i["shifts"][2:3], o[f"gs{h}"], h_slots[2 * h], o[f"sc{h}"],
            )
            passed.append(cores.start(h_slots[2 * h], h_slots[2 * h + 1], core))
            flush(f"gs{h}", f"sc{h}", f"h{2 * h}")

        norm_half(0)
        grads = Grads(turned, stage, stores)
        grads.turn([i["y0"], i["y1"], i["y2"], i["y3"]])
        grads.put([low[0], low[1]], o["tc"], 0)
        norm_half(1)
        f0.forward(b, local)
        grads.turn([i["c0"], i["c1"], i["c2"], i["c3"]])
        for c in range(2):
            grads.put([dckv[:, c * wide : (c + 1) * wide]], o["tc"], (1 + c) * wide)
        grads.turn(e)
        grads.put([i["cattn0"][...], i["cattn1"][...]], o["tc"], 3 * wide)
        c_last.wait_recv()
        o["ctx_grad"][...] = (c_chips[own_half].astype(F32) + c_far[...].astype(F32)).astype(BF)
        grads.finish()
        f0.total(a, result, o["s0"], stores.at[0], b, local)
        f1.pair(a, b, local)
        copy = pltpu.make_async_copy(a, o["p1"], stores.at[0])
        copy.start()
        copy.wait()
        for copy in passed:
            copy.wait_recv()
        cores.settle()
        xs.settle()

    scratch = [
        pltpu.VMEM((half, wide), BF),
        pltpu.VMEM((half, wide), F32),
        pltpu.VMEM((4 * texts, wide), F32),
        pltpu.VMEM((4 * texts, wide), F32),
        pltpu.VMEM((2, half, wide), BF),
        pltpu.VMEM((4 * texts, 2 * wide), BF),
        pltpu.VMEM((2, quarter, D), BF),
        pltpu.VMEM((2, quarter, D), BF),
        pltpu.VMEM((quarter, D), F32),
        pltpu.VMEM((2, quarter, D), BF),
        pltpu.VMEM((2, quarter, D), BF),
        pltpu.VMEM((2, texts, D), BF),
        pltpu.VMEM((2, texts, D), BF),
        pltpu.VMEM((2, texts, D), BF),
        pltpu.VMEM((texts, D), BF),
        pltpu.VMEM((2, 8, half), F32),
        pltpu.VMEM((8, 4 * texts), F32),
        pltpu.VMEM((4, 3, 8, half), F32),
        pltpu.VMEM((D, 2 * half), BF),
        pltpu.VMEM((2, D, GC), BF),
        pltpu.VMEM((n, r, W), BF),
        pltpu.VMEM((n, r, W), BF),
        pltpu.VMEM((n - 1, r, W) if n == 4 else (8, HEAD), BF),
        pltpu.VMEM((r, W), F32),
        pltpu.SemaphoreType.DMA((2, 8)),
        pltpu.SemaphoreType.DMA((2, 4)),
        pltpu.SemaphoreType.DMA((2, 12)),
        pltpu.SemaphoreType.DMA((2, 2, n)),
        pltpu.SemaphoreType.DMA((1, 2, n)),
        pltpu.SemaphoreType.DMA((2, n)),
        pltpu.SemaphoreType.DMA((2,)),
    ]
    return run_remote(kernel, outs, far_outs, blocks, far, scratch, 4, 4e10)


def self_backward(state, hidden, tables, sums_two, sums_five, n_dp, heads):
    quarter = hidden.shape[0]
    half, wide = 2 * quarter, heads * HEAD
    n, r = n_dp // 2, D // n_dp
    W, V = state["t2"].shape[1], 2 * wide
    g_cols = HEAD // n_dp
    outs = dict(
        hidden_grad=shape((quarter, D), BF), ss=shape((16, D), F32), self_gain=shape((8, wide), F32),
        time=shape((8, D), F32), tiny=shape((r, HEAD), F32),
    )
    far_outs = dict(
        s1=shape((r, W), F32), s2=shape((r, W), F32), s3=shape((r, W), F32), s4=shape((r, V), F32), s5=shape((r, V), F32),
        tv=shape((D, V), BF), tq=shape((D, V), BF),
        relay1=shape((2, r, W), BF), relay2=shape((2, r, W), BF), relay3=shape((2, r, W), BF), relay4=shape((2, r, V), BF),
        got2=shape((n, r, W), BF), got3=shape((n, r, W), BF), got4=shape((n, r, V), BF), got5=shape((n, r, V), BF),
    )
    if n != 4:
        far_outs["arrived"] = shape((3, n - 1, r, W), BF)
        far_outs["arrived_v"] = shape((2, n - 1, r, V), BF)
    given = (
        "h0", "h1", "h2", "h3", "q0", "q1", "k0", "k1", "v0", "v1", "lse0", "lse1", "qk0", "qk1", "stat0", "stat1",
        "gains", "shifts", "gs0", "gs1", "attn0", "attn1", "w_self", "sf0", "sf1", "sc0", "sc1", "cross_gain",
    )
    blocks = [state[name] for name in given] + [hidden, *tables, sums_two, sums_five]
    far = [state["p1"], state["t2"], state["tc"], *(state[f"x{p}"] for p in range(4))]
    names = [*outs, *far_outs]

    def kernel(*refs, flush):
        i = dict(zip(given, refs))
        hid, cos, sin, two, five, p1, t2, tc = refs[len(given) : len(given) + 8]
        xs_far = refs[len(given) + 8 : len(given) + 12]
        refs = refs[len(given) + 12 :]
        o = dict(zip(names, refs))
        (
            do, dq, dk, dv, low, theirs, landed, mine, chips, far_chip,
            dots, stats_in, turned, stage, a, b, arrived, arrived_v, result, four_sums, side, side_in,
            near, cross_x, near_sums, over, along, local, stores, slots, side_sems,
        ) = refs[len(names) :]
        t, core, across, diagonal = tensor_peers()
        first = t < 2
        cores, xs = Swap(near), Swap(cross_x)
        sums = Sums(stats_in, near_sums, (core, across, diagonal))
        held = pltpu.make_async_copy(p1, a.at[0], stores.at[0])
        held.start()
        x_copies = [pltpu.make_async_copy(xs_far[p], theirs.at[p % 2], slots.at[p]) for p in range(4)]
        for p in range(2):
            x_copies[p].start()
        greet(n_dp)
        arrived, arrived_v = o.get("arrived", arrived), o.get("arrived_v", arrived_v)
        f1 = Scatter(None, arrived.at[0], None, along.at[0], n)
        f2 = Scatter(o["got2"], arrived.at[1], over.at[0], along.at[1], n)
        fc = Scatter(o["got3"], arrived.at[2], over.at[1], along.at[2], n)
        fv = Scatter(o["got4"], arrived_v.at[0], over.at[2], along.at[3], n)
        fq = Scatter(o["got5"], arrived_v.at[1], over.at[3], along.at[4], n)
        f2.begin(t2)
        held.wait()
        f1.spread(a.at[0], o["relay1"])
        w = i["w_self"]
        hs = [i["h0"], i["h1"], i["h2"], i["h3"]]
        ks, vs = [i["k0"], i["k1"]], [i["v0"], i["v1"]]
        gain = [[i["gains"][g * heads + h : g * heads + h + 1] for h in range(heads)] for g in range(2)]
        o["self_gain"][...] = jnp.zeros_like(o["self_gain"])
        for h in range(2):
            for p in range(2):
                do[p * quarter : (p + 1) * quarter] = dot_nn(hs[2 * h + p][...], w[:, 3 * wide :]).astype(BF)
            attend_back_body(do, i[f"q{h}"], ks, vs, i[f"lse{h}"], None, dq.at[h], dk, dv, h == 0)
        collects = []
        for h in range(2):
            own = slice(h * half, (h + 1) * half)
            turns = (cos[own], sin[own])
            dk_half = dk.at[pl.ds(h * half, half)]
            columns = [
                dots_body(dq.at[h], i[f"qk{h}"], 0, i[f"stat{h}"], 0, gain[0], turns, o["self_gain"], 0, wide),
                dots_body(dk_half, i[f"qk{h}"], wide, i[f"stat{h}"], 1, gain[1], turns, o["self_gain"], 1, wide),
            ]
            dots[h] = to_rows(columns, half)
            collects.append(sums.start(dots.at[h]))
            low[h, :, 2 * wide :] = dv[own].astype(BF)

        grads = Grads(turned, stage, stores)
        for p in range(4):
            x_copies[p].wait()
            turned[:, p * quarter : (p + 1) * quarter] = jnp.transpose(theirs[p % 2])
            if p < 2:
                x_copies[p + 2].start()
        grads.put([low[0, :, 2 * wide :], low[1, :, 2 * wide :]], o["tv"], 0)
        fc.begin(tc)
        f1.forward(b, local)
        f2.pair(a.at[1], b, local)
        f2.spread(a.at[1], o["relay2"])
        sent = []

        def join(h):
            sent[h].wait_recv()
            join_body(mine, landed.at[h], chips.at[h])

        for h in range(2):
            collects[h]()
            dk_half = dk.at[pl.ds(h * half, half)]
            root_back_body(dq.at[h], i[f"qk{h}"], 0, i[f"stat{h}"], 0, dots.at[h], 0, gain[0], low.at[h], 0, wide)
            root_back_body(
                dk_half, i[f"qk{h}"], wide, i[f"stat{h}"], 1, dots.at[h], 1, gain[1], low.at[h], wide, wide
            )
            theirs[h] = dot_nt(low[h, quarter:], w[:, : 3 * wide]).astype(BF)
            sent.append(cores.start(theirs.at[h], landed.at[h], core))
            if h == 1:
                join(0)
            mine[...] = dot_nt(low[h, :quarter], w[:, : 3 * wide])
        join(1)
        own_half = jnp.where(first, 0, 1)
        last = xs.start(chips.at[1 - own_half], far_chip, across)
        for c in range(2):
            lanes = slice(c * wide, (c + 1) * wide)
            grads.put([low[0, :, lanes], low[1, :, lanes]], o["tq"], c * wide)
        grads.turn(hs)
        grads.put([i["attn0"][...], i["attn1"][...]], o["tv"], wide)
        grads.finish()
        f1.total(a.at[0], result, o["s1"], stores.at[0], b, local)
        fv.begin(o["tv"])

        last.wait_recv()
        m_row = 1.0 + i["shifts"][1:2]
        sum_ref = o["ss"]
        sum_ref[...] = jnp.zeros_like(sum_ref)

        def body(rows):
            da = chips[own_half, rows].astype(F32) + far_chip[rows].astype(F32)
            nv, rv = norm_of(hid[rows].astype(F32))
            dn = da * m_row
            mean = jnp.mean(dn, axis=-1, keepdims=True)
            proj = jnp.mean(dn * nv, axis=-1, keepdims=True)
            g = jnp.where(first, i["gs0"][rows], i["gs1"][rows])
            o["hidden_grad"][rows] = (g + rv * (dn - mean - nv * proj)).astype(BF)
            dan = da * nv
            for k in range(STEP // 8):
                sum_ref[:8] += da[k * 8 : k * 8 + 8]
                sum_ref[8:] += dan[k * 8 : k * 8 + 8]

        over_rows(quarter, body)
        flush("hidden_grad")

        def summed(ref, at):
            return jnp.sum(ref[at : at + 8], axis=0, keepdims=True)

        def own(name, at):
            return jnp.where(first, summed(i[name + "0"], at), summed(i[name + "1"], at))

        four_sums[0] = jnp.concatenate(
            [
                summed(sum_ref, 0), summed(sum_ref, 8), two[...], own("sf", 0), own("sf", 8), five[...],
                own("sc", 8), own("sc", 0),
            ]
        )
        cores.start(four_sums.at[0], four_sums.at[1], core).wait_recv()
        four_sums[2] = four_sums[0] + four_sums[1]
        xs.start(four_sums.at[2], four_sums.at[3], across).wait_recv()
        o["time"][...] = four_sums[2] + four_sums[3]
        flush("time", "ss", "self_gain")
        head_rows = [
            ref[g : g + 1, h * HEAD : (h + 1) * HEAD]
            for ref in (o["self_gain"], i["cross_gain"])
            for g in range(2)
            for h in range(heads)
        ]
        head_rows = jnp.concatenate([*head_rows, jnp.zeros((16 - 4 * heads, HEAD), F32)])
        at = lax.broadcasted_iota(jnp.int32, (D, HEAD), 0)
        to = lax.broadcasted_iota(jnp.int32, (D, HEAD), 1)
        pick = (at == (to // g_cols) * r + lax.rem(to, g_cols)).astype(F32)
        spread = dot_nt(head_rows.astype(BF), pick.astype(BF))
        both = jnp.concatenate([o["time"][...], spread, jnp.zeros((HEAD - 24, D), F32)])
        side[...] = jnp.transpose(both).astype(BF)
        d = lax.axis_index("dp")

        def side_block(k):
            return side.at[pl.ds(pl.multiple_of(lax.rem(d + k, n_dp) * r, 16), r)]

        side_copies = []
        for k in range(1, n_dp):
            copy = remote(
                side_block(k), side_in.at[k - 1], side_sems.at[0, k], side_sems.at[1, k], dp=lax.rem(d + k, n_dp)
            )
            copy.start()
            side_copies.append(copy)
        f2.forward(b, local)
        fq.begin(o["tq"])
        fc.pair(a.at[0], b, local)
        fc.spread(a.at[0], o["relay3"])
        f2.total(a.at[1], result, o["s2"], stores.at[0], b, local)
        a_v, a_q = (a.at[1, :, :, pl.ds(c * V, V)] for c in range(2))
        b_v = b.at[:, :, pl.ds(0, V)]
        fv.pair(a_v, b_v, local)
        fv.spread(a_v, o["relay4"])
        fc.forward(b, local)
        fv.forward(b_v, local)
        fq.pair(a_q, b_v, local)
        fq.spread(a_q)
        fc.total(a.at[0], result, o["s3"], stores.at[0], b, local)
        fv.total(a_v, result.at[:, pl.ds(0, V)], o["s4"], stores.at[0], b_v, local)
        small = side_block(0)[...].astype(F32)
        for k in range(1, n_dp):
            side_copies[k - 1].wait()
            small = small + side_in[k - 1].astype(F32)
        o["tiny"][...] = small
        flush("tiny")
        fq.total(a_q, result.at[:, pl.ds(0, V)], o["s5"], stores.at[0], b_v, local)
        cores.settle()
        xs.settle()

    scratch = [
        pltpu.VMEM((half, wide), BF),
        pltpu.VMEM((2, half, wide), F32),
        pltpu.VMEM((2 * half, wide), F32),
        pltpu.VMEM((2 * half, wide), F32),
        pltpu.VMEM((2, half, 3 * wide), BF),
        pltpu.VMEM((2, quarter, D), BF),
        pltpu.VMEM((2, quarter, D), BF),
        pltpu.VMEM((quarter, D), F32),
        pltpu.VMEM((2, quarter, D), BF),
        pltpu.VMEM((quarter, D), BF),
        pltpu.VMEM((2, 8, half), F32),
        pltpu.VMEM((2, 3, 8, half), F32),
        pltpu.VMEM((D, 2 * half), BF),
        pltpu.VMEM((2, D, GC), BF),
        pltpu.VMEM((2, n, r, W), BF),
        pltpu.VMEM((n, r, W), BF),
        pltpu.VMEM((3, n - 1, r, W) if n == 4 else (8, HEAD), BF),
        pltpu.VMEM((2, n - 1, r, V) if n == 4 else (8, HEAD), BF),
        pltpu.VMEM((r, W), F32),
        pltpu.VMEM((4, 8, D), F32),
        pltpu.VMEM((D, HEAD), BF),
        pltpu.VMEM((n_dp - 1, r, HEAD), BF),
        pltpu.SemaphoreType.DMA((2, 4)),
        pltpu.SemaphoreType.DMA((2, 4)),
        pltpu.SemaphoreType.DMA((2, 6)),
        pltpu.SemaphoreType.DMA((4, 2, n)),
        pltpu.SemaphoreType.DMA((5, 2, n)),
        pltpu.SemaphoreType.DMA((2, n)),
        pltpu.SemaphoreType.DMA((2,)),
        pltpu.SemaphoreType.DMA((4,)),
        pltpu.SemaphoreType.DMA((2, n_dp)),
    ]
    return run_remote(kernel, outs, far_outs, blocks, far, scratch, 5, 5e10)


def rotary_tables(positions, head_dim):
    pair_count = head_dim // 2
    side_pairs = pair_count // 3
    frame_pairs = pair_count - 2 * side_pairs
    pair_index = jnp.arange(pair_count)
    frame_mask = pair_index < frame_pairs
    height_mask = (pair_index >= frame_pairs) & (pair_index < frame_pairs + side_pairs)
    within = jnp.where(
        frame_mask,
        pair_index,
        jnp.where(height_mask, pair_index - frame_pairs, pair_index - frame_pairs - side_pairs),
    )
    extent = jnp.where(frame_mask, frame_pairs, side_pairs)
    frequency = jnp.power(10000.0, -within.astype(F32) / extent.astype(F32))
    coords = positions.astype(F32)
    coordinate = jnp.where(
        frame_mask[None, :],
        coords[0][:, None],
        jnp.where(height_mask[None, :], coords[1][:, None], coords[2][:, None]),
    )
    angles = jnp.repeat(coordinate * frequency[None, :], 2, axis=1)
    parity = jnp.arange(head_dim) % 2
    sign_pattern = jnp.where(parity == 0, -1.0, 1.0)
    return (jnp.cos(angles), jnp.sin(angles) * sign_pattern)


def solution(mesh):
    n_dp = mesh.shape["dp"]
    n_major = n_dp // 2
    pair_perm = [(i, i ^ 1) for i in range(n_dp)]
    ring_perm = {
        t: [((((i // 2) + t) % n_major) * 2 + i % 2, i) for i in range(n_dp)]
        for t in range(1, n_major)
    }
    back_perm = {t: [(b, a) for a, b in ring_perm[t]] for t in ring_perm}
    core_perm = [(i, i ^ 1) for i in range(4)]
    x_perm = [(i, i ^ 2) for i in range(4)]

    def core_swap(v):
        return lax.ppermute(v, "tensor", core_perm)

    def x_swap(v):
        return lax.ppermute(v, "tensor", x_perm)

    def gather_dp(block):
        pieces = []
        for t in range(n_major):
            piece = block if t == 0 else lax.ppermute(block, "dp", ring_perm[t])
            pieces += [piece, lax.ppermute(piece, "dp", pair_perm)]
        return pieces

    def scatter_dp(theirs, mine):
        major = lax.axis_index("dp") // 2
        got = lax.ppermute(theirs, "dp", pair_perm)

        def block(t):
            at = (major + t) % n_major
            a = lax.dynamic_slice_in_dim(mine, at, 1, axis=0)[0].astype(F32)
            return a + lax.dynamic_slice_in_dim(got, at, 1, axis=0)[0].astype(F32)

        arrived = [
            lax.ppermute(block(t).astype(BF), "dp", back_perm[t]) for t in range(1, n_major)
        ]
        total = block(0)
        for piece in arrived:
            total = total + piece.astype(F32)
        return total

    def join(mine, theirs):
        return (mine + core_swap(theirs).astype(F32)).astype(BF)

    def own_half(pair):
        first = lax.axis_index("tensor") < 2
        return jnp.where(first, pair[0], pair[1])

    def other_half(pair):
        first = lax.axis_index("tensor") < 2
        return jnp.where(first, pair[1], pair[0])

    def two_halves(own):
        got = x_swap(own)
        first = lax.axis_index("tensor") < 2
        return jnp.where(first, own, got), jnp.where(first, got, own)

    def sum_all(v):
        v = v + core_swap(v)
        return v + x_swap(v)

    def sum_vectors(v):
        h = v.shape[-1] // 2
        other = core_swap(v)
        v = v + jnp.concatenate([other[..., h:], other[..., :h]], -1)
        return v + x_swap(v)

    def sum_halves(pair):
        both = sum_vectors(jnp.stack(pair))
        return both[0], both[1]

    def quarters(values, axis):
        core = lax.axis_index("tensor") % 2
        step = values.shape[axis] // 4
        return jnp.concatenate(
            [
                lax.dynamic_slice_in_dim(values, at * step, step, axis)
                for at in (core, 1 - core, 2 + core, 3 - core)
            ],
            axis,
        )

    def on_device(
        hidden_in, context, time_emb, text_lengths, positions, modulation,
        self_query, self_key, self_value, self_output, self_query_gain, self_key_gain,
        cross_query, cross_key, cross_value, cross_output, cross_query_gain, cross_key_gain,
        norm_weight, norm_bias, ffn_up, ffn_down, out_cotangent,
    ):
        heads = self_query_gain.shape[0]
        half = positions.shape[1] // 2
        wide = heads * HEAD
        r_dp = self_query.shape[0]
        hid = ffn_up.shape[1]
        spare = -hid % HC

        texts = context.shape[1]
        quarter = half // 2
        g_cols = self_query_gain.shape[1]
        gains = [self_query_gain, self_key_gain, cross_query_gain, cross_key_gain]
        flat = jnp.concatenate([modulation, norm_weight[None], norm_bias[None]])
        side = jnp.pad(jnp.concatenate(gains), ((0, 0), (0, r_dp - g_cols)))
        small = jnp.concatenate([flat, side])
        small = jnp.pad(small, ((0, HEAD - small.shape[0]), (0, 0))).T.astype(BF)
        own_self = jnp.concatenate([self_query, self_key, self_value, self_output.T], axis=1).astype(BF)
        own_cross = jnp.concatenate([cross_query, cross_key, cross_value, cross_output.T], axis=1).astype(BF)
        padded = [jnp.pad(w, ((0, 0), (0, spare))) for w in (ffn_up.astype(BF), ffn_down.T.astype(BF))]
        hid_low = hid + spare
        own_ffn = [
            jnp.concatenate([w[:, j * HC : (j + 1) * HC] for w in padded], axis=1) for j in range(hid_low // HC)
        ]
        tables = rotary_tables(quarters(positions, 1), HEAD)
        text_bias = jnp.where(quarters(jnp.arange(4 * texts), 0) < text_lengths[0], 0.0, -1e30)
        text_bias = text_bias.astype(F32)[:, None]

        st = self_forward(
            hidden_in, context[0], out_cotangent, time_emb[0], tables, small,
            own_self, own_cross, own_ffn[0], n_dp, heads,
        )
        st |= cross_forward(st, out_cotangent, text_bias, own_ffn[1], own_ffn[2], n_dp, heads)
        d = lax.axis_index("dp")
        cosine, sine = ((t[:half], t[half:]) for t in tables)
        s0, s1, s2, s3, s4, s5, norm_gain, norm_shift = (st["shifts"][i : i + 1] for i in range(8))
        sq_gain, sk_gain, cq_gain, ck_gain = (
            st["gains"][i * heads : (i + 1) * heads].reshape(1, wide) for i in range(4)
        )
        ones = jnp.ones((1, D), F32)
        w_self, w_cross = [st["w_self"]], [st["w_cross"]]
        w_ffn = [st["f0"], st["f1"], st["f2"]]
        at_o, at_cq, at_ck, at_co = 3 * wide, 0, wide, 3 * wide

        def both(name):
            return [st[name + "0"], st[name + "1"]]

        def four(name):
            return [[st[name + "0"], st[name + "1"]], [st[name + "2"], st[name + "3"]]]

        first = lax.axis_index("tensor") < 2
        g = [jnp.where(first, out_cotangent, st["g_got"]), jnp.where(first, st["g_got"], out_cotangent)]
        ctx = [st[f"c{i}"] for i in range(4)]
        self_rows, cross_rows, ffn_rows = four("x"), four("y"), four("z")
        qk, v, stat, q, k, attn, lse = (both(name) for name in ("qk", "v", "stat", "q", "k", "attn", "lse"))
        self_chip, self_far, after_self = both("chip"), both("far"), both("after")
        ck_raw, cv, ck_stat, ck = st["ck_raw"], st["cv"], st["ck_stat"], st["ck"]
        cq_raw, cq_stat, cq, cattn, clse = (both(name) for name in ("cq_raw", "cq_stat", "cq", "cattn", "clse"))
        after_cross = both("after_c")

        def with_peer(rows):
            return [rows, core_swap(rows)]

        st |= feed_forward(st, out_cotangent, n_dp)
        g_c, sums_f = both("gc"), both("sf")

        st |= cross_backward(st, text_bias, n_dp, heads)
        g_own = own_half(both("gs"))
        self_branch = own_half(self_chip).astype(F32) + own_half(self_far).astype(F32)
        ffn_branch = st["branch"]
        sums_two = jnp.sum(g_own * self_branch, 0, keepdims=True)
        sums_five = jnp.sum(out_cotangent.astype(F32) * ffn_branch, 0, keepdims=True)
        st |= self_backward(st, hidden_in, tables, sums_two, sums_five, n_dp, heads)
        hid_grads = [st["s0"], st["s1"], st["s2"]]
        up_grad = jnp.concatenate([a[:, :HC] for a in hid_grads], axis=1)
        down_grad = jnp.concatenate([a[:, HC:] for a in hid_grads], axis=1)
        cross_grad = st["s3"]
        qkv_grad = [st["s5"][:, :wide], st["s5"][:, wide:], st["s4"][:, :wide]]
        oT_grad = st["s4"][:, wide:]
        hidden_grad, context_grad = st["hidden_grad"], st["ctx_grad"]

        block_out = (own_half(after_cross) + ffn_branch * s5).astype(BF)

        time_grad = st["time"][:6]
        eight = st["tiny"][:, :8].T
        gains_out = st["tiny"][:g_cols, 8 : 8 + 4 * heads].T.reshape(4, heads, g_cols)

        return (
            block_out,
            hidden_grad,
            context_grad[None],
            time_grad[None],
            eight[:6],
            qkv_grad[0],
            qkv_grad[1],
            qkv_grad[2],
            oT_grad.T,
            gains_out[0],
            gains_out[1],
            cross_grad[:, :wide],
            cross_grad[:, wide : 2 * wide],
            cross_grad[:, 2 * wide : 3 * wide],
            cross_grad[:, 3 * wide :].T,
            gains_out[2],
            gains_out[3],
            eight[6],
            eight[7],
            up_grad[:, :hid],
            down_grad[:, :hid].T,
        )

    rows = P(("dp", "tensor"), None)
    col = P("dp", "tensor")
    row = P("tensor", "dp")
    text = P("dp", "tensor", None)
    time = P("dp", None, None)
    one = P("dp")
    ins = (
        rows, text, time, one, P(None, "dp"), P(None, "dp"),
        col, col, col, row, row, row,
        col, col, col, row, row, row,
        one, one, col, row, rows,
    )
    outs = (
        rows, rows, text, time, P(None, "dp"),
        col, col, col, row, row, row,
        col, col, col, row, row, row,
        one, one, col, row,
    )
    return jax.shard_map(on_device, mesh=mesh, in_specs=ins, out_specs=outs, check_vma=False)
```

```python
import math

import jax
import jax.numpy as jnp
from jax import lax
from jax.experimental import pallas as pl
from jax.experimental.pallas import tpu as pltpu
from jax.sharding import PartitionSpec as P

D = 1536
HEAD = 128
EPS = 1e-6
BF = jnp.bfloat16
F32 = jnp.float32
FACTOR = 1.0 / math.sqrt(HEAD)
GELU = math.sqrt(2.0 / math.pi)
CUBE = 0.044715
MESH = pl.DeviceIdType.MESH


def dot_nn(a, b):
    return lax.dot_general(a, b, (((1,), (0,)), ((), ())), preferred_element_type=F32)


def dot_nt(a, b):
    return lax.dot_general(a, b, (((1,), (1,)), ((), ())), preferred_element_type=F32)


def dot_tn(a, b):
    return lax.dot_general(a, b, (((0,), (0,)), ((), ())), preferred_element_type=F32)


def shape(dims, dtype):
    return jax.ShapeDtypeStruct(dims, dtype)


def run(kernel, outs, blocks, far=(), scratch=(), flops=0, exps=0, limit=60):
    moved = sum(math.prod(v.shape) * v.dtype.itemsize for v in (*blocks, *far, *outs))
    return pl.pallas_call(
        kernel,
        out_shape=tuple(outs),
        in_specs=[pl.BlockSpec(memory_space=pltpu.VMEM)] * len(blocks)
        + [pl.BlockSpec(memory_space=pl.ANY)] * len(far),
        out_specs=tuple(pl.BlockSpec(memory_space=pltpu.VMEM) for _ in outs),
        scratch_shapes=list(scratch),
        compiler_params=pltpu.CompilerParams(vmem_limit_bytes=limit * 2**20),
        cost_estimate=pl.CostEstimate(flops=int(flops), bytes_accessed=moved, transcendentals=int(exps)),
    )(*blocks, *far)


def load(pieces, w, sems, first=0):
    n = len(pieces)
    r, c = w.shape[0] // n, w.shape[1]
    if n == 1:
        copy = pltpu.make_async_copy(pieces[0].at[:, pl.ds(first, c)], w, sems.at[0])
        copy.start()
        return [copy]
    d = lax.axis_index("dp")
    major, minor = d // 2, d % 2
    copies = []
    for i, piece in enumerate(pieces):
        t, flip = i // 2, i % 2
        block = 2 * lax.rem(major + t, n // 2) + (1 - minor if flip else minor)
        rows = pl.ds(pl.multiple_of(block * r, 16), r)
        copy = pltpu.make_async_copy(piece.at[:, pl.ds(first, c)], w.at[rows], sems.at[i])
        copy.start()
        copies.append(copy)
    return copies


def wait(copies):
    for copy in copies:
        copy.wait()


def weight(n, c):
    return [pltpu.VMEM((D, c), BF), pltpu.SemaphoreType.DMA((n,))]


def to_rows(columns, count):
    lane = lax.broadcasted_iota(jnp.int32, (count, 128), 1)
    out = jnp.zeros((count, 128), F32)
    for i, column in enumerate(columns):
        out = jnp.where(lane == i, column, out)
    return jnp.transpose(out)[:8]


def to_columns(rows):
    return jnp.transpose(jnp.concatenate([rows] * 16, axis=0))


def turn(values, cosine, sine):
    even = lax.broadcasted_iota(jnp.int32, values.shape, 1) % 2 == 0
    partner = jnp.where(even, pltpu.roll(values, HEAD - 1, 1), pltpu.roll(values, 1, 1))
    return values * cosine + partner * sine


def norm_of(v):
    center = v - jnp.mean(v, axis=-1, keepdims=True)
    r = lax.rsqrt(jnp.mean(center * center, axis=-1, keepdims=True) + EPS)
    return center * r, r


STEP = 32


def over_rows(count, body):
    def one(i, carry):
        body(pl.ds(pl.multiple_of(i * STEP, STEP), STEP))
        return carry

    lax.fori_loop(0, count // STEP, one, 0)


def norm_first(v, m, t):
    def kernel(v_ref, m_ref, t_ref, rows_ref):
        def body(s):
            n, _ = norm_of(v_ref[s].astype(F32))
            rows_ref[s] = (n * m_ref[...] + t_ref[...]).astype(BF)

        over_rows(v_ref.shape[0], body)

    return run(kernel, [shape(v.shape, BF)], [v, m, t], flops=1e9)[0]


def norm_forward(v, chip, far_chip, s, m, t):
    def kernel(v_ref, a_ref, b_ref, s_ref, m_ref, t_ref, out_ref, rows_ref):
        def body(i):
            branch = a_ref[i].astype(F32) + b_ref[i].astype(F32)
            out = v_ref[i].astype(F32) + branch * s_ref[...]
            out_ref[i] = out
            n, _ = norm_of(out)
            rows_ref[i] = (n * m_ref[...] + t_ref[...]).astype(BF)

        over_rows(v_ref.shape[0], body)

    return run(
        kernel, [shape(v.shape, F32), shape(v.shape, BF)], [v, chip, far_chip, s, m, t], flops=1e9
    )


def norm_backward(g, v, chip, far_chip, m, s):
    def kernel(g_ref, v_ref, a_ref, b_ref, m_ref, s_ref, out_ref, rows_ref, sum_ref):
        sum_ref[...] = jnp.zeros_like(sum_ref)

        def body(i):
            da = a_ref[i].astype(F32) + b_ref[i].astype(F32)
            n, r = norm_of(v_ref[i].astype(F32))
            dn = da * m_ref[...]
            mean = jnp.mean(dn, axis=-1, keepdims=True)
            along = jnp.mean(dn * n, axis=-1, keepdims=True)
            out = g_ref[i].astype(F32) + r * (dn - mean - n * along)
            out_ref[i] = out
            rows_ref[i] = (out * s_ref[...]).astype(BF)
            dan = da * n
            for k in range(STEP // 8):
                sum_ref[:8] += da[k * 8 : k * 8 + 8]
                sum_ref[8:] += dan[k * 8 : k * 8 + 8]

        over_rows(g_ref.shape[0], body)

    return run(
        kernel,
        [shape(g.shape, F32), shape(g.shape, BF), shape((16, D), F32)],
        [g, v, chip, far_chip, m, s],
        flops=1e9,
    )


def hold(v, after):
    def kernel(v_ref, *refs):
        refs[-1][...] = v_ref[...]

    return run(kernel, [shape(v.shape, v.dtype)], [v], after)[0]


def project(xs, pieces, first, squares, lows, wide):
    total = sum(x.shape[0] for x in xs)
    cols = (squares + lows) * wide
    n = len(pieces)
    outs = [shape((total, squares * wide), F32)] * (squares > 0)
    outs += [shape((total, lows * wide), BF)] * (lows > 0)
    outs += [shape((8, total), F32)] * (squares > 0)

    def kernel(*refs):
        x_refs, refs = refs[: len(xs)], refs[len(xs) :]
        piece_refs, refs = refs[:n], refs[n:]
        out_refs, (w, sems) = list(refs[:-2]), refs[-2:]
        wait(load(piece_refs, w, sems, first))
        at = 0
        for x_ref in x_refs:
            m = x_ref.shape[0]
            value = dot_nn(x_ref[...], w[...])
            columns = []
            for i in range(squares):
                part = value[:, i * wide : (i + 1) * wide]
                columns.append(jnp.sum(part * part, axis=1, keepdims=True))
            if squares:
                out_refs[0][at : at + m] = value[:, : squares * wide]
                out_refs[-1][:, at : at + m] = to_rows(columns, m)
            if lows:
                out_refs[1 if squares else 0][at : at + m] = value[:, squares * wide :].astype(BF)
            at += m

    return run(kernel, outs, xs, pieces, weight(n, cols), flops=2 * total * D * cols)


def normalize(raws, stats, gains, tables, wide):
    count = len(gains)
    parts = len(raws)
    outs = [shape((r.shape[0], wide), BF) for r in raws for _ in range(count)]

    def kernel(*refs):
        raw_refs, refs = refs[:parts], refs[parts:]
        stat_refs, refs = refs[:parts], refs[parts:]
        gain_refs, refs = refs[:count], refs[count:]
        if tables:
            cos_refs, sin_refs, refs = refs[:parts], refs[parts : 2 * parts], refs[2 * parts :]
        for p in range(parts):
            scale = lax.rsqrt(to_columns(stat_refs[p][...]) / D + EPS)
            for i in range(count):
                for h in range(wide // HEAD):
                    lanes = slice(i * wide + h * HEAD, i * wide + (h + 1) * HEAD)
                    own = slice(h * HEAD, (h + 1) * HEAD)
                    value = raw_refs[p][:, lanes] * scale[:, i : i + 1] * gain_refs[i][:, own]
                    if tables:
                        value = turn(value, cos_refs[p][...], sin_refs[p][...])
                    refs[p * count + i][:, own] = value.astype(BF)

    args = [*raws, *stats, *gains]
    if tables:
        args += [*tables[0], *tables[1]]
    return run(kernel, outs, args, flops=1e9)


QB = 256


def attend(q, ks, vs, bias, pieces, first):
    rows, wide = q.shape
    heads = wide // HEAD
    nk = sum(k.shape[0] for k in ks)
    n = len(pieces)
    parts = len(ks)
    half = rows // 2
    biases = [] if bias is None else [bias]

    def kernel(*refs):
        q_ref, k_refs, v_refs = refs[0], refs[1 : 1 + parts], refs[1 + parts : 1 + 2 * parts]
        refs = refs[1 + 2 * parts :]
        b_refs, refs = refs[: len(biases)], refs[len(biases) :]
        piece_refs, (out_ref, lse_ref, mine_ref, theirs_ref, w, sems) = refs[:n], refs[n:]
        copies = load(piece_refs, w, sems, first)
        lse_ref[...] = jnp.zeros_like(lse_ref)
        for h in range(heads):
            lanes = slice(h * HEAD, (h + 1) * HEAD)
            k = jnp.concatenate([r[:, lanes] for r in k_refs]) if parts > 1 else k_refs[0][:, lanes]
            v = jnp.concatenate([r[:, lanes] for r in v_refs]) if parts > 1 else v_refs[0][:, lanes]
            for b in range(rows // QB):
                block = slice(b * QB, (b + 1) * QB)
                s = dot_nt(k, q_ref[block, lanes]) * FACTOR
                if biases:
                    s = s + b_refs[0][...]
                top = jnp.max(s, axis=0, keepdims=True)
                e = jnp.exp(s - top)
                total = jnp.sum(e, axis=0, keepdims=True)
                lse_ref[h : h + 1, block] = top + jnp.log(total)
                o = dot_tn(v, e.astype(BF)) * (1.0 / total)
                out_ref[block, lanes] = jnp.transpose(o).astype(BF)
        wait(copies)
        mine_ref[...] = dot_nt(out_ref[:half], w[...])
        theirs_ref[...] = dot_nt(out_ref[half:], w[...]).astype(BF)

    return run(
        kernel,
        [shape((rows, wide), BF), shape((8, rows), F32), shape((half, D), F32), shape((half, D), BF)],
        [q, *ks, *vs, *biases],
        pieces,
        weight(n, wide),
        flops=2 * rows * wide * (2 * nk + D),
        exps=rows * nk * heads,
    )


def attend_back(xs, pieces, first, q, ks, vs, bias, lse, sofar):
    rows, wide = q.shape
    heads = wide // HEAD
    nk = sum(k.shape[0] for k in ks)
    n = len(pieces)
    parts = len(ks)
    biases = [] if bias is None else [bias]

    def kernel(*refs):
        x_refs, q_ref, refs = refs[:2], refs[2], refs[3:]
        k_refs, v_refs, lse_ref, refs = refs[:parts], refs[parts : 2 * parts], refs[2 * parts], refs[2 * parts + 1 :]
        b_refs, refs = refs[: len(biases)], refs[len(biases) :]
        old_refs, refs = refs[: len(sofar)], refs[len(sofar) :]
        piece_refs, (dq_ref, dk_ref, dv_ref, w, sems, do_ref) = refs[:n], refs[n:]
        wait(load(piece_refs, w, sems, first))
        for i in range(2):
            m = x_refs[i].shape[0]
            do_ref[i * m : (i + 1) * m] = dot_nn(x_refs[i][...], w[...]).astype(BF)
        for h in range(heads):
            lanes = slice(h * HEAD, (h + 1) * HEAD)
            k = jnp.concatenate([r[:, lanes] for r in k_refs]) if parts > 1 else k_refs[0][:, lanes]
            v = jnp.concatenate([r[:, lanes] for r in v_refs]) if parts > 1 else v_refs[0][:, lanes]
            for b in range(rows // QB):
                block = slice(b * QB, (b + 1) * QB)
                qb = q_ref[block, lanes]
                do = do_ref[block, lanes]
                s = dot_nt(k, qb) * FACTOR
                if biases:
                    s = s + b_refs[0][...]
                p = jnp.exp(s - lse_ref[h : h + 1, block])
                dp = dot_nt(v, do)
                center = jnp.sum(p * dp, axis=0, keepdims=True)
                ds = (p * (dp - center)).astype(BF)
                dq_ref[block, lanes] = dot_tn(ds, k) * FACTOR
                dk = dot_nn(ds, qb) * FACTOR
                dv = dot_nn(p.astype(BF), do)
                if b == 0 and not sofar:
                    dk_ref[:, lanes] = dk
                    dv_ref[:, lanes] = dv
                elif b == 0:
                    dk_ref[:, lanes] = old_refs[0][:, lanes] + dk
                    dv_ref[:, lanes] = old_refs[1][:, lanes] + dv
                else:
                    dk_ref[:, lanes] += dk
                    dv_ref[:, lanes] += dv

    return run(
        kernel,
        [shape((rows, wide), F32), shape((nk, wide), F32), shape((nk, wide), F32)],
        [*xs, q, *ks, *vs, lse, *biases, *sofar],
        pieces,
        weight(n, wide) + [pltpu.VMEM((rows, wide), BF)],
        flops=2 * rows * wide * (5 * nk + D),
        exps=rows * nk * heads,
    )


def root_dots(dys, raws, stats, gains, tables, wide):
    count = len(gains)
    outs = [shape(dy.shape, F32) for dy in dys] if tables else []
    outs += [shape((8, dy.shape[0]), F32) for dy in dys]
    outs += [shape((8, wide), F32)]

    def kernel(*refs):
        dy_refs, refs = refs[:count], refs[count:]
        raw_refs, refs = refs[:count], refs[count:]
        stat_refs, refs = refs[:count], refs[count:]
        gain_refs, refs = refs[:count], refs[count:]
        if tables:
            cos_ref, sin_ref, refs = refs[0], refs[1], refs[2:]
            turned, refs = refs[:count], refs[count:]
        dot_refs, grad_ref = refs[:count], refs[count]
        grad_ref[...] = jnp.zeros_like(grad_ref)
        for i in range(count):
            row = raws[i][2]
            m = dy_refs[i].shape[0]
            scale = lax.rsqrt(to_columns(stat_refs[i][...]) / D + EPS)[:, row : row + 1]
            dots = jnp.zeros((m, 1), F32)
            for h in range(wide // HEAD):
                own = slice(h * HEAD, (h + 1) * HEAD)
                dy = dy_refs[i][:, own]
                if tables:
                    dy = turn(dy, cos_ref[...], -sin_ref[...])
                    turned[i][:, own] = dy
                c = raws[i][1] + h * HEAD
                both = raw_refs[i][:, c : c + HEAD] * dy
                dots = dots + jnp.sum(both * gain_refs[i][:, own], axis=1, keepdims=True)
                grad_ref[i : i + 1, own] = jnp.sum(both * scale, axis=0, keepdims=True)
            dot_refs[i][...] = to_rows([dots], m)

    args = [*dys, *(r[0] for r in raws), *stats, *gains]
    if tables:
        args += [*tables]
    return run(kernel, outs, args, flops=1e9)


def root_back(dys, raws, stats, dots, gains, dv, pieces, first, wide, halves):
    count = len(gains)
    extra = 0 if dv is None else 1
    rows = dys[0].shape[0]
    cols = (count + extra) * wide
    n = len(pieces)
    part = rows // (2 * halves)
    vs = [] if dv is None else [dv]

    def kernel(*refs):
        dy_refs, refs = refs[:count], refs[count:]
        raw_refs, refs = refs[:count], refs[count:]
        stat_refs, refs = refs[:count], refs[count:]
        dot_refs, refs = refs[:count], refs[count:]
        gain_refs, refs = refs[:count], refs[count:]
        v_refs, refs = refs[:extra], refs[extra:]
        piece_refs, refs = refs[:n], refs[n:]
        low_ref, refs = refs[0], refs[1:]
        mine_refs, their_refs, (w, sems) = refs[:halves], refs[halves : 2 * halves], refs[2 * halves :]
        copies = load(piece_refs, w, sems, first)
        for i in range(count):
            row = raws[i][2]
            scale = lax.rsqrt(to_columns(stat_refs[i][...]) / D + EPS)[:, row : row + 1]
            along = scale * scale * scale * to_columns(dot_refs[i][...])[:, 0:1] / D
            for h in range(wide // HEAD):
                own = slice(h * HEAD, (h + 1) * HEAD)
                c = raws[i][1] + h * HEAD
                dx = scale * gain_refs[i][:, own] * dy_refs[i][:, own] - raw_refs[i][:, c : c + HEAD] * along
                low_ref[:, i * wide + h * HEAD : i * wide + (h + 1) * HEAD] = dx.astype(BF)
        if extra:
            low_ref[:, count * wide :] = v_refs[0][...].astype(BF)
        wait(copies)
        for j in range(halves):
            at = 2 * part * j
            mine_refs[j][...] = dot_nt(low_ref[at : at + part], w[...])
            their_refs[j][...] = dot_nt(low_ref[at + part : at + 2 * part], w[...]).astype(BF)

    return run(
        kernel,
        [shape((rows, cols), BF)]
        + [shape((part, D), F32)] * halves
        + [shape((part, D), BF)] * halves,
        [*dys, *(r[0] for r in raws), *stats, *dots, *gains, *vs],
        pieces,
        weight(n, cols),
        flops=2 * rows * cols * D,
    )


HC = 768


def expand(xs, pieces, first, hid):
    rows = sum(x.shape[0] for x in xs)
    n = len(pieces)

    def kernel(*refs):
        x_refs, piece_refs, (out_ref, w, sems) = refs[: len(xs)], refs[len(xs) : len(xs) + n], refs[len(xs) + n :]
        chunks = [load(piece_refs[j : j + 1], w.at[j], sems.at[j], first) for j in range(hid // HC)]
        for j in range(hid // HC):
            wait(chunks[j])
            at = 0
            for x_ref in x_refs:
                m = x_ref.shape[0]
                out_ref[at : at + m, j * HC : (j + 1) * HC] = dot_nn(x_ref[...], w[j]).astype(BF)
                at += m

    return run(
        kernel,
        [shape((rows, hid), BF)],
        xs,
        pieces,
        [pltpu.VMEM((hid // HC, D, HC), BF), pltpu.SemaphoreType.DMA((hid // HC, 1))],
        flops=2 * rows * D * hid,
    )[0]


def feed(xs, dact, pieces, first):
    rows, hid = dact.shape
    n = len(pieces)
    m = rows // 2

    def kernel(*refs):
        x_refs, dact_ref, piece_refs = refs[:2], refs[2], refs[3 : 3 + n]
        act_ref, dpre_ref, mine_ref, theirs_ref, w, sems = refs[3 + n :]
        chunks = [load(piece_refs[j : j + 1], w.at[j], sems.at[j], first) for j in range(hid // HC)]
        for j in range(hid // HC):
            cols = slice(j * HC, (j + 1) * HC)
            wait(chunks[j])
            for i in range(2):
                own = slice(i * m, (i + 1) * m)
                u = dot_nn(x_refs[i][...], w[j])
                sq = u * u
                th = jnp.tanh(u * (GELU + GELU * CUBE * sq))
                near = 0.5 + 0.5 * th
                act_ref[own, cols] = (u * near).astype(BF)
                slope = near + u * near * (1.0 - th) * (GELU + 3 * GELU * CUBE * sq)
                dpre_ref[own, cols] = (dact_ref[own, cols].astype(F32) * slope).astype(BF)
        for i in range(2):
            own = slice(i * m, (i + 1) * m)
            total = dot_nt(dpre_ref[own, :HC], w[0])
            for j in range(1, hid // HC):
                total = total + dot_nt(dpre_ref[own, j * HC : (j + 1) * HC], w[j])
            if i == 0:
                mine_ref[...] = total
            else:
                theirs_ref[...] = total.astype(BF)

    return run(
        kernel,
        [shape((rows, hid), BF), shape((rows, hid), BF), shape((m, D), F32), shape((m, D), BF)],
        [*xs, dact],
        pieces,
        [pltpu.VMEM((hid // HC, D, HC), BF), pltpu.SemaphoreType.DMA((hid // HC, 1))],
        flops=4 * rows * D * hid,
        exps=rows * hid,
        limit=60,
    )


def contract(act, pieces, first):
    rows, hid = act.shape
    n = len(pieces)
    m = rows // 2

    def kernel(*refs):
        act_ref, piece_refs, (mine_ref, theirs_ref, w, sems) = refs[0], refs[1 : 1 + n], refs[1 + n :]
        chunks = [load(piece_refs[j : j + 1], w.at[j], sems.at[j], first) for j in range(hid // HC)]
        for chunk in chunks:
            wait(chunk)
        for i in range(2):
            own = slice(i * m, (i + 1) * m)
            total = dot_nt(act_ref[own, :HC], w[0])
            for j in range(1, hid // HC):
                total = total + dot_nt(act_ref[own, j * HC : (j + 1) * HC], w[j])
            if i == 0:
                mine_ref[...] = total
            else:
                theirs_ref[...] = total.astype(BF)

    return run(
        kernel,
        [shape((m, D), F32), shape((m, D), BF)],
        [act],
        pieces,
        [pltpu.VMEM((hid // HC, D, HC), BF), pltpu.SemaphoreType.DMA((hid // HC, 1))],
        flops=2 * rows * D * hid,
    )


GC = 384


def full_grads(xs, ys):
    cols = ys[0].shape[1]
    most = sum(x.shape[0] for x in xs)

    def kernel(*refs):
        x_refs, y_refs, (out_ref, turned) = refs[: len(xs)], refs[len(xs) : -2], refs[-2:]
        row = 0
        for x_ref in x_refs:
            m = x_ref.shape[0]
            turned[:, row : row + m] = jnp.transpose(x_ref[...])
            row += m
        for c in range(0, cols, HC):
            lanes = slice(c, c + HC)
            for k in range(0, D, 512):
                row = 0
                total = None
                for y_ref in y_refs:
                    m = y_ref.shape[0]
                    term = dot_nn(turned[k : k + 512, row : row + m], y_ref[:, lanes])
                    total = term if total is None else total + term
                    row += m
                out_ref[k : k + 512, lanes] = total.astype(BF)

    return run(
        kernel,
        [shape((D, cols), BF)],
        [*xs, *ys],
        (),
        [pltpu.VMEM((D, most), BF)],
        flops=2 * most * D * cols,
        limit=60,
    )[0]


def weight_grads(pairs, n, after=()):
    widths = [ys[0].shape[1] for _, ys in pairs]
    cols = sum(widths)
    r = D // n
    flat = [a for xs, ys in pairs for a in (*xs, *ys)]
    out = shape((n // 2, r, cols), BF)
    most = max(sum(x.shape[0] for x in xs) for xs, _ in pairs)

    def kernel(*refs):
        ins, refs = refs[: len(flat)], refs[len(flat) + len(after) :]
        theirs_ref, mine_ref, total_ref, turned, sems = refs
        minor = lax.axis_index("dp") % 2
        at = 0
        col = 0
        copies = []
        for p, (xs, ys) in enumerate(pairs):
            x_refs, y_refs = ins[at : at + len(xs)], ins[at + len(xs) : at + len(xs) + len(ys)]
            at += len(xs) + len(ys)
            row = 0
            for x_ref in x_refs:
                m = x_ref.shape[0]
                turned[:, row : row + m] = jnp.transpose(x_ref[...])
                row += m
            for c in range(0, widths[p], GC):
                lanes = slice(c, c + GC)
                for k in range(0, D, 512):
                    row = 0
                    total = None
                    for y_ref in y_refs:
                        m = y_ref.shape[0]
                        term = dot_nn(turned[k : k + 512, row : row + m], y_ref[:, lanes])
                        total = term if total is None else total + term
                        row += m
                    total_ref[k : k + 512, col + c : col + c + GC] = total.astype(BF)
                for j in range(n // 2):
                    for flip, ref in ((1, theirs_ref), (0, mine_ref)):
                        block = 2 * j + (1 - minor if flip else minor)
                        copy = pltpu.make_async_copy(
                            total_ref.at[
                                pl.ds(pl.multiple_of(block * r, 16), r), pl.ds(col + c, GC)
                            ],
                            ref.at[j, :, pl.ds(col + c, GC)],
                            sems.at[(col + c) // GC, 2 * j + flip],
                        )
                        copy.start()
                        copies.append(copy)
            col += widths[p]
        wait(copies)

    moved = sum(math.prod(v.shape) * 2 for v in flat) + 2 * D * cols
    return pl.pallas_call(
        kernel,
        out_shape=(out, out),
        in_specs=[pl.BlockSpec(memory_space=pltpu.VMEM)] * len(flat)
        + [pl.BlockSpec(memory_space=pl.ANY)] * len(after),
        out_specs=(pl.BlockSpec(memory_space=pl.ANY),) * 2,
        scratch_shapes=[
            pltpu.VMEM((D, cols), BF),
            pltpu.VMEM((D, most), BF),
            pltpu.SemaphoreType.DMA((cols // GC, n)),
        ],
        compiler_params=pltpu.CompilerParams(vmem_limit_bytes=60 * 2**20),
        cost_estimate=pl.CostEstimate(
            flops=int(2 * most * D * cols), bytes_accessed=moved, transcendentals=0
        ),
    )(*flat, *after)


class Flush:
    def __init__(self, names, held, outs, sems):
        self.copies = {
            name: pltpu.make_async_copy(held[j], outs[j], sems.at[j]) for j, name in enumerate(names)
        }
        self.gone = []

    def __call__(self, *names):
        for name in names:
            self.copies[name].start()
            self.gone.append(name)

    def finish(self):
        self(*[name for name in self.copies if name not in self.gone])
        for copy in self.copies.values():
            copy.wait()


def run_remote(kernel, outs, far_outs, blocks, far, scratch, cid, flops):
    moved = sum(math.prod(v.shape) * v.dtype.itemsize for v in (*blocks, *outs.values()))
    vmem, hbm = pl.BlockSpec(memory_space=pltpu.VMEM), pl.BlockSpec(memory_space=pl.ANY)
    n_in, n_out, n_far = len(blocks) + len(far), len(outs), len(far_outs)

    def body(*refs):
        given, refs = refs[:n_in], refs[n_in:]
        results, refs = refs[:n_out], refs[n_out:]
        beyond, refs = refs[:n_far], refs[n_far:]
        held, sems, rest = refs[:n_out], refs[n_out], refs[n_out + 1 :]
        flush = Flush(list(outs), held, results, sems)
        kernel(*given, *held, *beyond, *rest, flush=flush)
        flush.finish()

    got = pl.pallas_call(
        body,
        out_shape=(*outs.values(), *far_outs.values()),
        in_specs=[vmem] * len(blocks) + [hbm] * len(far),
        out_specs=(hbm,) * (n_out + n_far),
        scratch_shapes=[
            *(pltpu.VMEM(v.shape, v.dtype) for v in outs.values()),
            pltpu.SemaphoreType.DMA((n_out,)),
            *scratch,
        ],
        compiler_params=pltpu.CompilerParams(
            vmem_limit_bytes=61 * 2**20, collective_id=cid, has_side_effects=True
        ),
        cost_estimate=pl.CostEstimate(flops=int(flops), bytes_accessed=moved, transcendentals=0),
    )(*blocks, *far)
    return dict(zip([*outs, *far_outs], got))


def tensor_peers():
    t = lax.axis_index("tensor")
    core = t + 1 - 2 * lax.rem(t, 2)
    across = lax.rem(t + 2, 4)
    return t, core, across, 3 - t


def greet(n_dp):
    d = lax.axis_index("dp")
    barrier = pltpu.get_barrier_semaphore()
    for k in range(1, n_dp):
        pl.semaphore_signal(
            barrier, inc=1, device_id={"dp": lax.rem(d + k, n_dp)}, device_id_type=MESH
        )
    for peer in tensor_peers()[1:]:
        pl.semaphore_signal(barrier, inc=1, device_id={"tensor": peer}, device_id_type=MESH)
    pl.semaphore_wait(barrier, n_dp + 2)


def remote(src, dst, send, recv, **place):
    return pltpu.make_async_remote_copy(
        src_ref=src, dst_ref=dst, send_sem=send, recv_sem=recv, device_id=place, device_id_type=MESH
    )


class Gather:
    def __init__(self, ref, sems, n):
        d = lax.axis_index("dp")
        self.z, self.y = d // 2, lax.rem(d, 2)
        self.ref, self.sems, self.n, self.r = ref, sems, n, ref.shape[0] // (2 * n)
        self.cols = (0, ref.shape[1])
        self.near = (0, ref.shape[1] - 256)
        self.last = (ref.shape[1] - 256, ref.shape[1])

    def copy(self, o, kind, index, z, y, own, cols):
        start = (2 * o + (self.y if own else 1 - self.y)) * self.r
        block = self.ref.at[pl.ds(pl.multiple_of(start, 16), self.r), pl.ds(cols[0], cols[1] - cols[0])]
        sems = self.sems
        return remote(block, block, sems.at[2 * kind, index], sems.at[2 * kind + 1, index], dp=2 * z + y)

    def along(self, way, s, own=True):
        kind = (0 if way > 0 else 1) + (0 if own else 3)
        cols = self.cols if own else self.last
        return self.copy(self.z - way * s, kind, s, self.z + way, self.y, own, cols)

    def came(self, way, s, own=True):
        kind = (0 if way > 0 else 1) + (0 if own else 3)
        cols = self.cols if own else self.last
        return self.copy(self.z - way * (s + 1), kind, s, self.z - way, self.y, own, cols)

    def over(self, o, cols):
        return self.copy(o, 2, o, self.z, 1 - self.y, True, cols)

    def inside(self, o):
        return (o >= 0) & (o <= self.n - 1)

    def start(self, own, sem):
        start = (2 * self.z + self.y) * self.r
        copy = pltpu.make_async_copy(own, self.ref.at[pl.ds(pl.multiple_of(start, 16), self.r)], sem)
        copy.start()
        copy.wait()
        for way in (1, -1):
            pl.when(self.inside(self.z + way))(lambda way=way: self.along(way, 0).start())
        self.over(self.z, self.cols).start()

    def step(self, s):
        for way in (1, -1):

            @pl.when(self.inside(self.z - way * (s + 1)))
            def _(way=way):
                self.came(way, s).wait_recv()
                pl.when(self.inside(self.z + way))(lambda: self.along(way, s + 1).start())
                self.over(self.z - way * (s + 1), self.near).start()

        self.rest(s)

    def rest(self, s):
        if s == 0:
            self.copy(self.z, 2, self.z, self.z, 1 - self.y, False, self.cols).wait_recv()
        for way in (1, -1):
            if s == 0:
                pl.when(self.inside(self.z + way))(lambda way=way: self.along(way, 0, False).start())
            else:

                @pl.when(self.inside(self.z - way * s))
                def _(way=way):
                    self.came(way, s - 1, False).wait_recv()
                    if s < self.n - 1:
                        pl.when(self.inside(self.z + way))(lambda: self.along(way, s, False).start())

    def finish(self):
        self.rest(self.n - 1)
        for o in range(self.n):
            pl.when(self.z != o)(
                lambda o=o: self.copy(o, 2, o, self.z, 1 - self.y, False, self.near).wait_recv()
            )

    def drain(self):
        for own in (True, False):
            for s in range(self.n - 1):
                for way in (1, -1):
                    pl.when(self.inside(self.z - way * s) & self.inside(self.z + way))(
                        lambda s=s, way=way, own=own: self.along(way, s, own).wait_send()
                    )
        for o in range(self.n):
            pl.when(self.z == o)(lambda: self.over(self.z, self.cols).wait_send())
            pl.when(self.z != o)(lambda o=o: self.over(o, self.near).wait_send())


class Swap:
    def __init__(self, sems):
        self.sems, self.used, self.sent = sems, 0, []

    def start(self, src, dst, peer):
        k = self.used
        self.used += 1
        copy = remote(src, dst, self.sems.at[0, k], self.sems.at[1, k], tensor=peer)
        copy.start()
        self.sent.append(copy)
        return copy

    def settle(self):
        for copy in self.sent:
            copy.wait_send()
        self.sent = []


class Sums:
    def __init__(self, landed, sems, peers):
        self.landed, self.peers, self.used = landed, peers, 0
        self.swap = Swap(sems)

    def start(self, ref):
        k, c = self.used, ref.shape[1]
        self.used += 1
        copies = [
            self.swap.start(ref, self.landed.at[k, p, :, pl.ds(0, c)], peer)
            for p, peer in enumerate(self.peers)
        ]

        def collect():
            for copy in copies:
                copy.wait()
            stat_sum(ref, [self.landed[k, p, :, :c] for p in range(3)])

        return collect


def project_body(x_refs, w, first, out_ref, low_ref, stat_ref, squares, lows, wide):
    at = 0
    for x_ref in x_refs:
        m = x_ref.shape[0]
        value = dot_nn(x_ref[...], w[:, first : first + (squares + lows) * wide])
        columns = []
        for i in range(squares):
            part = value[:, i * wide : (i + 1) * wide]
            columns.append(jnp.sum(part * part, axis=1, keepdims=True))
        out_ref[at : at + m] = value[:, : squares * wide]
        stat_ref[:, at : at + m] = to_rows(columns, m)
        if lows:
            low_ref[at : at + m] = value[:, squares * wide :].astype(BF)
        at += m


def normalize_body(raw_ref, stat_ref, gains, cos, sin, out_refs, wide):
    scale = lax.rsqrt(to_columns(stat_ref[...]) / D + EPS)
    for i, out_ref in enumerate(out_refs):
        for h in range(wide // HEAD):
            lanes = slice(i * wide + h * HEAD, i * wide + (h + 1) * HEAD)
            value = raw_ref[:, lanes] * scale[:, i : i + 1] * gains[i][h]
            if cos is not None:
                value = turn(value, cos, sin)
            out_ref[:, h * HEAD : (h + 1) * HEAD] = value.astype(BF)


def attend_body(q_ref, k_refs, v_refs, bias_ref, out_ref, lse_ref):
    rows, wide = q_ref.shape
    lse_ref[...] = jnp.zeros_like(lse_ref)
    for h in range(wide // HEAD):
        lanes = slice(h * HEAD, (h + 1) * HEAD)
        k = jnp.concatenate([r[:, lanes] for r in k_refs]) if len(k_refs) > 1 else k_refs[0][:, lanes]
        v = jnp.concatenate([r[:, lanes] for r in v_refs]) if len(v_refs) > 1 else v_refs[0][:, lanes]
        for b in range(rows // QB):
            block = slice(b * QB, (b + 1) * QB)
            s = dot_nt(k, q_ref[block, lanes]) * FACTOR
            if bias_ref is not None:
                s = s + bias_ref[...]
            top = jnp.max(s, axis=0, keepdims=True)
            e = jnp.exp(s - top)
            total = jnp.sum(e, axis=0, keepdims=True)
            lse_ref[h : h + 1, block] = top + jnp.log(total)
            o = dot_tn(v, e.astype(BF)) * (1.0 / total)
            out_ref[block, lanes] = jnp.transpose(o).astype(BF)


def stat_sum(stat_ref, landed):
    h = stat_ref.shape[1] // 2
    other = landed[0] + landed[2]
    total = stat_ref[...] + landed[1]
    stat_ref[:, :h] = total[:, :h] + other[:, h:]
    stat_ref[:, h:] = total[:, h:] + other[:, :h]


def join_body(mine, got, chip):
    def body(i):
        chip[i] = (mine[i] + got[i].astype(F32)).astype(BF)

    over_rows(mine.shape[0], body)


def stream_body(base, chip, far, s, m, t, out_ref, rows_ref):
    def body(i):
        out = base(i) + (chip[i].astype(F32) + far[i].astype(F32)) * s
        out_ref[i] = out
        n, _ = norm_of(out)
        rows_ref[i] = (n * m + t).astype(BF)

    over_rows(rows_ref.shape[0], body)


def self_forward(hidden, context, cotangent, time_rows, tables, small, own_self, own_cross, own_first, n_dp, heads):
    quarter, texts = hidden.shape[0], context.shape[0]
    half, wide = 2 * quarter, heads * HEAD
    n = n_dp // 2
    r = D // n_dp
    g_cols = HEAD // n_dp
    rows = shape((quarter, D), BF)
    outs = dict(
        w_self=shape((D, 4 * wide), BF), w_cross=shape((D, 4 * wide), BF), got=rows,
        c0=shape((texts, D), BF), c1=shape((texts, D), BF), c2=shape((texts, D), BF), c3=shape((texts, D), BF),
        shifts=shape((8, D), F32), gains=shape((16, HEAD), F32),
        x0=rows, x1=rows, x2=rows, x3=rows,
        qk0=shape((half, 2 * wide), F32), qk1=shape((half, 2 * wide), F32),
        v0=shape((half, wide), BF), v1=shape((half, wide), BF),
        stat0=shape((8, half), F32), stat1=shape((8, half), F32),
        q0=shape((half, wide), BF), q1=shape((half, wide), BF),
        k0=shape((half, wide), BF), k1=shape((half, wide), BF),
        attn0=shape((half, wide), BF), attn1=shape((half, wide), BF),
        lse0=shape((8, half), F32), lse1=shape((8, half), F32),
        chip0=rows, chip1=rows, far0=rows, far1=rows,
        after0=shape((quarter, D), F32), after1=shape((quarter, D), F32),
        y0=rows, y1=rows, y2=rows, y3=rows,
        ck_raw=shape((4 * texts, wide), F32), cv=shape((4 * texts, wide), BF),
        ck_stat=shape((8, 4 * texts), F32), ck=shape((4 * texts, wide), BF),
        f0=shape((D, own_first.shape[1]), BF),
    )
    far_outs = dict(g_got=rows)
    blocks = [hidden, context, time_rows, tables[0], tables[1], small]
    far = [own_self, own_cross, own_first, cotangent]
    names = [*outs, *far_outs]

    def kernel(*refs, flush):
        hid, ctx, times, cos, sin, small_ref = refs[:6]
        own1, own2, own3, cot = refs[6:10]
        o = dict(zip(names, refs[10 : 10 + len(names)]))
        all_small, ctx_got, theirs, landed, mine, stats_in, ring, near, cross_x, near_sums, small_sems, local = refs[
            10 + len(names) :
        ]
        t, core, across, diagonal = tensor_peers()
        first = t < 2
        d = lax.axis_index("dp")
        cores, xs = Swap(near), Swap(cross_x)
        greet(n_dp)

        g1 = Gather(o["w_self"], ring.at[0], n)
        g2 = Gather(o["w_cross"], ring.at[1], n)
        g3 = Gather(o["f0"], ring.at[2], n)
        g1.start(own1, local.at[0])
        own_small = all_small.at[pl.ds(pl.multiple_of(d * r, 16), r)]
        own_small[...] = small_ref[...]
        small_copies = []
        for k in range(1, n_dp):
            copy = remote(
                own_small, own_small, small_sems.at[0, k], small_sems.at[1, k], dp=lax.rem(d + k, n_dp)
            )
            copy.start()
            small_copies.append(copy)
        hid_copy = xs.start(hid, o["got"], across)
        ctx_copy = xs.start(ctx, ctx_got, across)
        g_copy = xs.start(cot, o["g_got"], across)

        for k in range(1, n_dp):
            source = lax.rem(d - k + n_dp, n_dp)
            block = all_small.at[pl.ds(pl.multiple_of(source * r, 16), r)]
            remote(block, block, small_sems.at[0, k], small_sems.at[1, k], dp=source).wait_recv()
        turned = jnp.transpose(all_small[...].astype(F32))
        o["shifts"][:6] = turned[:6] + times[...]
        o["shifts"][6:] = turned[6:8]
        at = lax.broadcasted_iota(jnp.int32, (D, HEAD), 0)
        to = lax.broadcasted_iota(jnp.int32, (D, HEAD), 1)
        pick = (at == (to // g_cols) * r + lax.rem(to, g_cols)).astype(F32)
        o["gains"][...] = dot_nn(turned[8:24].astype(BF), pick.astype(BF))
        g1.step(0)

        hid_copy.wait_recv()
        m_row, t_row = 1.0 + o["shifts"][1:2], o["shifts"][0:1]
        slots = [o["x0"], o["x1"], o["x2"], o["x3"]]

        def base(j):
            def pick_rows(i):
                own, other = hid[i].astype(F32), o["got"][i].astype(F32)
                return jnp.where(first, own, other) if j == 0 else jnp.where(first, other, own)

            return pick_rows

        arrivals = []
        for j in range(2):

            def body(i, j=j):
                v, _ = norm_of(base(j)(i))
                slots[2 * j][i] = (v * m_row + t_row).astype(BF)

            over_rows(quarter, body)
            arrivals.append(cores.start(slots[2 * j], slots[2 * j + 1], core))
        g1.step(1)
        ctx_copy.wait_recv()
        c_slots = [o["c0"], o["c1"], o["c2"], o["c3"]]
        a, b = ctx[...].astype(F32), ctx_got[...].astype(F32)
        c_slots[0][...] = jnp.where(first, a, b).astype(BF)
        c_slots[2][...] = jnp.where(first, b, a).astype(BF)
        c_arrivals = [cores.start(c_slots[2 * j], c_slots[2 * j + 1], core) for j in range(2)]
        for s in range(2, n - 1):
            g1.step(s)
        g2.start(own2, local.at[0])
        g1.finish()
        g2.step(0)

        qk, v = [o["qk0"], o["qk1"]], [o["v0"], o["v1"]]
        stat = [o["stat0"], o["stat1"]]
        w_self, w_cross = o["w_self"], o["w_cross"]

        sums = Sums(stats_in, near_sums, (core, across, diagonal))
        shared = []
        for j in range(2):
            arrivals[j].wait_recv()
            project_body(slots[2 * j : 2 * j + 2], w_self, 0, qk[j], v[j], stat[j], 2, 1, wide)
            shared.append(sums.start(stat[j]))
            if j == 0 and n > 2:
                g2.step(1)
        flush("shifts", "gains", "got", "x0", "x1", "x2", "x3", "qk0", "qk1", "v0", "v1")
        q, k = [o["q0"], o["q1"]], [o["k0"], o["k1"]]
        gain = [[o["gains"][i * heads + h : i * heads + h + 1] for h in range(heads)] for i in range(4)]
        for s in range(2, n - 1):
            g2.step(s)
        g3.start(own3, local.at[0])
        for j in range(2):
            shared[j]()
            own = slice(j * half, (j + 1) * half)
            normalize_body(qk[j], stat[j], gain[:2], cos[own], sin[own], [q[j], k[j]], wide)

        flush("stat0", "stat1", "q0", "q1", "k0", "k1")

        attn, lse = [o["attn0"], o["attn1"]], [o["lse0"], o["lse1"]]
        sent = []
        for j in range(2):
            attend_body(q[j], k, v, None, attn[j], lse[j])
            w_out = w_self[:, 3 * wide :]
            theirs[j] = dot_nt(attn[j][quarter:], w_out).astype(BF)
            sent.append(cores.start(theirs.at[j], landed.at[j], core))
            mine[j] = dot_nt(attn[j][:quarter], w_out)
            if j == 0:
                g3.step(0)
        chip, far_refs = [o["chip0"], o["chip1"]], [o["far0"], o["far1"]]
        crossed = []
        for j in range(2):
            sent[j].wait_recv()
            join_body(mine.at[j], landed.at[j], chip[j])
            crossed.append(xs.start(chip[j], far_refs[j], across))
        flush("attn0", "attn1", "lse0", "lse1", "w_self", "chip0", "chip1")
        if n > 2:
            g3.step(1)

        g2.finish()
        for copy in c_arrivals:
            copy.wait_recv()
        project_body(c_slots, w_cross, wide, o["ck_raw"], o["cv"], o["ck_stat"], 1, 1, wide)
        halves = 2 * texts
        for j in range(2):
            part = o["ck_stat"].at[:, pl.ds(j * halves, halves)]
            sums.start(part)()
        normalize_body(o["ck_raw"], o["ck_stat"], gain[3:], None, None, [o["ck"]], wide)

        flush("w_cross", "c0", "c1", "c2", "c3", "ck_raw", "cv", "ck_stat", "ck")

        after = [o["after0"], o["after1"]]
        y_slots = [o["y0"], o["y1"], o["y2"], o["y3"]]
        shifts = o["shifts"]
        passed = []
        for j in range(2):
            crossed[j].wait_recv()
            stream_body(
                base(j), chip[j], far_refs[j], shifts[2:3], shifts[6:7], shifts[7:8], after[j], y_slots[2 * j]
            )
            passed.append(cores.start(y_slots[2 * j], y_slots[2 * j + 1], core))
            flush(f"far{j}", f"after{j}", f"y{2 * j}")
            if j == 0:
                for s in range(2, n - 1):
                    g3.step(s)
        for copy in passed:
            copy.wait_recv()
        flush("y1", "y3")
        g_copy.wait_recv()
        g3.finish()
        for g in (g1, g2, g3):
            g.drain()
        for copy in small_copies:
            copy.wait_send()
        cores.settle()
        xs.settle()

    scratch = [
        pltpu.VMEM((D, HEAD), BF),
        pltpu.VMEM((texts, D), BF),
        pltpu.VMEM((2, quarter, D), BF),
        pltpu.VMEM((2, quarter, D), BF),
        pltpu.VMEM((2, quarter, D), F32),
        pltpu.VMEM((4, 3, 8, half), F32),
        pltpu.SemaphoreType.DMA((3, 10, n)),
        pltpu.SemaphoreType.DMA((2, 8)),
        pltpu.SemaphoreType.DMA((2, 8)),
        pltpu.SemaphoreType.DMA((2, 12)),
        pltpu.SemaphoreType.DMA((2, n_dp)),
        pltpu.SemaphoreType.DMA((1,)),
    ]
    return run_remote(kernel, outs, far_outs, blocks, far, scratch, 1, 2e10)


def cross_forward(state, cotangent, bias, own_second, own_third, n_dp, heads):
    quarter = state["y0"].shape[0]
    half, wide = 2 * quarter, heads * HEAD
    n = n_dp // 2
    rows = shape((quarter, D), BF)
    outs = dict(
        cq_raw0=shape((half, wide), F32), cq_raw1=shape((half, wide), F32),
        cq_stat0=shape((8, half), F32), cq_stat1=shape((8, half), F32),
        cq0=shape((half, wide), BF), cq1=shape((half, wide), BF),
        cattn0=shape((half, wide), BF), cattn1=shape((half, wide), BF),
        clse0=shape((8, half), F32), clse1=shape((8, half), F32),
        after_c0=shape((quarter, D), F32), after_c1=shape((quarter, D), F32),
        z0=rows, z1=rows, z2=rows, z3=rows, d0=rows, d1=rows, d2=rows, d3=rows,
        dpre0=shape((2 * half, HC), BF), dpre1=shape((2 * half, HC), BF),
        act0=shape((2 * half, HC), BF), act1=shape((2 * half, HC), BF),
        f1=shape((D, own_second.shape[1]), BF), f2=shape((D, own_third.shape[1]), BF),
    )
    far_outs = {}
    given = ("w_cross", "after0", "after1", "y0", "y1", "y2", "y3", "ck", "cv", "shifts", "gains", "g_got")
    blocks = [state[name] for name in given] + [bias, cotangent]
    far = [own_second, own_third, state["f0"]]
    names = [*outs, *far_outs]

    def kernel(*refs, flush):
        i = dict(zip(given, refs))
        bias_ref, cot, own1, own2, f0 = refs[len(given) : len(given) + 5]
        refs = refs[len(given) + 5 :]
        o = dict(zip(names, refs))
        theirs, landed, mine, chips, fars, stats_in, w_down, ring, near, cross_x, near_sums, local = refs[len(names) :]
        t, core, across, diagonal = tensor_peers()
        cores, xs = Swap(near), Swap(cross_x)
        sums = Sums(stats_in, near_sums, (core, across, diagonal))
        greet(n_dp)
        g1 = Gather(o["f1"], ring.at[0], n)
        g2 = Gather(o["f2"], ring.at[1], n)
        g1.start(own1, local.at[0])
        first_down = pltpu.make_async_copy(f0.at[:, pl.ds(HC, HC)], w_down, local.at[1])
        first_down.start()
        d_slots = [o["d0"], o["d1"], o["d2"], o["d3"]]
        s_five = i["shifts"][5:6]
        first = t < 2
        sent_d = []

        def act_grad(part):
            down = o["f1"][:, HC:] if part else w_down[...]
            for p, slot in enumerate(d_slots):
                o[f"dpre{part}"][p * quarter : (p + 1) * quarter] = dot_nn(slot[...], down).astype(BF)

        def activate(part, h):
            up = o["f1"][:, :HC] if part else w_down[...]
            act_ref, dpre_ref = o[f"act{part}"], o[f"dpre{part}"]
            for p in (2 * h, 2 * h + 1):
                own = slice(p * quarter, (p + 1) * quarter)
                u = dot_nn(z_slots[p][...], up)
                act_ref[own], slope = gelu_of(u)
                dpre_ref[own] = (dpre_ref[own].astype(F32) * slope).astype(BF)

        w = i["w_cross"]
        slots = [i["y0"], i["y1"], i["y2"], i["y3"]]
        raw, stat = [o["cq_raw0"], o["cq_raw1"]], [o["cq_stat0"], o["cq_stat1"]]
        q = [o["cq0"], o["cq1"]]
        attn, lse = [o["cattn0"], o["cattn1"]], [o["clse0"], o["clse1"]]
        gain = [i["gains"][2 * heads + h : 2 * heads + h + 1] for h in range(heads)]
        shared = []
        for j in range(2):
            project_body(slots[2 * j : 2 * j + 2], w, 0, raw[j], None, stat[j], 1, 0, wide)
            shared.append(sums.start(stat[j]))

            def scaled(rows, j=j):
                own, other = cot[rows].astype(F32), i["g_got"][rows].astype(F32)
                g = jnp.where(first, own, other) if j == 0 else jnp.where(first, other, own)
                d_slots[2 * j][rows] = (g * s_five).astype(BF)

            over_rows(quarter, scaled)
            sent_d.append(cores.start(d_slots[2 * j], d_slots[2 * j + 1], core))
        sent = []
        for j in range(2):
            shared[j]()
            normalize_body(raw[j], stat[j], [gain], None, None, [q[j]], wide)
            attend_body(q[j], [i["ck"]], [i["cv"]], bias_ref, attn[j], lse[j])
            w_out = w[:, 3 * wide :]
            theirs[j] = dot_nt(attn[j][quarter:], w_out).astype(BF)
            sent.append(cores.start(theirs.at[j], landed.at[j], core))
            mine[j] = dot_nt(attn[j][:quarter], w_out)
            if j == 0:
                g1.step(0)
        crossed = []
        for j in range(2):
            sent[j].wait_recv()
            join_body(mine.at[j], landed.at[j], chips.at[j])
            crossed.append(xs.start(chips.at[j], fars.at[j], across))
        for s in range(1, n - 2):
            g1.step(s)
        for copy in sent_d:
            copy.wait_recv()
        flush("cq_raw0", "cq_raw1", "cq_stat0", "cq_stat1", "cq0", "cq1", "cattn0", "cattn1", "clse0", "clse1")
        first_down.wait()
        act_grad(0)
        first_up = pltpu.make_async_copy(f0.at[:, pl.ds(0, HC)], w_down, local.at[2])
        first_up.start()
        flush("d0", "d1", "d2", "d3")
        g1.step(n - 2)
        g2.start(own2, local.at[0])
        base = [i["after0"], i["after1"]]
        after = [o["after_c0"], o["after_c1"]]
        z_slots = [o["z0"], o["z1"], o["z2"], o["z3"]]
        m_row, t_row = 1.0 + i["shifts"][4:5], i["shifts"][3:4]
        passed = []
        for j in range(2):
            crossed[j].wait_recv()
            stream_body(
                lambda rows, j=j: base[j][rows], chips.at[j], fars.at[j], 1.0, m_row, t_row, after[j], z_slots[2 * j]
            )
            passed.append(cores.start(z_slots[2 * j], z_slots[2 * j + 1], core))
            flush(f"after_c{j}", f"z{2 * j}")
            if j == 0:
                g2.step(0)
        g1.finish()
        act_grad(1)
        flush("f1")
        if n > 2:
            g2.step(1)
        first_up.wait()
        for j in range(2):
            passed[j].wait_recv()
            activate(0, j)
        flush("z1", "z3", "act0", "dpre0")
        activate(1, 0)
        for s in range(2, n - 1):
            g2.step(s)
        activate(1, 1)
        flush("act1", "dpre1")
        g2.finish()
        for g in (g1, g2):
            g.drain()
        cores.settle()
        xs.settle()

    scratch = [
        pltpu.VMEM((2, quarter, D), BF),
        pltpu.VMEM((2, quarter, D), BF),
        pltpu.VMEM((2, quarter, D), F32),
        pltpu.VMEM((2, quarter, D), BF),
        pltpu.VMEM((2, quarter, D), BF),
        pltpu.VMEM((2, 3, 8, half), F32),
        pltpu.VMEM((D, HC), BF),
        pltpu.SemaphoreType.DMA((2, 10, n)),
        pltpu.SemaphoreType.DMA((2, 8)),
        pltpu.SemaphoreType.DMA((2, 8)),
        pltpu.SemaphoreType.DMA((2, 6)),
        pltpu.SemaphoreType.DMA((3,)),
    ]
    return run_remote(kernel, outs, far_outs, blocks, far, scratch, 2, 1e10)


def gelu_of(u):
    sq = u * u
    th = jnp.tanh(u * (GELU + GELU * CUBE * sq))
    near = 0.5 + 0.5 * th
    slope = near + u * near * (1.0 - th) * (GELU + 3 * GELU * CUBE * sq)
    return (u * near).astype(BF), slope


def back_body(g, v, chip, far, m, s, out_ref, rows_ref, sum_ref):
    sum_ref[...] = jnp.zeros_like(sum_ref)

    def body(i):
        da = chip[i].astype(F32) + far[i].astype(F32)
        n, r = norm_of(v[i].astype(F32))
        dn = da * m
        mean = jnp.mean(dn, axis=-1, keepdims=True)
        along = jnp.mean(dn * n, axis=-1, keepdims=True)
        out = g(i) + r * (dn - mean - n * along)
        out_ref[i] = out
        rows_ref[i] = (out * s).astype(BF)
        dan = da * n
        for k in range(STEP // 8):
            sum_ref[:8] += da[k * 8 : k * 8 + 8]
            sum_ref[8:] += dan[k * 8 : k * 8 + 8]

    over_rows(v.shape[0], body)


def feed_forward(state, cotangent, n_dp):
    quarter = state["z0"].shape[0]
    half = 2 * quarter
    rows = shape((quarter, D), BF)
    whole = shape((quarter, D), F32)
    outs = dict(
        gc0=whole, gc1=whole, e0=rows, e1=rows, e2=rows, e3=rows,
        sf0=shape((16, D), F32), sf1=shape((16, D), F32), branch=whole,
    )
    far_outs = {f"t{j}": shape((D, 2 * HC), BF) for j in range(3)}
    given = ("z0", "z1", "z2", "z3", "d0", "d1", "d2", "d3", "after_c0", "after_c1", "shifts", "g_got")
    blocks = [state[name] for name in given] + [cotangent]
    far = [state[name] for name in ("f0", "f1", "f2", "dpre0", "dpre1", "act0", "act1")]
    names = [*outs, *far_outs]

    def kernel(*refs, flush):
        i = dict(zip(given, refs))
        cot, f, early, refs = refs[len(given)], refs[len(given) + 1 :][:3], refs[len(given) + 4 :][:4], refs[len(given) + 8 :]
        o = dict(zip(names, refs))
        (
            w, act, dpre, theirs, landed, mine, chips, fars, turned, near, cross_x, local,
        ) = refs[len(names) :]
        t, core, across, diagonal = tensor_peers()
        first = t < 2
        cores, xs = Swap(near), Swap(cross_x)
        loads = [pltpu.make_async_copy(f[j], w.at[j], local.at[j]) for j in range(3)]
        places = (dpre.at[0], dpre.at[1], act.at[0], act.at[1])
        loads += [pltpu.make_async_copy(early[j], places[j], local.at[3 + j]) for j in range(4)]
        loads[2].start()
        greet(n_dp)
        z = [i["z0"], i["z1"], i["z2"], i["z3"]]
        ds = [i["d0"], i["d1"], i["d2"], i["d3"]]
        loads[2].wait()
        for copy in (*loads[:2], *loads[3:]):
            copy.start()
        for p in range(4):
            dpre[2, p * quarter : (p + 1) * quarter] = dot_nn(ds[p][...], w[2, :, HC:]).astype(BF)

        def pre_part(h, j):
            for p in (2 * h, 2 * h + 1):
                own = slice(p * quarter, (p + 1) * quarter)
                u = dot_nn(z[p][...], w[j, :, :HC])
                act[j, own], slope = gelu_of(u)
                dpre[j, own] = (dpre[j, own].astype(F32) * slope).astype(BF)

        def contracted(a, p, side):
            own = slice(p * quarter, (p + 1) * quarter)
            total = None
            for j in range(3):
                term = dot_nt(a[j, own], w[j, :, side * HC : (side + 1) * HC])
                total = term if total is None else total + term
            return total

        def back_half(h):
            theirs[h] = contracted(dpre, 2 * h + 1, 0).astype(BF)
            copy = cores.start(theirs.at[h], landed.at[h], core)
            mine[h] = contracted(dpre, 2 * h, 0)
            return copy

        def forward_half(h):
            theirs[2 + h] = contracted(act, 2 * h + 1, 1).astype(BF)
            copy = cores.start(theirs.at[2 + h], landed.at[2 + h], core)
            mine[h] = contracted(act, 2 * h, 1)
            return copy

        def join(k, copy):
            copy.wait_recv()
            join_body(mine.at[k % 2], landed.at[k], chips.at[k])

        pre_part(0, 2)
        for copy in (*loads[:2], *loads[3:]):
            copy.wait()
        sent = back_half(0)
        pre_part(1, 2)
        join(0, sent)
        crossed = [xs.start(chips.at[0], fars.at[0], across)]
        sent = back_half(1)
        sent_f = forward_half(0)
        join(1, sent)
        crossed.append(xs.start(chips.at[1], fars.at[1], across))
        join(2, sent_f)
        sent_f = forward_half(1)
        join(3, sent_f)
        own_half = jnp.where(first, 0, 1)
        last = xs.start(chips.at[3 - own_half], fars.at[2], across)

        def turn_rows(slots):
            for p in range(4):
                turned[:, p * quarter : (p + 1) * quarter] = jnp.transpose(slots[p][...])

        def weight_grad(j, side, right):
            for k in range(0, D, 512):
                w[j, k : k + 512, side * HC : (side + 1) * HC] = dot_nn(turned[k : k + 512], right[j]).astype(BF)

        def g_of(h):
            def rows_of(r):
                own, other = cot[r].astype(F32), i["g_got"][r].astype(F32)
                return jnp.where(first, own, other) if h == 0 else jnp.where(first, other, own)

            return rows_of

        e = [o["e0"], o["e1"], o["e2"], o["e3"]]
        passed = []

        def norm_half(h):
            crossed[h].wait_recv()
            back_body(
                g_of(h), i[f"after_c{h}"], chips.at[h], fars.at[h], 1.0 + i["shifts"][4:5], 1.0,
                o[f"gc{h}"], e[2 * h], o[f"sf{h}"],
            )
            passed.append(cores.start(e[2 * h], e[2 * h + 1], core))
            flush(f"gc{h}", f"sf{h}", f"e{2 * h}")

        turn_rows(z)
        weight_grad(0, 0, dpre)
        norm_half(0)
        weight_grad(1, 0, dpre)
        weight_grad(2, 0, dpre)
        turn_rows(ds)
        stores = []
        for j in range(3):
            weight_grad(j, 1, act)
            store = pltpu.make_async_copy(w.at[j], o[f"t{j}"], local.at[j])
            store.start()
            stores.append(store)
            if j == 0:
                norm_half(1)
        last.wait_recv()
        o["branch"][...] = chips[2 + own_half].astype(F32) + fars[2].astype(F32)
        for copy in passed:
            copy.wait_recv()
        for store in stores:
            store.wait()
        cores.settle()
        xs.settle()

    scratch = [
        pltpu.VMEM((3, D, 2 * HC), BF),
        pltpu.VMEM((3, 2 * half, HC), BF),
        pltpu.VMEM((3, 2 * half, HC), BF),
        pltpu.VMEM((4, quarter, D), BF),
        pltpu.VMEM((4, quarter, D), BF),
        pltpu.VMEM((2, quarter, D), F32),
        pltpu.VMEM((4, quarter, D), BF),
        pltpu.VMEM((3, quarter, D), BF),
        pltpu.VMEM((D, 2 * half), BF),
        pltpu.SemaphoreType.DMA((2, 8)),
        pltpu.SemaphoreType.DMA((2, 4)),
        pltpu.SemaphoreType.DMA((7,)),
    ]
    return run_remote(kernel, outs, far_outs, blocks, far, scratch, 3, 6e10)


class Scatter:
    def __init__(self, got, arrived, over, along, n):
        d = lax.axis_index("dp")
        self.z, self.y = d // 2, lax.rem(d, 2)
        self.got, self.arrived, self.sems_y, self.sems_z, self.n = got, arrived, over, along, n
        self.r = D // (2 * n)

    def block(self, full, o, own):
        start = (2 * o + (self.y if own else 1 - self.y)) * self.r
        return full.at[pl.ds(pl.multiple_of(start, 16), self.r)]

    def begin(self, full):
        self.full = full
        self.sent = []
        for o in range(self.n):
            copy = remote(
                self.block(full, o, False), self.got.at[o], self.sems_y.at[0, o], self.sems_y.at[1, o],
                dp=2 * self.z + 1 - self.y,
            )
            copy.start()
            self.sent.append(copy)

    def pair(self, a, b, local):
        loads = []
        for o in range(self.n):
            copy = pltpu.make_async_copy(self.block(self.full, o, True), a.at[o], local.at[0, o])
            copy.start()
            loads.append(copy)
        for o in range(self.n):
            self.sent[o].wait()
            copy = pltpu.make_async_copy(self.got.at[o], b.at[o], local.at[1, o])
            copy.start()
            loads.append(copy)
        for o in range(self.n):
            loads[o].wait()
            loads[self.n + o].wait()
            a[o] = (a[o].astype(F32) + b[o].astype(F32)).astype(BF)

    def spread(self, a, relay=None):
        self.a, self.relay = a, relay if self.n == 4 else None
        if self.relay is None:
            self.out = []
            for k in range(1, self.n):
                at = lax.rem(self.z + k, self.n)
                copy = self.send(at, at, self.arrived.at[k - 1], k, k)
                copy.start()
                self.out.append(copy)
            return
        z = self.z
        self.end = (z == 0) | (z == 3)
        self.inner = jnp.where(z < 2, 1, 2)
        self.edge = jnp.where(z < 2, 0, 3)

        @pl.when(self.end)
        def _():
            self.send(3 - z, self.inner, relay.at[0], 1, 1).start()
            self.send(3 - self.inner, self.inner, relay.at[1], 2, 2).start()
            self.send(self.inner, self.inner, self.arrived.at[0], 0, 0).start()

        @pl.when(jnp.logical_not(self.end))
        def _():
            self.send(self.edge, self.edge, self.arrived.at[0], 0, 0).start()

    def send(self, block, to, place, k, j):
        return remote(
            self.a.at[block], place, self.sems_z.at[0, k], self.sems_z.at[1, j], dp=2 * to + self.y
        )

    def forward(self, b, local):
        if self.relay is None:
            return

        @pl.when(jnp.logical_not(self.end))
        def _():
            loads = []
            for k in range(2):
                self.send(self.edge, self.edge, self.relay.at[k], 1 + k, 1 + k).wait_recv()
                copy = pltpu.make_async_copy(self.relay.at[k], b.at[k], local.at[0, k])
                copy.start()
                loads.append(copy)
            for k, to in enumerate((3 - self.edge, 3 - self.inner)):
                loads[k].wait()
                self.a[to] = (self.a[to].astype(F32) + b[k].astype(F32)).astype(BF)
                self.send(to, to, self.arrived.at[1], 1 + k, 3).start()

    def total(self, a, stage, result, sem, b, local):
        count = self.n - 1
        if self.relay is None:
            for copy in self.out:
                copy.wait()
        else:
            count = 2
            for slot, j in ((0, 0), (1, 3)):
                self.send(self.edge, self.edge, self.arrived.at[slot], j, j).wait_recv()
            for k in range(3):
                self.send(self.edge, self.edge, self.arrived.at[0], k, k).wait_send()
        arrived = self.arrived
        if self.n != 4:
            loads = [pltpu.make_async_copy(arrived.at[k], b.at[k], local.at[0, k]) for k in range(count)]
            for copy in loads:
                copy.start()
            wait(loads)
            arrived = b
        total = a[self.z].astype(F32)
        for k in range(count):
            total = total + arrived[k].astype(F32)
        stage[...] = total
        copy = pltpu.make_async_copy(stage, result, sem)
        copy.start()
        copy.wait()


def attend_back_body(do_ref, q_ref, k_refs, v_refs, lse_ref, bias_ref, dq_ref, dk_ref, dv_ref, fresh):
    rows, wide = q_ref.shape
    for h in range(wide // HEAD):
        lanes = slice(h * HEAD, (h + 1) * HEAD)
        k = jnp.concatenate([r[:, lanes] for r in k_refs]) if len(k_refs) > 1 else k_refs[0][:, lanes]
        v = jnp.concatenate([r[:, lanes] for r in v_refs]) if len(v_refs) > 1 else v_refs[0][:, lanes]
        for b in range(rows // QB):
            block = slice(b * QB, (b + 1) * QB)
            qb = q_ref[block, lanes]
            do = do_ref[block, lanes]
            s = dot_nt(k, qb) * FACTOR
            if bias_ref is not None:
                s = s + bias_ref[...]
            p = jnp.exp(s - lse_ref[h : h + 1, block])
            dp = dot_nt(v, do)
            center = jnp.sum(p * dp, axis=0, keepdims=True)
            ds = (p * (dp - center)).astype(BF)
            dq_ref[block, lanes] = dot_tn(ds, k) * FACTOR
            dk = dot_nn(ds, qb) * FACTOR
            dv = dot_nn(p.astype(BF), do)
            if b == 0 and fresh:
                dk_ref[:, lanes] = dk
                dv_ref[:, lanes] = dv
            else:
                dk_ref[:, lanes] += dk
                dv_ref[:, lanes] += dv


def dots_body(dy_ref, raw_ref, col, stat_ref, row, gain, tables, grad_ref, grad_row, wide):
    scale = lax.rsqrt(to_columns(stat_ref[...]) / D + EPS)[:, row : row + 1]
    dots = jnp.zeros((dy_ref.shape[0], 1), F32)
    for h in range(wide // HEAD):
        own = slice(h * HEAD, (h + 1) * HEAD)
        dy = dy_ref[:, own]
        if tables is not None:
            dy = turn(dy, tables[0], -tables[1])
            dy_ref[:, own] = dy
        both = raw_ref[:, col + h * HEAD : col + (h + 1) * HEAD] * dy
        dots = dots + jnp.sum(both * gain[h], axis=1, keepdims=True)
        grad_ref[grad_row : grad_row + 1, own] += jnp.sum(both * scale, axis=0, keepdims=True)
    return dots


def root_back_body(dy_ref, raw_ref, col, stat_ref, row, dots_ref, dots_row, gain, low_ref, at, wide):
    scale = lax.rsqrt(to_columns(stat_ref[...]) / D + EPS)[:, row : row + 1]
    along = scale * scale * scale * to_columns(dots_ref[...])[:, dots_row : dots_row + 1] / D
    for h in range(wide // HEAD):
        own = slice(h * HEAD, (h + 1) * HEAD)
        raw = raw_ref[:, col + h * HEAD : col + (h + 1) * HEAD]
        dx = scale * gain[h] * dy_ref[:, own] - raw * along
        low_ref[:, at + h * HEAD : at + (h + 1) * HEAD] = dx.astype(BF)


class Grads:
    def __init__(self, turned, stage, sems):
        self.turned, self.stage, self.sems = turned, stage, sems
        self.stores = [None, None]
        self.used = 0

    def turn(self, slots):
        at = 0
        for slot in slots:
            m = slot.shape[0]
            self.turned[:, at : at + m] = jnp.transpose(slot[...])
            at += m

    def put(self, ys, full, col):
        i = self.used % 2
        self.used += 1
        if self.stores[i] is not None:
            self.stores[i].wait()
        for k in range(0, D, 512):
            total, at = None, 0
            for y in ys:
                m = y.shape[0]
                term = dot_nn(self.turned[k : k + 512, at : at + m], y)
                total = term if total is None else total + term
                at += m
            self.stage[i, k : k + 512] = total.astype(BF)
        store = pltpu.make_async_copy(self.stage.at[i], full.at[:, pl.ds(col, GC)], self.sems.at[i])
        store.start()
        self.stores[i] = store

    def finish(self):
        for i in range(2):
            if self.stores[i] is not None:
                self.stores[i].wait()
                self.stores[i] = None


def cross_backward(state, bias, n_dp, heads):
    quarter, texts = state["e0"].shape[0], state["c0"].shape[0]
    half, wide = 2 * quarter, heads * HEAD
    n, r = n_dp // 2, D // n_dp
    W = state["t0"].shape[1]
    rows = shape((quarter, D), BF)
    whole = shape((quarter, D), F32)
    sums_shape = shape((16, D), F32)
    outs = dict(
        gs0=whole, gs1=whole, h0=rows, h1=rows, h2=rows, h3=rows, sc0=sums_shape, sc1=sums_shape,
        cross_gain=shape((8, wide), F32), ctx_grad=shape((texts, D), BF),
    )
    far_outs = dict(
        tc=shape((D, 4 * wide), BF), p1=shape((n, r, W), BF), s0=shape((r, W), F32), relay0=shape((2, r, W), BF),
        got0=shape((n, r, W), BF), got1=shape((n, r, W), BF),
    )
    if n != 4:
        far_outs["arrived"] = shape((n - 1, r, W), BF)
    given = (
        "e0", "e1", "e2", "e3", "cq0", "cq1", "ck", "cv", "clse0", "clse1", "cq_raw0", "cq_raw1", "ck_raw",
        "cq_stat0", "cq_stat1", "ck_stat", "gains", "shifts", "gc0", "gc1", "after0", "after1", "w_cross",
        "cattn0", "cattn1", "y0", "y1", "y2", "y3", "c0", "c1", "c2", "c3",
    )
    blocks = [state[name] for name in given] + [bias]
    far = [state["t0"], state["t1"]]
    names = [*outs, *far_outs]

    def kernel(*refs, flush):
        i = dict(zip(given, refs))
        bias_ref, t0, t1 = refs[len(given) : len(given) + 3]
        refs = refs[len(given) + 3 :]
        o = dict(zip(names, refs))
        (
            do, dq, dk, dv, low, dckv, theirs, landed, mine, chips, fars, c_theirs, c_landed, c_chips, c_far,
            dots, ck_dots, stats_in, turned, stage, a, b, arrived, result,
            near, cross_x, near_sums, over, along, local, stores,
        ) = refs[len(names) :]
        t, core, across, diagonal = tensor_peers()
        first = t < 2
        cores, xs = Swap(near), Swap(cross_x)
        sums = Sums(stats_in, near_sums, (core, across, diagonal))
        greet(n_dp)
        arrived = o.get("arrived", arrived)
        f0 = Scatter(o["got0"], arrived, over.at[0], along.at[0], n)
        f1 = Scatter(o["got1"], arrived, over.at[1], along.at[0], n)
        f0.begin(t0)
        w = i["w_cross"]
        e = [i["e0"], i["e1"], i["e2"], i["e3"]]
        gain_q = [i["gains"][2 * heads + h : 2 * heads + h + 1] for h in range(heads)]
        gain_k = [i["gains"][3 * heads + h : 3 * heads + h + 1] for h in range(heads)]
        o["cross_gain"][...] = jnp.zeros_like(o["cross_gain"])

        def back(h):
            for p in range(2):
                do[p * quarter : (p + 1) * quarter] = dot_nn(e[2 * h + p][...], w[:, 3 * wide :]).astype(BF)
            attend_back_body(
                do, i[f"cq{h}"], [i["ck"]], [i["cv"]], i[f"clse{h}"], bias_ref, dq, dk, dv, h == 0
            )
            column = dots_body(
                dq, i[f"cq_raw{h}"], 0, i[f"cq_stat{h}"], 0, gain_q, None, o["cross_gain"], 0, wide
            )
            dots[h] = to_rows([column], half)
            return sums.start(dots.at[h])

        def send(h):
            root_back_body(
                dq, i[f"cq_raw{h}"], 0, i[f"cq_stat{h}"], 0, dots.at[h], 0, gain_q, low.at[h], 0, wide
            )
            theirs[h] = dot_nt(low[h, quarter:], w[:, :wide]).astype(BF)
            copy = cores.start(theirs.at[h], landed.at[h], core)
            mine[...] = dot_nt(low[h, :quarter], w[:, :wide])
            return copy

        def join(h, copy):
            copy.wait_recv()
            join_body(mine, landed.at[h], chips.at[h])
            return xs.start(chips.at[h], fars.at[h], across)

        collect = back(0)
        collect()
        sent0 = send(0)
        collect = back(1)
        crossed = [join(0, sent0)]
        column = dots_body(dk, i["ck_raw"], 0, i["ck_stat"], 0, gain_k, None, o["cross_gain"], 1, wide)
        ck_dots[...] = to_rows([column], 4 * texts)
        collect_k = [sums.start(ck_dots.at[:, pl.ds(j * 2 * texts, 2 * texts)]) for j in range(2)]
        collect()
        sent1 = send(1)
        crossed.append(join(1, sent1))
        f1.begin(t1)
        for part in collect_k:
            part()
        f0.pair(a, b, local)
        f0.spread(a, o["relay0"])

        root_back_body(dk, i["ck_raw"], 0, i["ck_stat"], 0, ck_dots, 0, gain_k, dckv, 0, wide)
        dckv[:, wide:] = dv[...].astype(BF)
        c_sent = []
        for j in range(2):
            at = 2 * texts * j
            c_theirs[j] = dot_nt(dckv[at + texts : at + 2 * texts], w[:, wide : 3 * wide]).astype(BF)
            c_sent.append(cores.start(c_theirs.at[j], c_landed.at[j], core))
        for j in range(2):
            at = 2 * texts * j
            part = dot_nt(dckv[at : at + texts], w[:, wide : 3 * wide])
            c_sent[j].wait_recv()
            c_chips[j] = (part + c_landed[j].astype(F32)).astype(BF)
        own_half = jnp.where(first, 0, 1)
        c_last = xs.start(c_chips.at[1 - own_half], c_far, across)

        h_slots = [o["h0"], o["h1"], o["h2"], o["h3"]]
        passed = []

        def norm_half(h):
            crossed[h].wait_recv()
            back_body(
                lambda rows: i[f"gc{h}"][rows], i[f"after{h}"], chips.at[h], fars.at[h], i["shifts"][6:7],
                i["shifts"][2:3], o[f"gs{h}"], h_slots[2 * h], o[f"sc{h}"],
            )
            passed.append(cores.start(h_slots[2 * h], h_slots[2 * h + 1], core))
            flush(f"gs{h}", f"sc{h}", f"h{2 * h}")

        norm_half(0)
        grads = Grads(turned, stage, stores)
        grads.turn([i["y0"], i["y1"], i["y2"], i["y3"]])
        grads.put([low[0], low[1]], o["tc"], 0)
        norm_half(1)
        f0.forward(b, local)
        grads.turn([i["c0"], i["c1"], i["c2"], i["c3"]])
        for c in range(2):
            grads.put([dckv[:, c * wide : (c + 1) * wide]], o["tc"], (1 + c) * wide)
        grads.turn(e)
        grads.put([i["cattn0"][...], i["cattn1"][...]], o["tc"], 3 * wide)
        c_last.wait_recv()
        o["ctx_grad"][...] = (c_chips[own_half].astype(F32) + c_far[...].astype(F32)).astype(BF)
        grads.finish()
        f0.total(a, result, o["s0"], stores.at[0], b, local)
        f1.pair(a, b, local)
        copy = pltpu.make_async_copy(a, o["p1"], stores.at[0])
        copy.start()
        copy.wait()
        for copy in passed:
            copy.wait_recv()
        cores.settle()
        xs.settle()

    scratch = [
        pltpu.VMEM((half, wide), BF),
        pltpu.VMEM((half, wide), F32),
        pltpu.VMEM((4 * texts, wide), F32),
        pltpu.VMEM((4 * texts, wide), F32),
        pltpu.VMEM((2, half, wide), BF),
        pltpu.VMEM((4 * texts, 2 * wide), BF),
        pltpu.VMEM((2, quarter, D), BF),
        pltpu.VMEM((2, quarter, D), BF),
        pltpu.VMEM((quarter, D), F32),
        pltpu.VMEM((2, quarter, D), BF),
        pltpu.VMEM((2, quarter, D), BF),
        pltpu.VMEM((2, texts, D), BF),
        pltpu.VMEM((2, texts, D), BF),
        pltpu.VMEM((2, texts, D), BF),
        pltpu.VMEM((texts, D), BF),
        pltpu.VMEM((2, 8, half), F32),
        pltpu.VMEM((8, 4 * texts), F32),
        pltpu.VMEM((4, 3, 8, half), F32),
        pltpu.VMEM((D, 2 * half), BF),
        pltpu.VMEM((2, D, GC), BF),
        pltpu.VMEM((n, r, W), BF),
        pltpu.VMEM((n, r, W), BF),
        pltpu.VMEM((n - 1, r, W) if n == 4 else (8, HEAD), BF),
        pltpu.VMEM((r, W), F32),
        pltpu.SemaphoreType.DMA((2, 8)),
        pltpu.SemaphoreType.DMA((2, 4)),
        pltpu.SemaphoreType.DMA((2, 12)),
        pltpu.SemaphoreType.DMA((2, 2, n)),
        pltpu.SemaphoreType.DMA((1, 2, n)),
        pltpu.SemaphoreType.DMA((2, n)),
        pltpu.SemaphoreType.DMA((2,)),
    ]
    return run_remote(kernel, outs, far_outs, blocks, far, scratch, 4, 4e10)


def self_backward(state, hidden, tables, sums_two, sums_five, n_dp, heads):
    quarter = hidden.shape[0]
    half, wide = 2 * quarter, heads * HEAD
    n, r = n_dp // 2, D // n_dp
    W, V = state["t2"].shape[1], 2 * wide
    g_cols = HEAD // n_dp
    outs = dict(
        hidden_grad=shape((quarter, D), BF), ss=shape((16, D), F32), self_gain=shape((8, wide), F32),
        time=shape((8, D), F32), tiny=shape((r, HEAD), F32),
    )
    far_outs = dict(
        s1=shape((r, W), F32), s2=shape((r, W), F32), s3=shape((r, W), F32), s4=shape((r, V), F32), s5=shape((r, V), F32),
        tv=shape((D, V), BF), tq=shape((D, V), BF),
        relay1=shape((2, r, W), BF), relay2=shape((2, r, W), BF), relay3=shape((2, r, W), BF), relay4=shape((2, r, V), BF),
        got2=shape((n, r, W), BF), got3=shape((n, r, W), BF), got4=shape((n, r, V), BF), got5=shape((n, r, V), BF),
    )
    if n != 4:
        far_outs["arrived"] = shape((3, n - 1, r, W), BF)
        far_outs["arrived_v"] = shape((2, n - 1, r, V), BF)
    given = (
        "h0", "h1", "h2", "h3", "q0", "q1", "k0", "k1", "v0", "v1", "lse0", "lse1", "qk0", "qk1", "stat0", "stat1",
        "gains", "shifts", "gs0", "gs1", "attn0", "attn1", "w_self", "sf0", "sf1", "sc0", "sc1", "cross_gain",
    )
    blocks = [state[name] for name in given] + [hidden, *tables, sums_two, sums_five]
    far = [state["p1"], state["t2"], state["tc"], *(state[f"x{p}"] for p in range(4))]
    names = [*outs, *far_outs]

    def kernel(*refs, flush):
        i = dict(zip(given, refs))
        hid, cos, sin, two, five, p1, t2, tc = refs[len(given) : len(given) + 8]
        xs_far = refs[len(given) + 8 : len(given) + 12]
        refs = refs[len(given) + 12 :]
        o = dict(zip(names, refs))
        (
            do, dq, dk, dv, low, theirs, landed, mine, chips, far_chip,
            dots, stats_in, turned, stage, a, b, arrived, arrived_v, result, four_sums, side, side_in,
            near, cross_x, near_sums, over, along, local, stores, slots, side_sems,
        ) = refs[len(names) :]
        t, core, across, diagonal = tensor_peers()
        first = t < 2
        cores, xs = Swap(near), Swap(cross_x)
        sums = Sums(stats_in, near_sums, (core, across, diagonal))
        held = pltpu.make_async_copy(p1, a.at[0], stores.at[0])
        held.start()
        x_copies = [pltpu.make_async_copy(xs_far[p], theirs.at[p % 2], slots.at[p]) for p in range(4)]
        for p in range(2):
            x_copies[p].start()
        greet(n_dp)
        arrived, arrived_v = o.get("arrived", arrived), o.get("arrived_v", arrived_v)
        f1 = Scatter(None, arrived.at[0], None, along.at[0], n)
        f2 = Scatter(o["got2"], arrived.at[1], over.at[0], along.at[1], n)
        fc = Scatter(o["got3"], arrived.at[2], over.at[1], along.at[2], n)
        fv = Scatter(o["got4"], arrived_v.at[0], over.at[2], along.at[3], n)
        fq = Scatter(o["got5"], arrived_v.at[1], over.at[3], along.at[4], n)
        f2.begin(t2)
        held.wait()
        f1.spread(a.at[0], o["relay1"])
        w = i["w_self"]
        hs = [i["h0"], i["h1"], i["h2"], i["h3"]]
        ks, vs = [i["k0"], i["k1"]], [i["v0"], i["v1"]]
        gain = [[i["gains"][g * heads + h : g * heads + h + 1] for h in range(heads)] for g in range(2)]
        o["self_gain"][...] = jnp.zeros_like(o["self_gain"])
        for h in range(2):
            for p in range(2):
                do[p * quarter : (p + 1) * quarter] = dot_nn(hs[2 * h + p][...], w[:, 3 * wide :]).astype(BF)
            attend_back_body(do, i[f"q{h}"], ks, vs, i[f"lse{h}"], None, dq.at[h], dk, dv, h == 0)
        collects = []
        for h in range(2):
            own = slice(h * half, (h + 1) * half)
            turns = (cos[own], sin[own])
            dk_half = dk.at[pl.ds(h * half, half)]
            columns = [
                dots_body(dq.at[h], i[f"qk{h}"], 0, i[f"stat{h}"], 0, gain[0], turns, o["self_gain"], 0, wide),
                dots_body(dk_half, i[f"qk{h}"], wide, i[f"stat{h}"], 1, gain[1], turns, o["self_gain"], 1, wide),
            ]
            dots[h] = to_rows(columns, half)
            collects.append(sums.start(dots.at[h]))
            low[h, :, 2 * wide :] = dv[own].astype(BF)

        grads = Grads(turned, stage, stores)
        for p in range(4):
            x_copies[p].wait()
            turned[:, p * quarter : (p + 1) * quarter] = jnp.transpose(theirs[p % 2])
            if p < 2:
                x_copies[p + 2].start()
        grads.put([low[0, :, 2 * wide :], low[1, :, 2 * wide :]], o["tv"], 0)
        fc.begin(tc)
        f1.forward(b, local)
        f2.pair(a.at[1], b, local)
        f2.spread(a.at[1], o["relay2"])
        sent = []

        def join(h):
            sent[h].wait_recv()
            join_body(mine, landed.at[h], chips.at[h])

        for h in range(2):
            collects[h]()
            dk_half = dk.at[pl.ds(h * half, half)]
            root_back_body(dq.at[h], i[f"qk{h}"], 0, i[f"stat{h}"], 0, dots.at[h], 0, gain[0], low.at[h], 0, wide)
            root_back_body(
                dk_half, i[f"qk{h}"], wide, i[f"stat{h}"], 1, dots.at[h], 1, gain[1], low.at[h], wide, wide
            )
            theirs[h] = dot_nt(low[h, quarter:], w[:, : 3 * wide]).astype(BF)
            sent.append(cores.start(theirs.at[h], landed.at[h], core))
            if h == 1:
                join(0)
            mine[...] = dot_nt(low[h, :quarter], w[:, : 3 * wide])
        join(1)
        own_half = jnp.where(first, 0, 1)
        last = xs.start(chips.at[1 - own_half], far_chip, across)
        for c in range(2):
            lanes = slice(c * wide, (c + 1) * wide)
            grads.put([low[0, :, lanes], low[1, :, lanes]], o["tq"], c * wide)
        grads.turn(hs)
        grads.put([i["attn0"][...], i["attn1"][...]], o["tv"], wide)
        grads.finish()
        f1.total(a.at[0], result, o["s1"], stores.at[0], b, local)
        fv.begin(o["tv"])

        last.wait_recv()
        m_row = 1.0 + i["shifts"][1:2]
        sum_ref = o["ss"]
        sum_ref[...] = jnp.zeros_like(sum_ref)

        def body(rows):
            da = chips[own_half, rows].astype(F32) + far_chip[rows].astype(F32)
            nv, rv = norm_of(hid[rows].astype(F32))
            dn = da * m_row
            mean = jnp.mean(dn, axis=-1, keepdims=True)
            proj = jnp.mean(dn * nv, axis=-1, keepdims=True)
            g = jnp.where(first, i["gs0"][rows], i["gs1"][rows])
            o["hidden_grad"][rows] = (g + rv * (dn - mean - nv * proj)).astype(BF)
            dan = da * nv
            for k in range(STEP // 8):
                sum_ref[:8] += da[k * 8 : k * 8 + 8]
                sum_ref[8:] += dan[k * 8 : k * 8 + 8]

        over_rows(quarter, body)
        flush("hidden_grad")

        def summed(ref, at):
            return jnp.sum(ref[at : at + 8], axis=0, keepdims=True)

        def own(name, at):
            return jnp.where(first, summed(i[name + "0"], at), summed(i[name + "1"], at))

        four_sums[0] = jnp.concatenate(
            [
                summed(sum_ref, 0), summed(sum_ref, 8), two[...], own("sf", 0), own("sf", 8), five[...],
                own("sc", 8), own("sc", 0),
            ]
        )
        cores.start(four_sums.at[0], four_sums.at[1], core).wait_recv()
        four_sums[2] = four_sums[0] + four_sums[1]
        xs.start(four_sums.at[2], four_sums.at[3], across).wait_recv()
        o["time"][...] = four_sums[2] + four_sums[3]
        flush("time", "ss", "self_gain")
        head_rows = [
            ref[g : g + 1, h * HEAD : (h + 1) * HEAD]
            for ref in (o["self_gain"], i["cross_gain"])
            for g in range(2)
            for h in range(heads)
        ]
        head_rows = jnp.concatenate([*head_rows, jnp.zeros((16 - 4 * heads, HEAD), F32)])
        at = lax.broadcasted_iota(jnp.int32, (D, HEAD), 0)
        to = lax.broadcasted_iota(jnp.int32, (D, HEAD), 1)
        pick = (at == (to // g_cols) * r + lax.rem(to, g_cols)).astype(F32)
        spread = dot_nt(head_rows.astype(BF), pick.astype(BF))
        both = jnp.concatenate([o["time"][...], spread, jnp.zeros((HEAD - 24, D), F32)])
        side[...] = jnp.transpose(both).astype(BF)
        d = lax.axis_index("dp")

        def side_block(k):
            return side.at[pl.ds(pl.multiple_of(lax.rem(d + k, n_dp) * r, 16), r)]

        side_copies = []
        for k in range(1, n_dp):
            copy = remote(
                side_block(k), side_in.at[k - 1], side_sems.at[0, k], side_sems.at[1, k], dp=lax.rem(d + k, n_dp)
            )
            copy.start()
            side_copies.append(copy)
        f2.forward(b, local)
        fq.begin(o["tq"])
        fc.pair(a.at[0], b, local)
        fc.spread(a.at[0], o["relay3"])
        f2.total(a.at[1], result, o["s2"], stores.at[0], b, local)
        a_v, a_q = (a.at[1, :, :, pl.ds(c * V, V)] for c in range(2))
        b_v = b.at[:, :, pl.ds(0, V)]
        fv.pair(a_v, b_v, local)
        fv.spread(a_v, o["relay4"])
        fc.forward(b, local)
        fv.forward(b_v, local)
        fq.pair(a_q, b_v, local)
        fq.spread(a_q)
        fc.total(a.at[0], result, o["s3"], stores.at[0], b, local)
        fv.total(a_v, result.at[:, pl.ds(0, V)], o["s4"], stores.at[0], b_v, local)
        small = side_block(0)[...].astype(F32)
        for k in range(1, n_dp):
            side_copies[k - 1].wait()
            small = small + side_in[k - 1].astype(F32)
        o["tiny"][...] = small
        flush("tiny")
        fq.total(a_q, result.at[:, pl.ds(0, V)], o["s5"], stores.at[0], b_v, local)
        cores.settle()
        xs.settle()

    scratch = [
        pltpu.VMEM((half, wide), BF),
        pltpu.VMEM((2, half, wide), F32),
        pltpu.VMEM((2 * half, wide), F32),
        pltpu.VMEM((2 * half, wide), F32),
        pltpu.VMEM((2, half, 3 * wide), BF),
        pltpu.VMEM((2, quarter, D), BF),
        pltpu.VMEM((2, quarter, D), BF),
        pltpu.VMEM((quarter, D), F32),
        pltpu.VMEM((2, quarter, D), BF),
        pltpu.VMEM((quarter, D), BF),
        pltpu.VMEM((2, 8, half), F32),
        pltpu.VMEM((2, 3, 8, half), F32),
        pltpu.VMEM((D, 2 * half), BF),
        pltpu.VMEM((2, D, GC), BF),
        pltpu.VMEM((2, n, r, W), BF),
        pltpu.VMEM((n, r, W), BF),
        pltpu.VMEM((3, n - 1, r, W) if n == 4 else (8, HEAD), BF),
        pltpu.VMEM((2, n - 1, r, V) if n == 4 else (8, HEAD), BF),
        pltpu.VMEM((r, W), F32),
        pltpu.VMEM((4, 8, D), F32),
        pltpu.VMEM((D, HEAD), BF),
        pltpu.VMEM((n_dp - 1, r, HEAD), BF),
        pltpu.SemaphoreType.DMA((2, 4)),
        pltpu.SemaphoreType.DMA((2, 4)),
        pltpu.SemaphoreType.DMA((2, 6)),
        pltpu.SemaphoreType.DMA((4, 2, n)),
        pltpu.SemaphoreType.DMA((5, 2, n)),
        pltpu.SemaphoreType.DMA((2, n)),
        pltpu.SemaphoreType.DMA((2,)),
        pltpu.SemaphoreType.DMA((4,)),
        pltpu.SemaphoreType.DMA((2, n_dp)),
    ]
    return run_remote(kernel, outs, far_outs, blocks, far, scratch, 5, 5e10)


def rotary_tables(positions, head_dim):
    pair_count = head_dim // 2
    side_pairs = pair_count // 3
    frame_pairs = pair_count - 2 * side_pairs
    pair_index = jnp.arange(pair_count)
    frame_mask = pair_index < frame_pairs
    height_mask = (pair_index >= frame_pairs) & (pair_index < frame_pairs + side_pairs)
    within = jnp.where(
        frame_mask,
        pair_index,
        jnp.where(height_mask, pair_index - frame_pairs, pair_index - frame_pairs - side_pairs),
    )
    extent = jnp.where(frame_mask, frame_pairs, side_pairs)
    frequency = jnp.power(10000.0, -within.astype(F32) / extent.astype(F32))
    coords = positions.astype(F32)
    coordinate = jnp.where(
        frame_mask[None, :],
        coords[0][:, None],
        jnp.where(height_mask[None, :], coords[1][:, None], coords[2][:, None]),
    )
    angles = jnp.repeat(coordinate * frequency[None, :], 2, axis=1)
    parity = jnp.arange(head_dim) % 2
    sign_pattern = jnp.where(parity == 0, -1.0, 1.0)
    return (jnp.cos(angles), jnp.sin(angles) * sign_pattern)


def solution(mesh):
    n_dp = mesh.shape["dp"]
    n_major = n_dp // 2
    pair_perm = [(i, i ^ 1) for i in range(n_dp)]
    ring_perm = {
        t: [((((i // 2) + t) % n_major) * 2 + i % 2, i) for i in range(n_dp)]
        for t in range(1, n_major)
    }
    back_perm = {t: [(b, a) for a, b in ring_perm[t]] for t in ring_perm}
    core_perm = [(i, i ^ 1) for i in range(4)]
    x_perm = [(i, i ^ 2) for i in range(4)]

    def core_swap(v):
        return lax.ppermute(v, "tensor", core_perm)

    def x_swap(v):
        return lax.ppermute(v, "tensor", x_perm)

    def gather_dp(block):
        pieces = []
        for t in range(n_major):
            piece = block if t == 0 else lax.ppermute(block, "dp", ring_perm[t])
            pieces += [piece, lax.ppermute(piece, "dp", pair_perm)]
        return pieces

    def scatter_dp(theirs, mine):
        major = lax.axis_index("dp") // 2
        got = lax.ppermute(theirs, "dp", pair_perm)

        def block(t):
            at = (major + t) % n_major
            a = lax.dynamic_slice_in_dim(mine, at, 1, axis=0)[0].astype(F32)
            return a + lax.dynamic_slice_in_dim(got, at, 1, axis=0)[0].astype(F32)

        arrived = [
            lax.ppermute(block(t).astype(BF), "dp", back_perm[t]) for t in range(1, n_major)
        ]
        total = block(0)
        for piece in arrived:
            total = total + piece.astype(F32)
        return total

    def join(mine, theirs):
        return (mine + core_swap(theirs).astype(F32)).astype(BF)

    def own_half(pair):
        first = lax.axis_index("tensor") < 2
        return jnp.where(first, pair[0], pair[1])

    def other_half(pair):
        first = lax.axis_index("tensor") < 2
        return jnp.where(first, pair[1], pair[0])

    def two_halves(own):
        got = x_swap(own)
        first = lax.axis_index("tensor") < 2
        return jnp.where(first, own, got), jnp.where(first, got, own)

    def sum_all(v):
        v = v + core_swap(v)
        return v + x_swap(v)

    def sum_vectors(v):
        h = v.shape[-1] // 2
        other = core_swap(v)
        v = v + jnp.concatenate([other[..., h:], other[..., :h]], -1)
        return v + x_swap(v)

    def sum_halves(pair):
        both = sum_vectors(jnp.stack(pair))
        return both[0], both[1]

    def quarters(values, axis):
        core = lax.axis_index("tensor") % 2
        step = values.shape[axis] // 4
        return jnp.concatenate(
            [
                lax.dynamic_slice_in_dim(values, at * step, step, axis)
                for at in (core, 1 - core, 2 + core, 3 - core)
            ],
            axis,
        )

    def on_device(
        hidden_in, context, time_emb, text_lengths, positions, modulation,
        self_query, self_key, self_value, self_output, self_query_gain, self_key_gain,
        cross_query, cross_key, cross_value, cross_output, cross_query_gain, cross_key_gain,
        norm_weight, norm_bias, ffn_up, ffn_down, out_cotangent,
    ):
        heads = self_query_gain.shape[0]
        half = positions.shape[1] // 2
        wide = heads * HEAD
        r_dp = self_query.shape[0]
        hid = ffn_up.shape[1]
        spare = -hid % HC

        texts = context.shape[1]
        quarter = half // 2
        g_cols = self_query_gain.shape[1]
        gains = [self_query_gain, self_key_gain, cross_query_gain, cross_key_gain]
        flat = jnp.concatenate([modulation, norm_weight[None], norm_bias[None]])
        side = jnp.pad(jnp.concatenate(gains), ((0, 0), (0, r_dp - g_cols)))
        small = jnp.concatenate([flat, side])
        small = jnp.pad(small, ((0, HEAD - small.shape[0]), (0, 0))).T.astype(BF)
        own_self = jnp.concatenate([self_query, self_key, self_value, self_output.T], axis=1).astype(BF)
        own_cross = jnp.concatenate([cross_query, cross_key, cross_value, cross_output.T], axis=1).astype(BF)
        padded = [jnp.pad(w, ((0, 0), (0, spare))) for w in (ffn_up.astype(BF), ffn_down.T.astype(BF))]
        hid_low = hid + spare
        own_ffn = [
            jnp.concatenate([w[:, j * HC : (j + 1) * HC] for w in padded], axis=1) for j in range(hid_low // HC)
        ]
        tables = rotary_tables(quarters(positions, 1), HEAD)
        text_bias = jnp.where(quarters(jnp.arange(4 * texts), 0) < text_lengths[0], 0.0, -1e30)
        text_bias = text_bias.astype(F32)[:, None]

        st = self_forward(
            hidden_in, context[0], out_cotangent, time_emb[0], tables, small,
            own_self, own_cross, own_ffn[0], n_dp, heads,
        )
        st |= cross_forward(st, out_cotangent, text_bias, own_ffn[1], own_ffn[2], n_dp, heads)
        d = lax.axis_index("dp")
        cosine, sine = ((t[:half], t[half:]) for t in tables)
        s0, s1, s2, s3, s4, s5, norm_gain, norm_shift = (st["shifts"][i : i + 1] for i in range(8))
        sq_gain, sk_gain, cq_gain, ck_gain = (
            st["gains"][i * heads : (i + 1) * heads].reshape(1, wide) for i in range(4)
        )
        ones = jnp.ones((1, D), F32)
        w_self, w_cross = [st["w_self"]], [st["w_cross"]]
        w_ffn = [st["f0"], st["f1"], st["f2"]]
        at_o, at_cq, at_ck, at_co = 3 * wide, 0, wide, 3 * wide

        def both(name):
            return [st[name + "0"], st[name + "1"]]

        def four(name):
            return [[st[name + "0"], st[name + "1"]], [st[name + "2"], st[name + "3"]]]

        first = lax.axis_index("tensor") < 2
        g = [jnp.where(first, out_cotangent, st["g_got"]), jnp.where(first, st["g_got"], out_cotangent)]
        ctx = [st[f"c{i}"] for i in range(4)]
        self_rows, cross_rows, ffn_rows = four("x"), four("y"), four("z")
        qk, v, stat, q, k, attn, lse = (both(name) for name in ("qk", "v", "stat", "q", "k", "attn", "lse"))
        self_chip, self_far, after_self = both("chip"), both("far"), both("after")
        ck_raw, cv, ck_stat, ck = st["ck_raw"], st["cv"], st["ck_stat"], st["ck"]
        cq_raw, cq_stat, cq, cattn, clse = (both(name) for name in ("cq_raw", "cq_stat", "cq", "cattn", "clse"))
        after_cross = both("after_c")

        def with_peer(rows):
            return [rows, core_swap(rows)]

        st |= feed_forward(st, out_cotangent, n_dp)
        g_c, sums_f = both("gc"), both("sf")

        st |= cross_backward(st, text_bias, n_dp, heads)
        g_own = own_half(both("gs"))
        self_branch = own_half(self_chip).astype(F32) + own_half(self_far).astype(F32)
        ffn_branch = st["branch"]
        sums_two = jnp.sum(g_own * self_branch, 0, keepdims=True)
        sums_five = jnp.sum(out_cotangent.astype(F32) * ffn_branch, 0, keepdims=True)
        st |= self_backward(st, hidden_in, tables, sums_two, sums_five, n_dp, heads)
        hid_grads = [st["s0"], st["s1"], st["s2"]]
        up_grad = jnp.concatenate([a[:, :HC] for a in hid_grads], axis=1)
        down_grad = jnp.concatenate([a[:, HC:] for a in hid_grads], axis=1)
        cross_grad = st["s3"]
        qkv_grad = [st["s5"][:, :wide], st["s5"][:, wide:], st["s4"][:, :wide]]
        oT_grad = st["s4"][:, wide:]
        hidden_grad, context_grad = st["hidden_grad"], st["ctx_grad"]

        block_out = (own_half(after_cross) + ffn_branch * s5).astype(BF)

        time_grad = st["time"][:6]
        eight = st["tiny"][:, :8].T
        gains_out = st["tiny"][:g_cols, 8 : 8 + 4 * heads].T.reshape(4, heads, g_cols)

        return (
            block_out,
            hidden_grad,
            context_grad[None],
            time_grad[None],
            eight[:6],
            qkv_grad[0],
            qkv_grad[1],
            qkv_grad[2],
            oT_grad.T,
            gains_out[0],
            gains_out[1],
            cross_grad[:, :wide],
            cross_grad[:, wide : 2 * wide],
            cross_grad[:, 2 * wide : 3 * wide],
            cross_grad[:, 3 * wide :].T,
            gains_out[2],
            gains_out[3],
            eight[6],
            eight[7],
            up_grad[:, :hid],
            down_grad[:, :hid].T,
        )

    rows = P(("dp", "tensor"), None)
    col = P("dp", "tensor")
    row = P("tensor", "dp")
    text = P("dp", "tensor", None)
    time = P("dp", None, None)
    one = P("dp")
    ins = (
        rows, text, time, one, P(None, "dp"), P(None, "dp"),
        col, col, col, row, row, row,
        col, col, col, row, row, row,
        one, one, col, row, rows,
    )
    outs = (
        rows, rows, text, time, P(None, "dp"),
        col, col, col, row, row, row,
        col, col, col, row, row, row,
        one, one, col, row,
    )
    return jax.shard_map(on_device, mesh=mesh, in_specs=ins, out_specs=outs, check_vma=False)
```
